32 devices in a mesh: seq: 8 (over z, y), ch: 4 (over x, core).
Axes of the slice: x: 2, y: 2, z: 4, core: 2. Of those that a mesh axis runs over, the one named last changes fastest.
Arguments:
- inputs: bfloat16 [1024, 1024], P('ch', 'seq'), may hold values from -6 to 6
- out_grad: bfloat16 [1024, 1024], P('ch', 'seq'), may hold values from -6 to 6
- readout: float32 [2, 1024, 64], P(None, 'ch'), may hold values from -4 to 4
- log_step: float32 [1024], P('ch'), may hold values from -10.5 to -3
- decay_log: float32 [64], replicated, may hold values from -1.4 to 0
- rotation: float32 [64], replicated, may hold values from 0 to 200
Outputs:
- kernel_grad: float32 [1024, 1024], P('ch', 'seq')
- readout_grad: float32 [2, 1024, 64], P(None, 'ch')
- step_grad: float32 [1024], P('ch')
- state_grad: float32 [2, 64], replicated
The draws below stay inside these ranges and needn't reach their ends.
All inputs are finite; a program needn't handle non-finite values.
Results may differ from the reference program's by a relative error of at most 0.0005.
Values may be sent and summed in bfloat16 or wider, within the bound.
No kernel may reach another device: no remote copies, remote signals or barrier semaphores. Data moves between devices by JAX's collectives and lax.ppermute only.
A program may use at most 64 MiB of HBM per device.

```python
import math
import jax
import jax.numpy as jnp
from jax import lax

CHANNELS = 1024
STATES = 64
TOK_DEV = 128
SEQ = 1024
N_SEQ = 8


def steps_of(rng, dims, cuts, low, top_value):
    level, own = 1.0, jax.random.fold_in(rng, 6)
    for dim, parts in cuts:
        draws = jnp.exp(jax.random.uniform(jax.random.fold_in(own, dim), (parts,), jnp.float32, low / len(cuts), top_value / len(cuts)))
        level = level * jnp.repeat(draws, dims[dim] // parts).reshape([-1 if axis == dim else 1 for axis in range(len(dims))])
    return level


def scatter_about(rng, extent, scale, most, split=(), held_as=jnp.bfloat16):
    gain = steps_of(rng, extent, split, -0.22, 0.18) if split else 1.0
    result = jax.random.normal(rng, extent, jnp.float32) * scale * gain
    return jnp.minimum(jnp.maximum(result, -most), most).astype(held_as)


def setup_inputs(seed: int = 0) -> dict:
    keys = jax.random.split(jax.random.key(seed), 7)
    return {
        "inputs": scatter_about(keys[0], (CHANNELS, SEQ), 1.0, 6.0, ((0, 4), (1, 8))),
        "out_grad": scatter_about(keys[1], (CHANNELS, SEQ), 1.0, 6.0, ((0, 4), (1, 8))),
        "readout": scatter_about(keys[2], (2, CHANNELS, STATES), 1.0, 4.0, ((1, 4),), jnp.float32),
        "log_step": jnp.clip(-10.5 + 7.5 * jax.random.uniform(keys[3], (CHANNELS,), jnp.float32) ** steps_of(keys[3], (CHANNELS,), ((0, 4),), -0.2, 0.2), -10.5, -3.0),
        "decay_log": jnp.clip(jax.random.uniform(keys[4], (STATES,), jnp.float32, -1.4, 0.0), -1.4, 0.0),
        "rotation": jnp.clip(jax.random.uniform(keys[5], (STATES,), jnp.float32, 0.0, 200.0), 0.0, 200.0),
    }


precise = lax.Precision.HIGHEST

def discretize(readout, log_step, decay_log, rotation):
    step_size = jnp.exp(log_step)[:, None]
    pole_real = -jnp.exp(decay_log)[None, :]
    pole_imag = rotation[None, :]
    rate_real = step_size * pole_real
    rate_imag = step_size * pole_imag
    lift_real = jnp.expm1(rate_real) * jnp.cos(rate_imag) - 2.0 * jnp.sin(0.5 * rate_imag) ** 2
    lift_imag = jnp.exp(rate_real) * jnp.sin(rate_imag)
    pole_norm = pole_real * pole_real + pole_imag * pole_imag
    ratio_real = (lift_real * pole_real + lift_imag * pole_imag) / pole_norm
    ratio_imag = (lift_imag * pole_real - lift_real * pole_imag) / pole_norm
    coef_real = readout[0] * ratio_real - readout[1] * ratio_imag
    coef_imag = readout[0] * ratio_imag + readout[1] * ratio_real
    return (coef_real, coef_imag, rate_real, rate_imag)

def parameter_grads(primal, backward, totals):
    coef_real, coef_imag = (primal[0], primal[1])
    cotangents = (2.0 * totals[0], -2.0 * totals[1], 2.0 * (coef_real * totals[2] - coef_imag * totals[3]), -2.0 * (coef_real * totals[3] + coef_imag * totals[2]))
    return backward(cotangents)

def shifted_totals(raw_sums, rate_real, rate_imag, block_start, norm_scale):
    decays = jnp.exp(rate_real * block_start)
    phases = rate_imag * block_start
    base_real = decays * jnp.cos(phases)
    base_imag = decays * jnp.sin(phases)
    near_real = block_start * raw_sums[0] + raw_sums[2]
    near_imag = block_start * raw_sums[1] + raw_sums[3]
    return jnp.stack([norm_scale * (base_real * raw_sums[0] - base_imag * raw_sums[1]), norm_scale * (base_real * raw_sums[1] + base_imag * raw_sums[0]), norm_scale * (base_real * near_real - base_imag * near_imag), norm_scale * (base_real * near_imag + base_imag * near_real)])

def reference(inputs, out_grad, readout, log_step, decay_log, rotation):
    norm_scale = 1.0 / math.sqrt(SEQ)
    group_size = math.gcd(CHANNELS, 64)
    group_count = CHANNELS // group_size

    def correlate(pieces):
        padded_in = jnp.pad(pieces[0].astype(jnp.float32), ((0, 0), (0, SEQ)))
        padded_out = jnp.pad(pieces[1].astype(jnp.float32), ((0, 0), (0, SEQ)))
        spectrum = jnp.fft.fft(padded_out, axis=-1) * jnp.conj(jnp.fft.fft(padded_in, axis=-1))
        lagged = jnp.real(jnp.fft.ifft(spectrum, axis=-1))[:, :SEQ]
        return (lagged * norm_scale).astype(jnp.float32)
    kernel_grad = lax.map(correlate, (inputs.reshape(group_count, group_size, SEQ), out_grad.reshape(group_count, group_size, SEQ))).reshape(CHANNELS, SEQ)
    primal, backward = jax.vjp(discretize, readout, log_step, decay_log, rotation)
    offsets = jnp.arange(TOK_DEV, dtype=jnp.int32).astype(jnp.float32)
    starts = (jnp.arange(N_SEQ, dtype=jnp.int32) * TOK_DEV).astype(jnp.float32)

    def block_totals(pieces):
        lag_rows, real_rate, imag_rate = pieces
        blocks = lag_rows.reshape(group_size, N_SEQ, TOK_DEV)
        decays = jnp.exp(real_rate[:, :, None] * offsets)
        phases = imag_rate[:, :, None] * offsets
        power_real = decays * jnp.cos(phases)
        power_imag = decays * jnp.sin(phases)
        weighted = blocks * offsets
        raw_sums = jnp.stack([jnp.einsum('gbj,gnj->gnb', blocks, power_real, precision=precise), jnp.einsum('gbj,gnj->gnb', blocks, power_imag, precision=precise), jnp.einsum('gbj,gnj->gnb', weighted, power_real, precision=precise), jnp.einsum('gbj,gnj->gnb', weighted, power_imag, precision=precise)])
        totals = shifted_totals(raw_sums, real_rate[:, :, None], imag_rate[:, :, None], starts, norm_scale)
        return lax.optimization_barrier(jnp.sum(totals, axis=-1))
    totals = lax.map(block_totals, (kernel_grad.reshape(group_count, group_size, SEQ), primal[2].reshape(group_count, group_size, STATES), primal[3].reshape(group_count, group_size, STATES)))
    totals = jnp.transpose(totals, (1, 0, 2, 3)).reshape(4, CHANNELS, STATES)
    readout_grad, step_grad, decay_grad, rotation_grad = parameter_grads(primal, backward, totals)
    return (kernel_grad, readout_grad, step_grad, jnp.stack([decay_grad, rotation_grad]))
```

```python
import functools
import math

import jax
import jax.numpy as jnp
import numpy as np
from jax import lax
from jax.experimental import pallas as pl
from jax.experimental.pallas import tpu as pltpu
from jax.sharding import PartitionSpec as P

precise = lax.Precision.HIGHEST
two_pi = 2.0 * math.pi
LANES = 128
SUBLANES = 8


def angle_table(left_index, right_index, modulus, orient):
    product = left_index[:, None] * right_index[None, :] % modulus
    return orient * two_pi * product.astype(jnp.float32) / modulus


def rotate(real_part, imag_part, angles):
    cosine_table = jnp.cos(angles)
    sine_table = jnp.sin(angles)
    return (
        real_part * cosine_table - imag_part * sine_table,
        real_part * sine_table + imag_part * cosine_table,
    )


def last_transform(real_part, imag_part, orient):
    length = real_part.shape[-1]
    counter = jnp.arange(length, dtype=jnp.int32)
    angles = angle_table(counter, counter, length, orient)
    cosine_table = jnp.cos(angles)
    sine_table = jnp.sin(angles)
    dot = functools.partial(jnp.dot, precision=precise, preferred_element_type=jnp.float32)
    return (
        dot(real_part, cosine_table) - dot(imag_part, sine_table),
        dot(imag_part, cosine_table) + dot(real_part, sine_table),
    )


def discretize(readout, log_step, decay_log, rotation):
    step_size = jnp.exp(log_step)[:, None]
    pole_real = -jnp.exp(decay_log)[None, :]
    pole_imag = rotation[None, :]
    rate_real = step_size * pole_real
    rate_imag = step_size * pole_imag
    lift_real = jnp.expm1(rate_real) * jnp.cos(rate_imag) - 2.0 * jnp.sin(0.5 * rate_imag) ** 2
    lift_imag = jnp.exp(rate_real) * jnp.sin(rate_imag)
    pole_norm = pole_real * pole_real + pole_imag * pole_imag
    ratio_real = (lift_real * pole_real + lift_imag * pole_imag) / pole_norm
    ratio_imag = (lift_imag * pole_real - lift_real * pole_imag) / pole_norm
    coef_real = readout[0] * ratio_real - readout[1] * ratio_imag
    coef_imag = readout[0] * ratio_imag + readout[1] * ratio_real
    return (coef_real, coef_imag, rate_real, rate_imag)


def parameter_grads(primal, backward, totals):
    coef_real, coef_imag = (primal[0], primal[1])
    cotangents = (
        2.0 * totals[0],
        -2.0 * totals[1],
        2.0 * (coef_real * totals[2] - coef_imag * totals[3]),
        -2.0 * (coef_real * totals[3] + coef_imag * totals[2]),
    )
    return backward(cotangents)


def shifted_totals(raw_sums, rate_real, rate_imag, block_start, norm_scale):
    decays = jnp.exp(rate_real * block_start)
    phases = rate_imag * block_start
    base_real = decays * jnp.cos(phases)
    base_imag = decays * jnp.sin(phases)
    near_real = block_start * raw_sums[0] + raw_sums[2]
    near_imag = block_start * raw_sums[1] + raw_sums[3]
    return jnp.stack(
        [
            norm_scale * (base_real * raw_sums[0] - base_imag * raw_sums[1]),
            norm_scale * (base_real * raw_sums[1] + base_imag * raw_sums[0]),
            norm_scale * (base_real * near_real - base_imag * near_imag),
            norm_scale * (base_real * near_imag + base_imag * near_real),
        ]
    )


def whole_channel_totals(lag_rows, rate_real, rate_imag, norm_scale):
    owners, length = (lag_rows.shape[1], lag_rows.shape[2])
    offsets = jnp.arange(length, dtype=jnp.int32).astype(jnp.float32)
    decays = jnp.exp(rate_real[:, :, None] * offsets)
    phases = rate_imag[:, :, None] * offsets
    power_real = decays * jnp.cos(phases)
    power_imag = decays * jnp.sin(phases)
    weighted = lag_rows * offsets
    raw_sums = jnp.stack(
        [
            jnp.einsum("cbj,cnj->cnb", lag_rows, power_real, precision=precise),
            jnp.einsum("cbj,cnj->cnb", lag_rows, power_imag, precision=precise),
            jnp.einsum("cbj,cnj->cnb", weighted, power_real, precision=precise),
            jnp.einsum("cbj,cnj->cnb", weighted, power_imag, precision=precise),
        ]
    )
    starts = (jnp.arange(owners, dtype=jnp.int32) * length).astype(jnp.float32)
    totals = shifted_totals(
        raw_sums, rate_real[:, :, None], rate_imag[:, :, None], starts, norm_scale
    )
    return jnp.sum(totals, axis=-1)


def general_lags(whole, norm_scale):
    part_count, owners, length = whole.shape[1:]
    freq_width = 2 * owners
    modulus = freq_width * length
    row_index = jnp.arange(owners, dtype=jnp.int32)
    outer_index = jnp.arange(freq_width, dtype=jnp.int32)
    inner_index = jnp.arange(length, dtype=jnp.int32)
    first = angle_table(row_index, outer_index, freq_width, -1.0)
    spec_real = jnp.einsum("scba,bk->scka", whole, jnp.cos(first), precision=precise)
    spec_imag = jnp.einsum("scba,bk->scka", whole, jnp.sin(first), precision=precise)
    spec_real, spec_imag = rotate(
        spec_real, spec_imag, angle_table(outer_index, inner_index, modulus, -1.0)
    )
    freq_real, freq_imag = last_transform(spec_real, spec_imag, -1.0)
    prod_real = freq_real[1] * freq_real[0] + freq_imag[1] * freq_imag[0]
    prod_imag = freq_imag[1] * freq_real[0] - freq_real[1] * freq_imag[0]
    back_real, back_imag = last_transform(prod_real, prod_imag, 1.0)
    back_real, back_imag = rotate(
        back_real, back_imag, angle_table(outer_index, inner_index, modulus, 1.0)
    )
    final = angle_table(outer_index, row_index, freq_width, 1.0)
    lag_rows = jnp.einsum("cka,kb->cba", back_real, jnp.cos(final), precision=precise) - jnp.einsum(
        "cka,kb->cba", back_imag, jnp.sin(final), precision=precise
    )
    return lag_rows * (norm_scale / modulus)


def general_device(inputs, out_grad, readout, log_step, decay_log, rotation):
    owners = lax.axis_size("seq")
    channels, length = inputs.shape
    states = decay_log.shape[0]
    part_count = channels // owners
    norm_scale = 1.0 / math.sqrt(owners * length)
    pieces = jnp.concatenate(
        [a.reshape(owners, part_count, length) for a in (inputs, out_grad)], axis=1
    )
    pieces = lax.all_to_all(pieces, "seq", split_axis=0, concat_axis=0, tiled=True)
    whole = pieces.astype(jnp.float32).reshape(owners, 2, part_count, length)
    lag_rows = general_lags(whole.transpose(1, 2, 0, 3), norm_scale)
    first_channel = lax.axis_index("seq") * part_count
    own_readout = lax.dynamic_slice_in_dim(readout, first_channel, part_count, 1)
    own_step = lax.dynamic_slice_in_dim(log_step, first_channel, part_count, 0)
    primal, backward = jax.vjp(discretize, own_readout, own_step, decay_log, rotation)
    totals = whole_channel_totals(lag_rows, primal[2], primal[3], norm_scale)
    readout_part, step_part, decay_part, rotation_part = parameter_grads(primal, backward, totals)
    shared = jnp.concatenate(
        [readout_part.reshape(-1), step_part, decay_part, rotation_part]
    )
    sent = jnp.concatenate(
        [
            lag_rows.transpose(1, 0, 2).reshape(owners, -1),
            jnp.broadcast_to(shared, (owners, shared.shape[0])),
        ],
        axis=1,
    )
    got = lax.all_to_all(sent, "seq", split_axis=0, concat_axis=0, tiled=True)
    cuts = np.cumsum([part_count * length, 2 * part_count * states, part_count])
    lags, readouts, steps, state = jnp.split(got, cuts, axis=1)
    readouts = readouts.reshape(owners, 2, part_count, states).transpose(1, 0, 2, 3)
    return (
        lags.reshape(channels, length),
        readouts.reshape(2, channels, states),
        steps.reshape(channels),
        lax.psum(jnp.sum(state, axis=0), "ch").reshape(2, states),
    )


def split_halves(value):
    high = value.astype(jnp.bfloat16)
    return high, (value - high.astype(jnp.float32)).astype(jnp.bfloat16)


def cos_sin(angle):
    turns = jnp.floor(angle * (2.0 / math.pi) + 0.5)
    rest = angle - turns * 1.5703125
    rest = rest - turns * 4.837512969970703125e-4
    rest = rest - turns * 7.54978995489188216e-8
    quarter = turns.astype(jnp.int32)
    square = rest * rest
    sine = rest + rest * square * (
        -1.6666654611e-1 + square * (8.3321608736e-3 - square * 1.9515295891e-4)
    )
    cosine = (
        1.0
        - 0.5 * square
        + square
        * square
        * (
            4.166664568298827e-2
            + square * (-1.388731625493765e-3 + square * 2.443315711809948e-5)
        )
    )
    odd = (quarter & 1) == 1
    out_cos = jnp.where(odd, sine, cosine)
    out_sin = jnp.where(odd, cosine, sine)
    out_cos = jnp.where(((quarter + 1) & 2) == 2, -out_cos, out_cos)
    out_sin = jnp.where((quarter & 2) == 2, -out_sin, out_sin)
    return out_cos, out_sin


def grow(value):
    series = 1.0
    for term in range(9, 1, -1):
        series = 1.0 + series * value * (1.0 / term)
    return jnp.where(jnp.abs(value) < 0.35, series * value, jnp.exp(value) - 1.0)


def power(rate_real, rate_imag, offset):
    size = jnp.exp(rate_real * offset)
    cosine, sine = cos_sin(rate_imag * offset)
    return size * cosine, size * sine


def times(left, right):
    return (
        left[0] * right[0] - left[1] * right[1],
        left[0] * right[1] + left[1] * right[0],
    )


RATE, RATIO, COEF, READ, LIFTED, POLE, INVERSE, STEP = range(8)


def table_kernel(owners, length, readout, log_step, decay_log, rotation, powers, bases, params):
    pairs = log_step.shape[0]
    step = jnp.exp(log_step[...])
    pole = (jnp.broadcast_to(-jnp.exp(decay_log[...]), step.shape), jnp.broadcast_to(rotation[...], step.shape))
    rate = (step * pole[0], step * pole[1])
    size = jnp.exp(rate[0])
    cosine, sine = cos_sin(rate[1])
    half = cos_sin(0.5 * rate[1])[1]
    lift = (grow(rate[0]) * cosine - 2.0 * half * half, size * sine)
    norm = 1.0 / (pole[0] * pole[0] + pole[1] * pole[1])
    inverse = (pole[0] * norm, -pole[1] * norm)
    ratio = times(lift, inverse)
    read = (readout[0], readout[1])
    lifted = times((size * cosine, size * sine), inverse)
    zero = jnp.zeros_like(step)
    for place, value in (
        (RATE, rate),
        (RATIO, ratio),
        (COEF, times(read, ratio)),
        (READ, read),
        (LIFTED, lifted),
        (POLE, pole),
        (INVERSE, inverse),
        (STEP, (step, zero)),
    ):
        params[2 * place] = value[0]
        params[2 * place + 1] = value[1]
    row = lax.broadcasted_iota(jnp.int32, (SUBLANES, LANES), 0).astype(jnp.float32)
    doublings = []
    size = SUBLANES
    while size < length:
        doublings.append(size)
        size *= 2

    @pl.loop(0, pairs)
    def _(pair):
        rate_real = params[2 * RATE, pl.ds(pair, 1), :]
        rate_imag = params[2 * RATE + 1, pl.ds(pair, 1), :]
        steps = [power(rate_real, rate_imag, float(size)) for size in doublings]
        table = [power(rate_real, rate_imag, row)]
        for shift in steps:
            table += [times(block, shift) for block in table]
        for place in range(0, len(table), 2):
            spot = place * SUBLANES
            for side in range(2):
                value = jnp.concatenate([table[place][side], table[place + 1][side]], axis=0)
                high, low = split_halves(value)
                lanes = slice(side * LANES, (side + 1) * LANES)
                powers[pair, spot : spot + 2 * SUBLANES, lanes] = high
                powers[pair, length + spot : length + spot + 2 * SUBLANES, lanes] = low
        for spot in range(0, owners, SUBLANES):
            real, imag = power(rate_real, rate_imag, (row + spot) * float(length))
            bases[pair, spot : spot + SUBLANES, 0:LANES] = real
            bases[pair, spot : spot + SUBLANES, LANES : 2 * LANES] = imag


def weighted_sum(terms):
    total = None
    for weight, value in terms:
        if abs(weight) < 1e-12:
            continue
        if abs(abs(weight) - 1.0) < 1e-12:
            term = value if weight > 0 else -value
        else:
            term = value * weight
        total = term if total is None else total + term
    return total


def turn(count, width):
    angle = two_pi * (count % width) / width
    return math.cos(angle), math.sin(angle)


def precise_dot(value, matrix):
    high, low = split_halves(value)
    dot = functools.partial(jnp.dot, preferred_element_type=jnp.float32)
    return dot(high, matrix[0]) + dot(low, matrix[0]) + dot(high, matrix[1])


def main_kernel(
    part_count, norm_scale, got, matrix, twiddle, powers, bases, params, sent, lags, sums
):
    owners, rows, length = got.shape
    width = 2 * owners
    pairs = part_count // 2

    blocks = [got[s].astype(jnp.float32) for s in range(owners)]
    spectra = []
    for k in range(owners + 1):
        real = weighted_sum([(turn(k * s, width)[0], blocks[s]) for s in range(owners)])
        imag = weighted_sum([(-turn(k * s, width)[1], blocks[s]) for s in range(owners)])
        if imag is None:
            imag = jnp.zeros_like(real)
        if k:
            real, imag = times((real, imag), (twiddle[k, 0:1], twiddle[k, 1:2]))
        spectra.append(jnp.concatenate([real, imag], axis=1))
    freq = precise_dot(jnp.concatenate(spectra, axis=0), matrix)

    products = []
    for k in range(owners + 1):
        at_in = freq[k * rows : k * rows + part_count]
        at_out = freq[k * rows + part_count : (k + 1) * rows]
        ur, ui = at_in[:, :length], at_in[:, length:]
        gr, gi = at_out[:, :length], at_out[:, length:]
        products.append(jnp.concatenate([gr * ur + gi * ui, gr * ui - gi * ur], axis=1))
    back = precise_dot(jnp.concatenate(products, axis=0), matrix)

    turned = []
    for k in range(owners + 1):
        value = back[k * part_count : (k + 1) * part_count]
        value = (value[:, :length], value[:, length:])
        if k:
            value = times(value, (twiddle[k, 0:1], twiddle[k, 1:2]))
        turned.append(value)
    scale = norm_scale / (width * length)
    for b in range(owners):
        terms = []
        for k in range(owners + 1):
            weight = scale if k in (0, owners) else 2.0 * scale
            cosine, sine = turn(k * b, width)
            terms += [(weight * cosine, turned[k][0]), (weight * sine, turned[k][1])]
        block = weighted_sum(terms)
        sent[b, 0:part_count] = block
        lags[b * part_count : (b + 1) * part_count] = block

    offset = lax.broadcasted_iota(jnp.int32, (owners, length), 1).astype(jnp.float32)
    start = lax.broadcasted_iota(jnp.int32, (owners, LANES), 0).astype(jnp.float32) * float(length)
    first = lax.broadcasted_iota(jnp.int32, (owners, LANES), 1) < LANES // 2
    for p in range(pairs):
        one = lags[pl.ds(2 * p, owners, stride=part_count), :]
        two = lags[pl.ds(2 * p + 1, owners, stride=part_count), :]
        high, low = split_halves(
            jnp.concatenate([one, two, one * offset, two * offset], axis=0)
        )
        left = jnp.concatenate(
            [
                jnp.concatenate([high, high], axis=1),
                jnp.concatenate([low, jnp.zeros_like(low)], axis=1),
            ],
            axis=0,
        )
        raw = jnp.dot(left, powers[p], preferred_element_type=jnp.float32)
        raw = raw[: 4 * owners] + raw[4 * owners :]

        def pick(place, side):
            lanes = slice(side * LANES, (side + 1) * LANES)
            top = raw[2 * place * owners : (2 * place + 1) * owners, lanes]
            bottom = raw[(2 * place + 1) * owners : (2 * place + 2) * owners, lanes]
            return jnp.where(first, top, bottom)

        plain = (pick(0, 0), pick(0, 1))
        near = (start * plain[0] + pick(1, 0), start * plain[1] + pick(1, 1))
        base = (bases[p, :, 0:LANES], bases[p, :, LANES : 2 * LANES])
        for place, value in enumerate(times(base, plain) + times(base, near)):
            sums[place, p : p + 1] = jnp.sum(value, axis=0, keepdims=True)

    def param(place):
        return params[2 * place], params[2 * place + 1]

    total = (sums[0] * (2.0 * norm_scale), sums[1] * (2.0 * norm_scale))
    lag_total = (sums[2] * (2.0 * norm_scale), sums[3] * (2.0 * norm_scale))
    on_read = times(total, param(RATIO))
    on_rate = times(param(COEF), lag_total)
    through = times(times(total, param(READ)), param(LIFTED))
    on_rate = (on_rate[0] + through[0], on_rate[1] + through[1])
    direct = times(times(total, param(COEF)), param(INVERSE))
    step = params[2 * STEP]
    on_pole = (step * on_rate[0] - direct[0], step * on_rate[1] - direct[1])
    on_step = times(on_rate, param(RATE))[0]
    on_decay = on_pole[0] * params[2 * POLE]
    on_rotation = -on_pole[1]

    lane = lax.broadcasted_iota(jnp.int32, (pairs, LANES), 1)
    pair = lax.broadcasted_iota(jnp.int32, (pairs, LANES), 0)
    even = jnp.sum(jnp.where(lane < LANES // 2, on_step, 0.0), axis=1, keepdims=True)
    odd = jnp.sum(jnp.where(lane < LANES // 2, 0.0, on_step), axis=1, keepdims=True)
    spread = jnp.where(lane == 2 * pair, even, jnp.where(lane == 2 * pair + 1, odd, 0.0))
    step_row = jnp.sum(spread, axis=0, keepdims=True)
    decay_row = jnp.sum(on_decay, axis=0, keepdims=True)
    rotation_row = jnp.sum(on_rotation, axis=0, keepdims=True)
    decay_row = decay_row + pltpu.roll(decay_row, LANES // 2, 1)
    rotation_row = rotation_row + pltpu.roll(rotation_row, LANES // 2, 1)
    state_row = jnp.where(lane[0:1] < LANES // 2, decay_row, rotation_row)
    place = lax.broadcasted_iota(jnp.int32, (SUBLANES, LANES), 0)
    tail = jnp.where(place == 0, step_row, jnp.where(place == 1, state_row, 0.0))
    for b in range(owners):
        sent[b, part_count : part_count + pairs] = on_read[0]
        sent[b, part_count + pairs : 2 * part_count] = -on_read[1]
        sent[b, 2 * part_count : 2 * part_count + SUBLANES] = tail


def transform_tables(owners, length):
    width = 2 * owners
    counter = np.arange(length)
    angles = two_pi * (counter[:, None] * counter[None, :] % length) / length
    cosine, sine = np.cos(angles), np.sin(angles)
    matrix = np.block([[cosine, -sine], [sine, cosine]]).astype(np.float32)
    high = matrix.astype(jnp.bfloat16)
    low = (matrix - high.astype(np.float32)).astype(jnp.bfloat16)
    outer = np.arange(owners + 1)
    angles = two_pi * (outer[:, None] * counter[None, :]) / (width * length)
    twiddle = np.stack([np.cos(angles), -np.sin(angles)], axis=1).astype(np.float32)
    return np.stack([high, low]), twiddle


def sum_over(value, axis):
    size = lax.axis_size(axis)
    if size & (size - 1):
        return lax.psum(value, axis)
    reach = 1
    while reach < size:
        value = value + lax.ppermute(value, axis, [(i, i ^ reach) for i in range(size)])
        reach *= 2
    return value


def kernel_device(inputs, out_grad, readout, log_step, decay_log, rotation):
    owners = lax.axis_size("seq")
    channels, length = inputs.shape
    states = decay_log.shape[0]
    part_count = channels // owners
    pairs = part_count // 2
    norm_scale = 1.0 / math.sqrt(owners * length)
    vmem = pl.BlockSpec(memory_space=pltpu.VMEM)
    memory = pltpu.CompilerParams(vmem_limit_bytes=32 * 1024 * 1024)

    pieces = jnp.concatenate(
        [a.reshape(owners, part_count, length) for a in (inputs, out_grad)], axis=1
    )
    got = lax.all_to_all(pieces, "seq", split_axis=0, concat_axis=0, tiled=True)

    first_channel = lax.axis_index("seq") * part_count
    own_readout = lax.dynamic_slice_in_dim(readout, first_channel, part_count, 1)
    own_step = lax.dynamic_slice_in_dim(log_step, first_channel, part_count, 0)
    powers, bases, params = pl.pallas_call(
        functools.partial(table_kernel, owners, length),
        out_shape=[
            jax.ShapeDtypeStruct((pairs, 2 * length, 2 * LANES), jnp.bfloat16),
            jax.ShapeDtypeStruct((pairs, owners, 2 * LANES), jnp.float32),
            jax.ShapeDtypeStruct((16, pairs, LANES), jnp.float32),
        ],
        in_specs=[vmem] * 4,
        out_specs=[vmem] * 3,
        compiler_params=memory,
        cost_estimate=pl.CostEstimate(
            flops=pairs * length * LANES * 8, bytes_accessed=2**21, transcendentals=2**17
        ),
    )(
        own_readout.reshape(2, pairs, LANES),
        jnp.repeat(own_step.reshape(pairs, 2), states, axis=1),
        jnp.tile(decay_log, 2)[None],
        jnp.tile(rotation, 2)[None],
    )

    matrix, twiddle = transform_tables(owners, length)
    sent_rows = 2 * part_count + SUBLANES
    sent = pl.pallas_call(
        functools.partial(main_kernel, part_count, norm_scale),
        out_shape=jax.ShapeDtypeStruct((owners, sent_rows, LANES), jnp.float32),
        in_specs=[vmem] * 6,
        out_specs=vmem,
        scratch_shapes=[
            pltpu.VMEM((owners * part_count, length), jnp.float32),
            pltpu.VMEM((4, pairs, LANES), jnp.float32),
        ],
        compiler_params=memory,
        cost_estimate=pl.CostEstimate(
            flops=2**28, bytes_accessed=2**22, transcendentals=0
        ),
    )(got, jnp.asarray(matrix), jnp.asarray(twiddle), powers, bases, params)
    back = lax.all_to_all(sent, "seq", split_axis=0, concat_axis=0, tiled=True)

    kernel_grad = back[:, :part_count].reshape(channels, length)
    readout_grad = back[:, part_count : 2 * part_count].reshape(owners, 2, pairs, LANES)
    readout_grad = readout_grad.transpose(1, 0, 2, 3).reshape(2, channels, states)
    step_grad = back[:, 2 * part_count, :part_count].reshape(channels)
    state = jnp.sum(back[:, 2 * part_count + 1], axis=0).reshape(2, states)
    return kernel_grad, readout_grad, step_grad, sum_over(state, "ch")


def kernel_fits(mesh, inputs, decay_log):
    owners = mesh.shape["seq"]
    channels = inputs.shape[0] // mesh.shape["ch"]
    part_count = channels // owners
    return (
        inputs.shape[1] == owners * LANES
        and 2 * decay_log.shape[0] == LANES
        and owners in (SUBLANES, 2 * SUBLANES)
        and part_count % (2 * SUBLANES) == 0
        and part_count <= LANES
    )


def solution(mesh):
    def whole(inputs, out_grad, readout, log_step, decay_log, rotation):
        fits = kernel_fits(mesh, inputs, decay_log)
        return jax.shard_map(
            kernel_device if fits else general_device,
            mesh=mesh,
            in_specs=(P("ch", "seq"), P("ch", "seq"), P(None, "ch", None), P("ch"), P(), P()),
            out_specs=(P("ch", "seq"), P(None, "ch", None), P("ch"), P()),
            check_vma=False,
        )(inputs, out_grad, readout, log_step, decay_log, rotation)

    return whole
```

```python
import functools
import math

import jax
import jax.numpy as jnp
import numpy as np
from jax import lax
from jax.experimental import pallas as pl
from jax.experimental.pallas import tpu as pltpu
from jax.sharding import PartitionSpec as P

precise = lax.Precision.HIGHEST
two_pi = 2.0 * math.pi
LANES = 128
SUBLANES = 8


def angle_table(left_index, right_index, modulus, orient):
    product = left_index[:, None] * right_index[None, :] % modulus
    return orient * two_pi * product.astype(jnp.float32) / modulus


def rotate(real_part, imag_part, angles):
    cosine_table = jnp.cos(angles)
    sine_table = jnp.sin(angles)
    return (
        real_part * cosine_table - imag_part * sine_table,
        real_part * sine_table + imag_part * cosine_table,
    )


def last_transform(real_part, imag_part, orient):
    length = real_part.shape[-1]
    counter = jnp.arange(length, dtype=jnp.int32)
    angles = angle_table(counter, counter, length, orient)
    cosine_table = jnp.cos(angles)
    sine_table = jnp.sin(angles)
    dot = functools.partial(jnp.dot, precision=precise, preferred_element_type=jnp.float32)
    return (
        dot(real_part, cosine_table) - dot(imag_part, sine_table),
        dot(imag_part, cosine_table) + dot(real_part, sine_table),
    )


def discretize(readout, log_step, decay_log, rotation):
    step_size = jnp.exp(log_step)[:, None]
    pole_real = -jnp.exp(decay_log)[None, :]
    pole_imag = rotation[None, :]
    rate_real = step_size * pole_real
    rate_imag = step_size * pole_imag
    lift_real = jnp.expm1(rate_real) * jnp.cos(rate_imag) - 2.0 * jnp.sin(0.5 * rate_imag) ** 2
    lift_imag = jnp.exp(rate_real) * jnp.sin(rate_imag)
    pole_norm = pole_real * pole_real + pole_imag * pole_imag
    ratio_real = (lift_real * pole_real + lift_imag * pole_imag) / pole_norm
    ratio_imag = (lift_imag * pole_real - lift_real * pole_imag) / pole_norm
    coef_real = readout[0] * ratio_real - readout[1] * ratio_imag
    coef_imag = readout[0] * ratio_imag + readout[1] * ratio_real
    return (coef_real, coef_imag, rate_real, rate_imag)


def parameter_grads(primal, backward, totals):
    coef_real, coef_imag = (primal[0], primal[1])
    cotangents = (
        2.0 * totals[0],
        -2.0 * totals[1],
        2.0 * (coef_real * totals[2] - coef_imag * totals[3]),
        -2.0 * (coef_real * totals[3] + coef_imag * totals[2]),
    )
    return backward(cotangents)


def shifted_totals(raw_sums, rate_real, rate_imag, block_start, norm_scale):
    decays = jnp.exp(rate_real * block_start)
    phases = rate_imag * block_start
    base_real = decays * jnp.cos(phases)
    base_imag = decays * jnp.sin(phases)
    near_real = block_start * raw_sums[0] + raw_sums[2]
    near_imag = block_start * raw_sums[1] + raw_sums[3]
    return jnp.stack(
        [
            norm_scale * (base_real * raw_sums[0] - base_imag * raw_sums[1]),
            norm_scale * (base_real * raw_sums[1] + base_imag * raw_sums[0]),
            norm_scale * (base_real * near_real - base_imag * near_imag),
            norm_scale * (base_real * near_imag + base_imag * near_real),
        ]
    )


def whole_channel_totals(lag_rows, rate_real, rate_imag, norm_scale):
    owners, length = (lag_rows.shape[1], lag_rows.shape[2])
    offsets = jnp.arange(length, dtype=jnp.int32).astype(jnp.float32)
    decays = jnp.exp(rate_real[:, :, None] * offsets)
    phases = rate_imag[:, :, None] * offsets
    power_real = decays * jnp.cos(phases)
    power_imag = decays * jnp.sin(phases)
    weighted = lag_rows * offsets
    raw_sums = jnp.stack(
        [
            jnp.einsum("cbj,cnj->cnb", lag_rows, power_real, precision=precise),
            jnp.einsum("cbj,cnj->cnb", lag_rows, power_imag, precision=precise),
            jnp.einsum("cbj,cnj->cnb", weighted, power_real, precision=precise),
            jnp.einsum("cbj,cnj->cnb", weighted, power_imag, precision=precise),
        ]
    )
    starts = (jnp.arange(owners, dtype=jnp.int32) * length).astype(jnp.float32)
    totals = shifted_totals(
        raw_sums, rate_real[:, :, None], rate_imag[:, :, None], starts, norm_scale
    )
    return jnp.sum(totals, axis=-1)


def general_lags(whole, norm_scale):
    part_count, owners, length = whole.shape[1:]
    freq_width = 2 * owners
    modulus = freq_width * length
    row_index = jnp.arange(owners, dtype=jnp.int32)
    outer_index = jnp.arange(freq_width, dtype=jnp.int32)
    inner_index = jnp.arange(length, dtype=jnp.int32)
    first = angle_table(row_index, outer_index, freq_width, -1.0)
    spec_real = jnp.einsum("scba,bk->scka", whole, jnp.cos(first), precision=precise)
    spec_imag = jnp.einsum("scba,bk->scka", whole, jnp.sin(first), precision=precise)
    spec_real, spec_imag = rotate(
        spec_real, spec_imag, angle_table(outer_index, inner_index, modulus, -1.0)
    )
    freq_real, freq_imag = last_transform(spec_real, spec_imag, -1.0)
    prod_real = freq_real[1] * freq_real[0] + freq_imag[1] * freq_imag[0]
    prod_imag = freq_imag[1] * freq_real[0] - freq_real[1] * freq_imag[0]
    back_real, back_imag = last_transform(prod_real, prod_imag, 1.0)
    back_real, back_imag = rotate(
        back_real, back_imag, angle_table(outer_index, inner_index, modulus, 1.0)
    )
    final = angle_table(outer_index, row_index, freq_width, 1.0)
    lag_rows = jnp.einsum("cka,kb->cba", back_real, jnp.cos(final), precision=precise) - jnp.einsum(
        "cka,kb->cba", back_imag, jnp.sin(final), precision=precise
    )
    return lag_rows * (norm_scale / modulus)


def general_device(inputs, out_grad, readout, log_step, decay_log, rotation):
    owners = lax.axis_size("seq")
    channels, length = inputs.shape
    states = decay_log.shape[0]
    part_count = channels // owners
    norm_scale = 1.0 / math.sqrt(owners * length)
    pieces = jnp.concatenate(
        [a.reshape(owners, part_count, length) for a in (inputs, out_grad)], axis=1
    )
    pieces = lax.all_to_all(pieces, "seq", split_axis=0, concat_axis=0, tiled=True)
    whole = pieces.astype(jnp.float32).reshape(owners, 2, part_count, length)
    lag_rows = general_lags(whole.transpose(1, 2, 0, 3), norm_scale)
    first_channel = lax.axis_index("seq") * part_count
    own_readout = lax.dynamic_slice_in_dim(readout, first_channel, part_count, 1)
    own_step = lax.dynamic_slice_in_dim(log_step, first_channel, part_count, 0)
    primal, backward = jax.vjp(discretize, own_readout, own_step, decay_log, rotation)
    totals = whole_channel_totals(lag_rows, primal[2], primal[3], norm_scale)
    readout_part, step_part, decay_part, rotation_part = parameter_grads(primal, backward, totals)
    shared = jnp.concatenate(
        [readout_part.reshape(-1), step_part, decay_part, rotation_part]
    )
    sent = jnp.concatenate(
        [
            lag_rows.transpose(1, 0, 2).reshape(owners, -1),
            jnp.broadcast_to(shared, (owners, shared.shape[0])),
        ],
        axis=1,
    )
    got = lax.all_to_all(sent, "seq", split_axis=0, concat_axis=0, tiled=True)
    cuts = np.cumsum([part_count * length, 2 * part_count * states, part_count])
    lags, readouts, steps, state = jnp.split(got, cuts, axis=1)
    readouts = readouts.reshape(owners, 2, part_count, states).transpose(1, 0, 2, 3)
    return (
        lags.reshape(channels, length),
        readouts.reshape(2, channels, states),
        steps.reshape(channels),
        lax.psum(jnp.sum(state, axis=0), "ch").reshape(2, states),
    )


def split_halves(value):
    high = value.astype(jnp.bfloat16)
    return high, (value - high.astype(jnp.float32)).astype(jnp.bfloat16)


def cos_sin(angle):
    turns = jnp.floor(angle * (2.0 / math.pi) + 0.5)
    rest = angle - turns * 1.5703125
    rest = rest - turns * 4.837512969970703125e-4
    rest = rest - turns * 7.54978995489188216e-8
    quarter = turns.astype(jnp.int32)
    square = rest * rest
    sine = rest + rest * square * (
        -1.6666654611e-1 + square * (8.3321608736e-3 - square * 1.9515295891e-4)
    )
    cosine = (
        1.0
        - 0.5 * square
        + square
        * square
        * (
            4.166664568298827e-2
            + square * (-1.388731625493765e-3 + square * 2.443315711809948e-5)
        )
    )
    odd = (quarter & 1) == 1
    out_cos = jnp.where(odd, sine, cosine)
    out_sin = jnp.where(odd, cosine, sine)
    out_cos = jnp.where(((quarter + 1) & 2) == 2, -out_cos, out_cos)
    out_sin = jnp.where((quarter & 2) == 2, -out_sin, out_sin)
    return out_cos, out_sin


def grow(value):
    series = 1.0
    for term in range(9, 1, -1):
        series = 1.0 + series * value * (1.0 / term)
    return jnp.where(jnp.abs(value) < 0.35, series * value, jnp.exp(value) - 1.0)


def power(rate_real, rate_imag, offset):
    size = jnp.exp(rate_real * offset)
    cosine, sine = cos_sin(rate_imag * offset)
    return size * cosine, size * sine


def times(left, right):
    return (
        left[0] * right[0] - left[1] * right[1],
        left[0] * right[1] + left[1] * right[0],
    )


def weighted_sum(terms):
    total = None
    for weight, value in terms:
        if abs(weight) < 1e-12:
            continue
        if abs(abs(weight) - 1.0) < 1e-12:
            term = value if weight > 0 else -value
        else:
            term = value * weight
        total = term if total is None else total + term
    return total


def turn(count, width):
    angle = two_pi * (count % width) / width
    return math.cos(angle), math.sin(angle)


def precise_dot(value, matrix):
    high, low = split_halves(value)
    dot = functools.partial(jnp.dot, preferred_element_type=jnp.float32)
    return dot(high, matrix[0]) + dot(low, matrix[0]) + dot(high, matrix[1])


def transform_tables(owners, length):
    width = 2 * owners
    counter = np.arange(length)
    angles = two_pi * (counter[:, None] * counter[None, :] % length) / length
    cosine, sine = np.cos(angles), np.sin(angles)
    matrix = np.block([[cosine, -sine], [sine, cosine]]).astype(np.float32)
    high = matrix.astype(jnp.bfloat16)
    low = (matrix - high.astype(np.float32)).astype(jnp.bfloat16)
    outer = np.arange(owners + 1)
    angles = two_pi * (outer[:, None] * counter[None, :]) / (width * length)
    twiddle = np.stack([np.cos(angles), -np.sin(angles)], axis=1).astype(np.float32)
    return np.stack([high, low]), twiddle


def three_pieces(value):
    pieces = []
    for _ in range(3):
        piece = value.astype(jnp.bfloat16).astype(jnp.float32)
        pieces.append(piece)
        value = value - piece
    return pieces


def transposed(value):
    return jnp.concatenate(
        [value[:, spot : spot + LANES].T for spot in range(0, value.shape[1], LANES)], axis=0
    )


SIGNALS, READ, STEP, OUT_ROWS = 0, 16, 19, 24
LAGS, GRADS, STATE, STEPS, SCALES, BACK_ROWS = 0, 8, 16, 18, 20, 24


def pack_kernel(axis, inputs, out_grad, readout, log_step, out, rows, turned, peers_rows):
    peers = out.shape[0]
    own = lax.axis_index(axis)
    for place, signal in enumerate((inputs, out_grad)):
        value = signal[...].astype(jnp.float32).reshape(peers, SUBLANES, LANES)
        peers_rows[:, SIGNALS + place * SUBLANES : SIGNALS + (place + 1) * SUBLANES] = value
    turned[0] = transposed(readout[...])
    turned[1] = transposed(jnp.broadcast_to(log_step[...], (LANES, log_step.shape[1])))
    extra = []
    for place in range(2):
        value = turned[place, pl.ds(own, peers, stride=SUBLANES), :]
        extra += three_pieces(value)
    for place, value in enumerate(extra):
        rows[pl.ds(place, peers, stride=SUBLANES), :] = value
    zero = jnp.zeros((peers, LANES), jnp.float32)
    for place in range(len(extra), SUBLANES):
        rows[pl.ds(place, peers, stride=SUBLANES), :] = zero
    peers_rows[:, READ:OUT_ROWS] = rows[...].reshape(peers, SUBLANES, LANES)
    out[...] = peers_rows[...].astype(jnp.bfloat16)


def hold_kernel(matrix, twiddle, out_matrix, out_twiddle):
    out_matrix[...] = matrix[...]
    out_twiddle[...] = twiddle[...]


def scaled(value):
    most = jnp.max(jnp.max(jnp.abs(value), axis=1, keepdims=True), axis=0, keepdims=True)
    exponent = jnp.floor(jnp.log(jnp.maximum(most, 1e-30)) * (1.0 / math.log(2.0))) + 1.0
    return value * jnp.exp2(-exponent), exponent


def two_pieces(value):
    high = value.astype(jnp.bfloat16).astype(jnp.float32)
    return high, (value - high) * 256.0


def main_kernel(
    owners, norm_scale, got, matrix, twiddle, decay_log, rotation, sent, extra, lags, powers, sums
):
    peers, length = got.shape[0], got.shape[2]
    groups = peers // owners
    part_count = groups * SUBLANES
    rows = 2 * part_count
    width = 2 * owners
    pairs = part_count // 2
    half = pairs // SUBLANES
    got_rows = got[...].astype(jnp.float32)
    extra[...] = got_rows[:, READ:OUT_ROWS].reshape(peers * SUBLANES, LANES)

    def collect(first):
        tiles = []
        for group in range(groups):
            pieces = [
                extra[pl.ds(group * SUBLANES + first - READ + i, owners, stride=groups * SUBLANES), :]
                for i in range(3)
            ]
            tiles.append(pieces[0] + pieces[1] + pieces[2])
        return jnp.concatenate(tiles[:half], axis=0), jnp.concatenate(tiles[half:], axis=0)

    lane = lax.broadcasted_iota(jnp.int32, (pairs, LANES), 1)
    left = lane < LANES // 2

    def swap(value):
        return pltpu.roll(value, LANES // 2, 1)

    lower, upper = collect(READ)
    read = (jnp.where(left, lower, swap(upper)), jnp.where(left, swap(lower), upper))
    lower, upper = collect(STEP)
    step = jnp.exp(jnp.where(left, lower, upper))
    decay_row = jnp.concatenate([decay_log[...], decay_log[...]], axis=1)
    rotation_row = jnp.concatenate([rotation[...], rotation[...]], axis=1)
    pole = (
        jnp.broadcast_to(-jnp.exp(decay_row), step.shape),
        jnp.broadcast_to(rotation_row, step.shape),
    )
    rate = (step * pole[0], step * pole[1])

    row = lax.broadcasted_iota(jnp.int32, (SUBLANES, LANES), 0).astype(jnp.float32)
    doublings = []
    size = SUBLANES
    while size < length:
        doublings.append(size)
        size *= 2
    jumps = jnp.zeros((SUBLANES, LANES), jnp.float32)
    for place, jump in enumerate(doublings):
        jumps = jnp.where(row == place, float(jump), jumps)
    bases = []
    for p in range(pairs):
        rate_real, rate_imag = rate[0][p : p + 1], rate[1][p : p + 1]
        shifts = power(rate_real, rate_imag, jumps)
        table = [power(rate_real, rate_imag, row)]
        for place in range(len(doublings)):
            shift = (shifts[0][place : place + 1], shifts[1][place : place + 1])
            table += [times(block, shift) for block in table]
        for place in range(0, len(table), 2):
            spot = place * SUBLANES
            for side in range(2):
                value = jnp.concatenate([table[place][side], table[place + 1][side]], axis=0)
                high, low = split_halves(value)
                lanes = slice(side * LANES, (side + 1) * LANES)
                powers[p, spot : spot + 2 * SUBLANES, lanes] = high
                powers[p, length + spot : length + spot + 2 * SUBLANES, lanes] = low
        bases.append(power(rate_real, rate_imag, row * float(length)))

    blocks = []
    for s in range(owners):
        mine = got_rows[s * groups : (s + 1) * groups]
        blocks.append(
            jnp.concatenate(
                [mine[:, :SUBLANES], mine[:, SUBLANES : 2 * SUBLANES]], axis=0
            ).reshape(rows, length)
        )
    spectra = []
    for k in range(owners + 1):
        real = weighted_sum([(turn(k * s, width)[0], blocks[s]) for s in range(owners)])
        imag = weighted_sum([(-turn(k * s, width)[1], blocks[s]) for s in range(owners)])
        if imag is None:
            imag = jnp.zeros_like(real)
        if k:
            real, imag = times((real, imag), (twiddle[k, 0:1], twiddle[k, 1:2]))
        spectra.append(jnp.concatenate([real, imag], axis=1))
    freq = precise_dot(jnp.concatenate(spectra, axis=0), matrix)

    products = []
    for k in range(owners + 1):
        at_in = freq[k * rows : k * rows + part_count]
        at_out = freq[k * rows + part_count : (k + 1) * rows]
        ur, ui = at_in[:, :length], at_in[:, length:]
        gr, gi = at_out[:, :length], at_out[:, length:]
        products.append(jnp.concatenate([gr * ur + gi * ui, gr * ui - gi * ur], axis=1))
    back = precise_dot(jnp.concatenate(products, axis=0), matrix)

    turned = []
    for k in range(owners + 1):
        value = back[k * part_count : (k + 1) * part_count]
        value = (value[:, :length], value[:, length:])
        if k:
            value = times(value, (twiddle[k, 0:1], twiddle[k, 1:2]))
        turned.append(value)
    scale = norm_scale / (width * length)
    for b in range(owners):
        terms = []
        for k in range(owners + 1):
            weight = scale if k in (0, owners) else 2.0 * scale
            cosine, sine = turn(k * b, width)
            terms += [(weight * cosine, turned[k][0]), (weight * sine, turned[k][1])]
        lags[b * part_count : (b + 1) * part_count] = weighted_sum(terms)

    offset = lax.broadcasted_iota(jnp.int32, (owners, length), 1).astype(jnp.float32)
    start = row * float(length)
    first = left[:owners]
    for p in range(pairs):
        one = lags[pl.ds(p, owners, stride=part_count), :]
        two = lags[pl.ds(pairs + p, owners, stride=part_count), :]
        high, low = split_halves(
            jnp.concatenate([one, two, one * offset, two * offset], axis=0)
        )
        factor = jnp.concatenate(
            [
                jnp.concatenate([high, high], axis=1),
                jnp.concatenate([low, jnp.zeros_like(low)], axis=1),
            ],
            axis=0,
        )
        raw = jnp.dot(factor, powers[p], preferred_element_type=jnp.float32)
        raw = raw[: 4 * owners] + raw[4 * owners :]

        def pick(place, side):
            lanes = slice(side * LANES, (side + 1) * LANES)
            top = raw[2 * place * owners : (2 * place + 1) * owners, lanes]
            bottom = raw[(2 * place + 1) * owners : (2 * place + 2) * owners, lanes]
            return jnp.where(first, top, bottom)

        plain = (pick(0, 0), pick(0, 1))
        near = (start * plain[0] + pick(1, 0), start * plain[1] + pick(1, 1))
        for place, value in enumerate(times(bases[p], plain) + times(bases[p], near)):
            sums[place, p : p + 1] = jnp.sum(value, axis=0, keepdims=True)

    size = jnp.exp(rate[0])
    cosine, sine = cos_sin(rate[1])
    sine_half = cos_sin(0.5 * rate[1])[1]
    lift = (grow(rate[0]) * cosine - 2.0 * sine_half * sine_half, size * sine)
    norm = 1.0 / (pole[0] * pole[0] + pole[1] * pole[1])
    inverse = (pole[0] * norm, -pole[1] * norm)
    ratio = times(lift, inverse)
    coef = times(read, ratio)
    lifted = times((size * cosine, size * sine), inverse)
    total = (sums[0] * (2.0 * norm_scale), sums[1] * (2.0 * norm_scale))
    lag_total = (sums[2] * (2.0 * norm_scale), sums[3] * (2.0 * norm_scale))
    on_read = times(total, ratio)
    on_read = (on_read[0], -on_read[1])
    on_rate = times(coef, lag_total)
    through = times(times(total, read), lifted)
    on_rate = (on_rate[0] + through[0], on_rate[1] + through[1])
    direct = times(times(total, coef), inverse)
    on_pole = (step * on_rate[0] - direct[0], step * on_rate[1] - direct[1])
    on_step = times(on_rate, rate)[0]
    on_decay = jnp.sum(on_pole[0] * pole[0], axis=0, keepdims=True)
    on_rotation = -jnp.sum(on_pole[1], axis=0, keepdims=True)
    on_decay = on_decay + swap(on_decay)
    on_rotation = on_rotation + swap(on_rotation)
    state, state_exponent = scaled(jnp.where(left[0:1], on_decay, on_rotation))

    lag_values, lag_exponent = scaled(lags[...])
    lower = jnp.where(left, on_read[0], swap(on_read[1]))
    upper = jnp.where(left, swap(on_read[0]), on_read[1])
    grads, grad_exponent = scaled(jnp.concatenate([lower, upper], axis=0))
    step_column = jnp.concatenate(
        [
            jnp.sum(jnp.where(left, on_step, 0.0), axis=1, keepdims=True),
            jnp.sum(jnp.where(left, 0.0, on_step), axis=1, keepdims=True),
        ],
        axis=0,
    )
    step_column, step_exponent = scaled(step_column)
    place_row = lax.broadcasted_iota(jnp.int32, (SUBLANES, LANES), 0)
    place_lane = lax.broadcasted_iota(jnp.int32, (SUBLANES, LANES), 1)
    device = lax.axis_index("seq") * groups + lax.axis_index("ch")
    per_row = LANES // SUBLANES
    aim = lax.rem(device, per_row) * SUBLANES
    fixed = jnp.zeros((SUBLANES, LANES), jnp.float32)
    values = two_pieces(state) + (None, None)
    values += (lag_exponent, grad_exponent, state_exponent, step_exponent)
    for spot, value in enumerate(values):
        if value is not None:
            fixed = jnp.where(place_row == spot, value, fixed)
    tails = []
    for group in range(groups):
        column = step_column[group * SUBLANES : (group + 1) * SUBLANES]
        spread = jnp.where(place_lane == place_row + aim, column, 0.0)
        high, low = two_pieces(jnp.sum(spread, axis=0, keepdims=True))
        tail = jnp.where(place_row == STEPS - STATE, high, fixed)
        tails.append(jnp.where(place_row == STEPS - STATE + 1, low, tail))
    for b in range(owners):
        for group in range(groups):
            spot = b * part_count + group * SUBLANES
            peer = b * groups + group
            sent[peer, LAGS:GRADS] = lag_values[spot : spot + SUBLANES]
            sent[peer, GRADS:STATE] = grads[group * SUBLANES : (group + 1) * SUBLANES]
            sent[peer, STATE:BACK_ROWS] = tails[group]


def unpack_kernel(got, kernel_grad, readout_grad, step_grad, state_grad):
    peers = got.shape[0]
    scales = [jnp.exp2(got[:, SCALES + i : SCALES + i + 1, :]) for i in range(4)]
    channels = peers * SUBLANES
    kernel_grad[...] = (got[:, LAGS:GRADS, :] * scales[0]).reshape(channels, LANES)
    grads = (got[:, GRADS:STATE, :] * scales[1]).reshape(channels, LANES)
    for spot in range(0, channels, LANES):
        readout_grad[:, spot : spot + LANES] = grads[spot : spot + LANES].T

    def whole(place, scale):
        high, low = got[:, place : place + 1, :], got[:, place + 1 : place + 2, :]
        return (high + low * (1.0 / 256.0)) * scale

    state_grad[...] = jnp.sum(whole(STATE, scales[2]), axis=0)
    steps = whole(STEPS, scales[3])
    per_row = LANES // SUBLANES
    for spot in range(0, peers, per_row):
        lanes = slice(spot * SUBLANES, (spot + per_row) * SUBLANES)
        step_grad[:, lanes] = jnp.sum(steps[spot : spot + per_row], axis=0)


def kernel_device(inputs, out_grad, readout, log_step, decay_log, rotation):
    owners, groups = lax.axis_size("seq"), lax.axis_size("ch")
    peers = owners * groups
    channels, length = inputs.shape
    states = decay_log.shape[0]
    part_count = channels // owners
    pairs = part_count // 2
    norm_scale = 1.0 / math.sqrt(owners * length)
    vmem = pl.BlockSpec(memory_space=pltpu.VMEM)
    memory = pltpu.CompilerParams(vmem_limit_bytes=32 * 1024 * 1024)
    f32, bf16 = jnp.float32, jnp.bfloat16

    pieces = pl.pallas_call(
        functools.partial(pack_kernel, "seq"),
        out_shape=jax.ShapeDtypeStruct((peers, OUT_ROWS, length), bf16),
        in_specs=[vmem] * 4,
        out_specs=vmem,
        scratch_shapes=[
            pltpu.VMEM((peers * SUBLANES, LANES), f32),
            pltpu.VMEM((2, channels, LANES), f32),
            pltpu.VMEM((peers, OUT_ROWS, LANES), f32),
        ],
        compiler_params=memory,
    )(inputs, out_grad, readout.transpose(0, 2, 1).reshape(LANES, channels), log_step[None])
    got = lax.all_to_all(pieces, ("seq", "ch"), split_axis=0, concat_axis=0, tiled=True)

    tables = [jnp.asarray(table) for table in transform_tables(owners, length)]
    tables = pl.pallas_call(
        hold_kernel,
        out_shape=[jax.ShapeDtypeStruct(table.shape, table.dtype) for table in tables],
        in_specs=[vmem] * 2,
        out_specs=[vmem] * 2,
        compiler_params=memory,
    )(*tables)
    sent = pl.pallas_call(
        functools.partial(main_kernel, owners, norm_scale),
        out_shape=jax.ShapeDtypeStruct((peers, BACK_ROWS, LANES), f32),
        in_specs=[vmem] * 5,
        out_specs=vmem,
        scratch_shapes=[
            pltpu.VMEM((peers * SUBLANES, LANES), f32),
            pltpu.VMEM((owners * part_count, length), f32),
            pltpu.VMEM((pairs, 2 * length, 2 * LANES), bf16),
            pltpu.VMEM((4, pairs, LANES), f32),
        ],
        compiler_params=memory,
    )(got, *tables, decay_log[None], rotation[None])
    back = lax.all_to_all(
        sent.astype(jnp.float16), ("seq", "ch"), split_axis=0, concat_axis=0, tiled=True
    )
    kernel_grad, readout_grad, step_grad, state_grad = pl.pallas_call(
        unpack_kernel,
        out_shape=[
            jax.ShapeDtypeStruct((channels, length), f32),
            jax.ShapeDtypeStruct((LANES, channels), f32),
            jax.ShapeDtypeStruct((1, channels), f32),
            jax.ShapeDtypeStruct((1, LANES), f32),
        ],
        in_specs=[vmem],
        out_specs=[vmem] * 4,
        compiler_params=memory,
    )(back.astype(f32))
    return (
        kernel_grad,
        readout_grad.reshape(2, states, channels).transpose(0, 2, 1),
        step_grad.reshape(channels),
        state_grad.reshape(2, states),
    )


def kernel_fits(mesh, inputs, decay_log):
    owners, groups = mesh.shape["seq"], mesh.shape["ch"]
    channels = inputs.shape[0] // groups
    return (
        inputs.shape[1] == owners * LANES
        and 2 * decay_log.shape[0] == LANES
        and owners == SUBLANES
        and groups % 2 == 0
        and channels == owners * groups * SUBLANES
        and channels % LANES == 0
    )


def solution(mesh):
    def whole(inputs, out_grad, readout, log_step, decay_log, rotation):
        fits = kernel_fits(mesh, inputs, decay_log)
        return jax.shard_map(
            kernel_device if fits else general_device,
            mesh=mesh,
            in_specs=(P("ch", "seq"), P("ch", "seq"), P(None, "ch", None), P("ch"), P(), P()),
            out_specs=(P("ch", "seq"), P(None, "ch", None), P("ch"), P()),
            check_vma=False,
        )(inputs, out_grad, readout, log_step, decay_log, rotation)

    return whole
```

```python
import functools
import math

import jax
import jax.numpy as jnp
import numpy as np
from jax import lax
from jax.experimental import pallas as pl
from jax.experimental.pallas import tpu as pltpu
from jax.sharding import PartitionSpec as P

precise = lax.Precision.HIGHEST
two_pi = 2.0 * math.pi
LANES = 128
SUBLANES = 8


def angle_table(left_index, right_index, modulus, orient):
    product = left_index[:, None] * right_index[None, :] % modulus
    return orient * two_pi * product.astype(jnp.float32) / modulus


def rotate(real_part, imag_part, angles):
    cosine_table = jnp.cos(angles)
    sine_table = jnp.sin(angles)
    return (
        real_part * cosine_table - imag_part * sine_table,
        real_part * sine_table + imag_part * cosine_table,
    )


def last_transform(real_part, imag_part, orient):
    length = real_part.shape[-1]
    counter = jnp.arange(length, dtype=jnp.int32)
    angles = angle_table(counter, counter, length, orient)
    cosine_table = jnp.cos(angles)
    sine_table = jnp.sin(angles)
    dot = functools.partial(jnp.dot, precision=precise, preferred_element_type=jnp.float32)
    return (
        dot(real_part, cosine_table) - dot(imag_part, sine_table),
        dot(imag_part, cosine_table) + dot(real_part, sine_table),
    )


def discretize(readout, log_step, decay_log, rotation):
    step_size = jnp.exp(log_step)[:, None]
    pole_real = -jnp.exp(decay_log)[None, :]
    pole_imag = rotation[None, :]
    rate_real = step_size * pole_real
    rate_imag = step_size * pole_imag
    lift_real = jnp.expm1(rate_real) * jnp.cos(rate_imag) - 2.0 * jnp.sin(0.5 * rate_imag) ** 2
    lift_imag = jnp.exp(rate_real) * jnp.sin(rate_imag)
    pole_norm = pole_real * pole_real + pole_imag * pole_imag
    ratio_real = (lift_real * pole_real + lift_imag * pole_imag) / pole_norm
    ratio_imag = (lift_imag * pole_real - lift_real * pole_imag) / pole_norm
    coef_real = readout[0] * ratio_real - readout[1] * ratio_imag
    coef_imag = readout[0] * ratio_imag + readout[1] * ratio_real
    return (coef_real, coef_imag, rate_real, rate_imag)


def parameter_grads(primal, backward, totals):
    coef_real, coef_imag = (primal[0], primal[1])
    cotangents = (
        2.0 * totals[0],
        -2.0 * totals[1],
        2.0 * (coef_real * totals[2] - coef_imag * totals[3]),
        -2.0 * (coef_real * totals[3] + coef_imag * totals[2]),
    )
    return backward(cotangents)


def shifted_totals(raw_sums, rate_real, rate_imag, block_start, norm_scale):
    decays = jnp.exp(rate_real * block_start)
    phases = rate_imag * block_start
    base_real = decays * jnp.cos(phases)
    base_imag = decays * jnp.sin(phases)
    near_real = block_start * raw_sums[0] + raw_sums[2]
    near_imag = block_start * raw_sums[1] + raw_sums[3]
    return jnp.stack(
        [
            norm_scale * (base_real * raw_sums[0] - base_imag * raw_sums[1]),
            norm_scale * (base_real * raw_sums[1] + base_imag * raw_sums[0]),
            norm_scale * (base_real * near_real - base_imag * near_imag),
            norm_scale * (base_real * near_imag + base_imag * near_real),
        ]
    )


def whole_channel_totals(lag_rows, rate_real, rate_imag, norm_scale):
    owners, length = (lag_rows.shape[1], lag_rows.shape[2])
    offsets = jnp.arange(length, dtype=jnp.int32).astype(jnp.float32)
    decays = jnp.exp(rate_real[:, :, None] * offsets)
    phases = rate_imag[:, :, None] * offsets
    power_real = decays * jnp.cos(phases)
    power_imag = decays * jnp.sin(phases)
    weighted = lag_rows * offsets
    raw_sums = jnp.stack(
        [
            jnp.einsum("cbj,cnj->cnb", lag_rows, power_real, precision=precise),
            jnp.einsum("cbj,cnj->cnb", lag_rows, power_imag, precision=precise),
            jnp.einsum("cbj,cnj->cnb", weighted, power_real, precision=precise),
            jnp.einsum("cbj,cnj->cnb", weighted, power_imag, precision=precise),
        ]
    )
    starts = (jnp.arange(owners, dtype=jnp.int32) * length).astype(jnp.float32)
    totals = shifted_totals(
        raw_sums, rate_real[:, :, None], rate_imag[:, :, None], starts, norm_scale
    )
    return jnp.sum(totals, axis=-1)


def general_lags(whole, norm_scale):
    part_count, owners, length = whole.shape[1:]
    freq_width = 2 * owners
    modulus = freq_width * length
    row_index = jnp.arange(owners, dtype=jnp.int32)
    outer_index = jnp.arange(freq_width, dtype=jnp.int32)
    inner_index = jnp.arange(length, dtype=jnp.int32)
    first = angle_table(row_index, outer_index, freq_width, -1.0)
    spec_real = jnp.einsum("scba,bk->scka", whole, jnp.cos(first), precision=precise)
    spec_imag = jnp.einsum("scba,bk->scka", whole, jnp.sin(first), precision=precise)
    spec_real, spec_imag = rotate(
        spec_real, spec_imag, angle_table(outer_index, inner_index, modulus, -1.0)
    )
    freq_real, freq_imag = last_transform(spec_real, spec_imag, -1.0)
    prod_real = freq_real[1] * freq_real[0] + freq_imag[1] * freq_imag[0]
    prod_imag = freq_imag[1] * freq_real[0] - freq_real[1] * freq_imag[0]
    back_real, back_imag = last_transform(prod_real, prod_imag, 1.0)
    back_real, back_imag = rotate(
        back_real, back_imag, angle_table(outer_index, inner_index, modulus, 1.0)
    )
    final = angle_table(outer_index, row_index, freq_width, 1.0)
    lag_rows = jnp.einsum("cka,kb->cba", back_real, jnp.cos(final), precision=precise) - jnp.einsum(
        "cka,kb->cba", back_imag, jnp.sin(final), precision=precise
    )
    return lag_rows * (norm_scale / modulus)


def general_device(inputs, out_grad, readout, log_step, decay_log, rotation):
    owners = lax.axis_size("seq")
    channels, length = inputs.shape
    states = decay_log.shape[0]
    part_count = channels // owners
    norm_scale = 1.0 / math.sqrt(owners * length)
    pieces = jnp.concatenate(
        [a.reshape(owners, part_count, length) for a in (inputs, out_grad)], axis=1
    )
    pieces = lax.all_to_all(pieces, "seq", split_axis=0, concat_axis=0, tiled=True)
    whole = pieces.astype(jnp.float32).reshape(owners, 2, part_count, length)
    lag_rows = general_lags(whole.transpose(1, 2, 0, 3), norm_scale)
    first_channel = lax.axis_index("seq") * part_count
    own_readout = lax.dynamic_slice_in_dim(readout, first_channel, part_count, 1)
    own_step = lax.dynamic_slice_in_dim(log_step, first_channel, part_count, 0)
    primal, backward = jax.vjp(discretize, own_readout, own_step, decay_log, rotation)
    totals = whole_channel_totals(lag_rows, primal[2], primal[3], norm_scale)
    readout_part, step_part, decay_part, rotation_part = parameter_grads(primal, backward, totals)
    shared = jnp.concatenate(
        [readout_part.reshape(-1), step_part, decay_part, rotation_part]
    )
    sent = jnp.concatenate(
        [
            lag_rows.transpose(1, 0, 2).reshape(owners, -1),
            jnp.broadcast_to(shared, (owners, shared.shape[0])),
        ],
        axis=1,
    )
    got = lax.all_to_all(sent, "seq", split_axis=0, concat_axis=0, tiled=True)
    cuts = np.cumsum([part_count * length, 2 * part_count * states, part_count])
    lags, readouts, steps, state = jnp.split(got, cuts, axis=1)
    readouts = readouts.reshape(owners, 2, part_count, states).transpose(1, 0, 2, 3)
    return (
        lags.reshape(channels, length),
        readouts.reshape(2, channels, states),
        steps.reshape(channels),
        lax.psum(jnp.sum(state, axis=0), "ch").reshape(2, states),
    )


def split_halves(value):
    high = value.astype(jnp.bfloat16)
    return high, (value - high.astype(jnp.float32)).astype(jnp.bfloat16)


def cos_sin(angle):
    turns = jnp.floor(angle * (2.0 / math.pi) + 0.5)
    rest = angle - turns * 1.5703125
    rest = rest - turns * 4.837512969970703125e-4
    rest = rest - turns * 7.54978995489188216e-8
    quarter = turns.astype(jnp.int32)
    square = rest * rest
    sine = rest + rest * square * (
        -1.6666654611e-1 + square * (8.3321608736e-3 - square * 1.9515295891e-4)
    )
    cosine = (
        1.0
        - 0.5 * square
        + square
        * square
        * (
            4.166664568298827e-2
            + square * (-1.388731625493765e-3 + square * 2.443315711809948e-5)
        )
    )
    odd = (quarter & 1) == 1
    out_cos = jnp.where(odd, sine, cosine)
    out_sin = jnp.where(odd, cosine, sine)
    out_cos = jnp.where(((quarter + 1) & 2) == 2, -out_cos, out_cos)
    out_sin = jnp.where((quarter & 2) == 2, -out_sin, out_sin)
    return out_cos, out_sin


def grow(value):
    series = 1.0
    for term in range(9, 1, -1):
        series = 1.0 + series * value * (1.0 / term)
    return jnp.where(jnp.abs(value) < 0.35, series * value, jnp.exp(value) - 1.0)


def power(rate_real, rate_imag, offset):
    size = jnp.exp(rate_real * offset)
    cosine, sine = cos_sin(rate_imag * offset)
    return size * cosine, size * sine


def times(left, right):
    return (
        left[0] * right[0] - left[1] * right[1],
        left[0] * right[1] + left[1] * right[0],
    )


def weighted_sum(terms):
    total = None
    for weight, value in terms:
        if abs(weight) < 1e-12:
            continue
        if abs(abs(weight) - 1.0) < 1e-12:
            term = value if weight > 0 else -value
        else:
            term = value * weight
        total = term if total is None else total + term
    return total


def turn(count, width):
    angle = two_pi * (count % width) / width
    return math.cos(angle), math.sin(angle)


def precise_dot(value, matrix):
    high, low = split_halves(value)
    dot = functools.partial(jnp.dot, preferred_element_type=jnp.float32)
    return dot(high, matrix[0]) + dot(low, matrix[0]) + dot(high, matrix[1])


def transform_tables(owners, length):
    width = 2 * owners
    counter = np.arange(length)
    angles = two_pi * (counter[:, None] * counter[None, :] % length) / length
    cosine, sine = np.cos(angles), np.sin(angles)
    matrix = np.block([[cosine, -sine], [sine, cosine]]).astype(np.float32)
    high = matrix.astype(jnp.bfloat16)
    low = (matrix - high.astype(np.float32)).astype(jnp.bfloat16)
    outer = np.arange(owners + 1)
    angles = two_pi * (outer[:, None] * counter[None, :]) / (width * length)
    twiddle = np.stack([np.cos(angles), -np.sin(angles)], axis=1).astype(np.float32)
    return np.stack([high, low]), twiddle


def three_pieces(value):
    pieces = []
    for _ in range(3):
        piece = value.astype(jnp.bfloat16).astype(jnp.float32)
        pieces.append(piece)
        value = value - piece
    return pieces


def transposed(value):
    return jnp.concatenate(
        [value[:, spot : spot + LANES].T for spot in range(0, value.shape[1], LANES)], axis=0
    )


READ, STEP, ROWS = 16, 19, 20
LAGS, GRADS, STATE, SINGLES = 0, 8, 16, 18
STEP_LANES, SCALE_LANES = (0, 8), (16, 17, 18, 19)


def pack_kernel(inputs, out_grad, readout, log_step, out, signals, read, step, turned, rows, sems):
    peers = out.shape[0] // ROWS
    copies = [
        pltpu.make_async_copy(source, target, sems.at[i])
        for i, (source, target) in enumerate(
            ((readout, read), (log_step, step), (inputs, signals.at[0]), (out_grad, signals.at[1]))
        )
    ]
    for copy in copies:
        copy.start()
    copies[0].wait()
    copies[1].wait()
    own = lax.axis_index("seq")
    turned[0] = transposed(read[...])
    turned[1] = transposed(jnp.broadcast_to(step[...], (LANES, step.shape[1])))
    for place, value in enumerate(
        three_pieces(turned[0, pl.ds(own, peers, stride=SUBLANES), :])
    ):
        rows[pl.ds(READ + place, peers, stride=ROWS), :] = value
    pieces = three_pieces(turned[1, pl.ds(own, peers, stride=SUBLANES), :])
    lane = lax.broadcasted_iota(jnp.int32, (peers, LANES), 1)
    value = jnp.where(lane == 0, pieces[0], jnp.where(lane == 1, pieces[1], pieces[2]))
    rows[pl.ds(STEP, peers, stride=ROWS), :] = value
    for place in range(2):
        copies[2 + place].wait()
        value = signals[place].astype(jnp.float32)
        for peer in range(peers):
            spot = peer * ROWS + place * SUBLANES
            rows[spot : spot + SUBLANES] = value[peer * SUBLANES : (peer + 1) * SUBLANES]
    out[...] = rows[...].astype(jnp.bfloat16)


def hold_kernel(*refs):
    for source, target in zip(refs[: len(refs) // 2], refs[len(refs) // 2 :]):
        target[...] = source[...]


def scaled(value):
    most = jnp.max(jnp.max(jnp.abs(value), axis=1, keepdims=True), axis=0, keepdims=True)
    exponent = jnp.floor(jnp.log(jnp.maximum(most, 1e-30)) * (1.0 / math.log(2.0))) + 1.0
    return value * jnp.exp2(-exponent), exponent


def two_pieces(value):
    high = value.astype(jnp.bfloat16).astype(jnp.float32)
    return high, (value - high) * 256.0


def main_kernel(
    owners, norm_scale, got, matrix, twiddle, decay_log, rotation, sent, rows_in, lags, powers, sums
):
    peers, length = got.shape[0] // ROWS, got.shape[1]
    groups = peers // owners
    part_count = groups * SUBLANES
    rows = 2 * part_count
    width = 2 * owners
    pairs = part_count // 2
    half = pairs // SUBLANES
    rows_in[...] = got[...].astype(jnp.float32)

    def collect(spot):
        tiles = [
            rows_in[pl.ds(group * ROWS + spot, owners, stride=groups * ROWS), :]
            for group in range(groups)
        ]
        return jnp.concatenate(tiles[:half], axis=0), jnp.concatenate(tiles[half:], axis=0)

    lane = lax.broadcasted_iota(jnp.int32, (pairs, LANES), 1)
    left = lane < LANES // 2

    def swap(value):
        return pltpu.roll(value, LANES // 2, 1)

    lower, upper = [sum(side) for side in zip(*(collect(READ + i) for i in range(3)))]
    read = (jnp.where(left, lower, swap(upper)), jnp.where(left, swap(lower), upper))
    lower, upper = [
        sum(side[:, i : i + 1] for i in range(3)) + jnp.zeros_like(side) for side in collect(STEP)
    ]
    step = jnp.exp(jnp.where(left, lower, upper))
    decay_row = jnp.concatenate([decay_log[...], decay_log[...]], axis=1)
    rotation_row = jnp.concatenate([rotation[...], rotation[...]], axis=1)
    pole = (
        jnp.broadcast_to(-jnp.exp(decay_row), step.shape),
        jnp.broadcast_to(rotation_row, step.shape),
    )
    rate = (step * pole[0], step * pole[1])

    row = lax.broadcasted_iota(jnp.int32, (SUBLANES, LANES), 0).astype(jnp.float32)
    doublings = []
    size = SUBLANES
    while size < length:
        doublings.append(size)
        size *= 2
    jumps = jnp.zeros((SUBLANES, LANES), jnp.float32)
    for place, jump in enumerate(doublings):
        jumps = jnp.where(row == place, float(jump), jumps)
    bases = []
    for p in range(pairs):
        rate_real, rate_imag = rate[0][p : p + 1], rate[1][p : p + 1]
        shifts = power(rate_real, rate_imag, jumps)
        table = [power(rate_real, rate_imag, row)]
        for place in range(len(doublings)):
            shift = (shifts[0][place : place + 1], shifts[1][place : place + 1])
            table += [times(block, shift) for block in table]
        for place in range(0, len(table), 2):
            spot = place * SUBLANES
            for side in range(2):
                value = jnp.concatenate([table[place][side], table[place + 1][side]], axis=0)
                high, low = split_halves(value)
                lanes = slice(side * LANES, (side + 1) * LANES)
                powers[p, spot : spot + 2 * SUBLANES, lanes] = high
                powers[p, length + spot : length + spot + 2 * SUBLANES, lanes] = low
        bases.append(power(rate_real, rate_imag, row * float(length)))

    blocks = []
    for s in range(owners):
        spots = [(s * groups + group) * ROWS for group in range(groups)]
        blocks.append(
            jnp.concatenate(
                [rows_in[spot : spot + SUBLANES] for spot in spots]
                + [rows_in[spot + SUBLANES : spot + 2 * SUBLANES] for spot in spots],
                axis=0,
            )
        )
    spectra = []
    for k in range(owners + 1):
        real = weighted_sum([(turn(k * s, width)[0], blocks[s]) for s in range(owners)])
        imag = weighted_sum([(-turn(k * s, width)[1], blocks[s]) for s in range(owners)])
        if imag is None:
            imag = jnp.zeros_like(real)
        if k:
            real, imag = times((real, imag), (twiddle[k, 0:1], twiddle[k, 1:2]))
        spectra.append(jnp.concatenate([real, imag], axis=1))
    freq = precise_dot(jnp.concatenate(spectra, axis=0), matrix)

    products = []
    for k in range(owners + 1):
        at_in = freq[k * rows : k * rows + part_count]
        at_out = freq[k * rows + part_count : (k + 1) * rows]
        ur, ui = at_in[:, :length], at_in[:, length:]
        gr, gi = at_out[:, :length], at_out[:, length:]
        products.append(jnp.concatenate([gr * ur + gi * ui, gr * ui - gi * ur], axis=1))
    back = precise_dot(jnp.concatenate(products, axis=0), matrix)

    turned = []
    for k in range(owners + 1):
        value = back[k * part_count : (k + 1) * part_count]
        value = (value[:, :length], value[:, length:])
        if k:
            value = times(value, (twiddle[k, 0:1], twiddle[k, 1:2]))
        turned.append(value)
    scale = norm_scale / (width * length)
    for b in range(owners):
        terms = []
        for k in range(owners + 1):
            weight = scale if k in (0, owners) else 2.0 * scale
            cosine, sine = turn(k * b, width)
            terms += [(weight * cosine, turned[k][0]), (weight * sine, turned[k][1])]
        lags[b * part_count : (b + 1) * part_count] = weighted_sum(terms)

    offset = lax.broadcasted_iota(jnp.int32, (owners, length), 1).astype(jnp.float32)
    start = row * float(length)
    first = left[:owners]
    for p in range(pairs):
        one = lags[pl.ds(p, owners, stride=part_count), :]
        two = lags[pl.ds(pairs + p, owners, stride=part_count), :]
        high, low = split_halves(
            jnp.concatenate([one, two, one * offset, two * offset], axis=0)
        )
        factor = jnp.concatenate(
            [
                jnp.concatenate([high, high], axis=1),
                jnp.concatenate([low, jnp.zeros_like(low)], axis=1),
            ],
            axis=0,
        )
        raw = jnp.dot(factor, powers[p], preferred_element_type=jnp.float32)
        raw = raw[: 4 * owners] + raw[4 * owners :]

        def pick(place, side):
            lanes = slice(side * LANES, (side + 1) * LANES)
            top = raw[2 * place * owners : (2 * place + 1) * owners, lanes]
            bottom = raw[(2 * place + 1) * owners : (2 * place + 2) * owners, lanes]
            return jnp.where(first, top, bottom)

        plain = (pick(0, 0), pick(0, 1))
        near = (start * plain[0] + pick(1, 0), start * plain[1] + pick(1, 1))
        for place, value in enumerate(times(bases[p], plain) + times(bases[p], near)):
            sums[place, p : p + 1] = jnp.sum(value, axis=0, keepdims=True)

    size = jnp.exp(rate[0])
    cosine, sine = cos_sin(rate[1])
    sine_half = cos_sin(0.5 * rate[1])[1]
    lift = (grow(rate[0]) * cosine - 2.0 * sine_half * sine_half, size * sine)
    norm = 1.0 / (pole[0] * pole[0] + pole[1] * pole[1])
    inverse = (pole[0] * norm, -pole[1] * norm)
    ratio = times(lift, inverse)
    coef = times(read, ratio)
    lifted = times((size * cosine, size * sine), inverse)
    total = (sums[0] * (2.0 * norm_scale), sums[1] * (2.0 * norm_scale))
    lag_total = (sums[2] * (2.0 * norm_scale), sums[3] * (2.0 * norm_scale))
    on_read = times(total, ratio)
    on_read = (on_read[0], -on_read[1])
    on_rate = times(coef, lag_total)
    through = times(times(total, read), lifted)
    on_rate = (on_rate[0] + through[0], on_rate[1] + through[1])
    direct = times(times(total, coef), inverse)
    on_pole = (step * on_rate[0] - direct[0], step * on_rate[1] - direct[1])
    on_step = times(on_rate, rate)[0]
    on_decay = jnp.sum(on_pole[0] * pole[0], axis=0, keepdims=True)
    on_rotation = -jnp.sum(on_pole[1], axis=0, keepdims=True)
    on_decay = on_decay + swap(on_decay)
    on_rotation = on_rotation + swap(on_rotation)
    state, state_exponent = scaled(jnp.where(left[0:1], on_decay, on_rotation))

    lag_values, lag_exponent = scaled(lags[...])
    lower = jnp.where(left, on_read[0], swap(on_read[1]))
    upper = jnp.where(left, swap(on_read[0]), on_read[1])
    grads, grad_exponent = scaled(jnp.concatenate([lower, upper], axis=0))
    step_column = jnp.concatenate(
        [
            jnp.sum(jnp.where(left, on_step, 0.0), axis=1, keepdims=True),
            jnp.sum(jnp.where(left, 0.0, on_step), axis=1, keepdims=True),
        ],
        axis=0,
    )
    step_column, step_exponent = scaled(step_column)
    place_row = lax.broadcasted_iota(jnp.int32, (SUBLANES, LANES), 0)
    place_lane = lax.broadcasted_iota(jnp.int32, (SUBLANES, LANES), 1)
    scales = jnp.zeros((1, LANES), jnp.float32)
    for spot, value in zip(
        SCALE_LANES, (lag_exponent, grad_exponent, state_exponent, step_exponent)
    ):
        scales = jnp.where(place_lane[0:1] == spot, value, scales)
    state_high, state_low = two_pieces(state)
    tails = []
    for group in range(groups):
        pieces = two_pieces(step_column[group * SUBLANES : (group + 1) * SUBLANES])
        spread = jnp.zeros((SUBLANES, LANES), jnp.float32)
        for spot, piece in zip(STEP_LANES, pieces):
            spread = jnp.where(place_lane == place_row + spot, piece, spread)
        singles = scales + jnp.sum(spread, axis=0, keepdims=True)
        tails.append(jnp.concatenate([state_high, state_low, singles, singles], axis=0))
    for b in range(owners):
        for group in range(groups):
            spot = b * part_count + group * SUBLANES
            place = (b * groups + group) * ROWS
            sent[place + LAGS : place + GRADS] = lag_values[spot : spot + SUBLANES]
            sent[place + GRADS : place + STATE] = grads[group * SUBLANES : (group + 1) * SUBLANES]
            sent[place + STATE : place + ROWS] = tails[group]


def unpack_kernel(got, kernel_grad, readout_grad, step_grad, state_grad, grads):
    peers = got.shape[0] // ROWS
    singles = got[pl.ds(SINGLES, peers, stride=ROWS), :]
    scales = [jnp.exp2(singles[:, spot : spot + 1]) for spot in SCALE_LANES]
    for peer in range(peers):
        spot = peer * ROWS
        lanes = slice(peer * SUBLANES, (peer + 1) * SUBLANES)
        kernel_grad[lanes] = got[spot + LAGS : spot + GRADS] * scales[0][peer : peer + 1]
        grads[lanes] = got[spot + GRADS : spot + STATE] * scales[1][peer : peer + 1]
    for spot in range(0, peers * SUBLANES, LANES):
        readout_grad[:, spot : spot + LANES] = grads[spot : spot + LANES].T
    high = got[pl.ds(STATE, peers, stride=ROWS), :]
    low = got[pl.ds(STATE + 1, peers, stride=ROWS), :]
    state = jnp.sum((high + low * (1.0 / 256.0)) * scales[2], axis=0, keepdims=True)
    states = state_grad.shape[1]
    state_grad[0:1] = state[:, :states]
    state_grad[1:2] = state[:, states:]
    per_row = LANES // SUBLANES
    lane = lax.broadcasted_iota(jnp.int32, (peers, LANES), 1)
    row = lax.broadcasted_iota(jnp.int32, (peers, LANES), 0)
    steps = pltpu.roll(singles, LANES - STEP_LANES[1], 1) * (1.0 / 256.0) + singles
    steps = jnp.where(lane < SUBLANES, steps * scales[3], 0.0)
    reach = SUBLANES
    while reach < LANES:
        steps = steps + pltpu.roll(steps, reach, 1)
        reach *= 2
    for spot in range(0, peers, per_row):
        mine = jnp.where(row - spot == lane // SUBLANES, steps, 0.0)
        step_grad[spot * SUBLANES : (spot + per_row) * SUBLANES] = jnp.sum(mine, axis=0)


def kernel_device(inputs, out_grad, readout, log_step, decay_log, rotation):
    owners, groups = lax.axis_size("seq"), lax.axis_size("ch")
    peers = owners * groups
    channels, length = inputs.shape
    states = decay_log.shape[0]
    part_count = channels // owners
    pairs = part_count // 2
    norm_scale = 1.0 / math.sqrt(owners * length)
    vmem = pl.BlockSpec(memory_space=pltpu.VMEM)
    memory = pltpu.CompilerParams(vmem_limit_bytes=32 * 1024 * 1024)
    f32, bf16 = jnp.float32, jnp.bfloat16

    def exchange(value):
        value = value.reshape(peers, ROWS // 2, 2, LANES)
        value = lax.all_to_all(value, ("seq", "ch"), split_axis=0, concat_axis=0, tiled=True)
        return value.reshape(peers * ROWS, LANES)

    anywhere = pl.BlockSpec(memory_space=pl.ANY)
    pieces = pl.pallas_call(
        pack_kernel,
        out_shape=jax.ShapeDtypeStruct((peers * ROWS, LANES), bf16),
        in_specs=[anywhere] * 4,
        out_specs=vmem,
        scratch_shapes=[
            pltpu.VMEM((2, channels, LANES), bf16),
            pltpu.VMEM((LANES, channels), f32),
            pltpu.VMEM((1, channels), f32),
            pltpu.VMEM((2, channels, LANES), f32),
            pltpu.VMEM((peers * ROWS, LANES), f32),
            pltpu.SemaphoreType.DMA((4,)),
        ],
        compiler_params=memory,
    )(inputs, out_grad, readout.transpose(0, 2, 1).reshape(LANES, channels), log_step[None])
    got = exchange(pieces)

    held = [jnp.asarray(table) for table in transform_tables(owners, length)]
    held += [decay_log[None], rotation[None]]
    held = pl.pallas_call(
        hold_kernel,
        out_shape=[jax.ShapeDtypeStruct(value.shape, value.dtype) for value in held],
        in_specs=[vmem] * 4,
        out_specs=[vmem] * 4,
        compiler_params=memory,
    )(*held)
    sent = pl.pallas_call(
        functools.partial(main_kernel, owners, norm_scale),
        out_shape=jax.ShapeDtypeStruct((peers * ROWS, LANES), f32),
        in_specs=[vmem] * 5,
        out_specs=vmem,
        scratch_shapes=[
            pltpu.VMEM((peers * ROWS, LANES), f32),
            pltpu.VMEM((owners * part_count, length), f32),
            pltpu.VMEM((pairs, 2 * length, 2 * LANES), bf16),
            pltpu.VMEM((4, pairs, LANES), f32),
        ],
        compiler_params=memory,
    )(got, *held)
    back = exchange(sent.astype(jnp.float16))
    kernel_grad, readout_grad, step_grad, state_grad = pl.pallas_call(
        unpack_kernel,
        out_shape=[
            jax.ShapeDtypeStruct((channels, length), f32),
            jax.ShapeDtypeStruct((LANES, channels), f32),
            jax.ShapeDtypeStruct((channels,), f32),
            jax.ShapeDtypeStruct((2, states), f32),
        ],
        in_specs=[vmem],
        out_specs=[vmem] * 4,
        scratch_shapes=[pltpu.VMEM((channels, LANES), f32)],
        compiler_params=memory,
    )(back.astype(f32))
    readout_grad = readout_grad.reshape(2, states, channels).transpose(0, 2, 1)
    return kernel_grad, readout_grad, step_grad, state_grad


def kernel_fits(mesh, inputs, decay_log):
    owners, groups = mesh.shape["seq"], mesh.shape["ch"]
    channels = inputs.shape[0] // groups
    return (
        inputs.shape[1] == owners * LANES
        and 2 * decay_log.shape[0] == LANES
        and owners == SUBLANES
        and groups % 2 == 0
        and channels == owners * groups * SUBLANES
        and channels % LANES == 0
    )


def solution(mesh):
    def whole(inputs, out_grad, readout, log_step, decay_log, rotation):
        fits = kernel_fits(mesh, inputs, decay_log)
        return jax.shard_map(
            kernel_device if fits else general_device,
            mesh=mesh,
            in_specs=(P("ch", "seq"), P("ch", "seq"), P(None, "ch", None), P("ch"), P(), P()),
            out_specs=(P("ch", "seq"), P(None, "ch", None), P("ch"), P()),
            check_vma=False,
        )(inputs, out_grad, readout, log_step, decay_log, rotation)

    return whole
```

```python
import functools
import math

import jax
import jax.numpy as jnp
import numpy as np
from jax import lax
from jax.experimental import pallas as pl
from jax.experimental.pallas import tpu as pltpu
from jax.sharding import PartitionSpec as P

precise = lax.Precision.HIGHEST
two_pi = 2.0 * math.pi
LANES = 128
SUBLANES = 8


def angle_table(left_index, right_index, modulus, orient):
    product = left_index[:, None] * right_index[None, :] % modulus
    return orient * two_pi * product.astype(jnp.float32) / modulus


def rotate(real_part, imag_part, angles):
    cosine_table = jnp.cos(angles)
    sine_table = jnp.sin(angles)
    return (
        real_part * cosine_table - imag_part * sine_table,
        real_part * sine_table + imag_part * cosine_table,
    )


def last_transform(real_part, imag_part, orient):
    length = real_part.shape[-1]
    counter = jnp.arange(length, dtype=jnp.int32)
    angles = angle_table(counter, counter, length, orient)
    cosine_table = jnp.cos(angles)
    sine_table = jnp.sin(angles)
    dot = functools.partial(jnp.dot, precision=precise, preferred_element_type=jnp.float32)
    return (
        dot(real_part, cosine_table) - dot(imag_part, sine_table),
        dot(imag_part, cosine_table) + dot(real_part, sine_table),
    )


def discretize(readout, log_step, decay_log, rotation):
    step_size = jnp.exp(log_step)[:, None]
    pole_real = -jnp.exp(decay_log)[None, :]
    pole_imag = rotation[None, :]
    rate_real = step_size * pole_real
    rate_imag = step_size * pole_imag
    lift_real = jnp.expm1(rate_real) * jnp.cos(rate_imag) - 2.0 * jnp.sin(0.5 * rate_imag) ** 2
    lift_imag = jnp.exp(rate_real) * jnp.sin(rate_imag)
    pole_norm = pole_real * pole_real + pole_imag * pole_imag
    ratio_real = (lift_real * pole_real + lift_imag * pole_imag) / pole_norm
    ratio_imag = (lift_imag * pole_real - lift_real * pole_imag) / pole_norm
    coef_real = readout[0] * ratio_real - readout[1] * ratio_imag
    coef_imag = readout[0] * ratio_imag + readout[1] * ratio_real
    return (coef_real, coef_imag, rate_real, rate_imag)


def parameter_grads(primal, backward, totals):
    coef_real, coef_imag = (primal[0], primal[1])
    cotangents = (
        2.0 * totals[0],
        -2.0 * totals[1],
        2.0 * (coef_real * totals[2] - coef_imag * totals[3]),
        -2.0 * (coef_real * totals[3] + coef_imag * totals[2]),
    )
    return backward(cotangents)


def shifted_totals(raw_sums, rate_real, rate_imag, block_start, norm_scale):
    decays = jnp.exp(rate_real * block_start)
    phases = rate_imag * block_start
    base_real = decays * jnp.cos(phases)
    base_imag = decays * jnp.sin(phases)
    near_real = block_start * raw_sums[0] + raw_sums[2]
    near_imag = block_start * raw_sums[1] + raw_sums[3]
    return jnp.stack(
        [
            norm_scale * (base_real * raw_sums[0] - base_imag * raw_sums[1]),
            norm_scale * (base_real * raw_sums[1] + base_imag * raw_sums[0]),
            norm_scale * (base_real * near_real - base_imag * near_imag),
            norm_scale * (base_real * near_imag + base_imag * near_real),
        ]
    )


def whole_channel_totals(lag_rows, rate_real, rate_imag, norm_scale):
    owners, length = (lag_rows.shape[1], lag_rows.shape[2])
    offsets = jnp.arange(length, dtype=jnp.int32).astype(jnp.float32)
    decays = jnp.exp(rate_real[:, :, None] * offsets)
    phases = rate_imag[:, :, None] * offsets
    power_real = decays * jnp.cos(phases)
    power_imag = decays * jnp.sin(phases)
    weighted = lag_rows * offsets
    raw_sums = jnp.stack(
        [
            jnp.einsum("cbj,cnj->cnb", lag_rows, power_real, precision=precise),
            jnp.einsum("cbj,cnj->cnb", lag_rows, power_imag, precision=precise),
            jnp.einsum("cbj,cnj->cnb", weighted, power_real, precision=precise),
            jnp.einsum("cbj,cnj->cnb", weighted, power_imag, precision=precise),
        ]
    )
    starts = (jnp.arange(owners, dtype=jnp.int32) * length).astype(jnp.float32)
    totals = shifted_totals(
        raw_sums, rate_real[:, :, None], rate_imag[:, :, None], starts, norm_scale
    )
    return jnp.sum(totals, axis=-1)


def general_lags(whole, norm_scale):
    part_count, owners, length = whole.shape[1:]
    freq_width = 2 * owners
    modulus = freq_width * length
    row_index = jnp.arange(owners, dtype=jnp.int32)
    outer_index = jnp.arange(freq_width, dtype=jnp.int32)
    inner_index = jnp.arange(length, dtype=jnp.int32)
    first = angle_table(row_index, outer_index, freq_width, -1.0)
    spec_real = jnp.einsum("scba,bk->scka", whole, jnp.cos(first), precision=precise)
    spec_imag = jnp.einsum("scba,bk->scka", whole, jnp.sin(first), precision=precise)
    spec_real, spec_imag = rotate(
        spec_real, spec_imag, angle_table(outer_index, inner_index, modulus, -1.0)
    )
    freq_real, freq_imag = last_transform(spec_real, spec_imag, -1.0)
    prod_real = freq_real[1] * freq_real[0] + freq_imag[1] * freq_imag[0]
    prod_imag = freq_imag[1] * freq_real[0] - freq_real[1] * freq_imag[0]
    back_real, back_imag = last_transform(prod_real, prod_imag, 1.0)
    back_real, back_imag = rotate(
        back_real, back_imag, angle_table(outer_index, inner_index, modulus, 1.0)
    )
    final = angle_table(outer_index, row_index, freq_width, 1.0)
    lag_rows = jnp.einsum("cka,kb->cba", back_real, jnp.cos(final), precision=precise) - jnp.einsum(
        "cka,kb->cba", back_imag, jnp.sin(final), precision=precise
    )
    return lag_rows * (norm_scale / modulus)


def general_device(inputs, out_grad, readout, log_step, decay_log, rotation):
    owners = lax.axis_size("seq")
    channels, length = inputs.shape
    states = decay_log.shape[0]
    part_count = channels // owners
    norm_scale = 1.0 / math.sqrt(owners * length)
    pieces = jnp.concatenate(
        [a.reshape(owners, part_count, length) for a in (inputs, out_grad)], axis=1
    )
    pieces = lax.all_to_all(pieces, "seq", split_axis=0, concat_axis=0, tiled=True)
    whole = pieces.astype(jnp.float32).reshape(owners, 2, part_count, length)
    lag_rows = general_lags(whole.transpose(1, 2, 0, 3), norm_scale)
    first_channel = lax.axis_index("seq") * part_count
    own_readout = lax.dynamic_slice_in_dim(readout, first_channel, part_count, 1)
    own_step = lax.dynamic_slice_in_dim(log_step, first_channel, part_count, 0)
    primal, backward = jax.vjp(discretize, own_readout, own_step, decay_log, rotation)
    totals = whole_channel_totals(lag_rows, primal[2], primal[3], norm_scale)
    readout_part, step_part, decay_part, rotation_part = parameter_grads(primal, backward, totals)
    shared = jnp.concatenate(
        [readout_part.reshape(-1), step_part, decay_part, rotation_part]
    )
    sent = jnp.concatenate(
        [
            lag_rows.transpose(1, 0, 2).reshape(owners, -1),
            jnp.broadcast_to(shared, (owners, shared.shape[0])),
        ],
        axis=1,
    )
    got = lax.all_to_all(sent, "seq", split_axis=0, concat_axis=0, tiled=True)
    cuts = np.cumsum([part_count * length, 2 * part_count * states, part_count])
    lags, readouts, steps, state = jnp.split(got, cuts, axis=1)
    readouts = readouts.reshape(owners, 2, part_count, states).transpose(1, 0, 2, 3)
    return (
        lags.reshape(channels, length),
        readouts.reshape(2, channels, states),
        steps.reshape(channels),
        lax.psum(jnp.sum(state, axis=0), "ch").reshape(2, states),
    )


def split_halves(value):
    high = value.astype(jnp.bfloat16)
    return high, (value - high.astype(jnp.float32)).astype(jnp.bfloat16)


def cos_sin(angle):
    turns = jnp.floor(angle * (2.0 / math.pi) + 0.5)
    rest = angle - turns * 1.5703125
    rest = rest - turns * 4.837512969970703125e-4
    rest = rest - turns * 7.54978995489188216e-8
    quarter = turns.astype(jnp.int32)
    square = rest * rest
    sine = rest + rest * square * (
        -1.6666654611e-1 + square * (8.3321608736e-3 - square * 1.9515295891e-4)
    )
    cosine = (
        1.0
        - 0.5 * square
        + square
        * square
        * (
            4.166664568298827e-2
            + square * (-1.388731625493765e-3 + square * 2.443315711809948e-5)
        )
    )
    odd = (quarter & 1) == 1
    out_cos = jnp.where(odd, sine, cosine)
    out_sin = jnp.where(odd, cosine, sine)
    out_cos = jnp.where(((quarter + 1) & 2) == 2, -out_cos, out_cos)
    out_sin = jnp.where((quarter & 2) == 2, -out_sin, out_sin)
    return out_cos, out_sin


def grow(value):
    series = 1.0
    for term in range(9, 1, -1):
        series = 1.0 + series * value * (1.0 / term)
    return jnp.where(jnp.abs(value) < 0.35, series * value, jnp.exp(value) - 1.0)


def power(rate_real, rate_imag, offset):
    size = jnp.exp(rate_real * offset)
    cosine, sine = cos_sin(rate_imag * offset)
    return size * cosine, size * sine


def times(left, right):
    return (
        left[0] * right[0] - left[1] * right[1],
        left[0] * right[1] + left[1] * right[0],
    )


def weighted_sum(terms):
    total = None
    for weight, value in terms:
        if abs(weight) < 1e-12:
            continue
        if abs(abs(weight) - 1.0) < 1e-12:
            term = value if weight > 0 else -value
        else:
            term = value * weight
        total = term if total is None else total + term
    return total


def turn(count, width):
    angle = two_pi * (count % width) / width
    return math.cos(angle), math.sin(angle)


def precise_dot(value, matrix):
    high, low = split_halves(value)
    dot = functools.partial(jnp.dot, preferred_element_type=jnp.float32)
    return dot(high, matrix[0]) + dot(low, matrix[0]) + dot(high, matrix[1])


def transform_tables(owners, length):
    width = 2 * owners
    counter = np.arange(length)
    angles = two_pi * (counter[:, None] * counter[None, :] % length) / length
    cosine, sine = np.cos(angles), np.sin(angles)
    matrix = np.block([[cosine, -sine], [sine, cosine]]).astype(np.float32)
    high = matrix.astype(jnp.bfloat16)
    low = (matrix - high.astype(np.float32)).astype(jnp.bfloat16)
    outer = np.arange(owners + 1)
    angles = two_pi * (outer[:, None] * counter[None, :]) / (width * length)
    twiddle = np.stack([np.cos(angles), -np.sin(angles)], axis=1).astype(np.float32)
    return np.stack([high, low]), twiddle


def three_pieces(value):
    pieces = []
    for _ in range(3):
        piece = value.astype(jnp.bfloat16).astype(jnp.float32)
        pieces.append(piece)
        value = value - piece
    return pieces


def transposed(value):
    return jnp.concatenate(
        [value[:, spot : spot + LANES].T for spot in range(0, value.shape[1], LANES)], axis=0
    )


READ, STEP, ROWS = 16, 19, 20
LAGS, GRADS, STATE, SINGLES = 0, 8, 16, 18
STEP_LANES, SCALE_LANES = (0, 8), (16, 17, 18, 19)


def pack_kernel(inputs, out_grad, readout, log_step, out, signals, read, step, turned, rows, sems):
    peers = out.shape[0] // ROWS
    copies = [
        pltpu.make_async_copy(source, target, sems.at[i])
        for i, (source, target) in enumerate(
            ((readout, read), (log_step, step), (inputs, signals.at[0]), (out_grad, signals.at[1]))
        )
    ]
    for copy in copies:
        copy.start()
    copies[0].wait()
    copies[1].wait()
    own = lax.axis_index("seq")
    turned[0] = transposed(read[...])
    turned[1] = transposed(jnp.broadcast_to(step[...], (LANES, step.shape[1])))
    for place, value in enumerate(
        three_pieces(turned[0, pl.ds(own, peers, stride=SUBLANES), :])
    ):
        rows[pl.ds(READ + place, peers, stride=ROWS), :] = value
    pieces = three_pieces(turned[1, pl.ds(own, peers, stride=SUBLANES), :])
    lane = lax.broadcasted_iota(jnp.int32, (peers, LANES), 1)
    value = jnp.where(lane == 0, pieces[0], jnp.where(lane == 1, pieces[1], pieces[2]))
    rows[pl.ds(STEP, peers, stride=ROWS), :] = value
    for place in range(2):
        copies[2 + place].wait()
        value = signals[place].astype(jnp.float32)
        for peer in range(peers):
            spot = peer * ROWS + place * SUBLANES
            rows[spot : spot + SUBLANES] = value[peer * SUBLANES : (peer + 1) * SUBLANES]
    out[...] = rows[...].astype(jnp.bfloat16)


def hold_kernel(*refs):
    for source, target in zip(refs[: len(refs) // 2], refs[len(refs) // 2 :]):
        target[...] = source[...]


def scaled(value):
    most = jnp.max(jnp.max(jnp.abs(value), axis=1, keepdims=True), axis=0, keepdims=True)
    exponent = jnp.floor(jnp.log(jnp.maximum(most, 1e-30)) * (1.0 / math.log(2.0))) + 1.0
    return value * jnp.exp2(-exponent), exponent


def two_pieces(value):
    high = value.astype(jnp.bfloat16).astype(jnp.float32)
    return high, (value - high) * 256.0


def main_kernel(
    owners, norm_scale, got, matrix, twiddle, decay_log, rotation, sent, rows_in, lags, powers, sums
):
    peers, length = got.shape[0] // ROWS, got.shape[1]
    groups = peers // owners
    part_count = groups * SUBLANES
    rows = 2 * part_count
    width = 2 * owners
    pairs = part_count // 2
    half = pairs // SUBLANES
    rows_in[...] = got[...].astype(jnp.float32)

    def collect(spot):
        tiles = [
            rows_in[pl.ds(group * ROWS + spot, owners, stride=groups * ROWS), :]
            for group in range(groups)
        ]
        return jnp.concatenate(tiles[:half], axis=0), jnp.concatenate(tiles[half:], axis=0)

    lane = lax.broadcasted_iota(jnp.int32, (pairs, LANES), 1)
    left = lane < LANES // 2

    def swap(value):
        return pltpu.roll(value, LANES // 2, 1)

    lower, upper = [sum(side) for side in zip(*(collect(READ + i) for i in range(3)))]
    read = (jnp.where(left, lower, swap(upper)), jnp.where(left, swap(lower), upper))
    lower, upper = [
        sum(side[:, i : i + 1] for i in range(3)) + jnp.zeros_like(side) for side in collect(STEP)
    ]
    step = jnp.exp(jnp.where(left, lower, upper))
    decay_row = jnp.concatenate([decay_log[...], decay_log[...]], axis=1)
    rotation_row = jnp.concatenate([rotation[...], rotation[...]], axis=1)
    pole = (
        jnp.broadcast_to(-jnp.exp(decay_row), step.shape),
        jnp.broadcast_to(rotation_row, step.shape),
    )
    rate = (step * pole[0], step * pole[1])

    row = lax.broadcasted_iota(jnp.int32, (SUBLANES, LANES), 0).astype(jnp.float32)
    doublings = []
    size = SUBLANES
    while size < length:
        doublings.append(size)
        size *= 2
    jumps = jnp.zeros((SUBLANES, LANES), jnp.float32)
    for place, jump in enumerate(doublings):
        jumps = jnp.where(row == place, float(jump), jumps)
    bases = []
    for p in range(pairs):
        rate_real, rate_imag = rate[0][p : p + 1], rate[1][p : p + 1]
        shifts = power(rate_real, rate_imag, jumps)
        table = [power(rate_real, rate_imag, row)]
        for place in range(len(doublings)):
            shift = (shifts[0][place : place + 1], shifts[1][place : place + 1])
            table += [times(block, shift) for block in table]
        for place in range(0, len(table), 2):
            spot = place * SUBLANES
            for side in range(2):
                value = jnp.concatenate([table[place][side], table[place + 1][side]], axis=0)
                high, low = split_halves(value)
                lanes = slice(side * LANES, (side + 1) * LANES)
                powers[p, spot : spot + 2 * SUBLANES, lanes] = high
                powers[p, length + spot : length + spot + 2 * SUBLANES, lanes] = low
        bases.append(power(rate_real, rate_imag, row * float(length)))

    blocks = []
    for s in range(owners):
        spots = [(s * groups + group) * ROWS for group in range(groups)]
        blocks.append(
            jnp.concatenate(
                [rows_in[spot : spot + SUBLANES] for spot in spots]
                + [rows_in[spot + SUBLANES : spot + 2 * SUBLANES] for spot in spots],
                axis=0,
            )
        )
    spectra = []
    for k in range(owners + 1):
        real = weighted_sum([(turn(k * s, width)[0], blocks[s]) for s in range(owners)])
        imag = weighted_sum([(-turn(k * s, width)[1], blocks[s]) for s in range(owners)])
        if imag is None:
            imag = jnp.zeros_like(real)
        if k:
            real, imag = times((real, imag), (twiddle[k, 0:1], twiddle[k, 1:2]))
        spectra.append(jnp.concatenate([real, imag], axis=1))
    freq = precise_dot(jnp.concatenate(spectra, axis=0), matrix)

    products = []
    for k in range(owners + 1):
        at_in = freq[k * rows : k * rows + part_count]
        at_out = freq[k * rows + part_count : (k + 1) * rows]
        ur, ui = at_in[:, :length], at_in[:, length:]
        gr, gi = at_out[:, :length], at_out[:, length:]
        products.append(jnp.concatenate([gr * ur + gi * ui, gr * ui - gi * ur], axis=1))
    back = precise_dot(jnp.concatenate(products, axis=0), matrix)

    turned = []
    for k in range(owners + 1):
        value = back[k * part_count : (k + 1) * part_count]
        value = (value[:, :length], value[:, length:])
        if k:
            value = times(value, (twiddle[k, 0:1], twiddle[k, 1:2]))
        turned.append(value)
    scale = norm_scale / (width * length)
    for b in range(owners):
        terms = []
        for k in range(owners + 1):
            weight = scale if k in (0, owners) else 2.0 * scale
            cosine, sine = turn(k * b, width)
            terms += [(weight * cosine, turned[k][0]), (weight * sine, turned[k][1])]
        lags[b * part_count : (b + 1) * part_count] = weighted_sum(terms)

    offset = lax.broadcasted_iota(jnp.int32, (owners, length), 1).astype(jnp.float32)
    start = row * float(length)
    first = left[:owners]
    for p in range(pairs):
        one = lags[pl.ds(p, owners, stride=part_count), :]
        two = lags[pl.ds(pairs + p, owners, stride=part_count), :]
        high, low = split_halves(
            jnp.concatenate([one, two, one * offset, two * offset], axis=0)
        )
        factor = jnp.concatenate(
            [
                jnp.concatenate([high, high], axis=1),
                jnp.concatenate([low, jnp.zeros_like(low)], axis=1),
            ],
            axis=0,
        )
        raw = jnp.dot(factor, powers[p], preferred_element_type=jnp.float32)
        raw = raw[: 4 * owners] + raw[4 * owners :]

        def pick(place, side):
            lanes = slice(side * LANES, (side + 1) * LANES)
            top = raw[2 * place * owners : (2 * place + 1) * owners, lanes]
            bottom = raw[(2 * place + 1) * owners : (2 * place + 2) * owners, lanes]
            return jnp.where(first, top, bottom)

        plain = (pick(0, 0), pick(0, 1))
        near = (start * plain[0] + pick(1, 0), start * plain[1] + pick(1, 1))
        for place, value in enumerate(times(bases[p], plain) + times(bases[p], near)):
            sums[place, p : p + 1] = jnp.sum(value, axis=0, keepdims=True)

    size = jnp.exp(rate[0])
    cosine, sine = cos_sin(rate[1])
    sine_half = cos_sin(0.5 * rate[1])[1]
    lift = (grow(rate[0]) * cosine - 2.0 * sine_half * sine_half, size * sine)
    norm = 1.0 / (pole[0] * pole[0] + pole[1] * pole[1])
    inverse = (pole[0] * norm, -pole[1] * norm)
    ratio = times(lift, inverse)
    coef = times(read, ratio)
    lifted = times((size * cosine, size * sine), inverse)
    total = (sums[0] * (2.0 * norm_scale), sums[1] * (2.0 * norm_scale))
    lag_total = (sums[2] * (2.0 * norm_scale), sums[3] * (2.0 * norm_scale))
    on_read = times(total, ratio)
    on_read = (on_read[0], -on_read[1])
    on_rate = times(coef, lag_total)
    through = times(times(total, read), lifted)
    on_rate = (on_rate[0] + through[0], on_rate[1] + through[1])
    direct = times(times(total, coef), inverse)
    on_pole = (step * on_rate[0] - direct[0], step * on_rate[1] - direct[1])
    on_step = times(on_rate, rate)[0]
    on_decay = jnp.sum(on_pole[0] * pole[0], axis=0, keepdims=True)
    on_rotation = -jnp.sum(on_pole[1], axis=0, keepdims=True)
    on_decay = on_decay + swap(on_decay)
    on_rotation = on_rotation + swap(on_rotation)
    state, state_exponent = scaled(jnp.where(left[0:1], on_decay, on_rotation))

    lag_values, lag_exponent = scaled(lags[...])
    lower = jnp.where(left, on_read[0], swap(on_read[1]))
    upper = jnp.where(left, swap(on_read[0]), on_read[1])
    grads, grad_exponent = scaled(jnp.concatenate([lower, upper], axis=0))
    step_column = jnp.concatenate(
        [
            jnp.sum(jnp.where(left, on_step, 0.0), axis=1, keepdims=True),
            jnp.sum(jnp.where(left, 0.0, on_step), axis=1, keepdims=True),
        ],
        axis=0,
    )
    step_column, step_exponent = scaled(step_column)
    place_row = lax.broadcasted_iota(jnp.int32, (SUBLANES, LANES), 0)
    place_lane = lax.broadcasted_iota(jnp.int32, (SUBLANES, LANES), 1)
    scales = jnp.zeros((1, LANES), jnp.float32)
    for spot, value in zip(
        SCALE_LANES, (lag_exponent, grad_exponent, state_exponent, step_exponent)
    ):
        scales = jnp.where(place_lane[0:1] == spot, value, scales)
    state_high, state_low = two_pieces(state)
    tails = []
    for group in range(groups):
        pieces = two_pieces(step_column[group * SUBLANES : (group + 1) * SUBLANES])
        spread = jnp.zeros((SUBLANES, LANES), jnp.float32)
        for spot, piece in zip(STEP_LANES, pieces):
            spread = jnp.where(place_lane == place_row + spot, piece, spread)
        singles = scales + jnp.sum(spread, axis=0, keepdims=True)
        tails.append(jnp.concatenate([state_high, state_low, singles, singles], axis=0))
    for b in range(owners):
        for group in range(groups):
            spot = b * part_count + group * SUBLANES
            place = (b * groups + group) * ROWS
            sent[place + LAGS : place + GRADS] = lag_values[spot : spot + SUBLANES]
            sent[place + GRADS : place + STATE] = grads[group * SUBLANES : (group + 1) * SUBLANES]
            sent[place + STATE : place + ROWS] = tails[group]


def unpack_kernel(got, kernel_grad, readout_grad, step_grad, state_grad, grads):
    peers = got.shape[0] // ROWS
    singles = got[pl.ds(SINGLES, peers, stride=ROWS), :]
    scales = [jnp.exp2(singles[:, spot : spot + 1]) for spot in SCALE_LANES]
    for peer in range(peers):
        spot = peer * ROWS
        lanes = slice(peer * SUBLANES, (peer + 1) * SUBLANES)
        kernel_grad[lanes] = got[spot + LAGS : spot + GRADS] * scales[0][peer : peer + 1]
        grads[lanes] = got[spot + GRADS : spot + STATE] * scales[1][peer : peer + 1]
    for spot in range(0, peers * SUBLANES, LANES):
        readout_grad[:, spot : spot + LANES] = grads[spot : spot + LANES].T
    high = got[pl.ds(STATE, peers, stride=ROWS), :]
    low = got[pl.ds(STATE + 1, peers, stride=ROWS), :]
    state = jnp.sum((high + low * (1.0 / 256.0)) * scales[2], axis=0, keepdims=True)
    states = state_grad.shape[1]
    state_grad[0:1] = state[:, :states]
    state_grad[1:2] = state[:, states:]
    per_row = LANES // SUBLANES
    lane = lax.broadcasted_iota(jnp.int32, (peers, LANES), 1)
    row = lax.broadcasted_iota(jnp.int32, (peers, LANES), 0)
    steps = pltpu.roll(singles, LANES - STEP_LANES[1], 1) * (1.0 / 256.0) + singles
    steps = jnp.where(lane < SUBLANES, steps * scales[3], 0.0)
    reach = SUBLANES
    while reach < LANES:
        steps = steps + pltpu.roll(steps, reach, 1)
        reach *= 2
    for spot in range(0, peers, per_row):
        mine = jnp.where(row - spot == lane // SUBLANES, steps, 0.0)
        step_grad[spot * SUBLANES : (spot + per_row) * SUBLANES] = jnp.sum(mine, axis=0)


def kernel_device(inputs, out_grad, readout, log_step, decay_log, rotation):
    owners, groups = lax.axis_size("seq"), lax.axis_size("ch")
    peers = owners * groups
    channels, length = inputs.shape
    states = decay_log.shape[0]
    part_count = channels // owners
    pairs = part_count // 2
    norm_scale = 1.0 / math.sqrt(owners * length)
    vmem = pl.BlockSpec(memory_space=pltpu.VMEM)
    memory = pltpu.CompilerParams(vmem_limit_bytes=32 * 1024 * 1024)
    f32, bf16 = jnp.float32, jnp.bfloat16

    def exchange(value):
        value = value.reshape(peers, ROWS // 2, 2, LANES)
        value = lax.all_to_all(value, ("seq", "ch"), split_axis=0, concat_axis=0, tiled=True)
        return value.reshape(peers * ROWS, LANES)

    anywhere = pl.BlockSpec(memory_space=pl.ANY)
    pieces = pl.pallas_call(
        pack_kernel,
        out_shape=jax.ShapeDtypeStruct((peers * ROWS, LANES), bf16),
        in_specs=[anywhere] * 4,
        out_specs=vmem,
        scratch_shapes=[
            pltpu.VMEM((2, channels, LANES), bf16),
            pltpu.VMEM((LANES, channels), f32),
            pltpu.VMEM((1, channels), f32),
            pltpu.VMEM((2, channels, LANES), f32),
            pltpu.VMEM((peers * ROWS, LANES), f32),
            pltpu.SemaphoreType.DMA((4,)),
        ],
        compiler_params=pltpu.CompilerParams(vmem_limit_bytes=60 * 1024 * 1024),
    )(inputs, out_grad, readout.transpose(0, 2, 1).reshape(LANES, channels), log_step[None])
    got = exchange(pieces)

    held = [jnp.asarray(table) for table in transform_tables(owners, length)]
    held += [decay_log[None], rotation[None]]
    held = pl.pallas_call(
        hold_kernel,
        out_shape=[jax.ShapeDtypeStruct(value.shape, value.dtype) for value in held],
        in_specs=[vmem] * 4,
        out_specs=[vmem] * 4,
        compiler_params=memory,
    )(*held)
    sent = pl.pallas_call(
        functools.partial(main_kernel, owners, norm_scale),
        out_shape=jax.ShapeDtypeStruct((peers * ROWS, LANES), f32),
        in_specs=[vmem] * 5,
        out_specs=vmem,
        scratch_shapes=[
            pltpu.VMEM((peers * ROWS, LANES), f32),
            pltpu.VMEM((owners * part_count, length), f32),
            pltpu.VMEM((pairs, 2 * length, 2 * LANES), bf16),
            pltpu.VMEM((4, pairs, LANES), f32),
        ],
        compiler_params=memory,
    )(got, *held)
    back = exchange(sent.astype(jnp.float16))
    kernel_grad, readout_grad, step_grad, state_grad = pl.pallas_call(
        unpack_kernel,
        out_shape=[
            jax.ShapeDtypeStruct((channels, length), f32),
            jax.ShapeDtypeStruct((LANES, channels), f32),
            jax.ShapeDtypeStruct((channels,), f32),
            jax.ShapeDtypeStruct((2, states), f32),
        ],
        in_specs=[vmem],
        out_specs=[vmem] * 4,
        scratch_shapes=[pltpu.VMEM((channels, LANES), f32)],
        compiler_params=memory,
    )(back.astype(f32))
    readout_grad = readout_grad.reshape(2, states, channels).transpose(0, 2, 1)
    return kernel_grad, readout_grad, step_grad, state_grad


def kernel_fits(mesh, inputs, decay_log):
    owners, groups = mesh.shape["seq"], mesh.shape["ch"]
    channels = inputs.shape[0] // groups
    return (
        inputs.shape[1] == owners * LANES
        and 2 * decay_log.shape[0] == LANES
        and owners == SUBLANES
        and groups % 2 == 0
        and channels == owners * groups * SUBLANES
        and channels % LANES == 0
    )


def solution(mesh):
    def whole(inputs, out_grad, readout, log_step, decay_log, rotation):
        fits = kernel_fits(mesh, inputs, decay_log)
        return jax.shard_map(
            kernel_device if fits else general_device,
            mesh=mesh,
            in_specs=(P("ch", "seq"), P("ch", "seq"), P(None, "ch", None), P("ch"), P(), P()),
            out_specs=(P("ch", "seq"), P(None, "ch", None), P("ch"), P()),
            check_vma=False,
        )(inputs, out_grad, readout, log_step, decay_log, rotation)

    return whole
```

```python
import functools
import math

import jax
import jax.numpy as jnp
import numpy as np
from jax import lax
from jax.experimental import pallas as pl
from jax.experimental.pallas import tpu as pltpu
from jax.sharding import PartitionSpec as P

precise = lax.Precision.HIGHEST
two_pi = 2.0 * math.pi
LANES = 128
SUBLANES = 8


def angle_table(left_index, right_index, modulus, orient):
    product = left_index[:, None] * right_index[None, :] % modulus
    return orient * two_pi * product.astype(jnp.float32) / modulus


def rotate(real_part, imag_part, angles):
    cosine_table = jnp.cos(angles)
    sine_table = jnp.sin(angles)
    return (
        real_part * cosine_table - imag_part * sine_table,
        real_part * sine_table + imag_part * cosine_table,
    )


def last_transform(real_part, imag_part, orient):
    length = real_part.shape[-1]
    counter = jnp.arange(length, dtype=jnp.int32)
    angles = angle_table(counter, counter, length, orient)
    cosine_table = jnp.cos(angles)
    sine_table = jnp.sin(angles)
    dot = functools.partial(jnp.dot, precision=precise, preferred_element_type=jnp.float32)
    return (
        dot(real_part, cosine_table) - dot(imag_part, sine_table),
        dot(imag_part, cosine_table) + dot(real_part, sine_table),
    )


def discretize(readout, log_step, decay_log, rotation):
    step_size = jnp.exp(log_step)[:, None]
    pole_real = -jnp.exp(decay_log)[None, :]
    pole_imag = rotation[None, :]
    rate_real = step_size * pole_real
    rate_imag = step_size * pole_imag
    lift_real = jnp.expm1(rate_real) * jnp.cos(rate_imag) - 2.0 * jnp.sin(0.5 * rate_imag) ** 2
    lift_imag = jnp.exp(rate_real) * jnp.sin(rate_imag)
    pole_norm = pole_real * pole_real + pole_imag * pole_imag
    ratio_real = (lift_real * pole_real + lift_imag * pole_imag) / pole_norm
    ratio_imag = (lift_imag * pole_real - lift_real * pole_imag) / pole_norm
    coef_real = readout[0] * ratio_real - readout[1] * ratio_imag
    coef_imag = readout[0] * ratio_imag + readout[1] * ratio_real
    return (coef_real, coef_imag, rate_real, rate_imag)


def parameter_grads(primal, backward, totals):
    coef_real, coef_imag = (primal[0], primal[1])
    cotangents = (
        2.0 * totals[0],
        -2.0 * totals[1],
        2.0 * (coef_real * totals[2] - coef_imag * totals[3]),
        -2.0 * (coef_real * totals[3] + coef_imag * totals[2]),
    )
    return backward(cotangents)


def shifted_totals(raw_sums, rate_real, rate_imag, block_start, norm_scale):
    decays = jnp.exp(rate_real * block_start)
    phases = rate_imag * block_start
    base_real = decays * jnp.cos(phases)
    base_imag = decays * jnp.sin(phases)
    near_real = block_start * raw_sums[0] + raw_sums[2]
    near_imag = block_start * raw_sums[1] + raw_sums[3]
    return jnp.stack(
        [
            norm_scale * (base_real * raw_sums[0] - base_imag * raw_sums[1]),
            norm_scale * (base_real * raw_sums[1] + base_imag * raw_sums[0]),
            norm_scale * (base_real * near_real - base_imag * near_imag),
            norm_scale * (base_real * near_imag + base_imag * near_real),
        ]
    )


def whole_channel_totals(lag_rows, rate_real, rate_imag, norm_scale):
    owners, length = (lag_rows.shape[1], lag_rows.shape[2])
    offsets = jnp.arange(length, dtype=jnp.int32).astype(jnp.float32)
    decays = jnp.exp(rate_real[:, :, None] * offsets)
    phases = rate_imag[:, :, None] * offsets
    power_real = decays * jnp.cos(phases)
    power_imag = decays * jnp.sin(phases)
    weighted = lag_rows * offsets
    raw_sums = jnp.stack(
        [
            jnp.einsum("cbj,cnj->cnb", lag_rows, power_real, precision=precise),
            jnp.einsum("cbj,cnj->cnb", lag_rows, power_imag, precision=precise),
            jnp.einsum("cbj,cnj->cnb", weighted, power_real, precision=precise),
            jnp.einsum("cbj,cnj->cnb", weighted, power_imag, precision=precise),
        ]
    )
    starts = (jnp.arange(owners, dtype=jnp.int32) * length).astype(jnp.float32)
    totals = shifted_totals(
        raw_sums, rate_real[:, :, None], rate_imag[:, :, None], starts, norm_scale
    )
    return jnp.sum(totals, axis=-1)


def general_lags(whole, norm_scale):
    part_count, owners, length = whole.shape[1:]
    freq_width = 2 * owners
    modulus = freq_width * length
    row_index = jnp.arange(owners, dtype=jnp.int32)
    outer_index = jnp.arange(freq_width, dtype=jnp.int32)
    inner_index = jnp.arange(length, dtype=jnp.int32)
    first = angle_table(row_index, outer_index, freq_width, -1.0)
    spec_real = jnp.einsum("scba,bk->scka", whole, jnp.cos(first), precision=precise)
    spec_imag = jnp.einsum("scba,bk->scka", whole, jnp.sin(first), precision=precise)
    spec_real, spec_imag = rotate(
        spec_real, spec_imag, angle_table(outer_index, inner_index, modulus, -1.0)
    )
    freq_real, freq_imag = last_transform(spec_real, spec_imag, -1.0)
    prod_real = freq_real[1] * freq_real[0] + freq_imag[1] * freq_imag[0]
    prod_imag = freq_imag[1] * freq_real[0] - freq_real[1] * freq_imag[0]
    back_real, back_imag = last_transform(prod_real, prod_imag, 1.0)
    back_real, back_imag = rotate(
        back_real, back_imag, angle_table(outer_index, inner_index, modulus, 1.0)
    )
    final = angle_table(outer_index, row_index, freq_width, 1.0)
    lag_rows = jnp.einsum("cka,kb->cba", back_real, jnp.cos(final), precision=precise) - jnp.einsum(
        "cka,kb->cba", back_imag, jnp.sin(final), precision=precise
    )
    return lag_rows * (norm_scale / modulus)


def general_device(inputs, out_grad, readout, log_step, decay_log, rotation):
    owners = lax.axis_size("seq")
    channels, length = inputs.shape
    states = decay_log.shape[0]
    part_count = channels // owners
    norm_scale = 1.0 / math.sqrt(owners * length)
    pieces = jnp.concatenate(
        [a.reshape(owners, part_count, length) for a in (inputs, out_grad)], axis=1
    )
    pieces = lax.all_to_all(pieces, "seq", split_axis=0, concat_axis=0, tiled=True)
    whole = pieces.astype(jnp.float32).reshape(owners, 2, part_count, length)
    lag_rows = general_lags(whole.transpose(1, 2, 0, 3), norm_scale)
    first_channel = lax.axis_index("seq") * part_count
    own_readout = lax.dynamic_slice_in_dim(readout, first_channel, part_count, 1)
    own_step = lax.dynamic_slice_in_dim(log_step, first_channel, part_count, 0)
    primal, backward = jax.vjp(discretize, own_readout, own_step, decay_log, rotation)
    totals = whole_channel_totals(lag_rows, primal[2], primal[3], norm_scale)
    readout_part, step_part, decay_part, rotation_part = parameter_grads(primal, backward, totals)
    shared = jnp.concatenate(
        [readout_part.reshape(-1), step_part, decay_part, rotation_part]
    )
    sent = jnp.concatenate(
        [
            lag_rows.transpose(1, 0, 2).reshape(owners, -1),
            jnp.broadcast_to(shared, (owners, shared.shape[0])),
        ],
        axis=1,
    )
    got = lax.all_to_all(sent, "seq", split_axis=0, concat_axis=0, tiled=True)
    cuts = np.cumsum([part_count * length, 2 * part_count * states, part_count])
    lags, readouts, steps, state = jnp.split(got, cuts, axis=1)
    readouts = readouts.reshape(owners, 2, part_count, states).transpose(1, 0, 2, 3)
    return (
        lags.reshape(channels, length),
        readouts.reshape(2, channels, states),
        steps.reshape(channels),
        lax.psum(jnp.sum(state, axis=0), "ch").reshape(2, states),
    )


def split_halves(value):
    high = value.astype(jnp.bfloat16)
    return high, (value - high.astype(jnp.float32)).astype(jnp.bfloat16)


def cos_sin(angle):
    turns = jnp.floor(angle * (2.0 / math.pi) + 0.5)
    rest = angle - turns * 1.5703125
    rest = rest - turns * 4.837512969970703125e-4
    rest = rest - turns * 7.54978995489188216e-8
    quarter = turns.astype(jnp.int32)
    square = rest * rest
    sine = rest + rest * square * (
        -1.6666654611e-1 + square * (8.3321608736e-3 - square * 1.9515295891e-4)
    )
    cosine = (
        1.0
        - 0.5 * square
        + square
        * square
        * (
            4.166664568298827e-2
            + square * (-1.388731625493765e-3 + square * 2.443315711809948e-5)
        )
    )
    odd = (quarter & 1) == 1
    out_cos = jnp.where(odd, sine, cosine)
    out_sin = jnp.where(odd, cosine, sine)
    out_cos = jnp.where(((quarter + 1) & 2) == 2, -out_cos, out_cos)
    out_sin = jnp.where((quarter & 2) == 2, -out_sin, out_sin)
    return out_cos, out_sin


def grow(value):
    series = 1.0
    for term in range(9, 1, -1):
        series = 1.0 + series * value * (1.0 / term)
    return jnp.where(jnp.abs(value) < 0.35, series * value, jnp.exp(value) - 1.0)


def power(rate_real, rate_imag, offset):
    size = jnp.exp(rate_real * offset)
    cosine, sine = cos_sin(rate_imag * offset)
    return size * cosine, size * sine


def times(left, right):
    return (
        left[0] * right[0] - left[1] * right[1],
        left[0] * right[1] + left[1] * right[0],
    )


def blocks_forward(x):
    root = math.sqrt(0.5)
    cosine, sine = math.cos(math.pi / 8), math.sin(math.pi / 8)
    total = [x[s] + x[s + 4] for s in range(4)]
    gap = [x[s] - x[s + 4] for s in range(4)]
    even, odd = total[0] + total[2], total[1] + total[3]
    real, imag = [None] * 9, [None] * 9
    real[0], real[8] = even + odd, even - odd
    imag[0] = imag[8] = jnp.zeros_like(even)
    real[4], imag[4] = total[0] - total[2], total[3] - total[1]
    less, more = root * (gap[1] - gap[3]), root * (gap[1] + gap[3])
    real[2], imag[2] = gap[0] + less, -gap[2] - more
    real[6], imag[6] = gap[0] - less, gap[2] - more
    less, more = root * (x[2] - x[6]), root * (x[2] + x[6])
    even1 = (x[0] + less, -x[4] - more)
    even3 = (x[0] - less, x[4] - more)
    p, q, r, t = x[1] - x[7], x[3] - x[5], x[1] + x[7], x[3] + x[5]
    odd1 = (cosine * p + sine * q, -sine * r - cosine * t)
    odd3 = (sine * p - cosine * q, sine * t - cosine * r)
    real[1], imag[1] = even1[0] + odd1[0], even1[1] + odd1[1]
    real[7], imag[7] = even1[0] - odd1[0], odd1[1] - even1[1]
    real[3], imag[3] = even3[0] + odd3[0], even3[1] + odd3[1]
    real[5], imag[5] = even3[0] - odd3[0], odd3[1] - even3[1]
    return list(zip(real, imag))


def blocks_back(z):
    root = math.sqrt(0.5)
    cosine, sine = math.cos(math.pi / 8), math.sin(math.pi / 8)
    real, imag = [v[0] for v in z], [v[1] for v in z]
    even, odd = real[0] + real[8], real[0] - real[8]
    total = [even + real[4], odd + imag[4], even - real[4], odd - imag[4]]
    less, more = root * (real[2] - real[6]), root * (imag[2] + imag[6])
    gap = [real[2] + real[6], less + more, imag[2] - imag[6], more - less]
    x = [total[s] + gap[s] for s in range(4)] + [total[s] - gap[s] for s in range(4)]
    even1 = (real[1] + real[7], imag[7] - imag[1])
    even3 = (real[3] + real[5], imag[5] - imag[3])
    odd1 = (real[1] - real[7], imag[1] + imag[7])
    odd3 = (real[3] - real[5], imag[3] + imag[5])
    less, more = root * (even1[0] - even3[0]), root * (even1[1] + even3[1])
    p = cosine * odd1[0] + sine * odd3[0]
    q = sine * odd1[0] - cosine * odd3[0]
    r = sine * odd1[1] + cosine * odd3[1]
    t = cosine * odd1[1] - sine * odd3[1]
    extra = [
        even1[0] + even3[0],
        p + r,
        less - more,
        q + t,
        even3[1] - even1[1],
        t - q,
        -less - more,
        r - p,
    ]
    return [v + w for v, w in zip(x, extra)]


def precise_dot(value, matrix):
    high, low = split_halves(value)
    dot = functools.partial(jnp.dot, preferred_element_type=jnp.float32)
    return dot(high, matrix[0]) + dot(low, matrix[0]) + dot(high, matrix[1])


def transform_tables(owners, length, norm_scale):
    width = 2 * owners
    counter = np.arange(length)
    angles = two_pi * (counter[:, None] * counter[None, :] % length) / length
    cosine, sine = np.cos(angles), np.sin(angles)
    matrix = np.block([[cosine, -sine], [sine, cosine]]).astype(np.float32)
    high = matrix.astype(jnp.bfloat16)
    low = (matrix - high.astype(np.float32)).astype(jnp.bfloat16)
    outer = np.arange(owners + 1)
    angles = two_pi * (outer[:, None] * counter[None, :]) / (width * length)
    twiddle = np.stack([np.cos(angles), -np.sin(angles)], axis=1)
    weight = np.where(outer % owners == 0, 1.0, 2.0) * norm_scale / (width * length)
    twiddle = np.concatenate([twiddle, twiddle * weight[:, None, None]], axis=1)
    return np.stack([high, low]), twiddle.astype(np.float32)


def three_pieces(value):
    pieces = []
    for _ in range(3):
        piece = value.astype(jnp.bfloat16).astype(jnp.float32)
        pieces.append(piece)
        value = value - piece
    return pieces


def transposed(value):
    return jnp.concatenate(
        [value[:, spot : spot + LANES].T for spot in range(0, value.shape[1], LANES)], axis=0
    )


READ, STEP, ROWS = 16, 19, 20
LAGS, GRADS, STATE, SINGLES = 0, 8, 16, 18
STEP_LANES, SCALE_LANES = (0, 8), (16, 17, 18, 19)


def pack_kernel(inputs, out_grad, readout, log_step, out, signals, read, step, turned, rows, sems):
    peers = out.shape[0] // ROWS
    copies = [
        pltpu.make_async_copy(source, target, sems.at[i])
        for i, (source, target) in enumerate(
            ((readout, read), (log_step, step), (inputs, signals.at[0]), (out_grad, signals.at[1]))
        )
    ]
    for copy in copies:
        copy.start()
    copies[0].wait()
    copies[1].wait()
    own = lax.axis_index("seq")
    turned[0] = transposed(read[...])
    turned[1] = transposed(jnp.broadcast_to(step[...], (LANES, step.shape[1])))
    for place, value in enumerate(
        three_pieces(turned[0, pl.ds(own, peers, stride=SUBLANES), :])
    ):
        rows[pl.ds(READ + place, peers, stride=ROWS), :] = value
    pieces = three_pieces(turned[1, pl.ds(own, peers, stride=SUBLANES), :])
    lane = lax.broadcasted_iota(jnp.int32, (peers, LANES), 1)
    value = jnp.where(lane == 0, pieces[0], jnp.where(lane == 1, pieces[1], pieces[2]))
    rows[pl.ds(STEP, peers, stride=ROWS), :] = value
    for place in range(2):
        copies[2 + place].wait()
        value = signals[place].astype(jnp.float32)
        for peer in range(peers):
            spot = peer * ROWS + place * SUBLANES
            rows[spot : spot + SUBLANES] = value[peer * SUBLANES : (peer + 1) * SUBLANES]
    out[...] = rows[...].astype(jnp.bfloat16)


def hold_kernel(*refs):
    for source, target in zip(refs[: len(refs) // 2], refs[len(refs) // 2 :]):
        target[...] = source[...]


def scaled(value):
    most = jnp.max(jnp.max(jnp.abs(value), axis=1, keepdims=True), axis=0, keepdims=True)
    exponent = jnp.floor(jnp.log(jnp.maximum(most, 1e-30)) * (1.0 / math.log(2.0))) + 1.0
    return value * jnp.exp2(-exponent), exponent


def two_pieces(value):
    high = value.astype(jnp.bfloat16).astype(jnp.float32)
    return high, (value - high) * 256.0


def main_kernel(
    owners, norm_scale, got, matrix, twiddle, decay_log, rotation, sent, rows_in, lags, powers, sums
):
    peers, length = got.shape[0] // ROWS, got.shape[1]
    groups = peers // owners
    part_count = groups * SUBLANES
    rows = 2 * part_count
    pairs = part_count // 2
    half = pairs // SUBLANES
    rows_in[...] = got[...].astype(jnp.float32)

    def collect(spot):
        tiles = [
            rows_in[pl.ds(group * ROWS + spot, owners, stride=groups * ROWS), :]
            for group in range(groups)
        ]
        return jnp.concatenate(tiles[:half], axis=0), jnp.concatenate(tiles[half:], axis=0)

    lane = lax.broadcasted_iota(jnp.int32, (pairs, LANES), 1)
    left = lane < LANES // 2

    def swap(value):
        return pltpu.roll(value, LANES // 2, 1)

    lower, upper = [sum(side) for side in zip(*(collect(READ + i) for i in range(3)))]
    read = (jnp.where(left, lower, swap(upper)), jnp.where(left, swap(lower), upper))
    lower, upper = [
        sum(side[:, i : i + 1] for i in range(3)) + jnp.zeros_like(side) for side in collect(STEP)
    ]
    step = jnp.exp(jnp.where(left, lower, upper))
    decay_row = jnp.concatenate([decay_log[...], decay_log[...]], axis=1)
    rotation_row = jnp.concatenate([rotation[...], rotation[...]], axis=1)
    pole = (
        jnp.broadcast_to(-jnp.exp(decay_row), step.shape),
        jnp.broadcast_to(rotation_row, step.shape),
    )
    rate = (step * pole[0], step * pole[1])

    reach = length // 2
    row = lax.broadcasted_iota(jnp.int32, (SUBLANES, LANES), 0)
    doubled = []
    size = 1
    while size < owners * length:
        doubled.append(power(rate[0], rate[1], float(size)))
        size *= 2
    block_bit, reach_bit = length.bit_length() - 1, reach.bit_length() - 1
    bits = [(row & (1 << i)) != 0 for i in range(SUBLANES.bit_length() - 1)]

    def by_rows(p, first):
        out = None
        for i, bit in enumerate(bits):
            real, imag = (side[p : p + 1] for side in doubled[first + i])
            value = (jnp.where(bit, real, 1.0), jnp.where(bit, imag, 0.0))
            out = value if out is None else times(out, value)
        return out

    bases = []
    for p in range(pairs):
        table = [by_rows(p, 0)]
        for i in range(len(bits), reach_bit):
            shift = tuple(side[p : p + 1] for side in doubled[i])
            table += [times(block, shift) for block in table]
        for place in range(0, len(table), 2):
            spot = place * SUBLANES
            for side in range(2):
                value = jnp.concatenate([table[place][side], table[place + 1][side]], axis=0)
                high, low = split_halves(value)
                lanes = slice(side * LANES, (side + 1) * LANES)
                powers[p, spot : spot + 2 * SUBLANES, lanes] = high
                powers[p, reach + spot : reach + spot + 2 * SUBLANES, lanes] = low
        base = by_rows(p, block_bit)
        bases.append((base, times(base, tuple(side[p : p + 1] for side in doubled[reach_bit]))))

    blocks = []
    for s in range(owners):
        spots = [(s * groups + group) * ROWS for group in range(groups)]
        blocks.append(
            jnp.concatenate(
                [rows_in[spot : spot + SUBLANES] for spot in spots]
                + [rows_in[spot + SUBLANES : spot + 2 * SUBLANES] for spot in spots],
                axis=0,
            )
        )
    spectra = []
    for k, value in enumerate(blocks_forward(blocks)):
        if k:
            value = times(value, (twiddle[k, 0:1], twiddle[k, 1:2]))
        spectra.append(jnp.concatenate(value, axis=1))
    freq = precise_dot(jnp.concatenate(spectra, axis=0), matrix)

    products = []
    for k in range(owners + 1):
        at_in = freq[k * rows : k * rows + part_count]
        at_out = freq[k * rows + part_count : (k + 1) * rows]
        ur, ui = at_in[:, :length], at_in[:, length:]
        gr, gi = at_out[:, :length], at_out[:, length:]
        products.append(jnp.concatenate([gr * ur + gi * ui, gr * ui - gi * ur], axis=1))
    back = precise_dot(jnp.concatenate(products, axis=0), matrix)

    turned = []
    for k in range(owners + 1):
        value = back[k * part_count : (k + 1) * part_count]
        value = (value[:, :length], value[:, length:])
        turned.append(times(value, (twiddle[k, 2:3], twiddle[k, 3:4])))
    for b, value in enumerate(blocks_back(turned)):
        lags[b * part_count : (b + 1) * part_count] = value

    lane = lax.broadcasted_iota(jnp.int32, (4 * owners, LANES), 1)
    left_rows = lane < reach
    left_both = left_rows[: 2 * owners]
    offset = jnp.where(left_rows, lane, lane - reach).astype(jnp.float32)
    start = row.astype(jnp.float32) * float(length)
    first = left[:owners]
    for p in range(pairs):
        one = lags[pl.ds(p, owners, stride=part_count), :]
        two = lags[pl.ds(pairs + p, owners, stride=part_count), :]
        both = jnp.concatenate([one, two], axis=0)
        turned_both = pltpu.roll(both, reach, 1)
        plain = jnp.concatenate(
            [jnp.where(left_both, both, turned_both), jnp.where(left_both, turned_both, both)], axis=0
        )
        factors = []
        for value in (plain, plain * offset):
            high = value.astype(jnp.bfloat16)
            low = jnp.where(left_rows, value - high.astype(jnp.float32), 0.0)
            factors.append((high, low.astype(jnp.bfloat16)))
        factor = jnp.concatenate([factors[i][j] for j in range(2) for i in range(2)], axis=0)
        raw = jnp.dot(factor, powers[p], preferred_element_type=jnp.float32)
        raw = raw[: 8 * owners] + raw[8 * owners :]

        def pick(place, side):
            lanes = slice(side * LANES, (side + 1) * LANES)
            top = raw[2 * place * owners : (2 * place + 1) * owners, lanes]
            bottom = raw[(2 * place + 1) * owners : (2 * place + 2) * owners, lanes]
            return jnp.where(first, top, bottom)

        found = [0.0] * 4
        for part, base in enumerate(bases[p]):
            near = start + float(part * reach)
            value = (pick(part, 0), pick(part, 1))
            lagged = (near * value[0] + pick(2 + part, 0), near * value[1] + pick(2 + part, 1))
            found = [x + y for x, y in zip(found, times(base, value) + times(base, lagged))]
        for place, value in enumerate(found):
            sums[place, p : p + 1] = jnp.sum(value, axis=0, keepdims=True)

    sine_half = cos_sin(0.5 * rate[1])[1]
    cosine = 1.0 - 2.0 * sine_half * sine_half
    lift = (grow(rate[0]) * cosine - 2.0 * sine_half * sine_half, doubled[0][1])
    norm = 1.0 / (pole[0] * pole[0] + pole[1] * pole[1])
    inverse = (pole[0] * norm, -pole[1] * norm)
    ratio = times(lift, inverse)
    coef = times(read, ratio)
    lifted = times(doubled[0], inverse)
    total = (sums[0] * (2.0 * norm_scale), sums[1] * (2.0 * norm_scale))
    lag_total = (sums[2] * (2.0 * norm_scale), sums[3] * (2.0 * norm_scale))
    on_read = times(total, ratio)
    on_read = (on_read[0], -on_read[1])
    on_rate = times(coef, lag_total)
    through = times(times(total, read), lifted)
    on_rate = (on_rate[0] + through[0], on_rate[1] + through[1])
    direct = times(times(total, coef), inverse)
    on_pole = (step * on_rate[0] - direct[0], step * on_rate[1] - direct[1])
    on_step = times(on_rate, rate)[0]
    on_decay = jnp.sum(on_pole[0] * pole[0], axis=0, keepdims=True)
    on_rotation = -jnp.sum(on_pole[1], axis=0, keepdims=True)
    on_decay = on_decay + swap(on_decay)
    on_rotation = on_rotation + swap(on_rotation)
    state, state_exponent = scaled(jnp.where(left[0:1], on_decay, on_rotation))

    lag_values, lag_exponent = scaled(lags[...])
    lower = jnp.where(left, on_read[0], swap(on_read[1]))
    upper = jnp.where(left, swap(on_read[0]), on_read[1])
    grads, grad_exponent = scaled(jnp.concatenate([lower, upper], axis=0))
    step_column = jnp.concatenate(
        [
            jnp.sum(jnp.where(left, on_step, 0.0), axis=1, keepdims=True),
            jnp.sum(jnp.where(left, 0.0, on_step), axis=1, keepdims=True),
        ],
        axis=0,
    )
    step_column, step_exponent = scaled(step_column)
    place_row = lax.broadcasted_iota(jnp.int32, (SUBLANES, LANES), 0)
    place_lane = lax.broadcasted_iota(jnp.int32, (SUBLANES, LANES), 1)
    scales = jnp.zeros((1, LANES), jnp.float32)
    for spot, value in zip(
        SCALE_LANES, (lag_exponent, grad_exponent, state_exponent, step_exponent)
    ):
        scales = jnp.where(place_lane[0:1] == spot, value, scales)
    state_high, state_low = two_pieces(state)
    tails = []
    for group in range(groups):
        pieces = two_pieces(step_column[group * SUBLANES : (group + 1) * SUBLANES])
        spread = jnp.zeros((SUBLANES, LANES), jnp.float32)
        for spot, piece in zip(STEP_LANES, pieces):
            spread = jnp.where(place_lane == place_row + spot, piece, spread)
        singles = scales + jnp.sum(spread, axis=0, keepdims=True)
        tails.append(jnp.concatenate([state_high, state_low, singles, singles], axis=0))
    for b in range(owners):
        for group in range(groups):
            spot = b * part_count + group * SUBLANES
            place = (b * groups + group) * ROWS
            sent[place + LAGS : place + GRADS] = lag_values[spot : spot + SUBLANES]
            sent[place + GRADS : place + STATE] = grads[group * SUBLANES : (group + 1) * SUBLANES]
            sent[place + STATE : place + ROWS] = tails[group]


def unpack_kernel(got, kernel_grad, readout_grad, step_grad, state_grad, grads):
    peers = got.shape[0] // ROWS
    singles = got[pl.ds(SINGLES, peers, stride=ROWS), :]
    scales = [jnp.exp2(singles[:, spot : spot + 1]) for spot in SCALE_LANES]
    for peer in range(peers):
        spot = peer * ROWS
        lanes = slice(peer * SUBLANES, (peer + 1) * SUBLANES)
        kernel_grad[lanes] = got[spot + LAGS : spot + GRADS] * scales[0][peer : peer + 1]
        grads[lanes] = got[spot + GRADS : spot + STATE] * scales[1][peer : peer + 1]
    for spot in range(0, peers * SUBLANES, LANES):
        readout_grad[:, spot : spot + LANES] = grads[spot : spot + LANES].T
    high = got[pl.ds(STATE, peers, stride=ROWS), :]
    low = got[pl.ds(STATE + 1, peers, stride=ROWS), :]
    state = jnp.sum((high + low * (1.0 / 256.0)) * scales[2], axis=0, keepdims=True)
    states = state_grad.shape[1]
    state_grad[0:1] = state[:, :states]
    state_grad[1:2] = state[:, states:]
    per_row = LANES // SUBLANES
    lane = lax.broadcasted_iota(jnp.int32, (peers, LANES), 1)
    row = lax.broadcasted_iota(jnp.int32, (peers, LANES), 0)
    steps = pltpu.roll(singles, LANES - STEP_LANES[1], 1) * (1.0 / 256.0) + singles
    steps = jnp.where(lane < SUBLANES, steps * scales[3], 0.0)
    reach = SUBLANES
    while reach < LANES:
        steps = steps + pltpu.roll(steps, reach, 1)
        reach *= 2
    for spot in range(0, peers, per_row):
        mine = jnp.where(row - spot == lane // SUBLANES, steps, 0.0)
        step_grad[spot * SUBLANES : (spot + per_row) * SUBLANES] = jnp.sum(mine, axis=0)


def kernel_device(inputs, out_grad, readout, log_step, decay_log, rotation):
    owners, groups = lax.axis_size("seq"), lax.axis_size("ch")
    peers = owners * groups
    channels, length = inputs.shape
    states = decay_log.shape[0]
    part_count = channels // owners
    pairs = part_count // 2
    norm_scale = 1.0 / math.sqrt(owners * length)
    vmem = pl.BlockSpec(memory_space=pltpu.VMEM)
    memory = pltpu.CompilerParams(vmem_limit_bytes=32 * 1024 * 1024)
    f32, bf16 = jnp.float32, jnp.bfloat16

    def exchange(value):
        value = value.reshape(peers, ROWS // 2, 2, LANES)
        value = lax.all_to_all(value, ("seq", "ch"), split_axis=0, concat_axis=0, tiled=True)
        return value.reshape(peers * ROWS, LANES)

    anywhere = pl.BlockSpec(memory_space=pl.ANY)
    pieces = pl.pallas_call(
        pack_kernel,
        out_shape=jax.ShapeDtypeStruct((peers * ROWS, LANES), bf16),
        in_specs=[anywhere] * 4,
        out_specs=vmem,
        scratch_shapes=[
            pltpu.VMEM((2, channels, LANES), bf16),
            pltpu.VMEM((LANES, channels), f32),
            pltpu.VMEM((1, channels), f32),
            pltpu.VMEM((2, channels, LANES), f32),
            pltpu.VMEM((peers * ROWS, LANES), f32),
            pltpu.SemaphoreType.DMA((4,)),
        ],
        compiler_params=pltpu.CompilerParams(vmem_limit_bytes=60 * 1024 * 1024),
    )(inputs, out_grad, readout.transpose(0, 2, 1).reshape(LANES, channels), log_step[None])
    got = exchange(pieces)

    held = [jnp.asarray(table) for table in transform_tables(owners, length, norm_scale)]
    held += [decay_log[None], rotation[None]]
    held = pl.pallas_call(
        hold_kernel,
        out_shape=[jax.ShapeDtypeStruct(value.shape, value.dtype) for value in held],
        in_specs=[vmem] * 4,
        out_specs=[vmem] * 4,
        compiler_params=memory,
    )(*held)
    sent = pl.pallas_call(
        functools.partial(main_kernel, owners, norm_scale),
        out_shape=jax.ShapeDtypeStruct((peers * ROWS, LANES), f32),
        in_specs=[vmem] * 5,
        out_specs=vmem,
        scratch_shapes=[
            pltpu.VMEM((peers * ROWS, LANES), f32),
            pltpu.VMEM((owners * part_count, length), f32),
            pltpu.VMEM((pairs, length, 2 * LANES), bf16),
            pltpu.VMEM((4, pairs, LANES), f32),
        ],
        compiler_params=memory,
    )(got, *held)
    back = exchange(sent.astype(jnp.float16))
    kernel_grad, readout_grad, step_grad, state_grad = pl.pallas_call(
        unpack_kernel,
        out_shape=[
            jax.ShapeDtypeStruct((channels, length), f32),
            jax.ShapeDtypeStruct((LANES, channels), f32),
            jax.ShapeDtypeStruct((channels,), f32),
            jax.ShapeDtypeStruct((2, states), f32),
        ],
        in_specs=[vmem],
        out_specs=[vmem] * 4,
        scratch_shapes=[pltpu.VMEM((channels, LANES), f32)],
        compiler_params=memory,
    )(back.astype(f32))
    readout_grad = readout_grad.reshape(2, states, channels).transpose(0, 2, 1)
    return kernel_grad, readout_grad, step_grad, state_grad


def kernel_fits(mesh, inputs, decay_log):
    owners, groups = mesh.shape["seq"], mesh.shape["ch"]
    channels = inputs.shape[0] // groups
    return (
        inputs.shape[1] == owners * LANES
        and 2 * decay_log.shape[0] == LANES
        and owners == SUBLANES
        and groups % 2 == 0
        and channels == owners * groups * SUBLANES
        and channels % LANES == 0
    )


def solution(mesh):
    def whole(inputs, out_grad, readout, log_step, decay_log, rotation):
        fits = kernel_fits(mesh, inputs, decay_log)
        return jax.shard_map(
            kernel_device if fits else general_device,
            mesh=mesh,
            in_specs=(P("ch", "seq"), P("ch", "seq"), P(None, "ch", None), P("ch"), P(), P()),
            out_specs=(P("ch", "seq"), P(None, "ch", None), P("ch"), P()),
            check_vma=False,
        )(inputs, out_grad, readout, log_step, decay_log, rotation)

    return whole
```

```python
import functools
import math

import jax
import jax.numpy as jnp
import numpy as np
from jax import lax
from jax.experimental import pallas as pl
from jax.experimental.pallas import tpu as pltpu
from jax.sharding import PartitionSpec as P

precise = lax.Precision.HIGHEST
two_pi = 2.0 * math.pi
LANES = 128
SUBLANES = 8


def angle_table(left_index, right_index, modulus, orient):
    product = left_index[:, None] * right_index[None, :] % modulus
    return orient * two_pi * product.astype(jnp.float32) / modulus


def rotate(real_part, imag_part, angles):
    cosine_table = jnp.cos(angles)
    sine_table = jnp.sin(angles)
    return (
        real_part * cosine_table - imag_part * sine_table,
        real_part * sine_table + imag_part * cosine_table,
    )


def last_transform(real_part, imag_part, orient):
    length = real_part.shape[-1]
    counter = jnp.arange(length, dtype=jnp.int32)
    angles = angle_table(counter, counter, length, orient)
    cosine_table = jnp.cos(angles)
    sine_table = jnp.sin(angles)
    dot = functools.partial(jnp.dot, precision=precise, preferred_element_type=jnp.float32)
    return (
        dot(real_part, cosine_table) - dot(imag_part, sine_table),
        dot(imag_part, cosine_table) + dot(real_part, sine_table),
    )


def discretize(readout, log_step, decay_log, rotation):
    step_size = jnp.exp(log_step)[:, None]
    pole_real = -jnp.exp(decay_log)[None, :]
    pole_imag = rotation[None, :]
    rate_real = step_size * pole_real
    rate_imag = step_size * pole_imag
    lift_real = jnp.expm1(rate_real) * jnp.cos(rate_imag) - 2.0 * jnp.sin(0.5 * rate_imag) ** 2
    lift_imag = jnp.exp(rate_real) * jnp.sin(rate_imag)
    pole_norm = pole_real * pole_real + pole_imag * pole_imag
    ratio_real = (lift_real * pole_real + lift_imag * pole_imag) / pole_norm
    ratio_imag = (lift_imag * pole_real - lift_real * pole_imag) / pole_norm
    coef_real = readout[0] * ratio_real - readout[1] * ratio_imag
    coef_imag = readout[0] * ratio_imag + readout[1] * ratio_real
    return (coef_real, coef_imag, rate_real, rate_imag)


def parameter_grads(primal, backward, totals):
    coef_real, coef_imag = (primal[0], primal[1])
    cotangents = (
        2.0 * totals[0],
        -2.0 * totals[1],
        2.0 * (coef_real * totals[2] - coef_imag * totals[3]),
        -2.0 * (coef_real * totals[3] + coef_imag * totals[2]),
    )
    return backward(cotangents)


def shifted_totals(raw_sums, rate_real, rate_imag, block_start, norm_scale):
    decays = jnp.exp(rate_real * block_start)
    phases = rate_imag * block_start
    base_real = decays * jnp.cos(phases)
    base_imag = decays * jnp.sin(phases)
    near_real = block_start * raw_sums[0] + raw_sums[2]
    near_imag = block_start * raw_sums[1] + raw_sums[3]
    return jnp.stack(
        [
            norm_scale * (base_real * raw_sums[0] - base_imag * raw_sums[1]),
            norm_scale * (base_real * raw_sums[1] + base_imag * raw_sums[0]),
            norm_scale * (base_real * near_real - base_imag * near_imag),
            norm_scale * (base_real * near_imag + base_imag * near_real),
        ]
    )


def whole_channel_totals(lag_rows, rate_real, rate_imag, norm_scale):
    owners, length = (lag_rows.shape[1], lag_rows.shape[2])
    offsets = jnp.arange(length, dtype=jnp.int32).astype(jnp.float32)
    decays = jnp.exp(rate_real[:, :, None] * offsets)
    phases = rate_imag[:, :, None] * offsets
    power_real = decays * jnp.cos(phases)
    power_imag = decays * jnp.sin(phases)
    weighted = lag_rows * offsets
    raw_sums = jnp.stack(
        [
            jnp.einsum("cbj,cnj->cnb", lag_rows, power_real, precision=precise),
            jnp.einsum("cbj,cnj->cnb", lag_rows, power_imag, precision=precise),
            jnp.einsum("cbj,cnj->cnb", weighted, power_real, precision=precise),
            jnp.einsum("cbj,cnj->cnb", weighted, power_imag, precision=precise),
        ]
    )
    starts = (jnp.arange(owners, dtype=jnp.int32) * length).astype(jnp.float32)
    totals = shifted_totals(
        raw_sums, rate_real[:, :, None], rate_imag[:, :, None], starts, norm_scale
    )
    return jnp.sum(totals, axis=-1)


def general_lags(whole, norm_scale):
    part_count, owners, length = whole.shape[1:]
    freq_width = 2 * owners
    modulus = freq_width * length
    row_index = jnp.arange(owners, dtype=jnp.int32)
    outer_index = jnp.arange(freq_width, dtype=jnp.int32)
    inner_index = jnp.arange(length, dtype=jnp.int32)
    first = angle_table(row_index, outer_index, freq_width, -1.0)
    spec_real = jnp.einsum("scba,bk->scka", whole, jnp.cos(first), precision=precise)
    spec_imag = jnp.einsum("scba,bk->scka", whole, jnp.sin(first), precision=precise)
    spec_real, spec_imag = rotate(
        spec_real, spec_imag, angle_table(outer_index, inner_index, modulus, -1.0)
    )
    freq_real, freq_imag = last_transform(spec_real, spec_imag, -1.0)
    prod_real = freq_real[1] * freq_real[0] + freq_imag[1] * freq_imag[0]
    prod_imag = freq_imag[1] * freq_real[0] - freq_real[1] * freq_imag[0]
    back_real, back_imag = last_transform(prod_real, prod_imag, 1.0)
    back_real, back_imag = rotate(
        back_real, back_imag, angle_table(outer_index, inner_index, modulus, 1.0)
    )
    final = angle_table(outer_index, row_index, freq_width, 1.0)
    lag_rows = jnp.einsum("cka,kb->cba", back_real, jnp.cos(final), precision=precise) - jnp.einsum(
        "cka,kb->cba", back_imag, jnp.sin(final), precision=precise
    )
    return lag_rows * (norm_scale / modulus)


def general_device(inputs, out_grad, readout, log_step, decay_log, rotation):
    owners = lax.axis_size("seq")
    channels, length = inputs.shape
    states = decay_log.shape[0]
    part_count = channels // owners
    norm_scale = 1.0 / math.sqrt(owners * length)
    pieces = jnp.concatenate(
        [a.reshape(owners, part_count, length) for a in (inputs, out_grad)], axis=1
    )
    pieces = lax.all_to_all(pieces, "seq", split_axis=0, concat_axis=0, tiled=True)
    whole = pieces.astype(jnp.float32).reshape(owners, 2, part_count, length)
    lag_rows = general_lags(whole.transpose(1, 2, 0, 3), norm_scale)
    first_channel = lax.axis_index("seq") * part_count
    own_readout = lax.dynamic_slice_in_dim(readout, first_channel, part_count, 1)
    own_step = lax.dynamic_slice_in_dim(log_step, first_channel, part_count, 0)
    primal, backward = jax.vjp(discretize, own_readout, own_step, decay_log, rotation)
    totals = whole_channel_totals(lag_rows, primal[2], primal[3], norm_scale)
    readout_part, step_part, decay_part, rotation_part = parameter_grads(primal, backward, totals)
    shared = jnp.concatenate(
        [readout_part.reshape(-1), step_part, decay_part, rotation_part]
    )
    sent = jnp.concatenate(
        [
            lag_rows.transpose(1, 0, 2).reshape(owners, -1),
            jnp.broadcast_to(shared, (owners, shared.shape[0])),
        ],
        axis=1,
    )
    got = lax.all_to_all(sent, "seq", split_axis=0, concat_axis=0, tiled=True)
    cuts = np.cumsum([part_count * length, 2 * part_count * states, part_count])
    lags, readouts, steps, state = jnp.split(got, cuts, axis=1)
    readouts = readouts.reshape(owners, 2, part_count, states).transpose(1, 0, 2, 3)
    return (
        lags.reshape(channels, length),
        readouts.reshape(2, channels, states),
        steps.reshape(channels),
        lax.psum(jnp.sum(state, axis=0), "ch").reshape(2, states),
    )


def split_halves(value):
    high = value.astype(jnp.bfloat16)
    return high, (value - high.astype(jnp.float32)).astype(jnp.bfloat16)


def cos_sin(angle):
    turns = jnp.floor(angle * (2.0 / math.pi) + 0.5)
    rest = angle - turns * 1.5703125
    rest = rest - turns * 4.837512969970703125e-4
    rest = rest - turns * 7.54978995489188216e-8
    quarter = turns.astype(jnp.int32)
    square = rest * rest
    sine = rest + rest * square * (
        -1.6666654611e-1 + square * (8.3321608736e-3 - square * 1.9515295891e-4)
    )
    cosine = (
        1.0
        - 0.5 * square
        + square
        * square
        * (
            4.166664568298827e-2
            + square * (-1.388731625493765e-3 + square * 2.443315711809948e-5)
        )
    )
    odd = (quarter & 1) == 1
    out_cos = jnp.where(odd, sine, cosine)
    out_sin = jnp.where(odd, cosine, sine)
    out_cos = jnp.where(((quarter + 1) & 2) == 2, -out_cos, out_cos)
    out_sin = jnp.where((quarter & 2) == 2, -out_sin, out_sin)
    return out_cos, out_sin


def grow(value):
    series = 1.0
    for term in range(9, 1, -1):
        series = 1.0 + series * value * (1.0 / term)
    return jnp.where(jnp.abs(value) < 0.35, series * value, jnp.exp(value) - 1.0)


def power(rate_real, rate_imag, offset):
    size = jnp.exp(rate_real * offset)
    cosine, sine = cos_sin(rate_imag * offset)
    return size * cosine, size * sine


def times(left, right):
    return (
        left[0] * right[0] - left[1] * right[1],
        left[0] * right[1] + left[1] * right[0],
    )


def blocks_forward(x):
    root = math.sqrt(0.5)
    cosine, sine = math.cos(math.pi / 8), math.sin(math.pi / 8)
    total = [x[s] + x[s + 4] for s in range(4)]
    gap = [x[s] - x[s + 4] for s in range(4)]
    even, odd = total[0] + total[2], total[1] + total[3]
    real, imag = [None] * 9, [None] * 9
    real[0], real[8] = even + odd, even - odd
    imag[0] = imag[8] = jnp.zeros_like(even)
    real[4], imag[4] = total[0] - total[2], total[3] - total[1]
    less, more = root * (gap[1] - gap[3]), root * (gap[1] + gap[3])
    real[2], imag[2] = gap[0] + less, -gap[2] - more
    real[6], imag[6] = gap[0] - less, gap[2] - more
    less, more = root * (x[2] - x[6]), root * (x[2] + x[6])
    even1 = (x[0] + less, -x[4] - more)
    even3 = (x[0] - less, x[4] - more)
    p, q, r, t = x[1] - x[7], x[3] - x[5], x[1] + x[7], x[3] + x[5]
    odd1 = (cosine * p + sine * q, -sine * r - cosine * t)
    odd3 = (sine * p - cosine * q, sine * t - cosine * r)
    real[1], imag[1] = even1[0] + odd1[0], even1[1] + odd1[1]
    real[7], imag[7] = even1[0] - odd1[0], odd1[1] - even1[1]
    real[3], imag[3] = even3[0] + odd3[0], even3[1] + odd3[1]
    real[5], imag[5] = even3[0] - odd3[0], odd3[1] - even3[1]
    return list(zip(real, imag))


def blocks_back(z):
    root = math.sqrt(0.5)
    cosine, sine = math.cos(math.pi / 8), math.sin(math.pi / 8)
    real, imag = [v[0] for v in z], [v[1] for v in z]
    even, odd = real[0] + real[8], real[0] - real[8]
    total = [even + real[4], odd + imag[4], even - real[4], odd - imag[4]]
    less, more = root * (real[2] - real[6]), root * (imag[2] + imag[6])
    gap = [real[2] + real[6], less + more, imag[2] - imag[6], more - less]
    x = [total[s] + gap[s] for s in range(4)] + [total[s] - gap[s] for s in range(4)]
    even1 = (real[1] + real[7], imag[7] - imag[1])
    even3 = (real[3] + real[5], imag[5] - imag[3])
    odd1 = (real[1] - real[7], imag[1] + imag[7])
    odd3 = (real[3] - real[5], imag[3] + imag[5])
    less, more = root * (even1[0] - even3[0]), root * (even1[1] + even3[1])
    p = cosine * odd1[0] + sine * odd3[0]
    q = sine * odd1[0] - cosine * odd3[0]
    r = sine * odd1[1] + cosine * odd3[1]
    t = cosine * odd1[1] - sine * odd3[1]
    extra = [
        even1[0] + even3[0],
        p + r,
        less - more,
        q + t,
        even3[1] - even1[1],
        t - q,
        -less - more,
        r - p,
    ]
    return [v + w for v, w in zip(x, extra)]


def transform_tables(owners, length, norm_scale):
    width = 2 * owners
    counter = np.arange(length)
    angles = two_pi * (counter[:, None] * counter[None, :] % length) / length
    cosine, sine = np.cos(angles), np.sin(angles)
    matrix = np.block([[cosine, -sine], [sine, cosine]]).astype(np.float32)
    high = matrix.astype(jnp.bfloat16)
    low = (matrix - high.astype(np.float32)).astype(jnp.bfloat16)
    outer = np.arange(owners + 1)
    angles = two_pi * (outer[:, None] * counter[None, :]) / (width * length)
    twiddle = np.stack([np.cos(angles), -np.sin(angles)], axis=1)
    weight = np.where(outer % owners == 0, 1.0, 2.0) * norm_scale / (width * length)
    twiddle = np.concatenate([twiddle, twiddle * weight[:, None, None]], axis=1)
    return np.stack([high, low]), twiddle.astype(np.float32)


def three_pieces(value):
    pieces = []
    for _ in range(3):
        piece = value.astype(jnp.bfloat16).astype(jnp.float32)
        pieces.append(piece)
        value = value - piece
    return pieces


def transposed(value):
    return jnp.concatenate(
        [value[:, spot : spot + LANES].T for spot in range(0, value.shape[1], LANES)], axis=0
    )


READ, STEP, ROWS = 16, 19, 20
LAGS, GRADS, STATE, SINGLES = 0, 8, 16, 18
STEP_LANES, SCALE_LANES = (0, 8), (16, 17, 18, 19)
SPARE = 15.0
PARTS = 4


def pack_kernel(inputs, out_grad, readout, log_step, out, signals, read, step, turned, rows, sems):
    peers = out.shape[0] // ROWS
    copies = [
        pltpu.make_async_copy(source, target, sems.at[i])
        for i, (source, target) in enumerate(
            ((readout, read), (log_step, step), (inputs, signals.at[0]), (out_grad, signals.at[1]))
        )
    ]
    for copy in copies:
        copy.start()
    copies[0].wait()
    copies[1].wait()
    own = lax.axis_index("seq")
    turned[0] = transposed(read[...])
    turned[1] = transposed(jnp.broadcast_to(step[...], (LANES, step.shape[1])))
    for place, value in enumerate(
        three_pieces(turned[0, pl.ds(own, peers, stride=SUBLANES), :])
    ):
        rows[pl.ds(READ + place, peers, stride=ROWS), :] = value
    pieces = three_pieces(turned[1, pl.ds(own, peers, stride=SUBLANES), :])
    lane = lax.broadcasted_iota(jnp.int32, (peers, LANES), 1)
    value = jnp.where(lane == 0, pieces[0], jnp.where(lane == 1, pieces[1], pieces[2]))
    rows[pl.ds(STEP, peers, stride=ROWS), :] = value
    for place in range(2):
        copies[2 + place].wait()
        value = signals[place].astype(jnp.float32)
        for peer in range(peers):
            spot = peer * ROWS + place * SUBLANES
            rows[spot : spot + SUBLANES] = value[peer * SUBLANES : (peer + 1) * SUBLANES]
    out[...] = rows[...].astype(jnp.bfloat16)


def hold_kernel(*refs):
    for source, target in zip(refs[: len(refs) // 2], refs[len(refs) // 2 :]):
        target[...] = source[...]


def exponent_of(bound):
    return jnp.floor(jnp.log(jnp.maximum(bound, 1e-30)) * (1.0 / math.log(2.0))) + (2.0 - SPARE)


def greatest(value):
    return jnp.max(jnp.max(value, axis=1, keepdims=True), axis=0, keepdims=True)


def size_of(value):
    return jnp.abs(value[0]) + jnp.abs(value[1])


def two_pieces(value):
    high = value.astype(jnp.bfloat16).astype(jnp.float32)
    return high, (value - high) * 256.0


def main_kernel(
    owners,
    norm_scale,
    got,
    matrix,
    twiddle,
    decay_log,
    rotation,
    sent,
    rows_in,
    spectra,
    freq,
    back,
    params,
    doubled,
    bases,
    powers,
    lags,
    sums,
):
    peers, length = got.shape[0] // ROWS, got.shape[1]
    groups = peers // owners
    part_count = groups * SUBLANES
    rows = 2 * part_count
    pairs = part_count // 2
    half = pairs // SUBLANES
    reach = length // 2
    device = lax.axis_index("seq") * groups + lax.axis_index("ch")
    lane = lax.broadcasted_iota(jnp.int32, (pairs, LANES), 1)
    left = lane < LANES // 2
    row = lax.broadcasted_iota(jnp.int32, (SUBLANES, LANES), 0)

    def swap(value):
        return pltpu.roll(value, LANES // 2, 1)

    def lanes_of(side):
        return slice(side * LANES, (side + 1) * LANES)

    def collect(spot):
        tiles = [
            rows_in[pl.ds(group * ROWS + spot, owners, stride=groups * ROWS), :]
            for group in range(groups)
        ]
        return jnp.concatenate(tiles[:half], axis=0), jnp.concatenate(tiles[half:], axis=0)

    def make_params():
        lower, upper = [sum(side) for side in zip(*(collect(READ + i) for i in range(3)))]
        read = (jnp.where(left, lower, swap(upper)), jnp.where(left, swap(lower), upper))
        lower, upper = [
            sum(side[:, i : i + 1] for i in range(3)) + jnp.zeros_like(side)
            for side in collect(STEP)
        ]
        step = jnp.exp(jnp.where(left, lower, upper))
        decay_row = jnp.concatenate([decay_log[...], decay_log[...]], axis=1)
        rotation_row = jnp.concatenate([rotation[...], rotation[...]], axis=1)
        pole = (
            jnp.broadcast_to(-jnp.exp(decay_row), step.shape),
            jnp.broadcast_to(rotation_row, step.shape),
        )
        rate = (step * pole[0], step * pole[1])
        place, size = 0, 1
        while size < owners * length:
            doubled[place], doubled[place + 1] = power(rate[0], rate[1], float(size))
            place, size = place + 2, size * 2
        sine = cos_sin(0.5 * rate[1])[1]
        cosine = 1.0 - 2.0 * sine * sine
        lift = (grow(rate[0]) * cosine - 2.0 * sine * sine, doubled[1])
        norm = 1.0 / (pole[0] * pole[0] + pole[1] * pole[1])
        inverse = (pole[0] * norm, -pole[1] * norm)
        ratio = times(lift, inverse)
        coef = times(read, ratio)
        lifted = times((doubled[0], doubled[1]), inverse)
        values = (rate, ratio, coef, times(read, lifted), pole, times(coef, inverse), (step, step))
        for place, value in enumerate(values):
            params[2 * place], params[2 * place + 1] = value

    block_bit, reach_bit = length.bit_length() - 1, reach.bit_length() - 1
    bits = [(row & (1 << i)) != 0 for i in range(SUBLANES.bit_length() - 1)]

    def doubled_row(p, i):
        return doubled[2 * i, p : p + 1, :], doubled[2 * i + 1, p : p + 1, :]

    def by_rows(p, first):
        out = None
        for i, bit in enumerate(bits):
            real, imag = doubled_row(p, first + i)
            value = (jnp.where(bit, real, 1.0), jnp.where(bit, imag, 0.0))
            out = value if out is None else times(out, value)
        return out

    def make_tables():
        for p in range(pairs):
            table = [by_rows(p, 0)]
            for i in range(len(bits), reach_bit):
                table += [times(block, doubled_row(p, i)) for block in table]
            for place in range(0, len(table), 2):
                for side in range(2):
                    value = jnp.concatenate([table[place][side], table[place + 1][side]], axis=0)
                    for i, piece in enumerate(split_halves(value)):
                        spot = 2 * i * reach + place * SUBLANES
                        powers[p, spot : spot + 2 * SUBLANES, lanes_of(side)] = piece
                        spot += reach
                        powers[p, spot : spot + 2 * SUBLANES, lanes_of(side)] = piece
            base = by_rows(p, block_bit)
            bases[p, 0], bases[p, 1] = base
            bases[p, 2], bases[p, 3] = times(base, doubled_row(p, reach_bit))

    def transform(source, target, count):
        dot = functools.partial(jnp.dot, preferred_element_type=jnp.float32)
        cuts = [(owners + 1) * i // PARTS * count for i in range(PARTS + 1)]
        for part in map(slice, cuts, cuts[1:]):
            low = source[1, part]
            target[part] = (
                dot(source[0, part], matrix[0]) + dot(low, matrix[0]) + dot(source[0, part], matrix[1])
            )

    def spread_blocks():
        rows_in[...] = got[...].astype(jnp.float32)
        blocks = []
        for s in range(owners):
            spots = [(s * groups + group) * ROWS for group in range(groups)]
            blocks.append(
                jnp.concatenate(
                    [rows_in[spot : spot + SUBLANES] for spot in spots]
                    + [rows_in[spot + SUBLANES : spot + 2 * SUBLANES] for spot in spots],
                    axis=0,
                )
            )
        for k, value in enumerate(blocks_forward(blocks)):
            if k:
                value = times(value, (twiddle[k, 0:1], twiddle[k, 1:2]))
            for side in range(2):
                for i, piece in enumerate(split_halves(value[side])):
                    spectra[i, k * rows : (k + 1) * rows, lanes_of(side)] = piece

    def to_frequencies():
        transform(spectra, freq, rows)
        make_params()
        make_tables()

    def to_lags():
        for k in range(owners + 1):
            at_in = freq[k * rows : k * rows + part_count]
            at_out = freq[k * rows + part_count : (k + 1) * rows]
            ur, ui = at_in[:, :length], at_in[:, length:]
            gr, gi = at_out[:, :length], at_out[:, length:]
            for side, value in enumerate((gr * ur + gi * ui, gr * ui - gi * ur)):
                for i, piece in enumerate(split_halves(value)):
                    spectra[i, k * part_count : (k + 1) * part_count, lanes_of(side)] = piece
        transform(spectra, back, part_count)

    def finish():
        turned = []
        for k in range(owners + 1):
            spots = slice(k * part_count, (k + 1) * part_count)
            value = (back[spots, lanes_of(0)], back[spots, lanes_of(1)])
            turned.append(times(value, (twiddle[k, 2:3], twiddle[k, 3:4])))
        blocks = blocks_back(turned)

        most = jnp.zeros((part_count, LANES), jnp.float32)
        for b, block in enumerate(blocks):
            most = jnp.maximum(most, jnp.abs(block))
            lags[b * part_count : (b + 1) * part_count] = block

        def param(place):
            return params[2 * place], params[2 * place + 1]

        rate, ratio, coef, through, pole, direct, (step, _) = (param(i) for i in range(7))
        most = greatest(most)
        whole = 2.0 * math.sqrt(owners * length)
        on_rate = size_of(coef) * float(owners * length) + size_of(through)
        on_pole = step * on_rate + size_of(direct)
        lag_exponent = exponent_of(most)
        grad_exponent = exponent_of(most * (whole * greatest(size_of(ratio))))
        state_exponent = exponent_of(
            most * (whole * part_count * greatest(on_pole * (1.0 - pole[0])))
        )
        step_exponent = exponent_of(
            most * (whole * (LANES // 2) * greatest(on_rate * size_of(rate)))
        )
        lag_scale = jnp.exp2(-lag_exponent)
        for b, block in enumerate(blocks):
            for group in range(groups):
                place = (b * groups + group) * ROWS
                value = block[group * SUBLANES : (group + 1) * SUBLANES]
                sent[place + LAGS : place + GRADS] = value * lag_scale

        start = row.astype(jnp.float32) * float(length)
        first = left[:owners]
        wide = lax.broadcasted_iota(jnp.int32, (4 * owners, LANES), 1)
        wide_left = wide < reach
        offset = jnp.where(wide_left, wide, wide - reach).astype(jnp.float32)
        both_left = wide_left[: 2 * owners]
        for p in range(pairs):
            both = jnp.concatenate(
                [
                    lags[pl.ds(first_row, owners, stride=part_count), :]
                    for first_row in (p, pairs + p)
                ],
                axis=0,
            )
            swapped = swap(both)
            plain = jnp.concatenate(
                [jnp.where(both_left, both, swapped), jnp.where(both_left, swapped, both)], axis=0
            )
            factor = []
            for value in (plain, plain * offset):
                high = value.astype(jnp.bfloat16).astype(jnp.float32)
                factor.append(jnp.where(wide_left, high, value - high))
            factor = jnp.concatenate(factor, axis=0).astype(jnp.bfloat16)
            raw = jnp.dot(
                jnp.concatenate([factor, factor], axis=1),
                powers[p],
                preferred_element_type=jnp.float32,
            )

            def pick(place, side):
                top = raw[2 * place * owners : (2 * place + 1) * owners, lanes_of(side)]
                bottom = raw[(2 * place + 1) * owners : (2 * place + 2) * owners, lanes_of(side)]
                return jnp.where(first, top, bottom)

            found = None
            for part in range(2):
                base = (bases[p, 2 * part], bases[p, 2 * part + 1])
                near = start + float(part * reach)
                value = (pick(part, 0), pick(part, 1))
                lagged = (near * value[0] + pick(2 + part, 0), near * value[1] + pick(2 + part, 1))
                terms = times(base, value) + times(base, lagged)
                found = terms if found is None else [x + y for x, y in zip(found, terms)]
            for place, value in enumerate(found):
                sums[place, p : p + 1] = jnp.sum(value, axis=0, keepdims=True)

        total = (sums[0] * (2.0 * norm_scale), sums[1] * (2.0 * norm_scale))
        lag_total = (sums[2] * (2.0 * norm_scale), sums[3] * (2.0 * norm_scale))
        on_read = times(total, ratio)
        on_read = (on_read[0], -on_read[1])
        on_rate = times(coef, lag_total)
        more = times(total, through)
        on_rate = (on_rate[0] + more[0], on_rate[1] + more[1])
        less = times(total, direct)
        on_pole = (step * on_rate[0] - less[0], step * on_rate[1] - less[1])
        on_step = times(on_rate, rate)[0]
        on_decay = jnp.sum(on_pole[0] * pole[0], axis=0, keepdims=True)
        on_rotation = -jnp.sum(on_pole[1], axis=0, keepdims=True)
        on_decay = on_decay + swap(on_decay)
        on_rotation = on_rotation + swap(on_rotation)
        state = jnp.where(left[0:1], on_decay, on_rotation) * jnp.exp2(-state_exponent)

        grad_scale = jnp.exp2(-grad_exponent)
        on_read = (on_read[0] * grad_scale, on_read[1] * grad_scale)
        lower = jnp.where(left, on_read[0], swap(on_read[1]))
        upper = jnp.where(left, swap(on_read[0]), on_read[1])
        grads = jnp.concatenate([lower, upper], axis=0)
        step_column = jnp.concatenate(
            [
                jnp.sum(jnp.where(left, on_step, 0.0), axis=1, keepdims=True),
                jnp.sum(jnp.where(left, 0.0, on_step), axis=1, keepdims=True),
            ],
            axis=0,
        ) * jnp.exp2(-step_exponent)
        place_lane = lax.broadcasted_iota(jnp.int32, (SUBLANES, LANES), 1)
        scales = jnp.zeros((1, LANES), jnp.float32)
        for spot, value in zip(
            SCALE_LANES, (lag_exponent, grad_exponent, state_exponent, step_exponent)
        ):
            scales = jnp.where(place_lane[0:1] == spot, value, scales)
        state_high, state_low = two_pieces(state)
        tails = []
        for group in range(groups):
            pieces = two_pieces(step_column[group * SUBLANES : (group + 1) * SUBLANES])
            spread = jnp.zeros((SUBLANES, LANES), jnp.float32)
            for spot, piece in zip(STEP_LANES, pieces):
                spread = jnp.where(place_lane == row + spot, piece, spread)
            singles = scales + jnp.sum(spread, axis=0, keepdims=True)
            tails.append(jnp.concatenate([state_high, state_low, singles, singles], axis=0))
        for b in range(owners):
            for group in range(groups):
                place = (b * groups + group) * ROWS
                sent[place + GRADS : place + STATE] = grads[
                    group * SUBLANES : (group + 1) * SUBLANES
                ]
                sent[place + STATE : place + ROWS] = tails[group]

    for section in (spread_blocks, to_frequencies, to_lags, finish):
        section()


def unpack_kernel(got, kernel_grad, readout_grad, step_grad, state_grad, wide, grads):
    peers = got.shape[0] // ROWS
    per_row = LANES // SUBLANES
    singles = got[pl.ds(SINGLES, peers, stride=ROWS), :]
    exponents = [jnp.broadcast_to(singles[:, spot : spot + 1], (peers, LANES)) for spot in SCALE_LANES]
    scales = [jnp.exp2(value) for value in exponents]
    for i in range(2):
        wide[i] = scales[i]
    for spot in range(0, peers, per_row):
        part = slice(spot * SUBLANES, (spot + per_row) * SUBLANES)
        for i, first, target in ((1, GRADS, grads), (0, LAGS, kernel_grad)):
            for peer in range(spot, spot + per_row):
                place = peer * ROWS + first
                target[peer * SUBLANES : (peer + 1) * SUBLANES] = (
                    got[place : place + SUBLANES] * wide[i, peer : peer + 1, :]
                )
        readout_grad[:, part] = grads[part].T

    high = got[pl.ds(STATE, peers, stride=ROWS), :]
    low = got[pl.ds(STATE + 1, peers, stride=ROWS), :]
    total = jnp.sum((high + low * (1.0 / 256.0)) * scales[2], axis=0, keepdims=True)
    states = state_grad.shape[1]
    state_grad[0:1] = total[:, :states]
    state_grad[1:2] = total[:, states:]
    lane = lax.broadcasted_iota(jnp.int32, (peers, LANES), 1)
    row = lax.broadcasted_iota(jnp.int32, (peers, LANES), 0)
    high, low = (
        jnp.take_along_axis(singles, lane % SUBLANES + first, axis=1) for first in STEP_LANES
    )
    value = (high + low * (1.0 / 256.0)) * scales[3]
    for spot in range(0, peers, per_row):
        mine = jnp.where(row - spot == lane // SUBLANES, value, 0.0)
        step_grad[spot * SUBLANES : (spot + per_row) * SUBLANES] = jnp.sum(mine, axis=0)


def kernel_device(inputs, out_grad, readout, log_step, decay_log, rotation):
    owners, groups = lax.axis_size("seq"), lax.axis_size("ch")
    peers = owners * groups
    channels, length = inputs.shape
    states = decay_log.shape[0]
    part_count = channels // owners
    pairs = part_count // 2
    norm_scale = 1.0 / math.sqrt(owners * length)
    vmem = pl.BlockSpec(memory_space=pltpu.VMEM)
    memory = pltpu.CompilerParams(vmem_limit_bytes=32 * 1024 * 1024)
    f32, bf16 = jnp.float32, jnp.bfloat16

    def exchange(value):
        value = value.reshape(peers, ROWS // 2, 2, LANES)
        value = lax.all_to_all(value, ("seq", "ch"), split_axis=0, concat_axis=0, tiled=True)
        return value.reshape(peers * ROWS, LANES)

    anywhere = pl.BlockSpec(memory_space=pl.ANY)
    pieces = pl.pallas_call(
        pack_kernel,
        out_shape=jax.ShapeDtypeStruct((peers * ROWS, LANES), bf16),
        in_specs=[anywhere] * 4,
        out_specs=vmem,
        scratch_shapes=[
            pltpu.VMEM((2, channels, LANES), bf16),
            pltpu.VMEM((LANES, channels), f32),
            pltpu.VMEM((1, channels), f32),
            pltpu.VMEM((2, channels, LANES), f32),
            pltpu.VMEM((peers * ROWS, LANES), f32),
            pltpu.SemaphoreType.DMA((4,)),
        ],
        compiler_params=pltpu.CompilerParams(vmem_limit_bytes=60 * 1024 * 1024),
    )(inputs, out_grad, readout.transpose(0, 2, 1).reshape(LANES, channels), log_step[None])
    got = exchange(pieces)

    held = [jnp.asarray(table) for table in transform_tables(owners, length, norm_scale)]
    held += [decay_log[None], rotation[None]]
    held = pl.pallas_call(
        hold_kernel,
        out_shape=[jax.ShapeDtypeStruct(value.shape, value.dtype) for value in held],
        in_specs=[vmem] * 4,
        out_specs=[vmem] * 4,
        compiler_params=memory,
    )(*held)
    sent = pl.pallas_call(
        functools.partial(main_kernel, owners, norm_scale),
        out_shape=jax.ShapeDtypeStruct((peers * ROWS, LANES), f32),
        in_specs=[vmem] * 5,
        out_specs=vmem,
        scratch_shapes=[
            pltpu.VMEM((peers * ROWS, LANES), f32),
            pltpu.VMEM((2, (owners + 1) * 2 * part_count, 2 * LANES), bf16),
            pltpu.VMEM(((owners + 1) * 2 * part_count, 2 * LANES), f32),
            pltpu.VMEM(((owners + 1) * part_count, 2 * LANES), f32),
            pltpu.VMEM((14, pairs, LANES), f32),
            pltpu.VMEM((2 * (owners * length).bit_length(), pairs, LANES), f32),
            pltpu.VMEM((pairs, 4, owners, LANES), f32),
            pltpu.VMEM((pairs, 2 * length, 2 * LANES), bf16),
            pltpu.VMEM((owners * part_count, length), f32),
            pltpu.VMEM((4, pairs, LANES), f32),
        ],
        compiler_params=memory,
    )(got, *held)
    back = exchange(sent.astype(jnp.float16))
    kernel_grad, readout_grad, step_grad, state_grad = pl.pallas_call(
        unpack_kernel,
        out_shape=[
            jax.ShapeDtypeStruct((channels, length), f32),
            jax.ShapeDtypeStruct((LANES, channels), f32),
            jax.ShapeDtypeStruct((channels,), f32),
            jax.ShapeDtypeStruct((2, states), f32),
        ],
        in_specs=[vmem],
        out_specs=[vmem] * 4,
        scratch_shapes=[
            pltpu.VMEM((2, peers, LANES), f32),
            pltpu.VMEM((channels, LANES), f32),
        ],
        compiler_params=memory,
    )(back.astype(f32))
    readout_grad = readout_grad.reshape(2, states, channels).transpose(0, 2, 1)
    return kernel_grad, readout_grad, step_grad, state_grad


def kernel_fits(mesh, inputs, decay_log):
    owners, groups = mesh.shape["seq"], mesh.shape["ch"]
    channels = inputs.shape[0] // groups
    return (
        inputs.shape[1] == owners * LANES
        and 2 * decay_log.shape[0] == LANES
        and owners == SUBLANES
        and groups % 2 == 0
        and channels == owners * groups * SUBLANES
        and channels % LANES == 0
    )


def solution(mesh):
    def whole(inputs, out_grad, readout, log_step, decay_log, rotation):
        fits = kernel_fits(mesh, inputs, decay_log)
        return jax.shard_map(
            kernel_device if fits else general_device,
            mesh=mesh,
            in_specs=(P("ch", "seq"), P("ch", "seq"), P(None, "ch", None), P("ch"), P(), P()),
            out_specs=(P("ch", "seq"), P(None, "ch", None), P("ch"), P()),
            check_vma=False,
        )(inputs, out_grad, readout, log_step, decay_log, rotation)

    return whole
```

```python
import functools
import math

import jax
import jax.numpy as jnp
import numpy as np
from jax import lax
from jax.experimental import pallas as pl
from jax.experimental.pallas import tpu as pltpu
from jax.sharding import PartitionSpec as P

precise = lax.Precision.HIGHEST
two_pi = 2.0 * math.pi
LANES = 128
SUBLANES = 8


def angle_table(left_index, right_index, modulus, orient):
    product = left_index[:, None] * right_index[None, :] % modulus
    return orient * two_pi * product.astype(jnp.float32) / modulus


def rotate(real_part, imag_part, angles):
    cosine_table = jnp.cos(angles)
    sine_table = jnp.sin(angles)
    return (
        real_part * cosine_table - imag_part * sine_table,
        real_part * sine_table + imag_part * cosine_table,
    )


def last_transform(real_part, imag_part, orient):
    length = real_part.shape[-1]
    counter = jnp.arange(length, dtype=jnp.int32)
    angles = angle_table(counter, counter, length, orient)
    cosine_table = jnp.cos(angles)
    sine_table = jnp.sin(angles)
    dot = functools.partial(jnp.dot, precision=precise, preferred_element_type=jnp.float32)
    return (
        dot(real_part, cosine_table) - dot(imag_part, sine_table),
        dot(imag_part, cosine_table) + dot(real_part, sine_table),
    )


def discretize(readout, log_step, decay_log, rotation):
    step_size = jnp.exp(log_step)[:, None]
    pole_real = -jnp.exp(decay_log)[None, :]
    pole_imag = rotation[None, :]
    rate_real = step_size * pole_real
    rate_imag = step_size * pole_imag
    lift_real = jnp.expm1(rate_real) * jnp.cos(rate_imag) - 2.0 * jnp.sin(0.5 * rate_imag) ** 2
    lift_imag = jnp.exp(rate_real) * jnp.sin(rate_imag)
    pole_norm = pole_real * pole_real + pole_imag * pole_imag
    ratio_real = (lift_real * pole_real + lift_imag * pole_imag) / pole_norm
    ratio_imag = (lift_imag * pole_real - lift_real * pole_imag) / pole_norm
    coef_real = readout[0] * ratio_real - readout[1] * ratio_imag
    coef_imag = readout[0] * ratio_imag + readout[1] * ratio_real
    return (coef_real, coef_imag, rate_real, rate_imag)


def parameter_grads(primal, backward, totals):
    coef_real, coef_imag = (primal[0], primal[1])
    cotangents = (
        2.0 * totals[0],
        -2.0 * totals[1],
        2.0 * (coef_real * totals[2] - coef_imag * totals[3]),
        -2.0 * (coef_real * totals[3] + coef_imag * totals[2]),
    )
    return backward(cotangents)


def shifted_totals(raw_sums, rate_real, rate_imag, block_start, norm_scale):
    decays = jnp.exp(rate_real * block_start)
    phases = rate_imag * block_start
    base_real = decays * jnp.cos(phases)
    base_imag = decays * jnp.sin(phases)
    near_real = block_start * raw_sums[0] + raw_sums[2]
    near_imag = block_start * raw_sums[1] + raw_sums[3]
    return jnp.stack(
        [
            norm_scale * (base_real * raw_sums[0] - base_imag * raw_sums[1]),
            norm_scale * (base_real * raw_sums[1] + base_imag * raw_sums[0]),
            norm_scale * (base_real * near_real - base_imag * near_imag),
            norm_scale * (base_real * near_imag + base_imag * near_real),
        ]
    )


def whole_channel_totals(lag_rows, rate_real, rate_imag, norm_scale):
    owners, length = (lag_rows.shape[1], lag_rows.shape[2])
    offsets = jnp.arange(length, dtype=jnp.int32).astype(jnp.float32)
    decays = jnp.exp(rate_real[:, :, None] * offsets)
    phases = rate_imag[:, :, None] * offsets
    power_real = decays * jnp.cos(phases)
    power_imag = decays * jnp.sin(phases)
    weighted = lag_rows * offsets
    raw_sums = jnp.stack(
        [
            jnp.einsum("cbj,cnj->cnb", lag_rows, power_real, precision=precise),
            jnp.einsum("cbj,cnj->cnb", lag_rows, power_imag, precision=precise),
            jnp.einsum("cbj,cnj->cnb", weighted, power_real, precision=precise),
            jnp.einsum("cbj,cnj->cnb", weighted, power_imag, precision=precise),
        ]
    )
    starts = (jnp.arange(owners, dtype=jnp.int32) * length).astype(jnp.float32)
    totals = shifted_totals(
        raw_sums, rate_real[:, :, None], rate_imag[:, :, None], starts, norm_scale
    )
    return jnp.sum(totals, axis=-1)


def general_lags(whole, norm_scale):
    part_count, owners, length = whole.shape[1:]
    freq_width = 2 * owners
    modulus = freq_width * length
    row_index = jnp.arange(owners, dtype=jnp.int32)
    outer_index = jnp.arange(freq_width, dtype=jnp.int32)
    inner_index = jnp.arange(length, dtype=jnp.int32)
    first = angle_table(row_index, outer_index, freq_width, -1.0)
    spec_real = jnp.einsum("scba,bk->scka", whole, jnp.cos(first), precision=precise)
    spec_imag = jnp.einsum("scba,bk->scka", whole, jnp.sin(first), precision=precise)
    spec_real, spec_imag = rotate(
        spec_real, spec_imag, angle_table(outer_index, inner_index, modulus, -1.0)
    )
    freq_real, freq_imag = last_transform(spec_real, spec_imag, -1.0)
    prod_real = freq_real[1] * freq_real[0] + freq_imag[1] * freq_imag[0]
    prod_imag = freq_imag[1] * freq_real[0] - freq_real[1] * freq_imag[0]
    back_real, back_imag = last_transform(prod_real, prod_imag, 1.0)
    back_real, back_imag = rotate(
        back_real, back_imag, angle_table(outer_index, inner_index, modulus, 1.0)
    )
    final = angle_table(outer_index, row_index, freq_width, 1.0)
    lag_rows = jnp.einsum("cka,kb->cba", back_real, jnp.cos(final), precision=precise) - jnp.einsum(
        "cka,kb->cba", back_imag, jnp.sin(final), precision=precise
    )
    return lag_rows * (norm_scale / modulus)


def general_device(inputs, out_grad, readout, log_step, decay_log, rotation):
    owners = lax.axis_size("seq")
    channels, length = inputs.shape
    states = decay_log.shape[0]
    part_count = channels // owners
    norm_scale = 1.0 / math.sqrt(owners * length)
    pieces = jnp.concatenate(
        [a.reshape(owners, part_count, length) for a in (inputs, out_grad)], axis=1
    )
    pieces = lax.all_to_all(pieces, "seq", split_axis=0, concat_axis=0, tiled=True)
    whole = pieces.astype(jnp.float32).reshape(owners, 2, part_count, length)
    lag_rows = general_lags(whole.transpose(1, 2, 0, 3), norm_scale)
    first_channel = lax.axis_index("seq") * part_count
    own_readout = lax.dynamic_slice_in_dim(readout, first_channel, part_count, 1)
    own_step = lax.dynamic_slice_in_dim(log_step, first_channel, part_count, 0)
    primal, backward = jax.vjp(discretize, own_readout, own_step, decay_log, rotation)
    totals = whole_channel_totals(lag_rows, primal[2], primal[3], norm_scale)
    readout_part, step_part, decay_part, rotation_part = parameter_grads(primal, backward, totals)
    shared = jnp.concatenate(
        [readout_part.reshape(-1), step_part, decay_part, rotation_part]
    )
    sent = jnp.concatenate(
        [
            lag_rows.transpose(1, 0, 2).reshape(owners, -1),
            jnp.broadcast_to(shared, (owners, shared.shape[0])),
        ],
        axis=1,
    )
    got = lax.all_to_all(sent, "seq", split_axis=0, concat_axis=0, tiled=True)
    cuts = np.cumsum([part_count * length, 2 * part_count * states, part_count])
    lags, readouts, steps, state = jnp.split(got, cuts, axis=1)
    readouts = readouts.reshape(owners, 2, part_count, states).transpose(1, 0, 2, 3)
    return (
        lags.reshape(channels, length),
        readouts.reshape(2, channels, states),
        steps.reshape(channels),
        lax.psum(jnp.sum(state, axis=0), "ch").reshape(2, states),
    )


def split_halves(value):
    high = value.astype(jnp.bfloat16)
    return high, (value - high.astype(jnp.float32)).astype(jnp.bfloat16)


def cos_sin(angle):
    turns = jnp.floor(angle * (2.0 / math.pi) + 0.5)
    rest = angle - turns * 1.5703125
    rest = rest - turns * 4.837512969970703125e-4
    rest = rest - turns * 7.54978995489188216e-8
    quarter = turns.astype(jnp.int32)
    square = rest * rest
    sine = rest + rest * square * (
        -1.6666654611e-1 + square * (8.3321608736e-3 - square * 1.9515295891e-4)
    )
    cosine = (
        1.0
        - 0.5 * square
        + square
        * square
        * (
            4.166664568298827e-2
            + square * (-1.388731625493765e-3 + square * 2.443315711809948e-5)
        )
    )
    odd = (quarter & 1) == 1
    out_cos = jnp.where(odd, sine, cosine)
    out_sin = jnp.where(odd, cosine, sine)
    out_cos = jnp.where(((quarter + 1) & 2) == 2, -out_cos, out_cos)
    out_sin = jnp.where((quarter & 2) == 2, -out_sin, out_sin)
    return out_cos, out_sin


def grow(value):
    series = 1.0
    for term in range(9, 1, -1):
        series = 1.0 + series * value * (1.0 / term)
    return jnp.where(jnp.abs(value) < 0.35, series * value, jnp.exp(value) - 1.0)


def power(rate_real, rate_imag, offset):
    size = jnp.exp(rate_real * offset)
    cosine, sine = cos_sin(rate_imag * offset)
    return size * cosine, size * sine


def times(left, right):
    return (
        left[0] * right[0] - left[1] * right[1],
        left[0] * right[1] + left[1] * right[0],
    )


def blocks_forward(x):
    root = math.sqrt(0.5)
    cosine, sine = math.cos(math.pi / 8), math.sin(math.pi / 8)
    total = [x[s] + x[s + 4] for s in range(4)]
    gap = [x[s] - x[s + 4] for s in range(4)]
    even, odd = total[0] + total[2], total[1] + total[3]
    real, imag = [None] * 9, [None] * 9
    real[0], real[8] = even + odd, even - odd
    imag[0] = imag[8] = jnp.zeros_like(even)
    real[4], imag[4] = total[0] - total[2], total[3] - total[1]
    less, more = root * (gap[1] - gap[3]), root * (gap[1] + gap[3])
    real[2], imag[2] = gap[0] + less, -gap[2] - more
    real[6], imag[6] = gap[0] - less, gap[2] - more
    less, more = root * (x[2] - x[6]), root * (x[2] + x[6])
    even1 = (x[0] + less, -x[4] - more)
    even3 = (x[0] - less, x[4] - more)
    p, q, r, t = x[1] - x[7], x[3] - x[5], x[1] + x[7], x[3] + x[5]
    odd1 = (cosine * p + sine * q, -sine * r - cosine * t)
    odd3 = (sine * p - cosine * q, sine * t - cosine * r)
    real[1], imag[1] = even1[0] + odd1[0], even1[1] + odd1[1]
    real[7], imag[7] = even1[0] - odd1[0], odd1[1] - even1[1]
    real[3], imag[3] = even3[0] + odd3[0], even3[1] + odd3[1]
    real[5], imag[5] = even3[0] - odd3[0], odd3[1] - even3[1]
    return list(zip(real, imag))


def blocks_back(z):
    root = math.sqrt(0.5)
    cosine, sine = math.cos(math.pi / 8), math.sin(math.pi / 8)
    real, imag = [v[0] for v in z], [v[1] for v in z]
    even, odd = real[0] + real[8], real[0] - real[8]
    total = [even + real[4], odd + imag[4], even - real[4], odd - imag[4]]
    less, more = root * (real[2] - real[6]), root * (imag[2] + imag[6])
    gap = [real[2] + real[6], less + more, imag[2] - imag[6], more - less]
    x = [total[s] + gap[s] for s in range(4)] + [total[s] - gap[s] for s in range(4)]
    even1 = (real[1] + real[7], imag[7] - imag[1])
    even3 = (real[3] + real[5], imag[5] - imag[3])
    odd1 = (real[1] - real[7], imag[1] + imag[7])
    odd3 = (real[3] - real[5], imag[3] + imag[5])
    less, more = root * (even1[0] - even3[0]), root * (even1[1] + even3[1])
    p = cosine * odd1[0] + sine * odd3[0]
    q = sine * odd1[0] - cosine * odd3[0]
    r = sine * odd1[1] + cosine * odd3[1]
    t = cosine * odd1[1] - sine * odd3[1]
    extra = [
        even1[0] + even3[0],
        p + r,
        less - more,
        q + t,
        even3[1] - even1[1],
        t - q,
        -less - more,
        r - p,
    ]
    return [v + w for v, w in zip(x, extra)]


def transform_tables(owners, length, norm_scale):
    width = 2 * owners
    counter = np.arange(length)
    angles = two_pi * (counter[:, None] * counter[None, :] % length) / length
    cosine, sine = np.cos(angles), np.sin(angles)
    matrix = np.block([[cosine, -sine], [sine, cosine]]).astype(np.float32)
    high = matrix.astype(jnp.bfloat16)
    low = (matrix - high.astype(np.float32)).astype(jnp.bfloat16)
    outer = np.arange(owners + 1)
    angles = two_pi * (outer[:, None] * counter[None, :]) / (width * length)
    twiddle = np.stack([np.cos(angles), -np.sin(angles)], axis=1)
    weight = np.where(outer % owners == 0, 1.0, 2.0) * norm_scale / (width * length)
    twiddle = np.concatenate([twiddle, twiddle * weight[:, None, None]], axis=1)
    return np.stack([high, low]), twiddle.astype(np.float32)


def three_pieces(value):
    pieces = []
    for _ in range(3):
        piece = value.astype(jnp.bfloat16).astype(jnp.float32)
        pieces.append(piece)
        value = value - piece
    return pieces


def transposed(value):
    return jnp.concatenate(
        [value[:, spot : spot + LANES].T for spot in range(0, value.shape[1], LANES)], axis=0
    )


READ, STEP, ROWS = 16, 19, 20
LAGS, GRADS, STATE, SINGLES = 0, 8, 16, 18
STEP_LANES, SCALE_LANES = (0, 8), (16, 17, 18, 19)
SPARE = 15.0
PARTS = 4


def pack_kernel(inputs, out_grad, readout, log_step, out, signals, read, step, turned, rows, sems):
    peers = out.shape[0] // ROWS
    copies = [
        pltpu.make_async_copy(source, target, sems.at[i])
        for i, (source, target) in enumerate(
            ((readout, read), (log_step, step), (inputs, signals.at[0]), (out_grad, signals.at[1]))
        )
    ]
    for copy in copies:
        copy.start()
    copies[0].wait()
    copies[1].wait()
    own = lax.axis_index("seq")
    turned[0] = transposed(read[...])
    turned[1] = transposed(jnp.broadcast_to(step[...], (LANES, step.shape[1])))
    for place, value in enumerate(
        three_pieces(turned[0, pl.ds(own, peers, stride=SUBLANES), :])
    ):
        rows[pl.ds(READ + place, peers, stride=ROWS), :] = value
    pieces = three_pieces(turned[1, pl.ds(own, peers, stride=SUBLANES), :])
    lane = lax.broadcasted_iota(jnp.int32, (peers, LANES), 1)
    value = jnp.where(lane == 0, pieces[0], jnp.where(lane == 1, pieces[1], pieces[2]))
    rows[pl.ds(STEP, peers, stride=ROWS), :] = value
    for place in range(2):
        copies[2 + place].wait()
        value = signals[place].astype(jnp.float32)
        for peer in range(peers):
            spot = peer * ROWS + place * SUBLANES
            rows[spot : spot + SUBLANES] = value[peer * SUBLANES : (peer + 1) * SUBLANES]
    out[...] = rows[...].astype(jnp.bfloat16)


def hold_kernel(*refs):
    for source, target in zip(refs[: len(refs) // 2], refs[len(refs) // 2 :]):
        target[...] = source[...]


def exponent_of(bound):
    return jnp.floor(jnp.log(jnp.maximum(bound, 1e-30)) * (1.0 / math.log(2.0))) + (2.0 - SPARE)


def greatest(value):
    return jnp.max(jnp.max(value, axis=1, keepdims=True), axis=0, keepdims=True)


def size_of(value):
    return jnp.abs(value[0]) + jnp.abs(value[1])


def two_pieces(value):
    high = value.astype(jnp.bfloat16).astype(jnp.float32)
    return high, (value - high) * 256.0


def main_kernel(
    owners,
    norm_scale,
    got,
    matrix,
    twiddle,
    decay_log,
    rotation,
    sent,
    rows_in,
    spectra,
    freq,
    back,
    params,
    doubled,
    bases,
    powers,
    lags,
    sums,
):
    peers, length = got.shape[0] // ROWS, got.shape[1]
    groups = peers // owners
    part_count = groups * SUBLANES
    rows = 2 * part_count
    pairs = part_count // 2
    half = pairs // SUBLANES
    reach = length // 2
    lane = lax.broadcasted_iota(jnp.int32, (pairs, LANES), 1)
    left = lane < LANES // 2
    row = lax.broadcasted_iota(jnp.int32, (SUBLANES, LANES), 0)

    def swap(value):
        return pltpu.roll(value, LANES // 2, 1)

    def lanes_of(side):
        return slice(side * LANES, (side + 1) * LANES)

    def collect(spot):
        tiles = [
            rows_in[pl.ds(group * owners * ROWS + spot, owners, stride=ROWS), :]
            for group in range(groups)
        ]
        return jnp.concatenate(tiles[:half], axis=0), jnp.concatenate(tiles[half:], axis=0)

    def make_params():
        lower, upper = [sum(side) for side in zip(*(collect(READ + i) for i in range(3)))]
        read = (jnp.where(left, lower, swap(upper)), jnp.where(left, swap(lower), upper))
        lower, upper = [
            sum(side[:, i : i + 1] for i in range(3)) + jnp.zeros_like(side)
            for side in collect(STEP)
        ]
        step = jnp.exp(jnp.where(left, lower, upper))
        decay_row = jnp.concatenate([decay_log[...], decay_log[...]], axis=1)
        rotation_row = jnp.concatenate([rotation[...], rotation[...]], axis=1)
        pole = (
            jnp.broadcast_to(-jnp.exp(decay_row), step.shape),
            jnp.broadcast_to(rotation_row, step.shape),
        )
        rate = (step * pole[0], step * pole[1])
        place, size = 0, 1
        while size < owners * length:
            doubled[place], doubled[place + 1] = power(rate[0], rate[1], float(size))
            place, size = place + 2, size * 2
        sine = cos_sin(0.5 * rate[1])[1]
        cosine = 1.0 - 2.0 * sine * sine
        lift = (grow(rate[0]) * cosine - 2.0 * sine * sine, doubled[1])
        norm = 1.0 / (pole[0] * pole[0] + pole[1] * pole[1])
        inverse = (pole[0] * norm, -pole[1] * norm)
        ratio = times(lift, inverse)
        coef = times(read, ratio)
        lifted = times((doubled[0], doubled[1]), inverse)
        values = (rate, ratio, coef, times(read, lifted), pole, times(coef, inverse), (step, step))
        for place, value in enumerate(values):
            params[2 * place], params[2 * place + 1] = value

    block_bit, reach_bit = length.bit_length() - 1, reach.bit_length() - 1
    bits = [(row & (1 << i)) != 0 for i in range(SUBLANES.bit_length() - 1)]

    def doubled_row(p, i):
        return doubled[2 * i, p : p + 1, :], doubled[2 * i + 1, p : p + 1, :]

    def by_rows(p, first):
        out = None
        for i, bit in enumerate(bits):
            real, imag = doubled_row(p, first + i)
            value = (jnp.where(bit, real, 1.0), jnp.where(bit, imag, 0.0))
            out = value if out is None else times(out, value)
        return out

    def make_tables():
        for p in range(pairs):
            table = [by_rows(p, 0)]
            for i in range(len(bits), reach_bit):
                table += [times(block, doubled_row(p, i)) for block in table]
            for place in range(0, len(table), 2):
                for side in range(2):
                    value = jnp.concatenate([table[place][side], table[place + 1][side]], axis=0)
                    for i, piece in enumerate(split_halves(value)):
                        spot = 2 * i * reach + place * SUBLANES
                        powers[p, spot : spot + 2 * SUBLANES, lanes_of(side)] = piece
                        spot += reach
                        powers[p, spot : spot + 2 * SUBLANES, lanes_of(side)] = piece
            base = by_rows(p, block_bit)
            bases[p, 0], bases[p, 1] = base
            bases[p, 2], bases[p, 3] = times(base, doubled_row(p, reach_bit))

    def transform(source, target, count):
        dot = functools.partial(jnp.dot, preferred_element_type=jnp.float32)
        cuts = [(owners + 1) * i // PARTS * count for i in range(PARTS + 1)]
        for part in map(slice, cuts, cuts[1:]):
            low = source[1, part]
            target[part] = (
                dot(source[0, part], matrix[0]) + dot(low, matrix[0]) + dot(source[0, part], matrix[1])
            )

    def spread_blocks():
        rows_in[...] = got[...].astype(jnp.float32)
        blocks = []
        for s in range(owners):
            spots = [(group * owners + s) * ROWS for group in range(groups)]
            blocks.append(
                jnp.concatenate(
                    [rows_in[spot : spot + SUBLANES] for spot in spots]
                    + [rows_in[spot + SUBLANES : spot + 2 * SUBLANES] for spot in spots],
                    axis=0,
                )
            )
        for k, value in enumerate(blocks_forward(blocks)):
            if k:
                value = times(value, (twiddle[k, 0:1], twiddle[k, 1:2]))
            for side in range(2):
                for i, piece in enumerate(split_halves(value[side])):
                    spectra[i, k * rows : (k + 1) * rows, lanes_of(side)] = piece

    def to_frequencies():
        transform(spectra, freq, rows)
        make_params()
        make_tables()

    def to_lags():
        for k in range(owners + 1):
            at_in = freq[k * rows : k * rows + part_count]
            at_out = freq[k * rows + part_count : (k + 1) * rows]
            ur, ui = at_in[:, :length], at_in[:, length:]
            gr, gi = at_out[:, :length], at_out[:, length:]
            for side, value in enumerate((gr * ur + gi * ui, gr * ui - gi * ur)):
                for i, piece in enumerate(split_halves(value)):
                    spectra[i, k * part_count : (k + 1) * part_count, lanes_of(side)] = piece
        transform(spectra, back, part_count)

    def finish():
        turned = []
        for k in range(owners + 1):
            spots = slice(k * part_count, (k + 1) * part_count)
            value = (back[spots, lanes_of(0)], back[spots, lanes_of(1)])
            turned.append(times(value, (twiddle[k, 2:3], twiddle[k, 3:4])))
        blocks = blocks_back(turned)

        most = jnp.zeros((part_count, LANES), jnp.float32)
        for b, block in enumerate(blocks):
            most = jnp.maximum(most, jnp.abs(block))
            lags[b * part_count : (b + 1) * part_count] = block

        def param(place):
            return params[2 * place], params[2 * place + 1]

        rate, ratio, coef, through, pole, direct, (step, _) = (param(i) for i in range(7))
        most = greatest(most)
        whole = 2.0 * math.sqrt(owners * length)
        on_rate = size_of(coef) * float(owners * length) + size_of(through)
        on_pole = step * on_rate + size_of(direct)
        lag_exponent = exponent_of(most)
        grad_exponent = exponent_of(most * (whole * greatest(size_of(ratio))))
        state_exponent = exponent_of(
            most * (whole * part_count * greatest(on_pole * (1.0 - pole[0])))
        )
        step_exponent = exponent_of(
            most * (whole * (LANES // 2) * greatest(on_rate * size_of(rate)))
        )
        lag_scale = jnp.exp2(-lag_exponent)
        for b, block in enumerate(blocks):
            for group in range(groups):
                place = (group * owners + b) * ROWS
                value = block[group * SUBLANES : (group + 1) * SUBLANES]
                sent[place + LAGS : place + GRADS] = value * lag_scale

        start = row.astype(jnp.float32) * float(length)
        first = left[:owners]
        wide = lax.broadcasted_iota(jnp.int32, (4 * owners, LANES), 1)
        wide_left = wide < reach
        offset = jnp.where(wide_left, wide, wide - reach).astype(jnp.float32)
        both_left = wide_left[: 2 * owners]
        for p in range(pairs):
            both = jnp.concatenate(
                [
                    lags[pl.ds(first_row, owners, stride=part_count), :]
                    for first_row in (p, pairs + p)
                ],
                axis=0,
            )
            swapped = swap(both)
            plain = jnp.concatenate(
                [jnp.where(both_left, both, swapped), jnp.where(both_left, swapped, both)], axis=0
            )
            factor = []
            for value in (plain, plain * offset):
                high = value.astype(jnp.bfloat16).astype(jnp.float32)
                factor.append(jnp.where(wide_left, high, value - high))
            factor = jnp.concatenate(factor, axis=0).astype(jnp.bfloat16)
            raw = jnp.dot(
                jnp.concatenate([factor, factor], axis=1),
                powers[p],
                preferred_element_type=jnp.float32,
            )

            def pick(place, side):
                top = raw[2 * place * owners : (2 * place + 1) * owners, lanes_of(side)]
                bottom = raw[(2 * place + 1) * owners : (2 * place + 2) * owners, lanes_of(side)]
                return jnp.where(first, top, bottom)

            found = None
            for part in range(2):
                base = (bases[p, 2 * part], bases[p, 2 * part + 1])
                near = start + float(part * reach)
                value = (pick(part, 0), pick(part, 1))
                lagged = (near * value[0] + pick(2 + part, 0), near * value[1] + pick(2 + part, 1))
                terms = times(base, value) + times(base, lagged)
                found = terms if found is None else [x + y for x, y in zip(found, terms)]
            for place, value in enumerate(found):
                sums[place, p : p + 1] = jnp.sum(value, axis=0, keepdims=True)

        total = (sums[0] * (2.0 * norm_scale), sums[1] * (2.0 * norm_scale))
        lag_total = (sums[2] * (2.0 * norm_scale), sums[3] * (2.0 * norm_scale))
        on_read = times(total, ratio)
        on_read = (on_read[0], -on_read[1])
        on_rate = times(coef, lag_total)
        more = times(total, through)
        on_rate = (on_rate[0] + more[0], on_rate[1] + more[1])
        less = times(total, direct)
        on_pole = (step * on_rate[0] - less[0], step * on_rate[1] - less[1])
        on_step = times(on_rate, rate)[0]
        on_decay = jnp.sum(on_pole[0] * pole[0], axis=0, keepdims=True)
        on_rotation = -jnp.sum(on_pole[1], axis=0, keepdims=True)
        on_decay = on_decay + swap(on_decay)
        on_rotation = on_rotation + swap(on_rotation)
        state = jnp.where(left[0:1], on_decay, on_rotation) * jnp.exp2(-state_exponent)

        grad_scale = jnp.exp2(-grad_exponent)
        on_read = (on_read[0] * grad_scale, on_read[1] * grad_scale)
        lower = jnp.where(left, on_read[0], swap(on_read[1]))
        upper = jnp.where(left, swap(on_read[0]), on_read[1])
        grads = jnp.concatenate([lower, upper], axis=0)
        step_column = jnp.concatenate(
            [
                jnp.sum(jnp.where(left, on_step, 0.0), axis=1, keepdims=True),
                jnp.sum(jnp.where(left, 0.0, on_step), axis=1, keepdims=True),
            ],
            axis=0,
        ) * jnp.exp2(-step_exponent)
        place_lane = lax.broadcasted_iota(jnp.int32, (SUBLANES, LANES), 1)
        scales = jnp.zeros((1, LANES), jnp.float32)
        for spot, value in zip(
            SCALE_LANES, (lag_exponent, grad_exponent, state_exponent, step_exponent)
        ):
            scales = jnp.where(place_lane[0:1] == spot, value, scales)
        state_high, state_low = two_pieces(state)
        tails = []
        for group in range(groups):
            pieces = two_pieces(step_column[group * SUBLANES : (group + 1) * SUBLANES])
            spread = jnp.zeros((SUBLANES, LANES), jnp.float32)
            for spot, piece in zip(STEP_LANES, pieces):
                spread = jnp.where(place_lane == row + spot, piece, spread)
            singles = scales + jnp.sum(spread, axis=0, keepdims=True)
            tails.append(jnp.concatenate([state_high, state_low, singles, singles], axis=0))
        for b in range(owners):
            for group in range(groups):
                place = (group * owners + b) * ROWS
                sent[place + GRADS : place + STATE] = grads[
                    group * SUBLANES : (group + 1) * SUBLANES
                ]
                sent[place + STATE : place + ROWS] = tails[group]

    for section in (spread_blocks, to_frequencies, to_lags, finish):
        section()


def unpack_kernel(got, kernel_grad, readout_grad, step_grad, state_grad, wide, grads):
    peers = got.shape[0] // ROWS
    per_row = LANES // SUBLANES
    singles = got[pl.ds(SINGLES, peers, stride=ROWS), :]
    exponents = [jnp.broadcast_to(singles[:, spot : spot + 1], (peers, LANES)) for spot in SCALE_LANES]
    scales = [jnp.exp2(value) for value in exponents]
    for i in range(2):
        wide[i] = scales[i]
    for spot in range(0, peers, per_row):
        part = slice(spot * SUBLANES, (spot + per_row) * SUBLANES)
        for i, first, target in ((1, GRADS, grads), (0, LAGS, kernel_grad)):
            for peer in range(spot, spot + per_row):
                place = peer * ROWS + first
                target[peer * SUBLANES : (peer + 1) * SUBLANES] = (
                    got[place : place + SUBLANES] * wide[i, peer : peer + 1, :]
                )
        readout_grad[:, part] = grads[part].T

    high = got[pl.ds(STATE, peers, stride=ROWS), :]
    low = got[pl.ds(STATE + 1, peers, stride=ROWS), :]
    total = jnp.sum((high + low * (1.0 / 256.0)) * scales[2], axis=0, keepdims=True)
    states = state_grad.shape[1]
    state_grad[0:1] = total[:, :states]
    state_grad[1:2] = total[:, states:]
    lane = lax.broadcasted_iota(jnp.int32, (peers, LANES), 1)
    row = lax.broadcasted_iota(jnp.int32, (peers, LANES), 0)
    high, low = (
        jnp.take_along_axis(singles, lane % SUBLANES + first, axis=1) for first in STEP_LANES
    )
    value = (high + low * (1.0 / 256.0)) * scales[3]
    for spot in range(0, peers, per_row):
        mine = jnp.where(row - spot == lane // SUBLANES, value, 0.0)
        step_grad[spot * SUBLANES : (spot + per_row) * SUBLANES] = jnp.sum(mine, axis=0)


def kernel_device(inputs, out_grad, readout, log_step, decay_log, rotation):
    owners, groups = lax.axis_size("seq"), lax.axis_size("ch")
    peers = owners * groups
    channels, length = inputs.shape
    states = decay_log.shape[0]
    part_count = channels // owners
    pairs = part_count // 2
    norm_scale = 1.0 / math.sqrt(owners * length)
    vmem = pl.BlockSpec(memory_space=pltpu.VMEM)
    memory = pltpu.CompilerParams(vmem_limit_bytes=32 * 1024 * 1024)
    f32, bf16 = jnp.float32, jnp.bfloat16

    def exchange(value):
        value = value.reshape(peers, ROWS // 2, 2, LANES)
        value = lax.all_to_all(value, ("ch", "seq"), split_axis=0, concat_axis=0, tiled=True)
        return value.reshape(peers * ROWS, LANES)

    anywhere = pl.BlockSpec(memory_space=pl.ANY)
    pieces = pl.pallas_call(
        pack_kernel,
        out_shape=jax.ShapeDtypeStruct((peers * ROWS, LANES), bf16),
        in_specs=[anywhere] * 4,
        out_specs=vmem,
        scratch_shapes=[
            pltpu.VMEM((2, channels, LANES), bf16),
            pltpu.VMEM((LANES, channels), f32),
            pltpu.VMEM((1, channels), f32),
            pltpu.VMEM((2, channels, LANES), f32),
            pltpu.VMEM((peers * ROWS, LANES), f32),
            pltpu.SemaphoreType.DMA((4,)),
        ],
        compiler_params=pltpu.CompilerParams(vmem_limit_bytes=60 * 1024 * 1024),
    )(inputs, out_grad, readout.transpose(0, 2, 1).reshape(LANES, channels), log_step[None])
    got = exchange(pieces)

    held = [jnp.asarray(table) for table in transform_tables(owners, length, norm_scale)]
    held += [decay_log[None], rotation[None]]
    held = pl.pallas_call(
        hold_kernel,
        out_shape=[jax.ShapeDtypeStruct(value.shape, value.dtype) for value in held],
        in_specs=[vmem] * 4,
        out_specs=[vmem] * 4,
        compiler_params=memory,
    )(*held)
    sent = pl.pallas_call(
        functools.partial(main_kernel, owners, norm_scale),
        out_shape=jax.ShapeDtypeStruct((peers * ROWS, LANES), f32),
        in_specs=[vmem] * 5,
        out_specs=vmem,
        scratch_shapes=[
            pltpu.VMEM((peers * ROWS, LANES), f32),
            pltpu.VMEM((2, (owners + 1) * 2 * part_count, 2 * LANES), bf16),
            pltpu.VMEM(((owners + 1) * 2 * part_count, 2 * LANES), f32),
            pltpu.VMEM(((owners + 1) * part_count, 2 * LANES), f32),
            pltpu.VMEM((14, pairs, LANES), f32),
            pltpu.VMEM((2 * (owners * length).bit_length(), pairs, LANES), f32),
            pltpu.VMEM((pairs, 4, owners, LANES), f32),
            pltpu.VMEM((pairs, 2 * length, 2 * LANES), bf16),
            pltpu.VMEM((owners * part_count, length), f32),
            pltpu.VMEM((4, pairs, LANES), f32),
        ],
        compiler_params=memory,
    )(got, *held)
    back = exchange(sent.astype(jnp.float16))
    kernel_grad, readout_grad, step_grad, state_grad = pl.pallas_call(
        unpack_kernel,
        out_shape=[
            jax.ShapeDtypeStruct((channels, length), f32),
            jax.ShapeDtypeStruct((LANES, channels), f32),
            jax.ShapeDtypeStruct((channels,), f32),
            jax.ShapeDtypeStruct((2, states), f32),
        ],
        in_specs=[vmem],
        out_specs=[vmem] * 4,
        scratch_shapes=[
            pltpu.VMEM((2, peers, LANES), f32),
            pltpu.VMEM((channels, LANES), f32),
        ],
        compiler_params=memory,
    )(back.astype(f32))
    readout_grad = readout_grad.reshape(2, states, channels).transpose(0, 2, 1)
    return kernel_grad, readout_grad, step_grad, state_grad


def kernel_fits(mesh, inputs, decay_log):
    owners, groups = mesh.shape["seq"], mesh.shape["ch"]
    channels = inputs.shape[0] // groups
    return (
        inputs.shape[1] == owners * LANES
        and 2 * decay_log.shape[0] == LANES
        and owners == SUBLANES
        and groups % 2 == 0
        and channels == owners * groups * SUBLANES
        and channels % LANES == 0
    )


def solution(mesh):
    def whole(inputs, out_grad, readout, log_step, decay_log, rotation):
        fits = kernel_fits(mesh, inputs, decay_log)
        return jax.shard_map(
            kernel_device if fits else general_device,
            mesh=mesh,
            in_specs=(P("ch", "seq"), P("ch", "seq"), P(None, "ch", None), P("ch"), P(), P()),
            out_specs=(P("ch", "seq"), P(None, "ch", None), P("ch"), P()),
            check_vma=False,
        )(inputs, out_grad, readout, log_step, decay_log, rotation)

    return whole
```

```python
import functools
import math

import jax
import jax.numpy as jnp
import numpy as np
from jax import lax
from jax.experimental import pallas as pl
from jax.experimental.pallas import tpu as pltpu
from jax.sharding import PartitionSpec as P

precise = lax.Precision.HIGHEST
two_pi = 2.0 * math.pi
LANES = 128
SUBLANES = 8


def angle_table(left_index, right_index, modulus, orient):
    product = left_index[:, None] * right_index[None, :] % modulus
    return orient * two_pi * product.astype(jnp.float32) / modulus


def rotate(real_part, imag_part, angles):
    cosine_table = jnp.cos(angles)
    sine_table = jnp.sin(angles)
    return (
        real_part * cosine_table - imag_part * sine_table,
        real_part * sine_table + imag_part * cosine_table,
    )


def last_transform(real_part, imag_part, orient):
    length = real_part.shape[-1]
    counter = jnp.arange(length, dtype=jnp.int32)
    angles = angle_table(counter, counter, length, orient)
    cosine_table = jnp.cos(angles)
    sine_table = jnp.sin(angles)
    dot = functools.partial(jnp.dot, precision=precise, preferred_element_type=jnp.float32)
    return (
        dot(real_part, cosine_table) - dot(imag_part, sine_table),
        dot(imag_part, cosine_table) + dot(real_part, sine_table),
    )


def discretize(readout, log_step, decay_log, rotation):
    step_size = jnp.exp(log_step)[:, None]
    pole_real = -jnp.exp(decay_log)[None, :]
    pole_imag = rotation[None, :]
    rate_real = step_size * pole_real
    rate_imag = step_size * pole_imag
    lift_real = jnp.expm1(rate_real) * jnp.cos(rate_imag) - 2.0 * jnp.sin(0.5 * rate_imag) ** 2
    lift_imag = jnp.exp(rate_real) * jnp.sin(rate_imag)
    pole_norm = pole_real * pole_real + pole_imag * pole_imag
    ratio_real = (lift_real * pole_real + lift_imag * pole_imag) / pole_norm
    ratio_imag = (lift_imag * pole_real - lift_real * pole_imag) / pole_norm
    coef_real = readout[0] * ratio_real - readout[1] * ratio_imag
    coef_imag = readout[0] * ratio_imag + readout[1] * ratio_real
    return (coef_real, coef_imag, rate_real, rate_imag)


def parameter_grads(primal, backward, totals):
    coef_real, coef_imag = (primal[0], primal[1])
    cotangents = (
        2.0 * totals[0],
        -2.0 * totals[1],
        2.0 * (coef_real * totals[2] - coef_imag * totals[3]),
        -2.0 * (coef_real * totals[3] + coef_imag * totals[2]),
    )
    return backward(cotangents)


def shifted_totals(raw_sums, rate_real, rate_imag, block_start, norm_scale):
    decays = jnp.exp(rate_real * block_start)
    phases = rate_imag * block_start
    base_real = decays * jnp.cos(phases)
    base_imag = decays * jnp.sin(phases)
    near_real = block_start * raw_sums[0] + raw_sums[2]
    near_imag = block_start * raw_sums[1] + raw_sums[3]
    return jnp.stack(
        [
            norm_scale * (base_real * raw_sums[0] - base_imag * raw_sums[1]),
            norm_scale * (base_real * raw_sums[1] + base_imag * raw_sums[0]),
            norm_scale * (base_real * near_real - base_imag * near_imag),
            norm_scale * (base_real * near_imag + base_imag * near_real),
        ]
    )


def whole_channel_totals(lag_rows, rate_real, rate_imag, norm_scale):
    owners, length = (lag_rows.shape[1], lag_rows.shape[2])
    offsets = jnp.arange(length, dtype=jnp.int32).astype(jnp.float32)
    decays = jnp.exp(rate_real[:, :, None] * offsets)
    phases = rate_imag[:, :, None] * offsets
    power_real = decays * jnp.cos(phases)
    power_imag = decays * jnp.sin(phases)
    weighted = lag_rows * offsets
    raw_sums = jnp.stack(
        [
            jnp.einsum("cbj,cnj->cnb", lag_rows, power_real, precision=precise),
            jnp.einsum("cbj,cnj->cnb", lag_rows, power_imag, precision=precise),
            jnp.einsum("cbj,cnj->cnb", weighted, power_real, precision=precise),
            jnp.einsum("cbj,cnj->cnb", weighted, power_imag, precision=precise),
        ]
    )
    starts = (jnp.arange(owners, dtype=jnp.int32) * length).astype(jnp.float32)
    totals = shifted_totals(
        raw_sums, rate_real[:, :, None], rate_imag[:, :, None], starts, norm_scale
    )
    return jnp.sum(totals, axis=-1)


def general_lags(whole, norm_scale):
    part_count, owners, length = whole.shape[1:]
    freq_width = 2 * owners
    modulus = freq_width * length
    row_index = jnp.arange(owners, dtype=jnp.int32)
    outer_index = jnp.arange(freq_width, dtype=jnp.int32)
    inner_index = jnp.arange(length, dtype=jnp.int32)
    first = angle_table(row_index, outer_index, freq_width, -1.0)
    spec_real = jnp.einsum("scba,bk->scka", whole, jnp.cos(first), precision=precise)
    spec_imag = jnp.einsum("scba,bk->scka", whole, jnp.sin(first), precision=precise)
    spec_real, spec_imag = rotate(
        spec_real, spec_imag, angle_table(outer_index, inner_index, modulus, -1.0)
    )
    freq_real, freq_imag = last_transform(spec_real, spec_imag, -1.0)
    prod_real = freq_real[1] * freq_real[0] + freq_imag[1] * freq_imag[0]
    prod_imag = freq_imag[1] * freq_real[0] - freq_real[1] * freq_imag[0]
    back_real, back_imag = last_transform(prod_real, prod_imag, 1.0)
    back_real, back_imag = rotate(
        back_real, back_imag, angle_table(outer_index, inner_index, modulus, 1.0)
    )
    final = angle_table(outer_index, row_index, freq_width, 1.0)
    lag_rows = jnp.einsum("cka,kb->cba", back_real, jnp.cos(final), precision=precise) - jnp.einsum(
        "cka,kb->cba", back_imag, jnp.sin(final), precision=precise
    )
    return lag_rows * (norm_scale / modulus)


def general_device(inputs, out_grad, readout, log_step, decay_log, rotation):
    owners = lax.axis_size("seq")
    channels, length = inputs.shape
    states = decay_log.shape[0]
    part_count = channels // owners
    norm_scale = 1.0 / math.sqrt(owners * length)
    pieces = jnp.concatenate(
        [a.reshape(owners, part_count, length) for a in (inputs, out_grad)], axis=1
    )
    pieces = lax.all_to_all(pieces, "seq", split_axis=0, concat_axis=0, tiled=True)
    whole = pieces.astype(jnp.float32).reshape(owners, 2, part_count, length)
    lag_rows = general_lags(whole.transpose(1, 2, 0, 3), norm_scale)
    first_channel = lax.axis_index("seq") * part_count
    own_readout = lax.dynamic_slice_in_dim(readout, first_channel, part_count, 1)
    own_step = lax.dynamic_slice_in_dim(log_step, first_channel, part_count, 0)
    primal, backward = jax.vjp(discretize, own_readout, own_step, decay_log, rotation)
    totals = whole_channel_totals(lag_rows, primal[2], primal[3], norm_scale)
    readout_part, step_part, decay_part, rotation_part = parameter_grads(primal, backward, totals)
    shared = jnp.concatenate(
        [readout_part.reshape(-1), step_part, decay_part, rotation_part]
    )
    sent = jnp.concatenate(
        [
            lag_rows.transpose(1, 0, 2).reshape(owners, -1),
            jnp.broadcast_to(shared, (owners, shared.shape[0])),
        ],
        axis=1,
    )
    got = lax.all_to_all(sent, "seq", split_axis=0, concat_axis=0, tiled=True)
    cuts = np.cumsum([part_count * length, 2 * part_count * states, part_count])
    lags, readouts, steps, state = jnp.split(got, cuts, axis=1)
    readouts = readouts.reshape(owners, 2, part_count, states).transpose(1, 0, 2, 3)
    return (
        lags.reshape(channels, length),
        readouts.reshape(2, channels, states),
        steps.reshape(channels),
        lax.psum(jnp.sum(state, axis=0), "ch").reshape(2, states),
    )


def split_halves(value):
    high = value.astype(jnp.bfloat16)
    return high, (value - high.astype(jnp.float32)).astype(jnp.bfloat16)


def cos_sin(angle):
    turns = jnp.floor(angle * (2.0 / math.pi) + 0.5)
    rest = angle - turns * 1.5703125
    rest = rest - turns * 4.837512969970703125e-4
    rest = rest - turns * 7.54978995489188216e-8
    quarter = turns.astype(jnp.int32)
    square = rest * rest
    sine = rest + rest * square * (
        -1.6666654611e-1 + square * (8.3321608736e-3 - square * 1.9515295891e-4)
    )
    cosine = (
        1.0
        - 0.5 * square
        + square
        * square
        * (
            4.166664568298827e-2
            + square * (-1.388731625493765e-3 + square * 2.443315711809948e-5)
        )
    )
    odd = (quarter & 1) == 1
    out_cos = jnp.where(odd, sine, cosine)
    out_sin = jnp.where(odd, cosine, sine)
    out_cos = jnp.where(((quarter + 1) & 2) == 2, -out_cos, out_cos)
    out_sin = jnp.where((quarter & 2) == 2, -out_sin, out_sin)
    return out_cos, out_sin


def grow(value):
    series = 1.0
    for term in range(9, 1, -1):
        series = 1.0 + series * value * (1.0 / term)
    return jnp.where(jnp.abs(value) < 0.35, series * value, jnp.exp(value) - 1.0)


def power(rate_real, rate_imag, offset):
    size = jnp.exp(rate_real * offset)
    cosine, sine = cos_sin(rate_imag * offset)
    return size * cosine, size * sine


def times(left, right):
    return (
        left[0] * right[0] - left[1] * right[1],
        left[0] * right[1] + left[1] * right[0],
    )


def blocks_forward(x):
    root = math.sqrt(0.5)
    cosine, sine = math.cos(math.pi / 8), math.sin(math.pi / 8)
    total = [x[s] + x[s + 4] for s in range(4)]
    gap = [x[s] - x[s + 4] for s in range(4)]
    even, odd = total[0] + total[2], total[1] + total[3]
    real, imag = [None] * 9, [None] * 9
    real[0], real[8] = even + odd, even - odd
    imag[0] = imag[8] = jnp.zeros_like(even)
    real[4], imag[4] = total[0] - total[2], total[3] - total[1]
    less, more = root * (gap[1] - gap[3]), root * (gap[1] + gap[3])
    real[2], imag[2] = gap[0] + less, -gap[2] - more
    real[6], imag[6] = gap[0] - less, gap[2] - more
    less, more = root * (x[2] - x[6]), root * (x[2] + x[6])
    even1 = (x[0] + less, -x[4] - more)
    even3 = (x[0] - less, x[4] - more)
    p, q, r, t = x[1] - x[7], x[3] - x[5], x[1] + x[7], x[3] + x[5]
    odd1 = (cosine * p + sine * q, -sine * r - cosine * t)
    odd3 = (sine * p - cosine * q, sine * t - cosine * r)
    real[1], imag[1] = even1[0] + odd1[0], even1[1] + odd1[1]
    real[7], imag[7] = even1[0] - odd1[0], odd1[1] - even1[1]
    real[3], imag[3] = even3[0] + odd3[0], even3[1] + odd3[1]
    real[5], imag[5] = even3[0] - odd3[0], odd3[1] - even3[1]
    return list(zip(real, imag))


def blocks_back(z):
    root = math.sqrt(0.5)
    cosine, sine = math.cos(math.pi / 8), math.sin(math.pi / 8)
    real, imag = [v[0] for v in z], [v[1] for v in z]
    even, odd = real[0] + real[8], real[0] - real[8]
    total = [even + real[4], odd + imag[4], even - real[4], odd - imag[4]]
    less, more = root * (real[2] - real[6]), root * (imag[2] + imag[6])
    gap = [real[2] + real[6], less + more, imag[2] - imag[6], more - less]
    x = [total[s] + gap[s] for s in range(4)] + [total[s] - gap[s] for s in range(4)]
    even1 = (real[1] + real[7], imag[7] - imag[1])
    even3 = (real[3] + real[5], imag[5] - imag[3])
    odd1 = (real[1] - real[7], imag[1] + imag[7])
    odd3 = (real[3] - real[5], imag[3] + imag[5])
    less, more = root * (even1[0] - even3[0]), root * (even1[1] + even3[1])
    p = cosine * odd1[0] + sine * odd3[0]
    q = sine * odd1[0] - cosine * odd3[0]
    r = sine * odd1[1] + cosine * odd3[1]
    t = cosine * odd1[1] - sine * odd3[1]
    extra = [
        even1[0] + even3[0],
        p + r,
        less - more,
        q + t,
        even3[1] - even1[1],
        t - q,
        -less - more,
        r - p,
    ]
    return [v + w for v, w in zip(x, extra)]


def transform_tables(owners, length, norm_scale):
    width = 2 * owners
    counter = np.arange(length)
    angles = two_pi * (counter[:, None] * counter[None, :] % length) / length
    cosine, sine = np.cos(angles), np.sin(angles)
    matrix = np.block([[cosine, -sine], [sine, cosine]]).astype(np.float32)
    high = matrix.astype(jnp.bfloat16)
    low = (matrix - high.astype(np.float32)).astype(jnp.bfloat16)
    outer = np.arange(owners + 1)
    angles = two_pi * (outer[:, None] * counter[None, :]) / (width * length)
    twiddle = np.stack([np.cos(angles), -np.sin(angles)], axis=1)
    weight = np.where(outer % owners == 0, 1.0, 2.0) * norm_scale / (width * length)
    twiddle = np.concatenate([twiddle, twiddle * weight[:, None, None]], axis=1)
    return np.stack([high, low]), twiddle.astype(np.float32)


def three_pieces(value):
    pieces = []
    for _ in range(3):
        piece = value.astype(jnp.bfloat16).astype(jnp.float32)
        pieces.append(piece)
        value = value - piece
    return pieces


def transposed(value):
    return jnp.concatenate(
        [value[:, spot : spot + LANES].T for spot in range(0, value.shape[1], LANES)], axis=0
    )


READ, STEP, ROWS = 16, 19, 20
LAGS, GRADS, STATE, SINGLES = 0, 8, 16, 18
STEP_LANES, SCALE_LANES = (0, 8), (16, 17, 18, 19)
SPARE = 15.0
PARTS = 4


def pack_kernel(inputs, out_grad, readout, log_step, *refs):
    count = (len(refs) - 7) // 2
    sources, (out, *held) = refs[:count], refs[count : 2 * count + 1]
    signals, read, step, turned, rows, sems = refs[2 * count + 1 :]
    peers = out.shape[0] // ROWS
    copies = [
        pltpu.make_async_copy(source, target, sems.at[i])
        for i, (source, target) in enumerate(
            (
                (readout, read),
                (log_step, step),
                (inputs, signals.at[0]),
                (out_grad, signals.at[1]),
                *zip(sources, held),
            )
        )
    ]
    for copy in copies:
        copy.start()
    copies[0].wait()
    copies[1].wait()
    own = lax.axis_index("seq")
    turned[0] = transposed(read[...])
    turned[1] = transposed(jnp.broadcast_to(step[...], (LANES, step.shape[1])))
    for place, value in enumerate(
        three_pieces(turned[0, pl.ds(own, peers, stride=SUBLANES), :])
    ):
        rows[pl.ds(READ + place, peers, stride=ROWS), :] = value
    pieces = three_pieces(turned[1, pl.ds(own, peers, stride=SUBLANES), :])
    lane = lax.broadcasted_iota(jnp.int32, (peers, LANES), 1)
    value = jnp.where(lane == 0, pieces[0], jnp.where(lane == 1, pieces[1], pieces[2]))
    rows[pl.ds(STEP, peers, stride=ROWS), :] = value
    for place in range(2):
        copies[2 + place].wait()
        value = signals[place].astype(jnp.float32)
        for peer in range(peers):
            spot = peer * ROWS + place * SUBLANES
            rows[spot : spot + SUBLANES] = value[peer * SUBLANES : (peer + 1) * SUBLANES]
    out[...] = rows[...].astype(jnp.bfloat16)
    for copy in copies[4:]:
        copy.wait()


def exponent_of(bound):
    return jnp.floor(jnp.log(jnp.maximum(bound, 1e-30)) * (1.0 / math.log(2.0))) + (2.0 - SPARE)


def greatest(value):
    return jnp.max(jnp.max(value, axis=1, keepdims=True), axis=0, keepdims=True)


def size_of(value):
    return jnp.abs(value[0]) + jnp.abs(value[1])


def two_pieces(value):
    high = value.astype(jnp.bfloat16).astype(jnp.float32)
    return high, (value - high) * 256.0


def main_kernel(
    owners,
    norm_scale,
    got,
    matrix,
    twiddle,
    decay_log,
    rotation,
    sent,
    rows_in,
    spectra,
    freq,
    back,
    params,
    doubled,
    bases,
    powers,
    lags,
    sums,
):
    peers, length = got.shape[0] // ROWS, got.shape[1]
    groups = peers // owners
    part_count = groups * SUBLANES
    rows = 2 * part_count
    pairs = part_count // 2
    half = pairs // SUBLANES
    reach = length // 2
    lane = lax.broadcasted_iota(jnp.int32, (pairs, LANES), 1)
    left = lane < LANES // 2
    row = lax.broadcasted_iota(jnp.int32, (SUBLANES, LANES), 0)

    def swap(value):
        return pltpu.roll(value, LANES // 2, 1)

    def lanes_of(side):
        return slice(side * LANES, (side + 1) * LANES)

    def collect(spot):
        tiles = [
            rows_in[pl.ds(group * owners * ROWS + spot, owners, stride=ROWS), :]
            for group in range(groups)
        ]
        return jnp.concatenate(tiles[:half], axis=0), jnp.concatenate(tiles[half:], axis=0)

    def make_params():
        lower, upper = [sum(side) for side in zip(*(collect(READ + i) for i in range(3)))]
        read = (jnp.where(left, lower, swap(upper)), jnp.where(left, swap(lower), upper))
        lower, upper = [
            sum(side[:, i : i + 1] for i in range(3)) + jnp.zeros_like(side)
            for side in collect(STEP)
        ]
        step = jnp.exp(jnp.where(left, lower, upper))
        decay_row = jnp.concatenate([decay_log[...], decay_log[...]], axis=1)
        rotation_row = jnp.concatenate([rotation[...], rotation[...]], axis=1)
        pole = (
            jnp.broadcast_to(-jnp.exp(decay_row), step.shape),
            jnp.broadcast_to(rotation_row, step.shape),
        )
        rate = (step * pole[0], step * pole[1])
        place, size = 0, 1
        while size < owners * length:
            doubled[place], doubled[place + 1] = power(rate[0], rate[1], float(size))
            place, size = place + 2, size * 2
        sine = cos_sin(0.5 * rate[1])[1]
        cosine = 1.0 - 2.0 * sine * sine
        lift = (grow(rate[0]) * cosine - 2.0 * sine * sine, doubled[1])
        norm = 1.0 / (pole[0] * pole[0] + pole[1] * pole[1])
        inverse = (pole[0] * norm, -pole[1] * norm)
        ratio = times(lift, inverse)
        coef = times(read, ratio)
        lifted = times((doubled[0], doubled[1]), inverse)
        values = (rate, ratio, coef, times(read, lifted), pole, times(coef, inverse), (step, step))
        for place, value in enumerate(values):
            params[2 * place], params[2 * place + 1] = value

    block_bit, reach_bit = length.bit_length() - 1, reach.bit_length() - 1
    bits = [(row & (1 << i)) != 0 for i in range(SUBLANES.bit_length() - 1)]

    def doubled_row(p, i):
        return doubled[2 * i, p : p + 1, :], doubled[2 * i + 1, p : p + 1, :]

    def by_rows(p, first):
        out = None
        for i, bit in enumerate(bits):
            real, imag = doubled_row(p, first + i)
            value = (jnp.where(bit, real, 1.0), jnp.where(bit, imag, 0.0))
            out = value if out is None else times(out, value)
        return out

    def make_tables():
        for p in range(pairs):
            table = [by_rows(p, 0)]
            for i in range(len(bits), reach_bit):
                table += [times(block, doubled_row(p, i)) for block in table]
            for place in range(0, len(table), 2):
                for side in range(2):
                    value = jnp.concatenate([table[place][side], table[place + 1][side]], axis=0)
                    for i, piece in enumerate(split_halves(value)):
                        spot = 2 * i * reach + place * SUBLANES
                        powers[p, spot : spot + 2 * SUBLANES, lanes_of(side)] = piece
                        spot += reach
                        powers[p, spot : spot + 2 * SUBLANES, lanes_of(side)] = piece
            base = by_rows(p, block_bit)
            bases[p, 0], bases[p, 1] = base
            bases[p, 2], bases[p, 3] = times(base, doubled_row(p, reach_bit))

    def transform(source, target, count):
        dot = functools.partial(jnp.dot, preferred_element_type=jnp.float32)
        cuts = [(owners + 1) * i // PARTS * count for i in range(PARTS + 1)]
        for part in map(slice, cuts, cuts[1:]):
            low = source[1, part]
            target[part] = (
                dot(source[0, part], matrix[0]) + dot(low, matrix[0]) + dot(source[0, part], matrix[1])
            )

    def spread_blocks():
        rows_in[...] = got[...].astype(jnp.float32)
        blocks = []
        for s in range(owners):
            spots = [(group * owners + s) * ROWS for group in range(groups)]
            blocks.append(
                jnp.concatenate(
                    [rows_in[spot : spot + SUBLANES] for spot in spots]
                    + [rows_in[spot + SUBLANES : spot + 2 * SUBLANES] for spot in spots],
                    axis=0,
                )
            )
        for k, value in enumerate(blocks_forward(blocks)):
            if k:
                value = times(value, (twiddle[k, 0:1], twiddle[k, 1:2]))
            for side in range(2):
                for i, piece in enumerate(split_halves(value[side])):
                    spectra[i, k * rows : (k + 1) * rows, lanes_of(side)] = piece

    def to_frequencies():
        transform(spectra, freq, rows)
        make_params()
        make_tables()

    def to_lags():
        for k in range(owners + 1):
            at_in = freq[k * rows : k * rows + part_count]
            at_out = freq[k * rows + part_count : (k + 1) * rows]
            ur, ui = at_in[:, :length], at_in[:, length:]
            gr, gi = at_out[:, :length], at_out[:, length:]
            for side, value in enumerate((gr * ur + gi * ui, gr * ui - gi * ur)):
                for i, piece in enumerate(split_halves(value)):
                    spectra[i, k * part_count : (k + 1) * part_count, lanes_of(side)] = piece
        transform(spectra, back, part_count)

    def finish():
        turned = []
        for k in range(owners + 1):
            spots = slice(k * part_count, (k + 1) * part_count)
            value = (back[spots, lanes_of(0)], back[spots, lanes_of(1)])
            turned.append(times(value, (twiddle[k, 2:3], twiddle[k, 3:4])))
        blocks = blocks_back(turned)

        most = jnp.zeros((part_count, LANES), jnp.float32)
        for b, block in enumerate(blocks):
            most = jnp.maximum(most, jnp.abs(block))
            lags[b * part_count : (b + 1) * part_count] = block

        def param(place):
            return params[2 * place], params[2 * place + 1]

        rate, ratio, coef, through, pole, direct, (step, _) = (param(i) for i in range(7))
        most = greatest(most)
        whole = 2.0 * math.sqrt(owners * length)
        on_rate = size_of(coef) * float(owners * length) + size_of(through)
        on_pole = step * on_rate + size_of(direct)
        lag_exponent = exponent_of(most)
        grad_exponent = exponent_of(most * (whole * greatest(size_of(ratio))))
        state_exponent = exponent_of(
            most * (whole * part_count * greatest(on_pole * (1.0 - pole[0])))
        )
        step_exponent = exponent_of(
            most * (whole * (LANES // 2) * greatest(on_rate * size_of(rate)))
        )
        lag_scale = jnp.exp2(-lag_exponent)
        for b, block in enumerate(blocks):
            for group in range(groups):
                place = (group * owners + b) * ROWS
                value = block[group * SUBLANES : (group + 1) * SUBLANES]
                sent[place + LAGS : place + GRADS] = value * lag_scale

        start = row.astype(jnp.float32) * float(length)
        first = left[:owners]
        wide = lax.broadcasted_iota(jnp.int32, (4 * owners, LANES), 1)
        wide_left = wide < reach
        offset = jnp.where(wide_left, wide, wide - reach).astype(jnp.float32)
        both_left = wide_left[: 2 * owners]
        for p in range(pairs):
            both = jnp.concatenate(
                [
                    lags[pl.ds(first_row, owners, stride=part_count), :]
                    for first_row in (p, pairs + p)
                ],
                axis=0,
            )
            swapped = swap(both)
            plain = jnp.concatenate(
                [jnp.where(both_left, both, swapped), jnp.where(both_left, swapped, both)], axis=0
            )
            factor = []
            for value in (plain, plain * offset):
                high = value.astype(jnp.bfloat16).astype(jnp.float32)
                factor.append(jnp.where(wide_left, high, value - high))
            factor = jnp.concatenate(factor, axis=0).astype(jnp.bfloat16)
            raw = jnp.dot(
                jnp.concatenate([factor, factor], axis=1),
                powers[p],
                preferred_element_type=jnp.float32,
            )

            def pick(place, side):
                top = raw[2 * place * owners : (2 * place + 1) * owners, lanes_of(side)]
                bottom = raw[(2 * place + 1) * owners : (2 * place + 2) * owners, lanes_of(side)]
                return jnp.where(first, top, bottom)

            found = None
            for part in range(2):
                base = (bases[p, 2 * part], bases[p, 2 * part + 1])
                near = start + float(part * reach)
                value = (pick(part, 0), pick(part, 1))
                lagged = (near * value[0] + pick(2 + part, 0), near * value[1] + pick(2 + part, 1))
                terms = times(base, value) + times(base, lagged)
                found = terms if found is None else [x + y for x, y in zip(found, terms)]
            for place, value in enumerate(found):
                sums[place, p : p + 1] = jnp.sum(value, axis=0, keepdims=True)

        total = (sums[0] * (2.0 * norm_scale), sums[1] * (2.0 * norm_scale))
        lag_total = (sums[2] * (2.0 * norm_scale), sums[3] * (2.0 * norm_scale))
        on_read = times(total, ratio)
        on_read = (on_read[0], -on_read[1])
        on_rate = times(coef, lag_total)
        more = times(total, through)
        on_rate = (on_rate[0] + more[0], on_rate[1] + more[1])
        less = times(total, direct)
        on_pole = (step * on_rate[0] - less[0], step * on_rate[1] - less[1])
        on_step = times(on_rate, rate)[0]
        on_decay = jnp.sum(on_pole[0] * pole[0], axis=0, keepdims=True)
        on_rotation = -jnp.sum(on_pole[1], axis=0, keepdims=True)
        on_decay = on_decay + swap(on_decay)
        on_rotation = on_rotation + swap(on_rotation)
        state = jnp.where(left[0:1], on_decay, on_rotation) * jnp.exp2(-state_exponent)

        grad_scale = jnp.exp2(-grad_exponent)
        on_read = (on_read[0] * grad_scale, on_read[1] * grad_scale)
        lower = jnp.where(left, on_read[0], swap(on_read[1]))
        upper = jnp.where(left, swap(on_read[0]), on_read[1])
        grads = jnp.concatenate([lower, upper], axis=0)
        step_column = jnp.concatenate(
            [
                jnp.sum(jnp.where(left, on_step, 0.0), axis=1, keepdims=True),
                jnp.sum(jnp.where(left, 0.0, on_step), axis=1, keepdims=True),
            ],
            axis=0,
        ) * jnp.exp2(-step_exponent)
        place_lane = lax.broadcasted_iota(jnp.int32, (SUBLANES, LANES), 1)
        scales = jnp.zeros((1, LANES), jnp.float32)
        for spot, value in zip(
            SCALE_LANES, (lag_exponent, grad_exponent, state_exponent, step_exponent)
        ):
            scales = jnp.where(place_lane[0:1] == spot, value, scales)
        state_high, state_low = two_pieces(state)
        tails = []
        for group in range(groups):
            pieces = two_pieces(step_column[group * SUBLANES : (group + 1) * SUBLANES])
            spread = jnp.zeros((SUBLANES, LANES), jnp.float32)
            for spot, piece in zip(STEP_LANES, pieces):
                spread = jnp.where(place_lane == row + spot, piece, spread)
            singles = scales + jnp.sum(spread, axis=0, keepdims=True)
            tails.append(jnp.concatenate([state_high, state_low, singles, singles], axis=0))
        for b in range(owners):
            for group in range(groups):
                place = (group * owners + b) * ROWS
                sent[place + GRADS : place + STATE] = grads[
                    group * SUBLANES : (group + 1) * SUBLANES
                ]
                sent[place + STATE : place + ROWS] = tails[group]

    for section in (spread_blocks, to_frequencies, to_lags, finish):
        section()


def unpack_kernel(got, kernel_grad, readout_grad, step_grad, state_grad, wide, grads):
    peers = got.shape[0] // ROWS
    per_row = LANES // SUBLANES
    singles = got[pl.ds(SINGLES, peers, stride=ROWS), :]
    exponents = [jnp.broadcast_to(singles[:, spot : spot + 1], (peers, LANES)) for spot in SCALE_LANES]
    scales = [jnp.exp2(value) for value in exponents]
    for i in range(2):
        wide[i] = scales[i]
    for spot in range(0, peers, per_row):
        part = slice(spot * SUBLANES, (spot + per_row) * SUBLANES)
        for i, first, target in ((1, GRADS, grads), (0, LAGS, kernel_grad)):
            for peer in range(spot, spot + per_row):
                place = peer * ROWS + first
                target[peer * SUBLANES : (peer + 1) * SUBLANES] = (
                    got[place : place + SUBLANES] * wide[i, peer : peer + 1, :]
                )
        readout_grad[:, part] = grads[part].T

    high = got[pl.ds(STATE, peers, stride=ROWS), :]
    low = got[pl.ds(STATE + 1, peers, stride=ROWS), :]
    total = jnp.sum((high + low * (1.0 / 256.0)) * scales[2], axis=0, keepdims=True)
    states = state_grad.shape[1]
    state_grad[0:1] = total[:, :states]
    state_grad[1:2] = total[:, states:]
    lane = lax.broadcasted_iota(jnp.int32, (peers, LANES), 1)
    row = lax.broadcasted_iota(jnp.int32, (peers, LANES), 0)
    high, low = (
        jnp.take_along_axis(singles, lane % SUBLANES + first, axis=1) for first in STEP_LANES
    )
    value = (high + low * (1.0 / 256.0)) * scales[3]
    for spot in range(0, peers, per_row):
        mine = jnp.where(row - spot == lane // SUBLANES, value, 0.0)
        step_grad[spot * SUBLANES : (spot + per_row) * SUBLANES] = jnp.sum(mine, axis=0)


def kernel_device(inputs, out_grad, readout, log_step, decay_log, rotation):
    owners, groups = lax.axis_size("seq"), lax.axis_size("ch")
    peers = owners * groups
    channels, length = inputs.shape
    states = decay_log.shape[0]
    part_count = channels // owners
    pairs = part_count // 2
    norm_scale = 1.0 / math.sqrt(owners * length)
    vmem = pl.BlockSpec(memory_space=pltpu.VMEM)
    memory = pltpu.CompilerParams(vmem_limit_bytes=32 * 1024 * 1024)
    f32, bf16 = jnp.float32, jnp.bfloat16

    def exchange(value):
        value = value.reshape(peers, ROWS // 2, 2, LANES)
        value = lax.all_to_all(value, ("ch", "seq"), split_axis=0, concat_axis=0, tiled=True)
        return value.reshape(peers * ROWS, LANES)

    anywhere = pl.BlockSpec(memory_space=pl.ANY)
    held = [jnp.asarray(table) for table in transform_tables(owners, length, norm_scale)]
    held += [decay_log[None], rotation[None]]
    sources = (
        inputs, out_grad, readout.transpose(0, 2, 1).reshape(LANES, channels), log_step[None], *held
    )
    pieces, *held = pl.pallas_call(
        pack_kernel,
        out_shape=[jax.ShapeDtypeStruct((peers * ROWS, LANES), bf16)]
        + [jax.ShapeDtypeStruct(value.shape, value.dtype) for value in held],
        in_specs=[anywhere] * len(sources),
        out_specs=[vmem] * (1 + len(held)),
        scratch_shapes=[
            pltpu.VMEM((2, channels, LANES), bf16),
            pltpu.VMEM((LANES, channels), f32),
            pltpu.VMEM((1, channels), f32),
            pltpu.VMEM((2, channels, LANES), f32),
            pltpu.VMEM((peers * ROWS, LANES), f32),
            pltpu.SemaphoreType.DMA((len(sources),)),
        ],
        compiler_params=memory,
    )(*(pltpu.with_memory_space_constraint(value, pltpu.HBM) for value in sources))
    got = exchange(pieces)
    sent = pl.pallas_call(
        functools.partial(main_kernel, owners, norm_scale),
        out_shape=jax.ShapeDtypeStruct((peers * ROWS, LANES), f32),
        in_specs=[vmem] * 5,
        out_specs=vmem,
        scratch_shapes=[
            pltpu.VMEM((peers * ROWS, LANES), f32),
            pltpu.VMEM((2, (owners + 1) * 2 * part_count, 2 * LANES), bf16),
            pltpu.VMEM(((owners + 1) * 2 * part_count, 2 * LANES), f32),
            pltpu.VMEM(((owners + 1) * part_count, 2 * LANES), f32),
            pltpu.VMEM((14, pairs, LANES), f32),
            pltpu.VMEM((2 * (owners * length).bit_length(), pairs, LANES), f32),
            pltpu.VMEM((pairs, 4, owners, LANES), f32),
            pltpu.VMEM((pairs, 2 * length, 2 * LANES), bf16),
            pltpu.VMEM((owners * part_count, length), f32),
            pltpu.VMEM((4, pairs, LANES), f32),
        ],
        compiler_params=memory,
    )(got, *held)
    back = exchange(sent.astype(jnp.float16))
    kernel_grad, readout_grad, step_grad, state_grad = pl.pallas_call(
        unpack_kernel,
        out_shape=[
            jax.ShapeDtypeStruct((channels, length), f32),
            jax.ShapeDtypeStruct((LANES, channels), f32),
            jax.ShapeDtypeStruct((channels,), f32),
            jax.ShapeDtypeStruct((2, states), f32),
        ],
        in_specs=[vmem],
        out_specs=[vmem] * 4,
        scratch_shapes=[
            pltpu.VMEM((2, peers, LANES), f32),
            pltpu.VMEM((channels, LANES), f32),
        ],
        compiler_params=memory,
    )(back.astype(f32))
    readout_grad = readout_grad.reshape(2, states, channels).transpose(0, 2, 1)
    return kernel_grad, readout_grad, step_grad, state_grad


def kernel_fits(mesh, inputs, decay_log):
    owners, groups = mesh.shape["seq"], mesh.shape["ch"]
    channels = inputs.shape[0] // groups
    return (
        inputs.shape[1] == owners * LANES
        and 2 * decay_log.shape[0] == LANES
        and owners == SUBLANES
        and groups % 2 == 0
        and channels == owners * groups * SUBLANES
        and channels % LANES == 0
    )


def solution(mesh):
    def whole(inputs, out_grad, readout, log_step, decay_log, rotation):
        fits = kernel_fits(mesh, inputs, decay_log)
        return jax.shard_map(
            kernel_device if fits else general_device,
            mesh=mesh,
            in_specs=(P("ch", "seq"), P("ch", "seq"), P(None, "ch", None), P("ch"), P(), P()),
            out_specs=(P("ch", "seq"), P(None, "ch", None), P("ch"), P()),
            check_vma=False,
        )(inputs, out_grad, readout, log_step, decay_log, rotation)

    return whole
```

```python
import functools
import math

import jax
import jax.numpy as jnp
import numpy as np
from jax import lax
from jax.experimental import pallas as pl
from jax.experimental.pallas import tpu as pltpu
from jax.sharding import PartitionSpec as P

precise = lax.Precision.HIGHEST
two_pi = 2.0 * math.pi
LANES = 128
SUBLANES = 8


def angle_table(left_index, right_index, modulus, orient):
    product = left_index[:, None] * right_index[None, :] % modulus
    return orient * two_pi * product.astype(jnp.float32) / modulus


def rotate(real_part, imag_part, angles):
    cosine_table = jnp.cos(angles)
    sine_table = jnp.sin(angles)
    return (
        real_part * cosine_table - imag_part * sine_table,
        real_part * sine_table + imag_part * cosine_table,
    )


def last_transform(real_part, imag_part, orient):
    length = real_part.shape[-1]
    counter = jnp.arange(length, dtype=jnp.int32)
    angles = angle_table(counter, counter, length, orient)
    cosine_table = jnp.cos(angles)
    sine_table = jnp.sin(angles)
    dot = functools.partial(jnp.dot, precision=precise, preferred_element_type=jnp.float32)
    return (
        dot(real_part, cosine_table) - dot(imag_part, sine_table),
        dot(imag_part, cosine_table) + dot(real_part, sine_table),
    )


def discretize(readout, log_step, decay_log, rotation):
    step_size = jnp.exp(log_step)[:, None]
    pole_real = -jnp.exp(decay_log)[None, :]
    pole_imag = rotation[None, :]
    rate_real = step_size * pole_real
    rate_imag = step_size * pole_imag
    lift_real = jnp.expm1(rate_real) * jnp.cos(rate_imag) - 2.0 * jnp.sin(0.5 * rate_imag) ** 2
    lift_imag = jnp.exp(rate_real) * jnp.sin(rate_imag)
    pole_norm = pole_real * pole_real + pole_imag * pole_imag
    ratio_real = (lift_real * pole_real + lift_imag * pole_imag) / pole_norm
    ratio_imag = (lift_imag * pole_real - lift_real * pole_imag) / pole_norm
    coef_real = readout[0] * ratio_real - readout[1] * ratio_imag
    coef_imag = readout[0] * ratio_imag + readout[1] * ratio_real
    return (coef_real, coef_imag, rate_real, rate_imag)


def parameter_grads(primal, backward, totals):
    coef_real, coef_imag = (primal[0], primal[1])
    cotangents = (
        2.0 * totals[0],
        -2.0 * totals[1],
        2.0 * (coef_real * totals[2] - coef_imag * totals[3]),
        -2.0 * (coef_real * totals[3] + coef_imag * totals[2]),
    )
    return backward(cotangents)


def shifted_totals(raw_sums, rate_real, rate_imag, block_start, norm_scale):
    decays = jnp.exp(rate_real * block_start)
    phases = rate_imag * block_start
    base_real = decays * jnp.cos(phases)
    base_imag = decays * jnp.sin(phases)
    near_real = block_start * raw_sums[0] + raw_sums[2]
    near_imag = block_start * raw_sums[1] + raw_sums[3]
    return jnp.stack(
        [
            norm_scale * (base_real * raw_sums[0] - base_imag * raw_sums[1]),
            norm_scale * (base_real * raw_sums[1] + base_imag * raw_sums[0]),
            norm_scale * (base_real * near_real - base_imag * near_imag),
            norm_scale * (base_real * near_imag + base_imag * near_real),
        ]
    )


def whole_channel_totals(lag_rows, rate_real, rate_imag, norm_scale):
    owners, length = (lag_rows.shape[1], lag_rows.shape[2])
    offsets = jnp.arange(length, dtype=jnp.int32).astype(jnp.float32)
    decays = jnp.exp(rate_real[:, :, None] * offsets)
    phases = rate_imag[:, :, None] * offsets
    power_real = decays * jnp.cos(phases)
    power_imag = decays * jnp.sin(phases)
    weighted = lag_rows * offsets
    raw_sums = jnp.stack(
        [
            jnp.einsum("cbj,cnj->cnb", lag_rows, power_real, precision=precise),
            jnp.einsum("cbj,cnj->cnb", lag_rows, power_imag, precision=precise),
            jnp.einsum("cbj,cnj->cnb", weighted, power_real, precision=precise),
            jnp.einsum("cbj,cnj->cnb", weighted, power_imag, precision=precise),
        ]
    )
    starts = (jnp.arange(owners, dtype=jnp.int32) * length).astype(jnp.float32)
    totals = shifted_totals(
        raw_sums, rate_real[:, :, None], rate_imag[:, :, None], starts, norm_scale
    )
    return jnp.sum(totals, axis=-1)


def general_lags(whole, norm_scale):
    part_count, owners, length = whole.shape[1:]
    freq_width = 2 * owners
    modulus = freq_width * length
    row_index = jnp.arange(owners, dtype=jnp.int32)
    outer_index = jnp.arange(freq_width, dtype=jnp.int32)
    inner_index = jnp.arange(length, dtype=jnp.int32)
    first = angle_table(row_index, outer_index, freq_width, -1.0)
    spec_real = jnp.einsum("scba,bk->scka", whole, jnp.cos(first), precision=precise)
    spec_imag = jnp.einsum("scba,bk->scka", whole, jnp.sin(first), precision=precise)
    spec_real, spec_imag = rotate(
        spec_real, spec_imag, angle_table(outer_index, inner_index, modulus, -1.0)
    )
    freq_real, freq_imag = last_transform(spec_real, spec_imag, -1.0)
    prod_real = freq_real[1] * freq_real[0] + freq_imag[1] * freq_imag[0]
    prod_imag = freq_imag[1] * freq_real[0] - freq_real[1] * freq_imag[0]
    back_real, back_imag = last_transform(prod_real, prod_imag, 1.0)
    back_real, back_imag = rotate(
        back_real, back_imag, angle_table(outer_index, inner_index, modulus, 1.0)
    )
    final = angle_table(outer_index, row_index, freq_width, 1.0)
    lag_rows = jnp.einsum("cka,kb->cba", back_real, jnp.cos(final), precision=precise) - jnp.einsum(
        "cka,kb->cba", back_imag, jnp.sin(final), precision=precise
    )
    return lag_rows * (norm_scale / modulus)


def general_device(inputs, out_grad, readout, log_step, decay_log, rotation):
    owners = lax.axis_size("seq")
    channels, length = inputs.shape
    states = decay_log.shape[0]
    part_count = channels // owners
    norm_scale = 1.0 / math.sqrt(owners * length)
    pieces = jnp.concatenate(
        [a.reshape(owners, part_count, length) for a in (inputs, out_grad)], axis=1
    )
    pieces = lax.all_to_all(pieces, "seq", split_axis=0, concat_axis=0, tiled=True)
    whole = pieces.astype(jnp.float32).reshape(owners, 2, part_count, length)
    lag_rows = general_lags(whole.transpose(1, 2, 0, 3), norm_scale)
    first_channel = lax.axis_index("seq") * part_count
    own_readout = lax.dynamic_slice_in_dim(readout, first_channel, part_count, 1)
    own_step = lax.dynamic_slice_in_dim(log_step, first_channel, part_count, 0)
    primal, backward = jax.vjp(discretize, own_readout, own_step, decay_log, rotation)
    totals = whole_channel_totals(lag_rows, primal[2], primal[3], norm_scale)
    readout_part, step_part, decay_part, rotation_part = parameter_grads(primal, backward, totals)
    shared = jnp.concatenate(
        [readout_part.reshape(-1), step_part, decay_part, rotation_part]
    )
    sent = jnp.concatenate(
        [
            lag_rows.transpose(1, 0, 2).reshape(owners, -1),
            jnp.broadcast_to(shared, (owners, shared.shape[0])),
        ],
        axis=1,
    )
    got = lax.all_to_all(sent, "seq", split_axis=0, concat_axis=0, tiled=True)
    cuts = np.cumsum([part_count * length, 2 * part_count * states, part_count])
    lags, readouts, steps, state = jnp.split(got, cuts, axis=1)
    readouts = readouts.reshape(owners, 2, part_count, states).transpose(1, 0, 2, 3)
    return (
        lags.reshape(channels, length),
        readouts.reshape(2, channels, states),
        steps.reshape(channels),
        lax.psum(jnp.sum(state, axis=0), "ch").reshape(2, states),
    )


def split_halves(value):
    high = value.astype(jnp.bfloat16)
    return high, (value - high.astype(jnp.float32)).astype(jnp.bfloat16)


def cos_sin(angle):
    turns = jnp.floor(angle * (2.0 / math.pi) + 0.5)
    rest = angle - turns * 1.5703125
    rest = rest - turns * 4.837512969970703125e-4
    rest = rest - turns * 7.54978995489188216e-8
    quarter = turns.astype(jnp.int32)
    square = rest * rest
    sine = rest + rest * square * (
        -1.6666654611e-1 + square * (8.3321608736e-3 - square * 1.9515295891e-4)
    )
    cosine = (
        1.0
        - 0.5 * square
        + square
        * square
        * (
            4.166664568298827e-2
            + square * (-1.388731625493765e-3 + square * 2.443315711809948e-5)
        )
    )
    odd = (quarter & 1) == 1
    out_cos = jnp.where(odd, sine, cosine)
    out_sin = jnp.where(odd, cosine, sine)
    out_cos = jnp.where(((quarter + 1) & 2) == 2, -out_cos, out_cos)
    out_sin = jnp.where((quarter & 2) == 2, -out_sin, out_sin)
    return out_cos, out_sin


def grow(value):
    series = 1.0
    for term in range(9, 1, -1):
        series = 1.0 + series * value * (1.0 / term)
    return jnp.where(jnp.abs(value) < 0.35, series * value, jnp.exp(value) - 1.0)


def power(rate_real, rate_imag, offset):
    size = jnp.exp(rate_real * offset)
    cosine, sine = cos_sin(rate_imag * offset)
    return size * cosine, size * sine


def times(left, right):
    return (
        left[0] * right[0] - left[1] * right[1],
        left[0] * right[1] + left[1] * right[0],
    )


def blocks_forward(x):
    root = math.sqrt(0.5)
    cosine, sine = math.cos(math.pi / 8), math.sin(math.pi / 8)
    total = [x[s] + x[s + 4] for s in range(4)]
    gap = [x[s] - x[s + 4] for s in range(4)]
    even, odd = total[0] + total[2], total[1] + total[3]
    real, imag = [None] * 9, [None] * 9
    real[0], real[8] = even + odd, even - odd
    imag[0] = imag[8] = jnp.zeros_like(even)
    real[4], imag[4] = total[0] - total[2], total[3] - total[1]
    less, more = root * (gap[1] - gap[3]), root * (gap[1] + gap[3])
    real[2], imag[2] = gap[0] + less, -gap[2] - more
    real[6], imag[6] = gap[0] - less, gap[2] - more
    less, more = root * (x[2] - x[6]), root * (x[2] + x[6])
    even1 = (x[0] + less, -x[4] - more)
    even3 = (x[0] - less, x[4] - more)
    p, q, r, t = x[1] - x[7], x[3] - x[5], x[1] + x[7], x[3] + x[5]
    odd1 = (cosine * p + sine * q, -sine * r - cosine * t)
    odd3 = (sine * p - cosine * q, sine * t - cosine * r)
    real[1], imag[1] = even1[0] + odd1[0], even1[1] + odd1[1]
    real[7], imag[7] = even1[0] - odd1[0], odd1[1] - even1[1]
    real[3], imag[3] = even3[0] + odd3[0], even3[1] + odd3[1]
    real[5], imag[5] = even3[0] - odd3[0], odd3[1] - even3[1]
    return list(zip(real, imag))


def blocks_back(z):
    root = math.sqrt(0.5)
    cosine, sine = math.cos(math.pi / 8), math.sin(math.pi / 8)
    real, imag = [v[0] for v in z], [v[1] for v in z]
    even, odd = real[0] + real[8], real[0] - real[8]
    total = [even + real[4], odd + imag[4], even - real[4], odd - imag[4]]
    less, more = root * (real[2] - real[6]), root * (imag[2] + imag[6])
    gap = [real[2] + real[6], less + more, imag[2] - imag[6], more - less]
    x = [total[s] + gap[s] for s in range(4)] + [total[s] - gap[s] for s in range(4)]
    even1 = (real[1] + real[7], imag[7] - imag[1])
    even3 = (real[3] + real[5], imag[5] - imag[3])
    odd1 = (real[1] - real[7], imag[1] + imag[7])
    odd3 = (real[3] - real[5], imag[3] + imag[5])
    less, more = root * (even1[0] - even3[0]), root * (even1[1] + even3[1])
    p = cosine * odd1[0] + sine * odd3[0]
    q = sine * odd1[0] - cosine * odd3[0]
    r = sine * odd1[1] + cosine * odd3[1]
    t = cosine * odd1[1] - sine * odd3[1]
    extra = [
        even1[0] + even3[0],
        p + r,
        less - more,
        q + t,
        even3[1] - even1[1],
        t - q,
        -less - more,
        r - p,
    ]
    return [v + w for v, w in zip(x, extra)]


def transform_tables(owners, length, norm_scale):
    width = 2 * owners
    counter = np.arange(length)
    angles = two_pi * (counter[:, None] * counter[None, :] % length) / length
    cosine, sine = np.cos(angles), np.sin(angles)
    matrix = np.block([[cosine, -sine], [sine, cosine]]).astype(np.float32)
    high = matrix.astype(jnp.bfloat16)
    low = (matrix - high.astype(np.float32)).astype(jnp.bfloat16)
    outer = np.arange(owners + 1)
    angles = two_pi * (outer[:, None] * counter[None, :]) / (width * length)
    twiddle = np.stack([np.cos(angles), -np.sin(angles)], axis=1)
    weight = np.where(outer % owners == 0, 1.0, 2.0) * norm_scale / (width * length)
    twiddle = np.concatenate([twiddle, twiddle * weight[:, None, None]], axis=1)
    return np.stack([high, low]), twiddle.astype(np.float32)


def three_pieces(value):
    pieces = []
    for _ in range(3):
        piece = value.astype(jnp.bfloat16).astype(jnp.float32)
        pieces.append(piece)
        value = value - piece
    return pieces


def transposed(value):
    return jnp.concatenate(
        [value[:, spot : spot + LANES].T for spot in range(0, value.shape[1], LANES)], axis=0
    )


READ, STEP, ROWS = 16, 19, 20
LAGS, GRADS, STATE, SINGLES = 0, 8, 16, 18
STEP_LANES, SCALE_LANES = (0, 8), (16, 17, 18, 19)
SPARE = 15.0
PARTS = 4
FRESH = 4


def pack_kernel(inputs, out_grad, readout, log_step, *refs):
    count = (len(refs) - 7) // 2
    sources, (out, *held) = refs[:count], refs[count : 2 * count + 1]
    signals, read, step, turned, rows, sems = refs[2 * count + 1 :]
    peers = out.shape[0] // ROWS
    copies = [
        pltpu.make_async_copy(source, target, sems.at[i])
        for i, (source, target) in enumerate(
            (
                (readout, read),
                (log_step, step),
                (inputs, signals.at[0]),
                (out_grad, signals.at[1]),
                *zip(sources, held),
            )
        )
    ]
    for copy in copies:
        copy.start()
    for copy in copies[:4]:
        copy.wait()
    own = lax.axis_index("seq")
    turned[...] = transposed(read[...])
    channels = step.shape[1]
    peer = lax.broadcasted_iota(jnp.int32, (peers, channels), 0)
    channel = lax.broadcasted_iota(jnp.int32, (peers, channels), 1)
    mine = jnp.where(channel == peer * SUBLANES + own, step[...], 0.0)
    mine = jnp.broadcast_to(jnp.sum(mine, axis=1, keepdims=True), (peers, LANES))
    for place, signal in enumerate((signals[0], signals[1])):
        value = signal.astype(jnp.float32)
        for peer in range(peers):
            spot = peer * ROWS + place * SUBLANES
            rows[spot : spot + SUBLANES] = value[peer * SUBLANES : (peer + 1) * SUBLANES]
    for place, value in enumerate(three_pieces(turned[pl.ds(own, peers, stride=SUBLANES), :])):
        rows[pl.ds(READ + place, peers, stride=ROWS), :] = value
    pieces = three_pieces(mine)
    lane = lax.broadcasted_iota(jnp.int32, (peers, LANES), 1)
    value = jnp.where(lane == 0, pieces[0], jnp.where(lane == 1, pieces[1], pieces[2]))
    rows[pl.ds(STEP, peers, stride=ROWS), :] = value
    out[...] = rows[...].astype(jnp.bfloat16)
    for copy in copies[4:]:
        copy.wait()


def exponent_of(bound):
    return jnp.floor(jnp.log(jnp.maximum(bound, 1e-30)) * (1.0 / math.log(2.0))) + (2.0 - SPARE)


def greatest(value):
    return jnp.max(jnp.max(value, axis=1, keepdims=True), axis=0, keepdims=True)


def size_of(value):
    return jnp.abs(value[0]) + jnp.abs(value[1])


def two_pieces(value):
    high = value.astype(jnp.bfloat16).astype(jnp.float32)
    return high, (value - high) * 256.0


def main_kernel(
    owners,
    norm_scale,
    got,
    matrix,
    twiddle,
    decay_log,
    rotation,
    sent,
    rows_in,
    spectra,
    freq,
    back,
    params,
    doubled,
    bases,
    powers,
    lags,
    sums,
):
    peers, length = got.shape[0] // ROWS, got.shape[1]
    groups = peers // owners
    part_count = groups * SUBLANES
    rows = 2 * part_count
    pairs = part_count // 2
    half = pairs // SUBLANES
    reach = length // 2
    lane = lax.broadcasted_iota(jnp.int32, (pairs, LANES), 1)
    left = lane < LANES // 2
    row = lax.broadcasted_iota(jnp.int32, (SUBLANES, LANES), 0)

    def swap(value):
        return pltpu.roll(value, LANES // 2, 1)

    def lanes_of(side):
        return slice(side * LANES, (side + 1) * LANES)

    def collect(spot):
        tiles = [
            rows_in[pl.ds(group * owners * ROWS + spot, owners, stride=ROWS), :]
            for group in range(groups)
        ]
        return jnp.concatenate(tiles[:half], axis=0), jnp.concatenate(tiles[half:], axis=0)

    def make_params():
        lower, upper = [sum(side) for side in zip(*(collect(READ + i) for i in range(3)))]
        read = (jnp.where(left, lower, swap(upper)), jnp.where(left, swap(lower), upper))
        lower, upper = [
            sum(side[:, i : i + 1] for i in range(3)) + jnp.zeros_like(side)
            for side in collect(STEP)
        ]
        step = jnp.exp(jnp.where(left, lower, upper))
        decay_row = jnp.concatenate([decay_log[...], decay_log[...]], axis=1)
        rotation_row = jnp.concatenate([rotation[...], rotation[...]], axis=1)
        pole = (
            jnp.broadcast_to(-jnp.exp(decay_row), step.shape),
            jnp.broadcast_to(rotation_row, step.shape),
        )
        rate = (step * pole[0], step * pole[1])
        place, size = 0, 1
        while size < owners * length:
            if place // 2 % FRESH == 0:
                value = power(rate[0], rate[1], float(size))
            else:
                value = (value[0] * value[0] - value[1] * value[1], 2.0 * value[0] * value[1])
            doubled[place], doubled[place + 1] = value
            place, size = place + 2, size * 2
        sine = cos_sin(0.5 * rate[1])[1]
        cosine = 1.0 - 2.0 * sine * sine
        lift = (grow(rate[0]) * cosine - 2.0 * sine * sine, doubled[1])
        norm = 1.0 / (pole[0] * pole[0] + pole[1] * pole[1])
        inverse = (pole[0] * norm, -pole[1] * norm)
        ratio = times(lift, inverse)
        coef = times(read, ratio)
        lifted = times((doubled[0], doubled[1]), inverse)
        values = (rate, ratio, coef, times(read, lifted), pole, times(coef, inverse), (step, step))
        for place, value in enumerate(values):
            params[2 * place], params[2 * place + 1] = value

    block_bit, reach_bit = length.bit_length() - 1, reach.bit_length() - 1
    bits = [(row & (1 << i)) != 0 for i in range(SUBLANES.bit_length() - 1)]

    def doubled_row(p, i):
        return doubled[2 * i, p : p + 1, :], doubled[2 * i + 1, p : p + 1, :]

    def by_rows(p, first):
        out = None
        for i, bit in enumerate(bits):
            real, imag = doubled_row(p, first + i)
            value = (jnp.where(bit, real, 1.0), jnp.where(bit, imag, 0.0))
            out = value if out is None else times(out, value)
        return out

    def make_tables():
        for p in range(pairs):
            table = [by_rows(p, 0)]
            for i in range(len(bits), reach_bit):
                table += [times(block, doubled_row(p, i)) for block in table]
            for place in range(0, len(table), 2):
                for side in range(2):
                    value = jnp.concatenate([table[place][side], table[place + 1][side]], axis=0)
                    for i, piece in enumerate(split_halves(value)):
                        spot = 2 * i * reach + place * SUBLANES
                        powers[p, spot : spot + 2 * SUBLANES, lanes_of(side)] = piece
                        spot += reach
                        powers[p, spot : spot + 2 * SUBLANES, lanes_of(side)] = piece
            base = by_rows(p, block_bit)
            bases[p, 0], bases[p, 1] = base
            bases[p, 2], bases[p, 3] = times(base, doubled_row(p, reach_bit))

    def transform(source, target, count):
        dot = functools.partial(jnp.dot, preferred_element_type=jnp.float32)
        cuts = [(owners + 1) * i // PARTS * count for i in range(PARTS + 1)]
        for part in map(slice, cuts, cuts[1:]):
            low = source[1, part]
            target[part] = (
                dot(source[0, part], matrix[0]) + dot(low, matrix[0]) + dot(source[0, part], matrix[1])
            )

    def spread_blocks():
        rows_in[...] = got[...].astype(jnp.float32)
        blocks = []
        for s in range(owners):
            spots = [(group * owners + s) * ROWS for group in range(groups)]
            blocks.append(
                jnp.concatenate(
                    [rows_in[spot : spot + SUBLANES] for spot in spots]
                    + [rows_in[spot + SUBLANES : spot + 2 * SUBLANES] for spot in spots],
                    axis=0,
                )
            )
        for k, value in enumerate(blocks_forward(blocks)):
            if k:
                value = times(value, (twiddle[k, 0:1], twiddle[k, 1:2]))
            for side in range(2):
                for i, piece in enumerate(split_halves(value[side])):
                    spectra[i, k * rows : (k + 1) * rows, lanes_of(side)] = piece

    def to_frequencies():
        transform(spectra, freq, rows)
        make_params()
        make_tables()

    def to_lags():
        for k in range(owners + 1):
            at_in = freq[k * rows : k * rows + part_count]
            at_out = freq[k * rows + part_count : (k + 1) * rows]
            ur, ui = at_in[:, :length], at_in[:, length:]
            gr, gi = at_out[:, :length], at_out[:, length:]
            for side, value in enumerate((gr * ur + gi * ui, gr * ui - gi * ur)):
                for i, piece in enumerate(split_halves(value)):
                    spectra[i, k * part_count : (k + 1) * part_count, lanes_of(side)] = piece
        transform(spectra, back, part_count)

    def finish():
        turned = []
        for k in range(owners + 1):
            spots = slice(k * part_count, (k + 1) * part_count)
            value = (back[spots, lanes_of(0)], back[spots, lanes_of(1)])
            turned.append(times(value, (twiddle[k, 2:3], twiddle[k, 3:4])))
        blocks = blocks_back(turned)

        most = jnp.zeros((part_count, LANES), jnp.float32)
        for b, block in enumerate(blocks):
            most = jnp.maximum(most, jnp.abs(block))
            lags[b * part_count : (b + 1) * part_count] = block

        def param(place):
            return params[2 * place], params[2 * place + 1]

        rate, ratio, coef, through, pole, direct, (step, _) = (param(i) for i in range(7))
        most = greatest(most)
        whole = 2.0 * math.sqrt(owners * length)
        on_rate = size_of(coef) * float(owners * length) + size_of(through)
        on_pole = step * on_rate + size_of(direct)
        lag_exponent = exponent_of(most)
        grad_exponent = exponent_of(most * (whole * greatest(size_of(ratio))))
        state_exponent = exponent_of(
            most * (whole * part_count * greatest(on_pole * (1.0 - pole[0])))
        )
        step_exponent = exponent_of(
            most * (whole * (LANES // 2) * greatest(on_rate * size_of(rate)))
        )
        lag_scale = jnp.exp2(-lag_exponent)
        for b, block in enumerate(blocks):
            for group in range(groups):
                place = (group * owners + b) * ROWS
                value = block[group * SUBLANES : (group + 1) * SUBLANES]
                sent[place + LAGS : place + GRADS] = value * lag_scale

        start = row.astype(jnp.float32) * float(length)
        first = left[:owners]
        wide = lax.broadcasted_iota(jnp.int32, (4 * owners, LANES), 1)
        wide_left = wide < reach
        offset = jnp.where(wide_left, wide, wide - reach).astype(jnp.float32)
        both_left = wide_left[: 2 * owners]
        for p in range(pairs):
            both = jnp.concatenate(
                [
                    lags[pl.ds(first_row, owners, stride=part_count), :]
                    for first_row in (p, pairs + p)
                ],
                axis=0,
            )
            swapped = swap(both)
            plain = jnp.concatenate(
                [jnp.where(both_left, both, swapped), jnp.where(both_left, swapped, both)], axis=0
            )
            factor = []
            for value in (plain, plain * offset):
                high = value.astype(jnp.bfloat16).astype(jnp.float32)
                factor.append(jnp.where(wide_left, high, value - high))
            factor = jnp.concatenate(factor, axis=0).astype(jnp.bfloat16)
            raw = jnp.dot(
                jnp.concatenate([factor, factor], axis=1),
                powers[p],
                preferred_element_type=jnp.float32,
            )

            def pick(place, side):
                top = raw[2 * place * owners : (2 * place + 1) * owners, lanes_of(side)]
                bottom = raw[(2 * place + 1) * owners : (2 * place + 2) * owners, lanes_of(side)]
                return jnp.where(first, top, bottom)

            found = None
            for part in range(2):
                base = (bases[p, 2 * part], bases[p, 2 * part + 1])
                near = start + float(part * reach)
                value = (pick(part, 0), pick(part, 1))
                lagged = (near * value[0] + pick(2 + part, 0), near * value[1] + pick(2 + part, 1))
                terms = times(base, value) + times(base, lagged)
                found = terms if found is None else [x + y for x, y in zip(found, terms)]
            for place, value in enumerate(found):
                sums[place, p : p + 1] = jnp.sum(value, axis=0, keepdims=True)

        total = (sums[0] * (2.0 * norm_scale), sums[1] * (2.0 * norm_scale))
        lag_total = (sums[2] * (2.0 * norm_scale), sums[3] * (2.0 * norm_scale))
        on_read = times(total, ratio)
        on_read = (on_read[0], -on_read[1])
        on_rate = times(coef, lag_total)
        more = times(total, through)
        on_rate = (on_rate[0] + more[0], on_rate[1] + more[1])
        less = times(total, direct)
        on_pole = (step * on_rate[0] - less[0], step * on_rate[1] - less[1])
        on_step = times(on_rate, rate)[0]
        on_decay = jnp.sum(on_pole[0] * pole[0], axis=0, keepdims=True)
        on_rotation = -jnp.sum(on_pole[1], axis=0, keepdims=True)
        on_decay = on_decay + swap(on_decay)
        on_rotation = on_rotation + swap(on_rotation)
        state = jnp.where(left[0:1], on_decay, on_rotation) * jnp.exp2(-state_exponent)

        grad_scale = jnp.exp2(-grad_exponent)
        on_read = (on_read[0] * grad_scale, on_read[1] * grad_scale)
        lower = jnp.where(left, on_read[0], swap(on_read[1]))
        upper = jnp.where(left, swap(on_read[0]), on_read[1])
        grads = jnp.concatenate([lower, upper], axis=0)
        step_scale = jnp.broadcast_to(jnp.exp2(-step_exponent), (pairs, LANES))
        step_columns = [
            jnp.broadcast_to(jnp.sum(value, axis=1, keepdims=True), (pairs, LANES)) * step_scale
            for value in (jnp.where(left, on_step, 0.0), jnp.where(left, 0.0, on_step))
        ]
        place_lane = lax.broadcasted_iota(jnp.int32, (SUBLANES, LANES), 1)
        scales = jnp.zeros((1, LANES), jnp.float32)
        for spot, value in zip(
            SCALE_LANES, (lag_exponent, grad_exponent, state_exponent, step_exponent)
        ):
            scales = jnp.where(place_lane[0:1] == spot, value, scales)
        state_high, state_low = two_pieces(state)
        tails = []
        for group in range(groups):
            spot = group % half * SUBLANES
            pieces = two_pieces(step_columns[group // half][spot : spot + SUBLANES])
            spread = jnp.zeros((SUBLANES, LANES), jnp.float32)
            for spot, piece in zip(STEP_LANES, pieces):
                spread = jnp.where(place_lane == row + spot, piece, spread)
            singles = scales + jnp.sum(spread, axis=0, keepdims=True)
            tails.append(jnp.concatenate([state_high, state_low, singles, singles], axis=0))
        for b in range(owners):
            for group in range(groups):
                place = (group * owners + b) * ROWS
                sent[place + GRADS : place + STATE] = grads[
                    group * SUBLANES : (group + 1) * SUBLANES
                ]
                sent[place + STATE : place + ROWS] = tails[group]

    for section in (spread_blocks, to_frequencies, to_lags, finish):
        section()


def unpack_kernel(got, kernel_grad, readout_grad, step_grad, state_grad, wide, grads):
    peers = got.shape[0] // ROWS
    per_row = LANES // SUBLANES
    singles = got[pl.ds(SINGLES, peers, stride=ROWS), :]
    exponents = [jnp.broadcast_to(singles[:, spot : spot + 1], (peers, LANES)) for spot in SCALE_LANES]
    scales = [jnp.exp2(value) for value in exponents]
    for i in range(2):
        wide[i] = scales[i]
    for spot in range(0, peers, per_row):
        part = slice(spot * SUBLANES, (spot + per_row) * SUBLANES)
        for i, first, target in ((1, GRADS, grads), (0, LAGS, kernel_grad)):
            for peer in range(spot, spot + per_row):
                place = peer * ROWS + first
                target[peer * SUBLANES : (peer + 1) * SUBLANES] = (
                    got[place : place + SUBLANES] * wide[i, peer : peer + 1, :]
                )
        readout_grad[:, part] = grads[part].T

    high = got[pl.ds(STATE, peers, stride=ROWS), :]
    low = got[pl.ds(STATE + 1, peers, stride=ROWS), :]
    total = jnp.sum((high + low * (1.0 / 256.0)) * scales[2], axis=0, keepdims=True)
    states = state_grad.shape[1]
    state_grad[0:1] = total[:, :states]
    state_grad[1:2] = total[:, states:]
    lane = lax.broadcasted_iota(jnp.int32, (peers, LANES), 1)
    row = lax.broadcasted_iota(jnp.int32, (peers, LANES), 0)
    high, low = (
        jnp.take_along_axis(singles, lane % SUBLANES + first, axis=1) for first in STEP_LANES
    )
    value = (high + low * (1.0 / 256.0)) * scales[3]
    for spot in range(0, peers, per_row):
        mine = jnp.where(row - spot == lane // SUBLANES, value, 0.0)
        step_grad[spot * SUBLANES : (spot + per_row) * SUBLANES] = jnp.sum(mine, axis=0)


def kernel_device(inputs, out_grad, readout, log_step, decay_log, rotation):
    owners, groups = lax.axis_size("seq"), lax.axis_size("ch")
    peers = owners * groups
    channels, length = inputs.shape
    states = decay_log.shape[0]
    part_count = channels // owners
    pairs = part_count // 2
    norm_scale = 1.0 / math.sqrt(owners * length)
    vmem = pl.BlockSpec(memory_space=pltpu.VMEM)
    memory = pltpu.CompilerParams(vmem_limit_bytes=32 * 1024 * 1024)
    f32, bf16 = jnp.float32, jnp.bfloat16

    def exchange(value):
        value = value.reshape(peers, ROWS // 2, 2, LANES)
        value = lax.all_to_all(value, ("ch", "seq"), split_axis=0, concat_axis=0, tiled=True)
        return value.reshape(peers * ROWS, LANES)

    anywhere = pl.BlockSpec(memory_space=pl.ANY)
    held = [jnp.asarray(table) for table in transform_tables(owners, length, norm_scale)]
    held += [decay_log[None], rotation[None]]
    sources = (
        inputs, out_grad, readout.transpose(0, 2, 1).reshape(LANES, channels), log_step[None], *held
    )
    pieces, *held = pl.pallas_call(
        pack_kernel,
        out_shape=[jax.ShapeDtypeStruct((peers * ROWS, LANES), bf16)]
        + [jax.ShapeDtypeStruct(value.shape, value.dtype) for value in held],
        in_specs=[anywhere] * len(sources),
        out_specs=[vmem] * (1 + len(held)),
        scratch_shapes=[
            pltpu.VMEM((2, channels, LANES), bf16),
            pltpu.VMEM((LANES, channels), f32),
            pltpu.VMEM((1, channels), f32),
            pltpu.VMEM((channels, LANES), f32),
            pltpu.VMEM((peers * ROWS, LANES), f32),
            pltpu.SemaphoreType.DMA((len(sources),)),
        ],
        compiler_params=memory,
    )(*(pltpu.with_memory_space_constraint(value, pltpu.HBM) for value in sources))
    got = exchange(pieces)
    sent = pl.pallas_call(
        functools.partial(main_kernel, owners, norm_scale),
        out_shape=jax.ShapeDtypeStruct((peers * ROWS, LANES), f32),
        in_specs=[vmem] * 5,
        out_specs=vmem,
        scratch_shapes=[
            pltpu.VMEM((peers * ROWS, LANES), f32),
            pltpu.VMEM((2, (owners + 1) * 2 * part_count, 2 * LANES), bf16),
            pltpu.VMEM(((owners + 1) * 2 * part_count, 2 * LANES), f32),
            pltpu.VMEM(((owners + 1) * part_count, 2 * LANES), f32),
            pltpu.VMEM((14, pairs, LANES), f32),
            pltpu.VMEM((2 * (owners * length).bit_length(), pairs, LANES), f32),
            pltpu.VMEM((pairs, 4, owners, LANES), f32),
            pltpu.VMEM((pairs, 2 * length, 2 * LANES), bf16),
            pltpu.VMEM((owners * part_count, length), f32),
            pltpu.VMEM((4, pairs, LANES), f32),
        ],
        compiler_params=memory,
    )(got, *held)
    back = exchange(sent.astype(jnp.float16))
    kernel_grad, readout_grad, step_grad, state_grad = pl.pallas_call(
        unpack_kernel,
        out_shape=[
            jax.ShapeDtypeStruct((channels, length), f32),
            jax.ShapeDtypeStruct((LANES, channels), f32),
            jax.ShapeDtypeStruct((channels,), f32),
            jax.ShapeDtypeStruct((2, states), f32),
        ],
        in_specs=[vmem],
        out_specs=[vmem] * 4,
        scratch_shapes=[
            pltpu.VMEM((2, peers, LANES), f32),
            pltpu.VMEM((channels, LANES), f32),
        ],
        compiler_params=memory,
    )(back.astype(f32))
    readout_grad = readout_grad.reshape(2, states, channels).transpose(0, 2, 1)
    return kernel_grad, readout_grad, step_grad, state_grad


def kernel_fits(mesh, inputs, decay_log):
    owners, groups = mesh.shape["seq"], mesh.shape["ch"]
    channels = inputs.shape[0] // groups
    return (
        inputs.shape[1] == owners * LANES
        and 2 * decay_log.shape[0] == LANES
        and owners == SUBLANES
        and groups % 2 == 0
        and channels == owners * groups * SUBLANES
        and channels % LANES == 0
    )


def solution(mesh):
    def whole(inputs, out_grad, readout, log_step, decay_log, rotation):
        fits = kernel_fits(mesh, inputs, decay_log)
        return jax.shard_map(
            kernel_device if fits else general_device,
            mesh=mesh,
            in_specs=(P("ch", "seq"), P("ch", "seq"), P(None, "ch", None), P("ch"), P(), P()),
            out_specs=(P("ch", "seq"), P(None, "ch", None), P("ch"), P()),
            check_vma=False,
        )(inputs, out_grad, readout, log_step, decay_log, rotation)

    return whole
```

```python
import functools
import math

import jax
import jax.numpy as jnp
import numpy as np
from jax import lax
from jax.experimental import pallas as pl
from jax.experimental.pallas import tpu as pltpu
from jax.sharding import PartitionSpec as P

precise = lax.Precision.HIGHEST
two_pi = 2.0 * math.pi
LANES = 128
SUBLANES = 8


def angle_table(left_index, right_index, modulus, orient):
    product = left_index[:, None] * right_index[None, :] % modulus
    return orient * two_pi * product.astype(jnp.float32) / modulus


def rotate(real_part, imag_part, angles):
    cosine_table = jnp.cos(angles)
    sine_table = jnp.sin(angles)
    return (
        real_part * cosine_table - imag_part * sine_table,
        real_part * sine_table + imag_part * cosine_table,
    )


def last_transform(real_part, imag_part, orient):
    length = real_part.shape[-1]
    counter = jnp.arange(length, dtype=jnp.int32)
    angles = angle_table(counter, counter, length, orient)
    cosine_table = jnp.cos(angles)
    sine_table = jnp.sin(angles)
    dot = functools.partial(jnp.dot, precision=precise, preferred_element_type=jnp.float32)
    return (
        dot(real_part, cosine_table) - dot(imag_part, sine_table),
        dot(imag_part, cosine_table) + dot(real_part, sine_table),
    )


def discretize(readout, log_step, decay_log, rotation):
    step_size = jnp.exp(log_step)[:, None]
    pole_real = -jnp.exp(decay_log)[None, :]
    pole_imag = rotation[None, :]
    rate_real = step_size * pole_real
    rate_imag = step_size * pole_imag
    lift_real = jnp.expm1(rate_real) * jnp.cos(rate_imag) - 2.0 * jnp.sin(0.5 * rate_imag) ** 2
    lift_imag = jnp.exp(rate_real) * jnp.sin(rate_imag)
    pole_norm = pole_real * pole_real + pole_imag * pole_imag
    ratio_real = (lift_real * pole_real + lift_imag * pole_imag) / pole_norm
    ratio_imag = (lift_imag * pole_real - lift_real * pole_imag) / pole_norm
    coef_real = readout[0] * ratio_real - readout[1] * ratio_imag
    coef_imag = readout[0] * ratio_imag + readout[1] * ratio_real
    return (coef_real, coef_imag, rate_real, rate_imag)


def parameter_grads(primal, backward, totals):
    coef_real, coef_imag = (primal[0], primal[1])
    cotangents = (
        2.0 * totals[0],
        -2.0 * totals[1],
        2.0 * (coef_real * totals[2] - coef_imag * totals[3]),
        -2.0 * (coef_real * totals[3] + coef_imag * totals[2]),
    )
    return backward(cotangents)


def shifted_totals(raw_sums, rate_real, rate_imag, block_start, norm_scale):
    decays = jnp.exp(rate_real * block_start)
    phases = rate_imag * block_start
    base_real = decays * jnp.cos(phases)
    base_imag = decays * jnp.sin(phases)
    near_real = block_start * raw_sums[0] + raw_sums[2]
    near_imag = block_start * raw_sums[1] + raw_sums[3]
    return jnp.stack(
        [
            norm_scale * (base_real * raw_sums[0] - base_imag * raw_sums[1]),
            norm_scale * (base_real * raw_sums[1] + base_imag * raw_sums[0]),
            norm_scale * (base_real * near_real - base_imag * near_imag),
            norm_scale * (base_real * near_imag + base_imag * near_real),
        ]
    )


def whole_channel_totals(lag_rows, rate_real, rate_imag, norm_scale):
    owners, length = (lag_rows.shape[1], lag_rows.shape[2])
    offsets = jnp.arange(length, dtype=jnp.int32).astype(jnp.float32)
    decays = jnp.exp(rate_real[:, :, None] * offsets)
    phases = rate_imag[:, :, None] * offsets
    power_real = decays * jnp.cos(phases)
    power_imag = decays * jnp.sin(phases)
    weighted = lag_rows * offsets
    raw_sums = jnp.stack(
        [
            jnp.einsum("cbj,cnj->cnb", lag_rows, power_real, precision=precise),
            jnp.einsum("cbj,cnj->cnb", lag_rows, power_imag, precision=precise),
            jnp.einsum("cbj,cnj->cnb", weighted, power_real, precision=precise),
            jnp.einsum("cbj,cnj->cnb", weighted, power_imag, precision=precise),
        ]
    )
    starts = (jnp.arange(owners, dtype=jnp.int32) * length).astype(jnp.float32)
    totals = shifted_totals(
        raw_sums, rate_real[:, :, None], rate_imag[:, :, None], starts, norm_scale
    )
    return jnp.sum(totals, axis=-1)


def general_lags(whole, norm_scale):
    part_count, owners, length = whole.shape[1:]
    freq_width = 2 * owners
    modulus = freq_width * length
    row_index = jnp.arange(owners, dtype=jnp.int32)
    outer_index = jnp.arange(freq_width, dtype=jnp.int32)
    inner_index = jnp.arange(length, dtype=jnp.int32)
    first = angle_table(row_index, outer_index, freq_width, -1.0)
    spec_real = jnp.einsum("scba,bk->scka", whole, jnp.cos(first), precision=precise)
    spec_imag = jnp.einsum("scba,bk->scka", whole, jnp.sin(first), precision=precise)
    spec_real, spec_imag = rotate(
        spec_real, spec_imag, angle_table(outer_index, inner_index, modulus, -1.0)
    )
    freq_real, freq_imag = last_transform(spec_real, spec_imag, -1.0)
    prod_real = freq_real[1] * freq_real[0] + freq_imag[1] * freq_imag[0]
    prod_imag = freq_imag[1] * freq_real[0] - freq_real[1] * freq_imag[0]
    back_real, back_imag = last_transform(prod_real, prod_imag, 1.0)
    back_real, back_imag = rotate(
        back_real, back_imag, angle_table(outer_index, inner_index, modulus, 1.0)
    )
    final = angle_table(outer_index, row_index, freq_width, 1.0)
    lag_rows = jnp.einsum("cka,kb->cba", back_real, jnp.cos(final), precision=precise) - jnp.einsum(
        "cka,kb->cba", back_imag, jnp.sin(final), precision=precise
    )
    return lag_rows * (norm_scale / modulus)


def general_device(inputs, out_grad, readout, log_step, decay_log, rotation):
    owners = lax.axis_size("seq")
    channels, length = inputs.shape
    states = decay_log.shape[0]
    part_count = channels // owners
    norm_scale = 1.0 / math.sqrt(owners * length)
    pieces = jnp.concatenate(
        [a.reshape(owners, part_count, length) for a in (inputs, out_grad)], axis=1
    )
    pieces = lax.all_to_all(pieces, "seq", split_axis=0, concat_axis=0, tiled=True)
    whole = pieces.astype(jnp.float32).reshape(owners, 2, part_count, length)
    lag_rows = general_lags(whole.transpose(1, 2, 0, 3), norm_scale)
    first_channel = lax.axis_index("seq") * part_count
    own_readout = lax.dynamic_slice_in_dim(readout, first_channel, part_count, 1)
    own_step = lax.dynamic_slice_in_dim(log_step, first_channel, part_count, 0)
    primal, backward = jax.vjp(discretize, own_readout, own_step, decay_log, rotation)
    totals = whole_channel_totals(lag_rows, primal[2], primal[3], norm_scale)
    readout_part, step_part, decay_part, rotation_part = parameter_grads(primal, backward, totals)
    shared = jnp.concatenate(
        [readout_part.reshape(-1), step_part, decay_part, rotation_part]
    )
    sent = jnp.concatenate(
        [
            lag_rows.transpose(1, 0, 2).reshape(owners, -1),
            jnp.broadcast_to(shared, (owners, shared.shape[0])),
        ],
        axis=1,
    )
    got = lax.all_to_all(sent, "seq", split_axis=0, concat_axis=0, tiled=True)
    cuts = np.cumsum([part_count * length, 2 * part_count * states, part_count])
    lags, readouts, steps, state = jnp.split(got, cuts, axis=1)
    readouts = readouts.reshape(owners, 2, part_count, states).transpose(1, 0, 2, 3)
    return (
        lags.reshape(channels, length),
        readouts.reshape(2, channels, states),
        steps.reshape(channels),
        lax.psum(jnp.sum(state, axis=0), "ch").reshape(2, states),
    )


def split_halves(value):
    high = value.astype(jnp.bfloat16)
    return high, (value - high.astype(jnp.float32)).astype(jnp.bfloat16)


def cos_sin(angle):
    turns = jnp.floor(angle * (2.0 / math.pi) + 0.5)
    rest = angle - turns * 1.5703125
    rest = rest - turns * 4.837512969970703125e-4
    rest = rest - turns * 7.54978995489188216e-8
    quarter = turns.astype(jnp.int32)
    square = rest * rest
    sine = rest + rest * square * (
        -1.6666654611e-1 + square * (8.3321608736e-3 - square * 1.9515295891e-4)
    )
    cosine = (
        1.0
        - 0.5 * square
        + square
        * square
        * (
            4.166664568298827e-2
            + square * (-1.388731625493765e-3 + square * 2.443315711809948e-5)
        )
    )
    odd = (quarter & 1) == 1
    out_cos = jnp.where(odd, sine, cosine)
    out_sin = jnp.where(odd, cosine, sine)
    out_cos = jnp.where(((quarter + 1) & 2) == 2, -out_cos, out_cos)
    out_sin = jnp.where((quarter & 2) == 2, -out_sin, out_sin)
    return out_cos, out_sin


def grow(value):
    series = 1.0
    for term in range(9, 1, -1):
        series = 1.0 + series * value * (1.0 / term)
    return jnp.where(jnp.abs(value) < 0.35, series * value, jnp.exp(value) - 1.0)


def power(rate_real, rate_imag, offset):
    size = jnp.exp(rate_real * offset)
    cosine, sine = cos_sin(rate_imag * offset)
    return size * cosine, size * sine


def times(left, right):
    return (
        left[0] * right[0] - left[1] * right[1],
        left[0] * right[1] + left[1] * right[0],
    )


def blocks_forward(x):
    root = math.sqrt(0.5)
    cosine, sine = math.cos(math.pi / 8), math.sin(math.pi / 8)
    total = [x[s] + x[s + 4] for s in range(4)]
    gap = [x[s] - x[s + 4] for s in range(4)]
    even, odd = total[0] + total[2], total[1] + total[3]
    real, imag = [None] * 9, [None] * 9
    real[0], real[8] = even + odd, even - odd
    imag[0] = imag[8] = jnp.zeros_like(even)
    real[4], imag[4] = total[0] - total[2], total[3] - total[1]
    less, more = root * (gap[1] - gap[3]), root * (gap[1] + gap[3])
    real[2], imag[2] = gap[0] + less, -gap[2] - more
    real[6], imag[6] = gap[0] - less, gap[2] - more
    less, more = root * (x[2] - x[6]), root * (x[2] + x[6])
    even1 = (x[0] + less, -x[4] - more)
    even3 = (x[0] - less, x[4] - more)
    p, q, r, t = x[1] - x[7], x[3] - x[5], x[1] + x[7], x[3] + x[5]
    odd1 = (cosine * p + sine * q, -sine * r - cosine * t)
    odd3 = (sine * p - cosine * q, sine * t - cosine * r)
    real[1], imag[1] = even1[0] + odd1[0], even1[1] + odd1[1]
    real[7], imag[7] = even1[0] - odd1[0], odd1[1] - even1[1]
    real[3], imag[3] = even3[0] + odd3[0], even3[1] + odd3[1]
    real[5], imag[5] = even3[0] - odd3[0], odd3[1] - even3[1]
    return list(zip(real, imag))


def blocks_back(z):
    root = math.sqrt(0.5)
    cosine, sine = math.cos(math.pi / 8), math.sin(math.pi / 8)
    real, imag = [v[0] for v in z], [v[1] for v in z]
    even, odd = real[0] + real[8], real[0] - real[8]
    total = [even + real[4], odd + imag[4], even - real[4], odd - imag[4]]
    less, more = root * (real[2] - real[6]), root * (imag[2] + imag[6])
    gap = [real[2] + real[6], less + more, imag[2] - imag[6], more - less]
    x = [total[s] + gap[s] for s in range(4)] + [total[s] - gap[s] for s in range(4)]
    even1 = (real[1] + real[7], imag[7] - imag[1])
    even3 = (real[3] + real[5], imag[5] - imag[3])
    odd1 = (real[1] - real[7], imag[1] + imag[7])
    odd3 = (real[3] - real[5], imag[3] + imag[5])
    less, more = root * (even1[0] - even3[0]), root * (even1[1] + even3[1])
    p = cosine * odd1[0] + sine * odd3[0]
    q = sine * odd1[0] - cosine * odd3[0]
    r = sine * odd1[1] + cosine * odd3[1]
    t = cosine * odd1[1] - sine * odd3[1]
    extra = [
        even1[0] + even3[0],
        p + r,
        less - more,
        q + t,
        even3[1] - even1[1],
        t - q,
        -less - more,
        r - p,
    ]
    return [v + w for v, w in zip(x, extra)]


def transform_tables(owners, length, norm_scale):
    width = 2 * owners
    counter = np.arange(length)
    angles = two_pi * (counter[:, None] * counter[None, :] % length) / length
    cosine, sine = np.cos(angles), np.sin(angles)
    matrix = np.block([[cosine, -sine], [sine, cosine]]).astype(np.float32)
    high = matrix.astype(jnp.bfloat16)
    low = (matrix - high.astype(np.float32)).astype(jnp.bfloat16)
    outer = np.arange(owners + 1)
    angles = two_pi * (outer[:, None] * counter[None, :]) / (width * length)
    twiddle = np.stack([np.cos(angles), -np.sin(angles)], axis=1)
    weight = np.where(outer % owners == 0, 1.0, 2.0) * norm_scale / (width * length)
    twiddle = np.concatenate([twiddle, twiddle * weight[:, None, None]], axis=1)
    return np.stack([high, low]), twiddle.astype(np.float32)


def three_pieces(value):
    pieces = []
    for _ in range(3):
        piece = value.astype(jnp.bfloat16).astype(jnp.float32)
        pieces.append(piece)
        value = value - piece
    return pieces


def swap(value):
    return pltpu.roll(value, LANES // 2, 1)


def rest_lanes(lane):
    return lane < 3, (lane >= LANES // 2) & (lane < LANES // 2 + 3)


def pack_rests(high, rest, pieces):
    lane = lax.broadcasted_iota(jnp.int32, high.shape, 1)
    shared, replaced = rest_lanes(lane)
    steps = jnp.where(high == 0.0, 0.0, rest / jnp.where(high == 0.0, 1.0, high))
    steps = jnp.floor(steps * (256.0 * REST_STEPS) + 0.5)
    rest = jnp.where(shared, steps * (2.0 * REST_STEPS + 1.0) + swap(steps), rest)
    for i, piece in enumerate(pieces):
        rest = jnp.where(lane == LANES // 2 + i, piece, rest)
    return rest


def unpack_rests(high, rest):
    lane = lax.broadcasted_iota(jnp.int32, high.shape, 1)
    shared, replaced = rest_lanes(lane)
    step = sum(rest[:, LANES // 2 + i : LANES // 2 + i + 1] for i in range(3))
    both = jnp.where(shared, rest, swap(rest))
    first = jnp.floor(both * (1.0 / (2.0 * REST_STEPS + 1.0)) + 0.5)
    second = both - first * (2.0 * REST_STEPS + 1.0)
    steps = jnp.where(shared, first, second) * (1.0 / (256.0 * REST_STEPS))
    return jnp.where(shared | replaced, high * steps, rest), jnp.broadcast_to(step, high.shape)


def transposed(value):
    return jnp.concatenate(
        [value[:, spot : spot + LANES].T for spot in range(0, value.shape[1], LANES)], axis=0
    )


READ, REST, OUT_ROWS = 16, 17, 18
REST_STEPS = 7.0
ROWS = 20
LAGS, GRADS, STATE, SINGLES = 0, 8, 16, 18
STEP_LANES, SCALE_LANES = (0, 8), (16, 17, 18, 19)
SPARE = 15.0
PARTS = 4
FRESH = 4


def pack_kernel(inputs, out_grad, readout, log_step, *refs):
    count = (len(refs) - 7) // 2
    sources, (out, *held) = refs[:count], refs[count : 2 * count + 1]
    signals, read, step, turned, rows, sems = refs[2 * count + 1 :]
    peers = out.shape[0] // OUT_ROWS
    copies = [
        pltpu.make_async_copy(source, target, sems.at[i])
        for i, (source, target) in enumerate(
            (
                (readout, read),
                (log_step, step),
                (inputs, signals.at[0]),
                (out_grad, signals.at[1]),
                *zip(sources, held),
            )
        )
    ]
    for copy in copies:
        copy.start()
    for copy in copies[:4]:
        copy.wait()
    own = lax.axis_index("seq")
    turned[...] = transposed(read[...])
    channels = step.shape[1]
    peer = lax.broadcasted_iota(jnp.int32, (peers, channels), 0)
    channel = lax.broadcasted_iota(jnp.int32, (peers, channels), 1)
    mine = jnp.where(channel == peer * SUBLANES + own, step[...], 0.0)
    mine = jnp.broadcast_to(jnp.sum(mine, axis=1, keepdims=True), (peers, LANES))
    for place, signal in enumerate((signals[0], signals[1])):
        value = signal.astype(jnp.float32)
        for peer in range(peers):
            spot = peer * OUT_ROWS + place * SUBLANES
            rows[spot : spot + SUBLANES] = value[peer * SUBLANES : (peer + 1) * SUBLANES]
    value = turned[pl.ds(own, peers, stride=SUBLANES), :]
    high = value.astype(jnp.bfloat16).astype(jnp.float32)
    rows[pl.ds(READ, peers, stride=OUT_ROWS), :] = high
    rows[pl.ds(REST, peers, stride=OUT_ROWS), :] = pack_rests(high, value - high, three_pieces(mine))
    out[...] = rows[...].astype(jnp.bfloat16)
    for copy in copies[4:]:
        copy.wait()


def exponent_of(bound):
    return jnp.floor(jnp.log(jnp.maximum(bound, 1e-30)) * (1.0 / math.log(2.0))) + (2.0 - SPARE)


def greatest(value):
    return jnp.max(jnp.max(value, axis=1, keepdims=True), axis=0, keepdims=True)


def size_of(value):
    return jnp.abs(value[0]) + jnp.abs(value[1])


def two_pieces(value):
    high = value.astype(jnp.bfloat16).astype(jnp.float32)
    return high, (value - high) * 256.0


def main_kernel(
    owners,
    norm_scale,
    got,
    matrix,
    twiddle,
    decay_log,
    rotation,
    sent,
    rows_in,
    spectra,
    freq,
    back,
    params,
    doubled,
    bases,
    powers,
    lags,
    sums,
):
    peers, length = got.shape[0] // OUT_ROWS, got.shape[1]
    groups = peers // owners
    part_count = groups * SUBLANES
    rows = 2 * part_count
    pairs = part_count // 2
    half = pairs // SUBLANES
    reach = length // 2
    lane = lax.broadcasted_iota(jnp.int32, (pairs, LANES), 1)
    left = lane < LANES // 2
    row = lax.broadcasted_iota(jnp.int32, (SUBLANES, LANES), 0)

    def lanes_of(side):
        return slice(side * LANES, (side + 1) * LANES)

    def collect(spot):
        tiles = [
            rows_in[pl.ds(group * owners * OUT_ROWS + spot, owners, stride=OUT_ROWS), :]
            for group in range(groups)
        ]
        return jnp.concatenate(tiles[:half], axis=0), jnp.concatenate(tiles[half:], axis=0)

    def make_params():
        sides = []
        for high, rest in zip(collect(READ), collect(REST)):
            rest, step = unpack_rests(high, rest)
            sides.append((high + rest, step))
        (lower, lower_step), (upper, upper_step) = sides
        read = (jnp.where(left, lower, swap(upper)), jnp.where(left, swap(lower), upper))
        step = jnp.exp(jnp.where(left, lower_step, upper_step))
        decay_row = jnp.concatenate([decay_log[...], decay_log[...]], axis=1)
        rotation_row = jnp.concatenate([rotation[...], rotation[...]], axis=1)
        pole = (
            jnp.broadcast_to(-jnp.exp(decay_row), step.shape),
            jnp.broadcast_to(rotation_row, step.shape),
        )
        rate = (step * pole[0], step * pole[1])
        place, size = 0, 1
        while size < owners * length:
            if place // 2 % FRESH == 0:
                value = power(rate[0], rate[1], float(size))
            else:
                value = (value[0] * value[0] - value[1] * value[1], 2.0 * value[0] * value[1])
            doubled[place], doubled[place + 1] = value
            place, size = place + 2, size * 2
        sine = cos_sin(0.5 * rate[1])[1]
        cosine = 1.0 - 2.0 * sine * sine
        lift = (grow(rate[0]) * cosine - 2.0 * sine * sine, doubled[1])
        norm = 1.0 / (pole[0] * pole[0] + pole[1] * pole[1])
        inverse = (pole[0] * norm, -pole[1] * norm)
        ratio = times(lift, inverse)
        coef = times(read, ratio)
        lifted = times((doubled[0], doubled[1]), inverse)
        values = (rate, ratio, coef, times(read, lifted), pole, times(coef, inverse), (step, step))
        for place, value in enumerate(values):
            params[2 * place], params[2 * place + 1] = value

    block_bit, reach_bit = length.bit_length() - 1, reach.bit_length() - 1
    bits = [(row & (1 << i)) != 0 for i in range(SUBLANES.bit_length() - 1)]

    def doubled_row(p, i):
        return doubled[2 * i, p : p + 1, :], doubled[2 * i + 1, p : p + 1, :]

    def by_rows(p, first):
        out = None
        for i, bit in enumerate(bits):
            real, imag = doubled_row(p, first + i)
            value = (jnp.where(bit, real, 1.0), jnp.where(bit, imag, 0.0))
            out = value if out is None else times(out, value)
        return out

    def make_tables():
        for p in range(pairs):
            table = [by_rows(p, 0)]
            for i in range(len(bits), reach_bit):
                table += [times(block, doubled_row(p, i)) for block in table]
            for place in range(0, len(table), 2):
                for side in range(2):
                    value = jnp.concatenate([table[place][side], table[place + 1][side]], axis=0)
                    for i, piece in enumerate(split_halves(value)):
                        spot = 2 * i * reach + place * SUBLANES
                        powers[p, spot : spot + 2 * SUBLANES, lanes_of(side)] = piece
                        spot += reach
                        powers[p, spot : spot + 2 * SUBLANES, lanes_of(side)] = piece
            base = by_rows(p, block_bit)
            bases[p, 0], bases[p, 1] = base
            bases[p, 2], bases[p, 3] = times(base, doubled_row(p, reach_bit))

    def transform(source, target, count):
        dot = functools.partial(jnp.dot, preferred_element_type=jnp.float32)
        cuts = [(owners + 1) * i // PARTS * count for i in range(PARTS + 1)]
        for part in map(slice, cuts, cuts[1:]):
            low = source[1, part]
            target[part] = (
                dot(source[0, part], matrix[0]) + dot(low, matrix[0]) + dot(source[0, part], matrix[1])
            )

    def spread_blocks():
        rows_in[...] = got[...].astype(jnp.float32)
        blocks = []
        for s in range(owners):
            spots = [(group * owners + s) * OUT_ROWS for group in range(groups)]
            blocks.append(
                jnp.concatenate(
                    [rows_in[spot : spot + SUBLANES] for spot in spots]
                    + [rows_in[spot + SUBLANES : spot + 2 * SUBLANES] for spot in spots],
                    axis=0,
                )
            )
        for k, value in enumerate(blocks_forward(blocks)):
            if k:
                value = times(value, (twiddle[k, 0:1], twiddle[k, 1:2]))
            for side in range(2):
                for i, piece in enumerate(split_halves(value[side])):
                    spectra[i, k * rows : (k + 1) * rows, lanes_of(side)] = piece

    def to_frequencies():
        transform(spectra, freq, rows)
        make_params()
        make_tables()

    def to_lags():
        for k in range(owners + 1):
            at_in = freq[k * rows : k * rows + part_count]
            at_out = freq[k * rows + part_count : (k + 1) * rows]
            ur, ui = at_in[:, :length], at_in[:, length:]
            gr, gi = at_out[:, :length], at_out[:, length:]
            for side, value in enumerate((gr * ur + gi * ui, gr * ui - gi * ur)):
                for i, piece in enumerate(split_halves(value)):
                    spectra[i, k * part_count : (k + 1) * part_count, lanes_of(side)] = piece
        transform(spectra, back, part_count)

    def finish():
        turned = []
        for k in range(owners + 1):
            spots = slice(k * part_count, (k + 1) * part_count)
            value = (back[spots, lanes_of(0)], back[spots, lanes_of(1)])
            turned.append(times(value, (twiddle[k, 2:3], twiddle[k, 3:4])))
        blocks = blocks_back(turned)

        most = jnp.zeros((part_count, LANES), jnp.float32)
        for b, block in enumerate(blocks):
            most = jnp.maximum(most, jnp.abs(block))
            lags[b * part_count : (b + 1) * part_count] = block

        def param(place):
            return params[2 * place], params[2 * place + 1]

        rate, ratio, coef, through, pole, direct, (step, _) = (param(i) for i in range(7))
        most = greatest(most)
        whole = 2.0 * math.sqrt(owners * length)
        on_rate = size_of(coef) * float(owners * length) + size_of(through)
        on_pole = step * on_rate + size_of(direct)
        lag_exponent = exponent_of(most)
        grad_exponent = exponent_of(most * (whole * greatest(size_of(ratio))))
        state_exponent = exponent_of(
            most * (whole * part_count * greatest(on_pole * (1.0 - pole[0])))
        )
        step_exponent = exponent_of(
            most * (whole * (LANES // 2) * greatest(on_rate * size_of(rate)))
        )
        lag_scale = jnp.exp2(-lag_exponent)
        for b, block in enumerate(blocks):
            for group in range(groups):
                place = (group * owners + b) * ROWS
                value = block[group * SUBLANES : (group + 1) * SUBLANES]
                sent[place + LAGS : place + GRADS] = value * lag_scale

        start = row.astype(jnp.float32) * float(length)
        first = left[:owners]
        wide = lax.broadcasted_iota(jnp.int32, (4 * owners, LANES), 1)
        wide_left = wide < reach
        offset = jnp.where(wide_left, wide, wide - reach).astype(jnp.float32)
        both_left = wide_left[: 2 * owners]
        for p in range(pairs):
            both = jnp.concatenate(
                [
                    lags[pl.ds(first_row, owners, stride=part_count), :]
                    for first_row in (p, pairs + p)
                ],
                axis=0,
            )
            swapped = swap(both)
            plain = jnp.concatenate(
                [jnp.where(both_left, both, swapped), jnp.where(both_left, swapped, both)], axis=0
            )
            factor = []
            for value in (plain, plain * offset):
                high = value.astype(jnp.bfloat16).astype(jnp.float32)
                factor.append(jnp.where(wide_left, high, value - high))
            factor = jnp.concatenate(factor, axis=0).astype(jnp.bfloat16)
            raw = jnp.dot(
                jnp.concatenate([factor, factor], axis=1),
                powers[p],
                preferred_element_type=jnp.float32,
            )

            def pick(place, side):
                top = raw[2 * place * owners : (2 * place + 1) * owners, lanes_of(side)]
                bottom = raw[(2 * place + 1) * owners : (2 * place + 2) * owners, lanes_of(side)]
                return jnp.where(first, top, bottom)

            found = None
            for part in range(2):
                base = (bases[p, 2 * part], bases[p, 2 * part + 1])
                near = start + float(part * reach)
                value = (pick(part, 0), pick(part, 1))
                lagged = (near * value[0] + pick(2 + part, 0), near * value[1] + pick(2 + part, 1))
                terms = times(base, value) + times(base, lagged)
                found = terms if found is None else [x + y for x, y in zip(found, terms)]
            for place, value in enumerate(found):
                sums[place, p : p + 1] = jnp.sum(value, axis=0, keepdims=True)

        total = (sums[0] * (2.0 * norm_scale), sums[1] * (2.0 * norm_scale))
        lag_total = (sums[2] * (2.0 * norm_scale), sums[3] * (2.0 * norm_scale))
        on_read = times(total, ratio)
        on_read = (on_read[0], -on_read[1])
        on_rate = times(coef, lag_total)
        more = times(total, through)
        on_rate = (on_rate[0] + more[0], on_rate[1] + more[1])
        less = times(total, direct)
        on_pole = (step * on_rate[0] - less[0], step * on_rate[1] - less[1])
        on_step = times(on_rate, rate)[0]
        on_decay = jnp.sum(on_pole[0] * pole[0], axis=0, keepdims=True)
        on_rotation = -jnp.sum(on_pole[1], axis=0, keepdims=True)
        on_decay = on_decay + swap(on_decay)
        on_rotation = on_rotation + swap(on_rotation)
        state = jnp.where(left[0:1], on_decay, on_rotation) * jnp.exp2(-state_exponent)

        grad_scale = jnp.exp2(-grad_exponent)
        on_read = (on_read[0] * grad_scale, on_read[1] * grad_scale)
        lower = jnp.where(left, on_read[0], swap(on_read[1]))
        upper = jnp.where(left, swap(on_read[0]), on_read[1])
        grads = jnp.concatenate([lower, upper], axis=0)
        step_scale = jnp.broadcast_to(jnp.exp2(-step_exponent), (pairs, LANES))
        step_columns = [
            jnp.broadcast_to(jnp.sum(value, axis=1, keepdims=True), (pairs, LANES)) * step_scale
            for value in (jnp.where(left, on_step, 0.0), jnp.where(left, 0.0, on_step))
        ]
        place_lane = lax.broadcasted_iota(jnp.int32, (SUBLANES, LANES), 1)
        scales = jnp.zeros((1, LANES), jnp.float32)
        for spot, value in zip(
            SCALE_LANES, (lag_exponent, grad_exponent, state_exponent, step_exponent)
        ):
            scales = jnp.where(place_lane[0:1] == spot, value, scales)
        state_high, state_low = two_pieces(state)
        tails = []
        for group in range(groups):
            spot = group % half * SUBLANES
            pieces = two_pieces(step_columns[group // half][spot : spot + SUBLANES])
            spread = jnp.zeros((SUBLANES, LANES), jnp.float32)
            for spot, piece in zip(STEP_LANES, pieces):
                spread = jnp.where(place_lane == row + spot, piece, spread)
            singles = scales + jnp.sum(spread, axis=0, keepdims=True)
            tails.append(jnp.concatenate([state_high, state_low, singles, singles], axis=0))
        for b in range(owners):
            for group in range(groups):
                place = (group * owners + b) * ROWS
                sent[place + GRADS : place + STATE] = grads[
                    group * SUBLANES : (group + 1) * SUBLANES
                ]
                sent[place + STATE : place + ROWS] = tails[group]

    for section in (spread_blocks, to_frequencies, to_lags, finish):
        section()


def unpack_kernel(got, kernel_grad, readout_grad, step_grad, state_grad, wide, grads):
    peers = got.shape[0] // ROWS
    per_row = LANES // SUBLANES
    singles = got[pl.ds(SINGLES, peers, stride=ROWS), :]
    exponents = [jnp.broadcast_to(singles[:, spot : spot + 1], (peers, LANES)) for spot in SCALE_LANES]
    scales = [jnp.exp2(value) for value in exponents]
    for i in range(2):
        wide[i] = scales[i]
    for spot in range(0, peers, per_row):
        part = slice(spot * SUBLANES, (spot + per_row) * SUBLANES)
        for i, first, target in ((1, GRADS, grads), (0, LAGS, kernel_grad)):
            for peer in range(spot, spot + per_row):
                place = peer * ROWS + first
                target[peer * SUBLANES : (peer + 1) * SUBLANES] = (
                    got[place : place + SUBLANES] * wide[i, peer : peer + 1, :]
                )
        readout_grad[:, part] = grads[part].T

    high = got[pl.ds(STATE, peers, stride=ROWS), :]
    low = got[pl.ds(STATE + 1, peers, stride=ROWS), :]
    total = jnp.sum((high + low * (1.0 / 256.0)) * scales[2], axis=0, keepdims=True)
    states = state_grad.shape[1]
    state_grad[0:1] = total[:, :states]
    state_grad[1:2] = total[:, states:]
    lane = lax.broadcasted_iota(jnp.int32, (peers, LANES), 1)
    row = lax.broadcasted_iota(jnp.int32, (peers, LANES), 0)
    high, low = (
        jnp.take_along_axis(singles, lane % SUBLANES + first, axis=1) for first in STEP_LANES
    )
    value = (high + low * (1.0 / 256.0)) * scales[3]
    for spot in range(0, peers, per_row):
        mine = jnp.where(row - spot == lane // SUBLANES, value, 0.0)
        step_grad[spot * SUBLANES : (spot + per_row) * SUBLANES] = jnp.sum(mine, axis=0)


def kernel_device(inputs, out_grad, readout, log_step, decay_log, rotation):
    owners, groups = lax.axis_size("seq"), lax.axis_size("ch")
    peers = owners * groups
    channels, length = inputs.shape
    states = decay_log.shape[0]
    part_count = channels // owners
    pairs = part_count // 2
    norm_scale = 1.0 / math.sqrt(owners * length)
    vmem = pl.BlockSpec(memory_space=pltpu.VMEM)
    memory = pltpu.CompilerParams(vmem_limit_bytes=32 * 1024 * 1024)
    f32, bf16 = jnp.float32, jnp.bfloat16

    def exchange(value):
        rows = value.shape[0] // peers
        value = value.reshape(peers, rows // 2, 2, LANES)
        value = lax.all_to_all(value, ("ch", "seq"), split_axis=0, concat_axis=0, tiled=True)
        return value.reshape(peers * rows, LANES)

    anywhere = pl.BlockSpec(memory_space=pl.ANY)
    held = [jnp.asarray(table) for table in transform_tables(owners, length, norm_scale)]
    held += [decay_log[None], rotation[None]]
    sources = (
        inputs, out_grad, readout.transpose(0, 2, 1).reshape(LANES, channels), log_step[None], *held
    )
    pieces, *held = pl.pallas_call(
        pack_kernel,
        out_shape=[jax.ShapeDtypeStruct((peers * OUT_ROWS, LANES), bf16)]
        + [jax.ShapeDtypeStruct(value.shape, value.dtype) for value in held],
        in_specs=[anywhere] * len(sources),
        out_specs=[vmem] * (1 + len(held)),
        scratch_shapes=[
            pltpu.VMEM((2, channels, LANES), bf16),
            pltpu.VMEM((LANES, channels), f32),
            pltpu.VMEM((1, channels), f32),
            pltpu.VMEM((channels, LANES), f32),
            pltpu.VMEM((peers * OUT_ROWS, LANES), f32),
            pltpu.SemaphoreType.DMA((len(sources),)),
        ],
        compiler_params=memory,
    )(*(pltpu.with_memory_space_constraint(value, pltpu.HBM) for value in sources))
    got = exchange(pieces)
    sent = pl.pallas_call(
        functools.partial(main_kernel, owners, norm_scale),
        out_shape=jax.ShapeDtypeStruct((peers * ROWS, LANES), f32),
        in_specs=[vmem] * 5,
        out_specs=vmem,
        scratch_shapes=[
            pltpu.VMEM((peers * OUT_ROWS, LANES), f32),
            pltpu.VMEM((2, (owners + 1) * 2 * part_count, 2 * LANES), bf16),
            pltpu.VMEM(((owners + 1) * 2 * part_count, 2 * LANES), f32),
            pltpu.VMEM(((owners + 1) * part_count, 2 * LANES), f32),
            pltpu.VMEM((14, pairs, LANES), f32),
            pltpu.VMEM((2 * (owners * length).bit_length(), pairs, LANES), f32),
            pltpu.VMEM((pairs, 4, owners, LANES), f32),
            pltpu.VMEM((pairs, 2 * length, 2 * LANES), bf16),
            pltpu.VMEM((owners * part_count, length), f32),
            pltpu.VMEM((4, pairs, LANES), f32),
        ],
        compiler_params=memory,
    )(got, *held)
    back = exchange(sent.astype(jnp.float16))
    kernel_grad, readout_grad, step_grad, state_grad = pl.pallas_call(
        unpack_kernel,
        out_shape=[
            jax.ShapeDtypeStruct((channels, length), f32),
            jax.ShapeDtypeStruct((LANES, channels), f32),
            jax.ShapeDtypeStruct((channels,), f32),
            jax.ShapeDtypeStruct((2, states), f32),
        ],
        in_specs=[vmem],
        out_specs=[vmem] * 4,
        scratch_shapes=[
            pltpu.VMEM((2, peers, LANES), f32),
            pltpu.VMEM((channels, LANES), f32),
        ],
        compiler_params=memory,
    )(back.astype(f32))
    readout_grad = readout_grad.reshape(2, states, channels).transpose(0, 2, 1)
    return kernel_grad, readout_grad, step_grad, state_grad


def kernel_fits(mesh, inputs, decay_log):
    owners, groups = mesh.shape["seq"], mesh.shape["ch"]
    channels = inputs.shape[0] // groups
    return (
        inputs.shape[1] == owners * LANES
        and 2 * decay_log.shape[0] == LANES
        and owners == SUBLANES
        and groups % 2 == 0
        and channels == owners * groups * SUBLANES
        and channels % LANES == 0
    )


def solution(mesh):
    def whole(inputs, out_grad, readout, log_step, decay_log, rotation):
        fits = kernel_fits(mesh, inputs, decay_log)
        return jax.shard_map(
            kernel_device if fits else general_device,
            mesh=mesh,
            in_specs=(P("ch", "seq"), P("ch", "seq"), P(None, "ch", None), P("ch"), P(), P()),
            out_specs=(P("ch", "seq"), P(None, "ch", None), P("ch"), P()),
            check_vma=False,
        )(inputs, out_grad, readout, log_step, decay_log, rotation)

    return whole
```

```python
import functools
import math

import jax
import jax.numpy as jnp
import numpy as np
from jax import lax
from jax.experimental import pallas as pl
from jax.experimental.pallas import tpu as pltpu
from jax.sharding import PartitionSpec as P

precise = lax.Precision.HIGHEST
two_pi = 2.0 * math.pi
LANES = 128
SUBLANES = 8


def angle_table(left_index, right_index, modulus, orient):
    product = left_index[:, None] * right_index[None, :] % modulus
    return orient * two_pi * product.astype(jnp.float32) / modulus


def rotate(real_part, imag_part, angles):
    cosine_table = jnp.cos(angles)
    sine_table = jnp.sin(angles)
    return (
        real_part * cosine_table - imag_part * sine_table,
        real_part * sine_table + imag_part * cosine_table,
    )


def last_transform(real_part, imag_part, orient):
    length = real_part.shape[-1]
    counter = jnp.arange(length, dtype=jnp.int32)
    angles = angle_table(counter, counter, length, orient)
    cosine_table = jnp.cos(angles)
    sine_table = jnp.sin(angles)
    dot = functools.partial(jnp.dot, precision=precise, preferred_element_type=jnp.float32)
    return (
        dot(real_part, cosine_table) - dot(imag_part, sine_table),
        dot(imag_part, cosine_table) + dot(real_part, sine_table),
    )


def discretize(readout, log_step, decay_log, rotation):
    step_size = jnp.exp(log_step)[:, None]
    pole_real = -jnp.exp(decay_log)[None, :]
    pole_imag = rotation[None, :]
    rate_real = step_size * pole_real
    rate_imag = step_size * pole_imag
    lift_real = jnp.expm1(rate_real) * jnp.cos(rate_imag) - 2.0 * jnp.sin(0.5 * rate_imag) ** 2
    lift_imag = jnp.exp(rate_real) * jnp.sin(rate_imag)
    pole_norm = pole_real * pole_real + pole_imag * pole_imag
    ratio_real = (lift_real * pole_real + lift_imag * pole_imag) / pole_norm
    ratio_imag = (lift_imag * pole_real - lift_real * pole_imag) / pole_norm
    coef_real = readout[0] * ratio_real - readout[1] * ratio_imag
    coef_imag = readout[0] * ratio_imag + readout[1] * ratio_real
    return (coef_real, coef_imag, rate_real, rate_imag)


def parameter_grads(primal, backward, totals):
    coef_real, coef_imag = (primal[0], primal[1])
    cotangents = (
        2.0 * totals[0],
        -2.0 * totals[1],
        2.0 * (coef_real * totals[2] - coef_imag * totals[3]),
        -2.0 * (coef_real * totals[3] + coef_imag * totals[2]),
    )
    return backward(cotangents)


def shifted_totals(raw_sums, rate_real, rate_imag, block_start, norm_scale):
    decays = jnp.exp(rate_real * block_start)
    phases = rate_imag * block_start
    base_real = decays * jnp.cos(phases)
    base_imag = decays * jnp.sin(phases)
    near_real = block_start * raw_sums[0] + raw_sums[2]
    near_imag = block_start * raw_sums[1] + raw_sums[3]
    return jnp.stack(
        [
            norm_scale * (base_real * raw_sums[0] - base_imag * raw_sums[1]),
            norm_scale * (base_real * raw_sums[1] + base_imag * raw_sums[0]),
            norm_scale * (base_real * near_real - base_imag * near_imag),
            norm_scale * (base_real * near_imag + base_imag * near_real),
        ]
    )


def whole_channel_totals(lag_rows, rate_real, rate_imag, norm_scale):
    owners, length = (lag_rows.shape[1], lag_rows.shape[2])
    offsets = jnp.arange(length, dtype=jnp.int32).astype(jnp.float32)
    decays = jnp.exp(rate_real[:, :, None] * offsets)
    phases = rate_imag[:, :, None] * offsets
    power_real = decays * jnp.cos(phases)
    power_imag = decays * jnp.sin(phases)
    weighted = lag_rows * offsets
    raw_sums = jnp.stack(
        [
            jnp.einsum("cbj,cnj->cnb", lag_rows, power_real, precision=precise),
            jnp.einsum("cbj,cnj->cnb", lag_rows, power_imag, precision=precise),
            jnp.einsum("cbj,cnj->cnb", weighted, power_real, precision=precise),
            jnp.einsum("cbj,cnj->cnb", weighted, power_imag, precision=precise),
        ]
    )
    starts = (jnp.arange(owners, dtype=jnp.int32) * length).astype(jnp.float32)
    totals = shifted_totals(
        raw_sums, rate_real[:, :, None], rate_imag[:, :, None], starts, norm_scale
    )
    return jnp.sum(totals, axis=-1)


def general_lags(whole, norm_scale):
    part_count, owners, length = whole.shape[1:]
    freq_width = 2 * owners
    modulus = freq_width * length
    row_index = jnp.arange(owners, dtype=jnp.int32)
    outer_index = jnp.arange(freq_width, dtype=jnp.int32)
    inner_index = jnp.arange(length, dtype=jnp.int32)
    first = angle_table(row_index, outer_index, freq_width, -1.0)
    spec_real = jnp.einsum("scba,bk->scka", whole, jnp.cos(first), precision=precise)
    spec_imag = jnp.einsum("scba,bk->scka", whole, jnp.sin(first), precision=precise)
    spec_real, spec_imag = rotate(
        spec_real, spec_imag, angle_table(outer_index, inner_index, modulus, -1.0)
    )
    freq_real, freq_imag = last_transform(spec_real, spec_imag, -1.0)
    prod_real = freq_real[1] * freq_real[0] + freq_imag[1] * freq_imag[0]
    prod_imag = freq_imag[1] * freq_real[0] - freq_real[1] * freq_imag[0]
    back_real, back_imag = last_transform(prod_real, prod_imag, 1.0)
    back_real, back_imag = rotate(
        back_real, back_imag, angle_table(outer_index, inner_index, modulus, 1.0)
    )
    final = angle_table(outer_index, row_index, freq_width, 1.0)
    lag_rows = jnp.einsum("cka,kb->cba", back_real, jnp.cos(final), precision=precise) - jnp.einsum(
        "cka,kb->cba", back_imag, jnp.sin(final), precision=precise
    )
    return lag_rows * (norm_scale / modulus)


def general_device(inputs, out_grad, readout, log_step, decay_log, rotation):
    owners = lax.axis_size("seq")
    channels, length = inputs.shape
    states = decay_log.shape[0]
    part_count = channels // owners
    norm_scale = 1.0 / math.sqrt(owners * length)
    pieces = jnp.concatenate(
        [a.reshape(owners, part_count, length) for a in (inputs, out_grad)], axis=1
    )
    pieces = lax.all_to_all(pieces, "seq", split_axis=0, concat_axis=0, tiled=True)
    whole = pieces.astype(jnp.float32).reshape(owners, 2, part_count, length)
    lag_rows = general_lags(whole.transpose(1, 2, 0, 3), norm_scale)
    first_channel = lax.axis_index("seq") * part_count
    own_readout = lax.dynamic_slice_in_dim(readout, first_channel, part_count, 1)
    own_step = lax.dynamic_slice_in_dim(log_step, first_channel, part_count, 0)
    primal, backward = jax.vjp(discretize, own_readout, own_step, decay_log, rotation)
    totals = whole_channel_totals(lag_rows, primal[2], primal[3], norm_scale)
    readout_part, step_part, decay_part, rotation_part = parameter_grads(primal, backward, totals)
    shared = jnp.concatenate(
        [readout_part.reshape(-1), step_part, decay_part, rotation_part]
    )
    sent = jnp.concatenate(
        [
            lag_rows.transpose(1, 0, 2).reshape(owners, -1),
            jnp.broadcast_to(shared, (owners, shared.shape[0])),
        ],
        axis=1,
    )
    got = lax.all_to_all(sent, "seq", split_axis=0, concat_axis=0, tiled=True)
    cuts = np.cumsum([part_count * length, 2 * part_count * states, part_count])
    lags, readouts, steps, state = jnp.split(got, cuts, axis=1)
    readouts = readouts.reshape(owners, 2, part_count, states).transpose(1, 0, 2, 3)
    return (
        lags.reshape(channels, length),
        readouts.reshape(2, channels, states),
        steps.reshape(channels),
        lax.psum(jnp.sum(state, axis=0), "ch").reshape(2, states),
    )


def split_halves(value):
    high = value.astype(jnp.bfloat16)
    return high, (value - high.astype(jnp.float32)).astype(jnp.bfloat16)


def cos_sin(angle):
    turns = jnp.floor(angle * (2.0 / math.pi) + 0.5)
    rest = angle - turns * 1.5703125
    rest = rest - turns * 4.837512969970703125e-4
    rest = rest - turns * 7.54978995489188216e-8
    quarter = turns.astype(jnp.int32)
    square = rest * rest
    sine = rest + rest * square * (
        -1.6666654611e-1 + square * (8.3321608736e-3 - square * 1.9515295891e-4)
    )
    cosine = (
        1.0
        - 0.5 * square
        + square
        * square
        * (
            4.166664568298827e-2
            + square * (-1.388731625493765e-3 + square * 2.443315711809948e-5)
        )
    )
    odd = (quarter & 1) == 1
    out_cos = jnp.where(odd, sine, cosine)
    out_sin = jnp.where(odd, cosine, sine)
    out_cos = jnp.where(((quarter + 1) & 2) == 2, -out_cos, out_cos)
    out_sin = jnp.where((quarter & 2) == 2, -out_sin, out_sin)
    return out_cos, out_sin


def grow(value):
    series = 1.0
    for term in range(9, 1, -1):
        series = 1.0 + series * value * (1.0 / term)
    return jnp.where(jnp.abs(value) < 0.35, series * value, jnp.exp(value) - 1.0)


def power(rate_real, rate_imag, offset):
    size = jnp.exp(rate_real * offset)
    cosine, sine = cos_sin(rate_imag * offset)
    return size * cosine, size * sine


def times(left, right):
    return (
        left[0] * right[0] - left[1] * right[1],
        left[0] * right[1] + left[1] * right[0],
    )


def blocks_forward(x):
    root = math.sqrt(0.5)
    cosine, sine = math.cos(math.pi / 8), math.sin(math.pi / 8)
    total = [x[s] + x[s + 4] for s in range(4)]
    gap = [x[s] - x[s + 4] for s in range(4)]
    even, odd = total[0] + total[2], total[1] + total[3]
    real, imag = [None] * 9, [None] * 9
    real[0], real[8] = even + odd, even - odd
    imag[0] = imag[8] = jnp.zeros_like(even)
    real[4], imag[4] = total[0] - total[2], total[3] - total[1]
    less, more = root * (gap[1] - gap[3]), root * (gap[1] + gap[3])
    real[2], imag[2] = gap[0] + less, -gap[2] - more
    real[6], imag[6] = gap[0] - less, gap[2] - more
    less, more = root * (x[2] - x[6]), root * (x[2] + x[6])
    even1 = (x[0] + less, -x[4] - more)
    even3 = (x[0] - less, x[4] - more)
    p, q, r, t = x[1] - x[7], x[3] - x[5], x[1] + x[7], x[3] + x[5]
    odd1 = (cosine * p + sine * q, -sine * r - cosine * t)
    odd3 = (sine * p - cosine * q, sine * t - cosine * r)
    real[1], imag[1] = even1[0] + odd1[0], even1[1] + odd1[1]
    real[7], imag[7] = even1[0] - odd1[0], odd1[1] - even1[1]
    real[3], imag[3] = even3[0] + odd3[0], even3[1] + odd3[1]
    real[5], imag[5] = even3[0] - odd3[0], odd3[1] - even3[1]
    return list(zip(real, imag))


def blocks_back(z):
    root = math.sqrt(0.5)
    cosine, sine = math.cos(math.pi / 8), math.sin(math.pi / 8)
    real, imag = [v[0] for v in z], [v[1] for v in z]
    even, odd = real[0] + real[8], real[0] - real[8]
    total = [even + real[4], odd + imag[4], even - real[4], odd - imag[4]]
    less, more = root * (real[2] - real[6]), root * (imag[2] + imag[6])
    gap = [real[2] + real[6], less + more, imag[2] - imag[6], more - less]
    x = [total[s] + gap[s] for s in range(4)] + [total[s] - gap[s] for s in range(4)]
    even1 = (real[1] + real[7], imag[7] - imag[1])
    even3 = (real[3] + real[5], imag[5] - imag[3])
    odd1 = (real[1] - real[7], imag[1] + imag[7])
    odd3 = (real[3] - real[5], imag[3] + imag[5])
    less, more = root * (even1[0] - even3[0]), root * (even1[1] + even3[1])
    p = cosine * odd1[0] + sine * odd3[0]
    q = sine * odd1[0] - cosine * odd3[0]
    r = sine * odd1[1] + cosine * odd3[1]
    t = cosine * odd1[1] - sine * odd3[1]
    extra = [
        even1[0] + even3[0],
        p + r,
        less - more,
        q + t,
        even3[1] - even1[1],
        t - q,
        -less - more,
        r - p,
    ]
    return [v + w for v, w in zip(x, extra)]


def transform_tables(owners, length, norm_scale):
    width = 2 * owners
    counter = np.arange(length)
    angles = two_pi * (counter[:, None] * counter[None, :] % length) / length
    cosine, sine = np.cos(angles), np.sin(angles)
    matrix = np.block([[cosine, -sine], [sine, cosine]]).astype(np.float32)
    high = matrix.astype(jnp.bfloat16)
    low = (matrix - high.astype(np.float32)).astype(jnp.bfloat16)
    outer = np.arange(owners + 1)
    angles = two_pi * (outer[:, None] * counter[None, :]) / (width * length)
    twiddle = np.stack([np.cos(angles), -np.sin(angles)], axis=1)
    weight = np.where(outer % owners == 0, 1.0, 2.0) * norm_scale / (width * length)
    twiddle = np.concatenate([twiddle, twiddle * weight[:, None, None]], axis=1)
    return np.stack([high, low]), twiddle.astype(np.float32)


def three_pieces(value):
    pieces = []
    for _ in range(3):
        piece = value.astype(jnp.bfloat16).astype(jnp.float32)
        pieces.append(piece)
        value = value - piece
    return pieces


def swap(value):
    return pltpu.roll(value, LANES // 2, 1)


def rest_lanes(lane):
    return lane < 3, (lane >= LANES // 2) & (lane < LANES // 2 + 3)


def pack_rests(high, rest, pieces):
    lane = lax.broadcasted_iota(jnp.int32, high.shape, 1)
    shared, replaced = rest_lanes(lane)
    steps = jnp.where(high == 0.0, 0.0, rest / jnp.where(high == 0.0, 1.0, high))
    steps = jnp.floor(steps * (256.0 * REST_STEPS) + 0.5)
    rest = jnp.where(shared, steps * (2.0 * REST_STEPS + 1.0) + swap(steps), rest)
    for i, piece in enumerate(pieces):
        rest = jnp.where(lane == LANES // 2 + i, piece, rest)
    return rest


def unpack_rests(high, rest):
    lane = lax.broadcasted_iota(jnp.int32, high.shape, 1)
    shared, replaced = rest_lanes(lane)
    step = sum(rest[:, LANES // 2 + i : LANES // 2 + i + 1] for i in range(3))
    both = jnp.where(shared, rest, swap(rest))
    first = jnp.floor(both * (1.0 / (2.0 * REST_STEPS + 1.0)) + 0.5)
    second = both - first * (2.0 * REST_STEPS + 1.0)
    steps = jnp.where(shared, first, second) * (1.0 / (256.0 * REST_STEPS))
    return jnp.where(shared | replaced, high * steps, rest), jnp.broadcast_to(step, high.shape)


def transposed(value):
    return jnp.concatenate(
        [value[:, spot : spot + LANES].T for spot in range(0, value.shape[1], LANES)], axis=0
    )


READ, REST, OUT_ROWS = 16, 17, 18
REST_STEPS = 7.0
ROWS = 20
LAGS, GRADS, STATE, SINGLES = 0, 8, 16, 18
STEP_LANES, SCALE_LANES = (0, 8), (16, 17, 18, 19)
SPARE = 15.0
PARTS = 4
FRESH = 5


def pack_kernel(inputs, out_grad, readout, log_step, *refs):
    count = (len(refs) - 7) // 2
    sources, (out, *held) = refs[:count], refs[count : 2 * count + 1]
    signals, read, step, turned, rows, sems = refs[2 * count + 1 :]
    peers = out.shape[0] // OUT_ROWS
    copies = [
        pltpu.make_async_copy(source, target, sems.at[i])
        for i, (source, target) in enumerate(
            (
                (readout, read),
                (log_step, step),
                (inputs, signals.at[0]),
                (out_grad, signals.at[1]),
                *zip(sources, held),
            )
        )
    ]
    for copy in copies:
        copy.start()
    for copy in copies[:4]:
        copy.wait()
    own = lax.axis_index("seq")
    turned[...] = transposed(read[...])
    channels = step.shape[1]
    peer = lax.broadcasted_iota(jnp.int32, (peers, channels), 0)
    channel = lax.broadcasted_iota(jnp.int32, (peers, channels), 1)
    mine = jnp.where(channel == peer * SUBLANES + own, step[...], 0.0)
    mine = jnp.broadcast_to(jnp.sum(mine, axis=1, keepdims=True), (peers, LANES))
    for place, signal in enumerate((signals[0], signals[1])):
        value = signal.astype(jnp.float32)
        for peer in range(peers):
            spot = peer * OUT_ROWS + place * SUBLANES
            rows[spot : spot + SUBLANES] = value[peer * SUBLANES : (peer + 1) * SUBLANES]
    value = turned[pl.ds(own, peers, stride=SUBLANES), :]
    high = value.astype(jnp.bfloat16).astype(jnp.float32)
    rows[pl.ds(READ, peers, stride=OUT_ROWS), :] = high
    rows[pl.ds(REST, peers, stride=OUT_ROWS), :] = pack_rests(high, value - high, three_pieces(mine))
    out[...] = rows[...].astype(jnp.bfloat16)
    for copy in copies[4:]:
        copy.wait()


def exponent_of(bound):
    return jnp.floor(jnp.log(jnp.maximum(bound, 1e-30)) * (1.0 / math.log(2.0))) + (2.0 - SPARE)


def greatest(value):
    return jnp.max(jnp.max(value, axis=1, keepdims=True), axis=0, keepdims=True)


def size_of(value):
    return jnp.abs(value[0]) + jnp.abs(value[1])


def two_pieces(value):
    high = value.astype(jnp.bfloat16).astype(jnp.float32)
    return high, (value - high) * 256.0


def main_kernel(
    owners,
    norm_scale,
    got,
    matrix,
    twiddle,
    decay_log,
    rotation,
    sent,
    rows_in,
    spectra,
    freq,
    back,
    params,
    doubled,
    bases,
    powers,
    lags,
    sums,
):
    peers, length = got.shape[0] // OUT_ROWS, got.shape[1]
    groups = peers // owners
    part_count = groups * SUBLANES
    rows = 2 * part_count
    pairs = part_count // 2
    half = pairs // SUBLANES
    reach = length // 2
    lane = lax.broadcasted_iota(jnp.int32, (pairs, LANES), 1)
    left = lane < LANES // 2
    row = lax.broadcasted_iota(jnp.int32, (SUBLANES, LANES), 0)

    def lanes_of(side):
        return slice(side * LANES, (side + 1) * LANES)

    def collect(spot):
        tiles = [
            rows_in[pl.ds(group * owners * OUT_ROWS + spot, owners, stride=OUT_ROWS), :]
            for group in range(groups)
        ]
        return jnp.concatenate(tiles[:half], axis=0), jnp.concatenate(tiles[half:], axis=0)

    def make_params():
        sides = []
        for high, rest in zip(collect(READ), collect(REST)):
            rest, step = unpack_rests(high, rest)
            sides.append((high + rest, step))
        (lower, lower_step), (upper, upper_step) = sides
        read = (jnp.where(left, lower, swap(upper)), jnp.where(left, swap(lower), upper))
        step = jnp.exp(jnp.where(left, lower_step, upper_step))
        decay_row = jnp.concatenate([decay_log[...], decay_log[...]], axis=1)
        rotation_row = jnp.concatenate([rotation[...], rotation[...]], axis=1)
        pole = (
            jnp.broadcast_to(-jnp.exp(decay_row), step.shape),
            jnp.broadcast_to(rotation_row, step.shape),
        )
        rate = (step * pole[0], step * pole[1])
        place, size = 0, 1
        while size < owners * length:
            if place // 2 % FRESH == 0:
                value = power(rate[0], rate[1], float(size))
            else:
                value = (value[0] * value[0] - value[1] * value[1], 2.0 * value[0] * value[1])
            doubled[place], doubled[place + 1] = value
            place, size = place + 2, size * 2
        sine = cos_sin(0.5 * rate[1])[1]
        cosine = 1.0 - 2.0 * sine * sine
        lift = (grow(rate[0]) * cosine - 2.0 * sine * sine, doubled[1])
        norm = 1.0 / (pole[0] * pole[0] + pole[1] * pole[1])
        inverse = (pole[0] * norm, -pole[1] * norm)
        ratio = times(lift, inverse)
        coef = times(read, ratio)
        lifted = times((doubled[0], doubled[1]), inverse)
        values = (rate, ratio, coef, times(read, lifted), pole, times(coef, inverse), (step, step))
        for place, value in enumerate(values):
            params[2 * place], params[2 * place + 1] = value

    block_bit, reach_bit = length.bit_length() - 1, reach.bit_length() - 1
    bits = [(row & (1 << i)) != 0 for i in range(SUBLANES.bit_length() - 1)]

    def doubled_row(p, i):
        return doubled[2 * i, p : p + 1, :], doubled[2 * i + 1, p : p + 1, :]

    def by_rows(p, first):
        out = None
        for i, bit in enumerate(bits):
            real, imag = doubled_row(p, first + i)
            value = (jnp.where(bit, real, 1.0), jnp.where(bit, imag, 0.0))
            out = value if out is None else times(out, value)
        return out

    def make_tables():
        for p in range(pairs):
            table = [by_rows(p, 0)]
            for i in range(len(bits), reach_bit):
                table += [times(block, doubled_row(p, i)) for block in table]
            for place in range(0, len(table), 2):
                for side in range(2):
                    value = jnp.concatenate([table[place][side], table[place + 1][side]], axis=0)
                    for i, piece in enumerate(split_halves(value)):
                        spot = 2 * i * reach + place * SUBLANES
                        powers[p, spot : spot + 2 * SUBLANES, lanes_of(side)] = piece
                        spot += reach
                        powers[p, spot : spot + 2 * SUBLANES, lanes_of(side)] = piece
            base = by_rows(p, block_bit)
            bases[p, 0], bases[p, 1] = base
            bases[p, 2], bases[p, 3] = times(base, doubled_row(p, reach_bit))

    def transform(source, target, count):
        dot = functools.partial(jnp.dot, preferred_element_type=jnp.float32)
        cuts = [(owners + 1) * i // PARTS * count for i in range(PARTS + 1)]
        for part in map(slice, cuts, cuts[1:]):
            low = source[1, part]
            target[part] = (
                dot(source[0, part], matrix[0]) + dot(low, matrix[0]) + dot(source[0, part], matrix[1])
            )

    def spread_blocks():
        rows_in[...] = got[...].astype(jnp.float32)
        blocks = []
        for s in range(owners):
            spots = [(group * owners + s) * OUT_ROWS for group in range(groups)]
            blocks.append(
                jnp.concatenate(
                    [rows_in[spot : spot + SUBLANES] for spot in spots]
                    + [rows_in[spot + SUBLANES : spot + 2 * SUBLANES] for spot in spots],
                    axis=0,
                )
            )
        for k, value in enumerate(blocks_forward(blocks)):
            if k:
                value = times(value, (twiddle[k, 0:1], twiddle[k, 1:2]))
            for side in range(2):
                for i, piece in enumerate(split_halves(value[side])):
                    spectra[i, k * rows : (k + 1) * rows, lanes_of(side)] = piece

    def to_frequencies():
        transform(spectra, freq, rows)
        make_params()
        make_tables()

    def to_lags():
        for k in range(owners + 1):
            at_in = freq[k * rows : k * rows + part_count]
            at_out = freq[k * rows + part_count : (k + 1) * rows]
            ur, ui = at_in[:, :length], at_in[:, length:]
            gr, gi = at_out[:, :length], at_out[:, length:]
            for side, value in enumerate((gr * ur + gi * ui, gr * ui - gi * ur)):
                for i, piece in enumerate(split_halves(value)):
                    spectra[i, k * part_count : (k + 1) * part_count, lanes_of(side)] = piece
        transform(spectra, back, part_count)

    def finish():
        turned = []
        for k in range(owners + 1):
            spots = slice(k * part_count, (k + 1) * part_count)
            value = (back[spots, lanes_of(0)], back[spots, lanes_of(1)])
            turned.append(times(value, (twiddle[k, 2:3], twiddle[k, 3:4])))
        blocks = blocks_back(turned)

        most = jnp.zeros((part_count, LANES), jnp.float32)
        for b, block in enumerate(blocks):
            most = jnp.maximum(most, jnp.abs(block))
            lags[b * part_count : (b + 1) * part_count] = block

        def param(place):
            return params[2 * place], params[2 * place + 1]

        rate, ratio, coef, through, pole, direct, (step, _) = (param(i) for i in range(7))
        most = greatest(most)
        whole = 2.0 * math.sqrt(owners * length)
        on_rate = size_of(coef) * float(owners * length) + size_of(through)
        on_pole = step * on_rate + size_of(direct)
        lag_exponent = exponent_of(most)
        grad_exponent = exponent_of(most * (whole * greatest(size_of(ratio))))
        state_exponent = exponent_of(
            most * (whole * part_count * greatest(on_pole * (1.0 - pole[0])))
        )
        step_exponent = exponent_of(
            most * (whole * (LANES // 2) * greatest(on_rate * size_of(rate)))
        )
        lag_scale = jnp.exp2(-lag_exponent)
        for b, block in enumerate(blocks):
            for group in range(groups):
                place = (group * owners + b) * ROWS
                value = block[group * SUBLANES : (group + 1) * SUBLANES]
                sent[place + LAGS : place + GRADS] = value * lag_scale

        start = row.astype(jnp.float32) * float(length)
        first = left[:owners]
        wide = lax.broadcasted_iota(jnp.int32, (4 * owners, LANES), 1)
        wide_left = wide < reach
        offset = jnp.where(wide_left, wide, wide - reach).astype(jnp.float32)
        both_left = wide_left[: 2 * owners]
        for p in range(pairs):
            both = jnp.concatenate(
                [
                    lags[pl.ds(first_row, owners, stride=part_count), :]
                    for first_row in (p, pairs + p)
                ],
                axis=0,
            )
            swapped = swap(both)
            plain = jnp.concatenate(
                [jnp.where(both_left, both, swapped), jnp.where(both_left, swapped, both)], axis=0
            )
            factor = []
            for value in (plain, plain * offset):
                high = value.astype(jnp.bfloat16).astype(jnp.float32)
                factor.append(jnp.where(wide_left, high, value - high))
            factor = jnp.concatenate(factor, axis=0).astype(jnp.bfloat16)
            raw = jnp.dot(
                jnp.concatenate([factor, factor], axis=1),
                powers[p],
                preferred_element_type=jnp.float32,
            )

            def pick(place, side):
                top = raw[2 * place * owners : (2 * place + 1) * owners, lanes_of(side)]
                bottom = raw[(2 * place + 1) * owners : (2 * place + 2) * owners, lanes_of(side)]
                return jnp.where(first, top, bottom)

            found = None
            for part in range(2):
                base = (bases[p, 2 * part], bases[p, 2 * part + 1])
                near = start + float(part * reach)
                value = (pick(part, 0), pick(part, 1))
                lagged = (near * value[0] + pick(2 + part, 0), near * value[1] + pick(2 + part, 1))
                terms = times(base, value) + times(base, lagged)
                found = terms if found is None else [x + y for x, y in zip(found, terms)]
            for place, value in enumerate(found):
                sums[place, p : p + 1] = jnp.sum(value, axis=0, keepdims=True)

        total = (sums[0] * (2.0 * norm_scale), sums[1] * (2.0 * norm_scale))
        lag_total = (sums[2] * (2.0 * norm_scale), sums[3] * (2.0 * norm_scale))
        on_read = times(total, ratio)
        on_read = (on_read[0], -on_read[1])
        on_rate = times(coef, lag_total)
        more = times(total, through)
        on_rate = (on_rate[0] + more[0], on_rate[1] + more[1])
        less = times(total, direct)
        on_pole = (step * on_rate[0] - less[0], step * on_rate[1] - less[1])
        on_step = times(on_rate, rate)[0]
        on_decay = jnp.sum(on_pole[0] * pole[0], axis=0, keepdims=True)
        on_rotation = -jnp.sum(on_pole[1], axis=0, keepdims=True)
        on_decay = on_decay + swap(on_decay)
        on_rotation = on_rotation + swap(on_rotation)
        state = jnp.where(left[0:1], on_decay, on_rotation) * jnp.exp2(-state_exponent)

        grad_scale = jnp.exp2(-grad_exponent)
        on_read = (on_read[0] * grad_scale, on_read[1] * grad_scale)
        lower = jnp.where(left, on_read[0], swap(on_read[1]))
        upper = jnp.where(left, swap(on_read[0]), on_read[1])
        grads = jnp.concatenate([lower, upper], axis=0)
        step_scale = jnp.broadcast_to(jnp.exp2(-step_exponent), (pairs, LANES))
        step_columns = [
            jnp.broadcast_to(jnp.sum(value, axis=1, keepdims=True), (pairs, LANES)) * step_scale
            for value in (jnp.where(left, on_step, 0.0), jnp.where(left, 0.0, on_step))
        ]
        place_lane = lax.broadcasted_iota(jnp.int32, (SUBLANES, LANES), 1)
        scales = jnp.zeros((1, LANES), jnp.float32)
        for spot, value in zip(
            SCALE_LANES, (lag_exponent, grad_exponent, state_exponent, step_exponent)
        ):
            scales = jnp.where(place_lane[0:1] == spot, value, scales)
        state_high, state_low = two_pieces(state)
        tails = []
        for group in range(groups):
            spot = group % half * SUBLANES
            pieces = two_pieces(step_columns[group // half][spot : spot + SUBLANES])
            spread = jnp.zeros((SUBLANES, LANES), jnp.float32)
            for spot, piece in zip(STEP_LANES, pieces):
                spread = jnp.where(place_lane == row + spot, piece, spread)
            singles = scales + jnp.sum(spread, axis=0, keepdims=True)
            tails.append(jnp.concatenate([state_high, state_low, singles, singles], axis=0))
        for b in range(owners):
            for group in range(groups):
                place = (group * owners + b) * ROWS
                sent[place + GRADS : place + STATE] = grads[
                    group * SUBLANES : (group + 1) * SUBLANES
                ]
                sent[place + STATE : place + ROWS] = tails[group]

    for section in (spread_blocks, to_frequencies, to_lags, finish):
        section()


def unpack_kernel(got, kernel_grad, readout_grad, step_grad, state_grad, wide, grads):
    peers = got.shape[0] // ROWS
    per_row = LANES // SUBLANES
    singles = got[pl.ds(SINGLES, peers, stride=ROWS), :]
    exponents = [jnp.broadcast_to(singles[:, spot : spot + 1], (peers, LANES)) for spot in SCALE_LANES]
    scales = [jnp.exp2(value) for value in exponents]
    wide[...] = scales[0]
    lane = lax.broadcasted_iota(jnp.int32, (peers, LANES), 1)
    row = lax.broadcasted_iota(jnp.int32, (peers, LANES), 0)

    def by_channel(value, spot):
        mine = jnp.where(row - spot == lane // SUBLANES, value, 0.0)
        return jnp.sum(mine, axis=0, keepdims=True)

    for spot in range(0, peers, per_row):
        part = slice(spot * SUBLANES, (spot + per_row) * SUBLANES)
        for peer in range(spot, spot + per_row):
            place, own = peer * ROWS, slice(peer * SUBLANES, (peer + 1) * SUBLANES)
            grads[own] = got[place + GRADS : place + STATE]
            kernel_grad[own] = got[place + LAGS : place + GRADS] * wide[peer : peer + 1, :]
        readout_grad[:, part] = grads[part].T * by_channel(scales[1], spot)

    high = got[pl.ds(STATE, peers, stride=ROWS), :]
    low = got[pl.ds(STATE + 1, peers, stride=ROWS), :]
    total = jnp.sum((high + low * (1.0 / 256.0)) * scales[2], axis=0, keepdims=True)
    states = state_grad.shape[1]
    state_grad[0:1] = total[:, :states]
    state_grad[1:2] = total[:, states:]
    high, low = (
        jnp.take_along_axis(singles, lane % SUBLANES + first, axis=1) for first in STEP_LANES
    )
    value = (high + low * (1.0 / 256.0)) * scales[3]
    for spot in range(0, peers, per_row):
        part = slice(spot * SUBLANES, (spot + per_row) * SUBLANES)
        step_grad[part] = by_channel(value, spot).reshape(LANES)


def kernel_device(inputs, out_grad, readout, log_step, decay_log, rotation):
    owners, groups = lax.axis_size("seq"), lax.axis_size("ch")
    peers = owners * groups
    channels, length = inputs.shape
    states = decay_log.shape[0]
    part_count = channels // owners
    pairs = part_count // 2
    norm_scale = 1.0 / math.sqrt(owners * length)
    vmem = pl.BlockSpec(memory_space=pltpu.VMEM)
    memory = pltpu.CompilerParams(vmem_limit_bytes=32 * 1024 * 1024)
    f32, bf16 = jnp.float32, jnp.bfloat16

    def exchange(value):
        rows = value.shape[0] // peers
        value = value.reshape(peers, rows // 2, 2, LANES)
        value = lax.all_to_all(value, ("ch", "seq"), split_axis=0, concat_axis=0, tiled=True)
        return value.reshape(peers * rows, LANES)

    anywhere = pl.BlockSpec(memory_space=pl.ANY)
    held = [jnp.asarray(table) for table in transform_tables(owners, length, norm_scale)]
    held += [decay_log[None], rotation[None]]
    sources = (
        inputs, out_grad, readout.transpose(0, 2, 1).reshape(LANES, channels), log_step[None], *held
    )
    pieces, *held = pl.pallas_call(
        pack_kernel,
        out_shape=[jax.ShapeDtypeStruct((peers * OUT_ROWS, LANES), bf16)]
        + [jax.ShapeDtypeStruct(value.shape, value.dtype) for value in held],
        in_specs=[anywhere] * len(sources),
        out_specs=[vmem] * (1 + len(held)),
        scratch_shapes=[
            pltpu.VMEM((2, channels, LANES), bf16),
            pltpu.VMEM((LANES, channels), f32),
            pltpu.VMEM((1, channels), f32),
            pltpu.VMEM((channels, LANES), f32),
            pltpu.VMEM((peers * OUT_ROWS, LANES), f32),
            pltpu.SemaphoreType.DMA((len(sources),)),
        ],
        compiler_params=memory,
    )(*(pltpu.with_memory_space_constraint(value, pltpu.HBM) for value in sources))
    got = exchange(pieces)
    sent = pl.pallas_call(
        functools.partial(main_kernel, owners, norm_scale),
        out_shape=jax.ShapeDtypeStruct((peers * ROWS, LANES), f32),
        in_specs=[vmem] * 5,
        out_specs=vmem,
        scratch_shapes=[
            pltpu.VMEM((peers * OUT_ROWS, LANES), f32),
            pltpu.VMEM((2, (owners + 1) * 2 * part_count, 2 * LANES), bf16),
            pltpu.VMEM(((owners + 1) * 2 * part_count, 2 * LANES), f32),
            pltpu.VMEM(((owners + 1) * part_count, 2 * LANES), f32),
            pltpu.VMEM((14, pairs, LANES), f32),
            pltpu.VMEM((2 * (owners * length).bit_length(), pairs, LANES), f32),
            pltpu.VMEM((pairs, 4, owners, LANES), f32),
            pltpu.VMEM((pairs, 2 * length, 2 * LANES), bf16),
            pltpu.VMEM((owners * part_count, length), f32),
            pltpu.VMEM((4, pairs, LANES), f32),
        ],
        compiler_params=memory,
    )(got, *held)
    back = exchange(sent.astype(jnp.float16))
    kernel_grad, readout_grad, step_grad, state_grad = pl.pallas_call(
        unpack_kernel,
        out_shape=[
            jax.ShapeDtypeStruct((channels, length), f32),
            jax.ShapeDtypeStruct((LANES, channels), f32),
            jax.ShapeDtypeStruct((channels,), f32),
            jax.ShapeDtypeStruct((2, states), f32),
        ],
        in_specs=[vmem],
        out_specs=[vmem] * 4,
        scratch_shapes=[
            pltpu.VMEM((peers, LANES), f32),
            pltpu.VMEM((channels, LANES), f32),
        ],
        compiler_params=memory,
    )(back.astype(f32))
    readout_grad = readout_grad.reshape(2, states, channels).transpose(0, 2, 1)
    return kernel_grad, readout_grad, step_grad, state_grad


def kernel_fits(mesh, inputs, decay_log):
    owners, groups = mesh.shape["seq"], mesh.shape["ch"]
    channels = inputs.shape[0] // groups
    return (
        inputs.shape[1] == owners * LANES
        and 2 * decay_log.shape[0] == LANES
        and owners == SUBLANES
        and groups % 2 == 0
        and channels == owners * groups * SUBLANES
        and channels % LANES == 0
    )


def solution(mesh):
    def whole(inputs, out_grad, readout, log_step, decay_log, rotation):
        fits = kernel_fits(mesh, inputs, decay_log)
        return jax.shard_map(
            kernel_device if fits else general_device,
            mesh=mesh,
            in_specs=(P("ch", "seq"), P("ch", "seq"), P(None, "ch", None), P("ch"), P(), P()),
            out_specs=(P("ch", "seq"), P(None, "ch", None), P("ch"), P()),
            check_vma=False,
        )(inputs, out_grad, readout, log_step, decay_log, rotation)

    return whole
```

```python
import functools
import math

import jax
import jax.numpy as jnp
import numpy as np
from jax import lax
from jax.experimental import pallas as pl
from jax.experimental.pallas import tpu as pltpu
from jax.sharding import PartitionSpec as P

precise = lax.Precision.HIGHEST
two_pi = 2.0 * math.pi
LANES = 128
SUBLANES = 8


def angle_table(left_index, right_index, modulus, orient):
    product = left_index[:, None] * right_index[None, :] % modulus
    return orient * two_pi * product.astype(jnp.float32) / modulus


def rotate(real_part, imag_part, angles):
    cosine_table = jnp.cos(angles)
    sine_table = jnp.sin(angles)
    return (
        real_part * cosine_table - imag_part * sine_table,
        real_part * sine_table + imag_part * cosine_table,
    )


def last_transform(real_part, imag_part, orient):
    length = real_part.shape[-1]
    counter = jnp.arange(length, dtype=jnp.int32)
    angles = angle_table(counter, counter, length, orient)
    cosine_table = jnp.cos(angles)
    sine_table = jnp.sin(angles)
    dot = functools.partial(jnp.dot, precision=precise, preferred_element_type=jnp.float32)
    return (
        dot(real_part, cosine_table) - dot(imag_part, sine_table),
        dot(imag_part, cosine_table) + dot(real_part, sine_table),
    )


def discretize(readout, log_step, decay_log, rotation):
    step_size = jnp.exp(log_step)[:, None]
    pole_real = -jnp.exp(decay_log)[None, :]
    pole_imag = rotation[None, :]
    rate_real = step_size * pole_real
    rate_imag = step_size * pole_imag
    lift_real = jnp.expm1(rate_real) * jnp.cos(rate_imag) - 2.0 * jnp.sin(0.5 * rate_imag) ** 2
    lift_imag = jnp.exp(rate_real) * jnp.sin(rate_imag)
    pole_norm = pole_real * pole_real + pole_imag * pole_imag
    ratio_real = (lift_real * pole_real + lift_imag * pole_imag) / pole_norm
    ratio_imag = (lift_imag * pole_real - lift_real * pole_imag) / pole_norm
    coef_real = readout[0] * ratio_real - readout[1] * ratio_imag
    coef_imag = readout[0] * ratio_imag + readout[1] * ratio_real
    return (coef_real, coef_imag, rate_real, rate_imag)


def parameter_grads(primal, backward, totals):
    coef_real, coef_imag = (primal[0], primal[1])
    cotangents = (
        2.0 * totals[0],
        -2.0 * totals[1],
        2.0 * (coef_real * totals[2] - coef_imag * totals[3]),
        -2.0 * (coef_real * totals[3] + coef_imag * totals[2]),
    )
    return backward(cotangents)


def shifted_totals(raw_sums, rate_real, rate_imag, block_start, norm_scale):
    decays = jnp.exp(rate_real * block_start)
    phases = rate_imag * block_start
    base_real = decays * jnp.cos(phases)
    base_imag = decays * jnp.sin(phases)
    near_real = block_start * raw_sums[0] + raw_sums[2]
    near_imag = block_start * raw_sums[1] + raw_sums[3]
    return jnp.stack(
        [
            norm_scale * (base_real * raw_sums[0] - base_imag * raw_sums[1]),
            norm_scale * (base_real * raw_sums[1] + base_imag * raw_sums[0]),
            norm_scale * (base_real * near_real - base_imag * near_imag),
            norm_scale * (base_real * near_imag + base_imag * near_real),
        ]
    )


def whole_channel_totals(lag_rows, rate_real, rate_imag, norm_scale):
    owners, length = (lag_rows.shape[1], lag_rows.shape[2])
    offsets = jnp.arange(length, dtype=jnp.int32).astype(jnp.float32)
    decays = jnp.exp(rate_real[:, :, None] * offsets)
    phases = rate_imag[:, :, None] * offsets
    power_real = decays * jnp.cos(phases)
    power_imag = decays * jnp.sin(phases)
    weighted = lag_rows * offsets
    raw_sums = jnp.stack(
        [
            jnp.einsum("cbj,cnj->cnb", lag_rows, power_real, precision=precise),
            jnp.einsum("cbj,cnj->cnb", lag_rows, power_imag, precision=precise),
            jnp.einsum("cbj,cnj->cnb", weighted, power_real, precision=precise),
            jnp.einsum("cbj,cnj->cnb", weighted, power_imag, precision=precise),
        ]
    )
    starts = (jnp.arange(owners, dtype=jnp.int32) * length).astype(jnp.float32)
    totals = shifted_totals(
        raw_sums, rate_real[:, :, None], rate_imag[:, :, None], starts, norm_scale
    )
    return jnp.sum(totals, axis=-1)


def general_lags(whole, norm_scale):
    part_count, owners, length = whole.shape[1:]
    freq_width = 2 * owners
    modulus = freq_width * length
    row_index = jnp.arange(owners, dtype=jnp.int32)
    outer_index = jnp.arange(freq_width, dtype=jnp.int32)
    inner_index = jnp.arange(length, dtype=jnp.int32)
    first = angle_table(row_index, outer_index, freq_width, -1.0)
    spec_real = jnp.einsum("scba,bk->scka", whole, jnp.cos(first), precision=precise)
    spec_imag = jnp.einsum("scba,bk->scka", whole, jnp.sin(first), precision=precise)
    spec_real, spec_imag = rotate(
        spec_real, spec_imag, angle_table(outer_index, inner_index, modulus, -1.0)
    )
    freq_real, freq_imag = last_transform(spec_real, spec_imag, -1.0)
    prod_real = freq_real[1] * freq_real[0] + freq_imag[1] * freq_imag[0]
    prod_imag = freq_imag[1] * freq_real[0] - freq_real[1] * freq_imag[0]
    back_real, back_imag = last_transform(prod_real, prod_imag, 1.0)
    back_real, back_imag = rotate(
        back_real, back_imag, angle_table(outer_index, inner_index, modulus, 1.0)
    )
    final = angle_table(outer_index, row_index, freq_width, 1.0)
    lag_rows = jnp.einsum("cka,kb->cba", back_real, jnp.cos(final), precision=precise) - jnp.einsum(
        "cka,kb->cba", back_imag, jnp.sin(final), precision=precise
    )
    return lag_rows * (norm_scale / modulus)


def general_device(inputs, out_grad, readout, log_step, decay_log, rotation):
    owners = lax.axis_size("seq")
    channels, length = inputs.shape
    states = decay_log.shape[0]
    part_count = channels // owners
    norm_scale = 1.0 / math.sqrt(owners * length)
    pieces = jnp.concatenate(
        [a.reshape(owners, part_count, length) for a in (inputs, out_grad)], axis=1
    )
    pieces = lax.all_to_all(pieces, "seq", split_axis=0, concat_axis=0, tiled=True)
    whole = pieces.astype(jnp.float32).reshape(owners, 2, part_count, length)
    lag_rows = general_lags(whole.transpose(1, 2, 0, 3), norm_scale)
    first_channel = lax.axis_index("seq") * part_count
    own_readout = lax.dynamic_slice_in_dim(readout, first_channel, part_count, 1)
    own_step = lax.dynamic_slice_in_dim(log_step, first_channel, part_count, 0)
    primal, backward = jax.vjp(discretize, own_readout, own_step, decay_log, rotation)
    totals = whole_channel_totals(lag_rows, primal[2], primal[3], norm_scale)
    readout_part, step_part, decay_part, rotation_part = parameter_grads(primal, backward, totals)
    shared = jnp.concatenate(
        [readout_part.reshape(-1), step_part, decay_part, rotation_part]
    )
    sent = jnp.concatenate(
        [
            lag_rows.transpose(1, 0, 2).reshape(owners, -1),
            jnp.broadcast_to(shared, (owners, shared.shape[0])),
        ],
        axis=1,
    )
    got = lax.all_to_all(sent, "seq", split_axis=0, concat_axis=0, tiled=True)
    cuts = np.cumsum([part_count * length, 2 * part_count * states, part_count])
    lags, readouts, steps, state = jnp.split(got, cuts, axis=1)
    readouts = readouts.reshape(owners, 2, part_count, states).transpose(1, 0, 2, 3)
    return (
        lags.reshape(channels, length),
        readouts.reshape(2, channels, states),
        steps.reshape(channels),
        lax.psum(jnp.sum(state, axis=0), "ch").reshape(2, states),
    )


def split_halves(value):
    high = value.astype(jnp.bfloat16)
    return high, (value - high.astype(jnp.float32)).astype(jnp.bfloat16)


def cos_sin(angle):
    turns = jnp.floor(angle * (2.0 / math.pi) + 0.5)
    rest = angle - turns * 1.5703125
    rest = rest - turns * 4.837512969970703125e-4
    rest = rest - turns * 7.54978995489188216e-8
    quarter = turns.astype(jnp.int32)
    square = rest * rest
    sine = rest + rest * square * (
        -1.6666654611e-1 + square * (8.3321608736e-3 - square * 1.9515295891e-4)
    )
    cosine = (
        1.0
        - 0.5 * square
        + square
        * square
        * (
            4.166664568298827e-2
            + square * (-1.388731625493765e-3 + square * 2.443315711809948e-5)
        )
    )
    odd = (quarter & 1) == 1
    out_cos = jnp.where(odd, sine, cosine)
    out_sin = jnp.where(odd, cosine, sine)
    out_cos = jnp.where(((quarter + 1) & 2) == 2, -out_cos, out_cos)
    out_sin = jnp.where((quarter & 2) == 2, -out_sin, out_sin)
    return out_cos, out_sin


def grow(value):
    series = 1.0
    for term in range(9, 1, -1):
        series = 1.0 + series * value * (1.0 / term)
    return jnp.where(jnp.abs(value) < 0.35, series * value, jnp.exp(value) - 1.0)


def power(rate_real, rate_imag, offset):
    size = jnp.exp(rate_real * offset)
    cosine, sine = cos_sin(rate_imag * offset)
    return size * cosine, size * sine


def times(left, right):
    return (
        left[0] * right[0] - left[1] * right[1],
        left[0] * right[1] + left[1] * right[0],
    )


def blocks_forward(x):
    root = math.sqrt(0.5)
    cosine, sine = math.cos(math.pi / 8), math.sin(math.pi / 8)
    total = [x[s] + x[s + 4] for s in range(4)]
    gap = [x[s] - x[s + 4] for s in range(4)]
    even, odd = total[0] + total[2], total[1] + total[3]
    real, imag = [None] * 9, [None] * 9
    real[0], real[8] = even + odd, even - odd
    imag[0] = imag[8] = jnp.zeros_like(even)
    real[4], imag[4] = total[0] - total[2], total[3] - total[1]
    less, more = root * (gap[1] - gap[3]), root * (gap[1] + gap[3])
    real[2], imag[2] = gap[0] + less, -gap[2] - more
    real[6], imag[6] = gap[0] - less, gap[2] - more
    less, more = root * (x[2] - x[6]), root * (x[2] + x[6])
    even1 = (x[0] + less, -x[4] - more)
    even3 = (x[0] - less, x[4] - more)
    p, q, r, t = x[1] - x[7], x[3] - x[5], x[1] + x[7], x[3] + x[5]
    odd1 = (cosine * p + sine * q, -sine * r - cosine * t)
    odd3 = (sine * p - cosine * q, sine * t - cosine * r)
    real[1], imag[1] = even1[0] + odd1[0], even1[1] + odd1[1]
    real[7], imag[7] = even1[0] - odd1[0], odd1[1] - even1[1]
    real[3], imag[3] = even3[0] + odd3[0], even3[1] + odd3[1]
    real[5], imag[5] = even3[0] - odd3[0], odd3[1] - even3[1]
    return list(zip(real, imag))


def blocks_back(z):
    root = math.sqrt(0.5)
    cosine, sine = math.cos(math.pi / 8), math.sin(math.pi / 8)
    real, imag = [v[0] for v in z], [v[1] for v in z]
    even, odd = real[0] + real[8], real[0] - real[8]
    total = [even + real[4], odd + imag[4], even - real[4], odd - imag[4]]
    less, more = root * (real[2] - real[6]), root * (imag[2] + imag[6])
    gap = [real[2] + real[6], less + more, imag[2] - imag[6], more - less]
    x = [total[s] + gap[s] for s in range(4)] + [total[s] - gap[s] for s in range(4)]
    even1 = (real[1] + real[7], imag[7] - imag[1])
    even3 = (real[3] + real[5], imag[5] - imag[3])
    odd1 = (real[1] - real[7], imag[1] + imag[7])
    odd3 = (real[3] - real[5], imag[3] + imag[5])
    less, more = root * (even1[0] - even3[0]), root * (even1[1] + even3[1])
    p = cosine * odd1[0] + sine * odd3[0]
    q = sine * odd1[0] - cosine * odd3[0]
    r = sine * odd1[1] + cosine * odd3[1]
    t = cosine * odd1[1] - sine * odd3[1]
    extra = [
        even1[0] + even3[0],
        p + r,
        less - more,
        q + t,
        even3[1] - even1[1],
        t - q,
        -less - more,
        r - p,
    ]
    return [v + w for v, w in zip(x, extra)]


def transform_tables(owners, length, norm_scale):
    width = 2 * owners
    counter = np.arange(length)
    angles = two_pi * (counter[:, None] * counter[None, :] % length) / length
    cosine, sine = np.cos(angles), np.sin(angles)
    matrix = np.block([[cosine, -sine], [sine, cosine]]).astype(np.float32)
    high = matrix.astype(jnp.bfloat16)
    low = (matrix - high.astype(np.float32)).astype(jnp.bfloat16)
    outer = np.arange(owners + 1)
    angles = two_pi * (outer[:, None] * counter[None, :]) / (width * length)
    twiddle = np.stack([np.cos(angles), -np.sin(angles)], axis=1)
    weight = np.where(outer % owners == 0, 1.0, 2.0) * norm_scale / (width * length)
    twiddle = np.concatenate([twiddle, twiddle * weight[:, None, None]], axis=1)
    return np.stack([high, low]), twiddle.astype(np.float32)


def three_pieces(value):
    pieces = []
    for _ in range(3):
        piece = value.astype(jnp.bfloat16).astype(jnp.float32)
        pieces.append(piece)
        value = value - piece
    return pieces


def swap(value):
    return pltpu.roll(value, LANES // 2, 1)


def rest_lanes(lane):
    return lane < 3, (lane >= LANES // 2) & (lane < LANES // 2 + 3)


def rest_steps(value):
    high = value.astype(jnp.bfloat16).astype(jnp.float32)
    steps = jnp.where(high == 0.0, 0.0, (value - high) / jnp.where(high == 0.0, 1.0, high))
    return jnp.floor(steps * (256.0 * REST_STEPS) + 0.5)


def unpack_rests(high, rest):
    lane = lax.broadcasted_iota(jnp.int32, high.shape, 1)
    shared, replaced = rest_lanes(lane)
    step = sum(rest[:, LANES // 2 + i : LANES // 2 + i + 1] for i in range(3))
    both = jnp.where(shared, rest, swap(rest))
    first = jnp.floor(both * (1.0 / (2.0 * REST_STEPS + 1.0)) + 0.5)
    second = both - first * (2.0 * REST_STEPS + 1.0)
    steps = jnp.where(shared, first, second) * (1.0 / (256.0 * REST_STEPS))
    return jnp.where(shared | replaced, high * steps, rest), jnp.broadcast_to(step, high.shape)


def transposed(value):
    return jnp.concatenate(
        [value[:, spot : spot + LANES].T for spot in range(0, value.shape[1], LANES)], axis=0
    )


READ, REST, OUT_ROWS = 16, 17, 18
REST_STEPS = 7.0
ROWS = 20
LAGS, GRADS, STATE, SINGLES = 0, 8, 16, 18
STEP_LANES, SCALE_LANES = (0, 8), (16, 17, 18, 19)
SPARE = 15.0
PARTS = 4
EARLY = 9
FRESH = 5


def pack_kernel(inputs, out_grad, readout, log_step, *refs):
    count = (len(refs) - 7) // 2
    sources, (out, *held) = refs[:count], refs[count : 2 * count + 1]
    signals, read, step, turned, rows, sems = refs[2 * count + 1 :]
    peers = out.shape[0] // OUT_ROWS
    copies = [
        pltpu.make_async_copy(source, target, sems.at[i])
        for i, (source, target) in enumerate(
            (
                (readout, read),
                (log_step, step),
                (inputs, signals.at[0]),
                (out_grad, signals.at[1]),
                *zip(sources, held),
            )
        )
    ]
    for copy in copies:
        copy.start()
    for copy in copies[:4]:
        copy.wait()
    own = lax.axis_index("seq")
    turned[...] = transposed(read[...])
    channels = step.shape[1]
    peer = lax.broadcasted_iota(jnp.int32, (peers, channels), 0)
    channel = lax.broadcasted_iota(jnp.int32, (peers, channels), 1)
    sent_channel = channel == peer * SUBLANES + own

    def pick(row):
        value = jnp.sum(jnp.where(sent_channel, row, 0.0), axis=1, keepdims=True)
        return jnp.broadcast_to(value, (peers, LANES))

    half = LANES // 2
    shared = rest_steps(read[0:SUBLANES]) * (2.0 * REST_STEPS + 1.0)
    shared = shared + rest_steps(read[half : half + SUBLANES])
    pieces = three_pieces(pick(step[...]))
    placed = [(i, pick(shared[i : i + 1])) for i in range(3)]
    placed += [(half + i, piece) for i, piece in enumerate(pieces)]
    for place, signal in enumerate((signals[0], signals[1])):
        value = signal.astype(jnp.float32)
        for peer in range(peers):
            spot = peer * OUT_ROWS + place * SUBLANES
            rows[spot : spot + SUBLANES] = value[peer * SUBLANES : (peer + 1) * SUBLANES]
    value = turned[pl.ds(own, peers, stride=SUBLANES), :]
    high = value.astype(jnp.bfloat16).astype(jnp.float32)
    rows[pl.ds(READ, peers, stride=OUT_ROWS), :] = high
    rest = value - high
    lane = lax.broadcasted_iota(jnp.int32, (peers, LANES), 1)
    for place, other in placed:
        rest = jnp.where(lane == place, other, rest)
    rows[pl.ds(REST, peers, stride=OUT_ROWS), :] = rest
    out[...] = rows[...].astype(jnp.bfloat16)
    for copy in copies[4:]:
        copy.wait()


def exponent_of(bound):
    return jnp.floor(jnp.log(jnp.maximum(bound, 1e-30)) * (1.0 / math.log(2.0))) + (2.0 - SPARE)


def greatest(value):
    return jnp.max(jnp.max(value, axis=1, keepdims=True), axis=0, keepdims=True)


def size_of(value):
    return jnp.abs(value[0]) + jnp.abs(value[1])


def two_pieces(value):
    high = value.astype(jnp.bfloat16).astype(jnp.float32)
    return high, (value - high) * 256.0


def main_kernel(
    owners,
    norm_scale,
    got,
    matrix,
    twiddle,
    decay_log,
    rotation,
    sent,
    rows_in,
    spectra,
    freq,
    back,
    params,
    doubled,
    bases,
    powers,
    early_powers,
    lags,
    sums,
):
    peers, length = got.shape[0] // OUT_ROWS, got.shape[1]
    groups = peers // owners
    part_count = groups * SUBLANES
    rows = 2 * part_count
    pairs = part_count // 2
    half = pairs // SUBLANES
    reach = length // 2
    lane = lax.broadcasted_iota(jnp.int32, (pairs, LANES), 1)
    left = lane < LANES // 2
    row = lax.broadcasted_iota(jnp.int32, (SUBLANES, LANES), 0)

    def lanes_of(side):
        return slice(side * LANES, (side + 1) * LANES)

    def collect(spot):
        tiles = [
            rows_in[pl.ds(group * owners * OUT_ROWS + spot, owners, stride=OUT_ROWS), :]
            for group in range(groups)
        ]
        return jnp.concatenate(tiles[:half], axis=0), jnp.concatenate(tiles[half:], axis=0)

    def make_params():
        sides = []
        for high, rest in zip(collect(READ), collect(REST)):
            rest, step = unpack_rests(high, rest)
            sides.append((high + rest, step))
        (lower, lower_step), (upper, upper_step) = sides
        read = (jnp.where(left, lower, swap(upper)), jnp.where(left, swap(lower), upper))
        step = jnp.exp(jnp.where(left, lower_step, upper_step))
        decay_row = jnp.concatenate([decay_log[...], decay_log[...]], axis=1)
        rotation_row = jnp.concatenate([rotation[...], rotation[...]], axis=1)
        pole = (
            jnp.broadcast_to(-jnp.exp(decay_row), step.shape),
            jnp.broadcast_to(rotation_row, step.shape),
        )
        rate = (step * pole[0], step * pole[1])
        place, size = 0, 1
        while size < owners * length:
            if place // 2 % FRESH == 0:
                value = power(rate[0], rate[1], float(size))
            else:
                value = (value[0] * value[0] - value[1] * value[1], 2.0 * value[0] * value[1])
            doubled[place], doubled[place + 1] = value
            place, size = place + 2, size * 2
        sine = cos_sin(0.5 * rate[1])[1]
        cosine = 1.0 - 2.0 * sine * sine
        lift = (grow(rate[0]) * cosine - 2.0 * sine * sine, doubled[1])
        norm = 1.0 / (pole[0] * pole[0] + pole[1] * pole[1])
        inverse = (pole[0] * norm, -pole[1] * norm)
        ratio = times(lift, inverse)
        coef = times(read, ratio)
        lifted = times((doubled[0], doubled[1]), inverse)
        values = (rate, ratio, coef, times(read, lifted), pole, times(coef, inverse), (step, step))
        for place, value in enumerate(values):
            params[2 * place], params[2 * place + 1] = value

    early = min(EARLY, pairs)
    products = 4 * early * reach
    nothing = twiddle[0, 1, 0].astype(jnp.int32) * (2 * SUBLANES)
    block_bit, reach_bit = length.bit_length() - 1, reach.bit_length() - 1
    bits = [(row & (1 << i)) != 0 for i in range(SUBLANES.bit_length() - 1)]

    def doubled_row(p, i):
        return doubled[2 * i, p : p + 1, :], doubled[2 * i + 1, p : p + 1, :]

    def by_rows(p, first):
        out = None
        for i, bit in enumerate(bits):
            real, imag = doubled_row(p, first + i)
            value = (jnp.where(bit, real, 1.0), jnp.where(bit, imag, 0.0))
            out = value if out is None else times(out, value)
        return out

    def make_tables():
        for p in range(pairs):
            table = [by_rows(p, 0)]
            for i in range(len(bits), reach_bit):
                table += [times(block, doubled_row(p, i)) for block in table]
            for place in range(0, len(table), 2):
                for side in range(2):
                    value = jnp.concatenate([table[place][side], table[place + 1][side]], axis=0)
                    for i, piece in enumerate(split_halves(value)):
                        for spot in (2 * i * reach, (2 * i + 1) * reach):
                            spot += p * 4 * reach + place * SUBLANES
                            if p < early:
                                rows_at = pl.multiple_of(nothing + spot, 2 * SUBLANES)
                                early_powers[pl.ds(rows_at, 2 * SUBLANES), lanes_of(side)] = piece
                            else:
                                powers[spot : spot + 2 * SUBLANES, lanes_of(side)] = piece
            base = by_rows(p, block_bit)
            bases[p, 0], bases[p, 1] = base
            bases[p, 2], bases[p, 3] = times(base, doubled_row(p, reach_bit))

    def transform(pieces, target, count):
        dot = functools.partial(jnp.dot, preferred_element_type=jnp.float32)
        cuts = [(owners + 1) * i // PARTS * count for i in range(PARTS + 1)]
        for part in map(slice, cuts, cuts[1:]):
            high, low = pieces(part)
            target[part] = dot(high, matrix[0]) + dot(low, matrix[0]) + dot(high, matrix[1])

    def spread_blocks():
        rows_in[...] = got[...].astype(jnp.float32)
        blocks = []
        for s in range(owners):
            spots = [(group * owners + s) * OUT_ROWS for group in range(groups)]
            blocks.append(
                jnp.concatenate(
                    [rows_in[spot : spot + SUBLANES] for spot in spots]
                    + [rows_in[spot + SUBLANES : spot + 2 * SUBLANES] for spot in spots],
                    axis=0,
                )
            )
        for k, value in enumerate(blocks_forward(blocks)):
            if k:
                value = times(value, (twiddle[k, 0:1], twiddle[k, 1:2]))
            for side in range(2):
                for i, piece in enumerate(split_halves(value[side])):
                    spectra[i, k * rows : (k + 1) * rows, lanes_of(side)] = piece

    def to_frequencies():
        transform(lambda part: (spectra[0, part], spectra[1, part]), freq, rows)
        make_params()
        make_tables()

    def to_lags():
        for k in range(owners + 1):
            at_in = freq[k * rows : k * rows + part_count]
            at_out = freq[k * rows + part_count : (k + 1) * rows]
            ur, ui = at_in[:, :length], at_in[:, length:]
            gr, gi = at_out[:, :length], at_out[:, length:]
            for side, value in enumerate((gr * ur + gi * ui, gr * ui - gi * ur)):
                for i, piece in enumerate(split_halves(value)):
                    spot = products + (i * (owners + 1) + k) * part_count
                    early_powers[spot : spot + part_count, lanes_of(side)] = piece

        def pieces(part):
            low = products + (owners + 1) * part_count
            return tuple(
                early_powers[first + part.start : first + part.stop] for first in (products, low)
            )

        transform(pieces, back, part_count)

    def finish():
        turned = []
        for k in range(owners + 1):
            spots = slice(k * part_count, (k + 1) * part_count)
            value = (back[spots, lanes_of(0)], back[spots, lanes_of(1)])
            turned.append(times(value, (twiddle[k, 2:3], twiddle[k, 3:4])))
        blocks = blocks_back(turned)

        most = jnp.zeros((part_count, LANES), jnp.float32)
        for b, block in enumerate(blocks):
            most = jnp.maximum(most, jnp.abs(block))
            lags[b * part_count : (b + 1) * part_count] = block

        def param(place):
            return params[2 * place], params[2 * place + 1]

        rate, ratio, coef, through, pole, direct, (step, _) = (param(i) for i in range(7))
        most = greatest(most)
        whole = 2.0 * math.sqrt(owners * length)
        on_rate = size_of(coef) * float(owners * length) + size_of(through)
        on_pole = step * on_rate + size_of(direct)
        lag_exponent = exponent_of(most)
        grad_exponent = exponent_of(most * (whole * greatest(size_of(ratio))))
        state_exponent = exponent_of(
            most * (whole * part_count * greatest(on_pole * (1.0 - pole[0])))
        )
        step_exponent = exponent_of(
            most * (whole * (LANES // 2) * greatest(on_rate * size_of(rate)))
        )
        lag_scale = jnp.exp2(-lag_exponent)
        for b, block in enumerate(blocks):
            for group in range(groups):
                place = (group * owners + b) * ROWS
                value = block[group * SUBLANES : (group + 1) * SUBLANES]
                sent[place + LAGS : place + GRADS] = value * lag_scale

        start = row.astype(jnp.float32) * float(length)
        first = left[:owners]
        wide = lax.broadcasted_iota(jnp.int32, (4 * owners, LANES), 1)
        wide_left = wide < reach
        offset = jnp.where(wide_left, wide, wide - reach).astype(jnp.float32)
        both_left = wide_left[: 2 * owners]
        for p in range(pairs):
            both = jnp.concatenate(
                [
                    lags[pl.ds(first_row, owners, stride=part_count), :]
                    for first_row in (p, pairs + p)
                ],
                axis=0,
            )
            swapped = swap(both)
            plain = jnp.concatenate(
                [jnp.where(both_left, both, swapped), jnp.where(both_left, swapped, both)], axis=0
            )
            factor = []
            for value in (plain, plain * offset):
                high = value.astype(jnp.bfloat16).astype(jnp.float32)
                factor.append(jnp.where(wide_left, high, value - high))
            factor = jnp.concatenate(factor, axis=0).astype(jnp.bfloat16)
            raw = jnp.dot(
                jnp.concatenate([factor, factor], axis=1),
                (early_powers if p < early else powers)[p * 4 * reach : (p + 1) * 4 * reach],
                preferred_element_type=jnp.float32,
            )

            def pick(place, side):
                top = raw[2 * place * owners : (2 * place + 1) * owners, lanes_of(side)]
                bottom = raw[(2 * place + 1) * owners : (2 * place + 2) * owners, lanes_of(side)]
                return jnp.where(first, top, bottom)

            found = None
            for part in range(2):
                base = (bases[p, 2 * part], bases[p, 2 * part + 1])
                near = start + float(part * reach)
                value = (pick(part, 0), pick(part, 1))
                lagged = (near * value[0] + pick(2 + part, 0), near * value[1] + pick(2 + part, 1))
                terms = times(base, value) + times(base, lagged)
                found = terms if found is None else [x + y for x, y in zip(found, terms)]
            for place, value in enumerate(found):
                sums[place, p : p + 1] = jnp.sum(value, axis=0, keepdims=True)

        total = (sums[0] * (2.0 * norm_scale), sums[1] * (2.0 * norm_scale))
        lag_total = (sums[2] * (2.0 * norm_scale), sums[3] * (2.0 * norm_scale))
        on_read = times(total, ratio)
        on_read = (on_read[0], -on_read[1])
        on_rate = times(coef, lag_total)
        more = times(total, through)
        on_rate = (on_rate[0] + more[0], on_rate[1] + more[1])
        less = times(total, direct)
        on_pole = (step * on_rate[0] - less[0], step * on_rate[1] - less[1])
        on_step = times(on_rate, rate)[0]
        on_decay = jnp.sum(on_pole[0] * pole[0], axis=0, keepdims=True)
        on_rotation = -jnp.sum(on_pole[1], axis=0, keepdims=True)
        on_decay = on_decay + swap(on_decay)
        on_rotation = on_rotation + swap(on_rotation)
        state = jnp.where(left[0:1], on_decay, on_rotation) * jnp.exp2(-state_exponent)

        grad_scale = jnp.exp2(-grad_exponent)
        on_read = (on_read[0] * grad_scale, on_read[1] * grad_scale)
        lower = jnp.where(left, on_read[0], swap(on_read[1]))
        upper = jnp.where(left, swap(on_read[0]), on_read[1])
        grads = jnp.concatenate([lower, upper], axis=0)
        step_scale = jnp.broadcast_to(jnp.exp2(-step_exponent), (pairs, LANES))
        step_columns = [
            jnp.broadcast_to(jnp.sum(value, axis=1, keepdims=True), (pairs, LANES)) * step_scale
            for value in (jnp.where(left, on_step, 0.0), jnp.where(left, 0.0, on_step))
        ]
        place_lane = lax.broadcasted_iota(jnp.int32, (SUBLANES, LANES), 1)
        scales = jnp.zeros((1, LANES), jnp.float32)
        for spot, value in zip(
            SCALE_LANES, (lag_exponent, grad_exponent, state_exponent, step_exponent)
        ):
            scales = jnp.where(place_lane[0:1] == spot, value, scales)
        state_high, state_low = two_pieces(state)
        tails = []
        for group in range(groups):
            spot = group % half * SUBLANES
            pieces = two_pieces(step_columns[group // half][spot : spot + SUBLANES])
            spread = jnp.zeros((SUBLANES, LANES), jnp.float32)
            for spot, piece in zip(STEP_LANES, pieces):
                spread = jnp.where(place_lane == row + spot, piece, spread)
            singles = scales + jnp.sum(spread, axis=0, keepdims=True)
            tails.append(jnp.concatenate([state_high, state_low, singles, singles], axis=0))
        for b in range(owners):
            for group in range(groups):
                place = (group * owners + b) * ROWS
                sent[place + GRADS : place + STATE] = grads[
                    group * SUBLANES : (group + 1) * SUBLANES
                ]
                sent[place + STATE : place + ROWS] = tails[group]

    for section in (spread_blocks, to_frequencies, to_lags, finish):
        section()


def unpack_kernel(got, kernel_grad, readout_grad, step_grad, state_grad, wide, grads):
    peers = got.shape[0] // ROWS
    per_row = LANES // SUBLANES
    singles = got[pl.ds(SINGLES, peers, stride=ROWS), :]
    exponents = [jnp.broadcast_to(singles[:, spot : spot + 1], (peers, LANES)) for spot in SCALE_LANES]
    scales = [jnp.exp2(value) for value in exponents]
    wide[...] = scales[0]
    lane = lax.broadcasted_iota(jnp.int32, (peers, LANES), 1)
    row = lax.broadcasted_iota(jnp.int32, (peers, LANES), 0)

    def by_channel(value, spot):
        mine = jnp.where(row - spot == lane // SUBLANES, value, 0.0)
        return jnp.sum(mine, axis=0, keepdims=True)

    for spot in range(0, peers, per_row):
        part = slice(spot * SUBLANES, (spot + per_row) * SUBLANES)
        for peer in range(spot, spot + per_row):
            place, own = peer * ROWS, slice(peer * SUBLANES, (peer + 1) * SUBLANES)
            grads[own] = got[place + GRADS : place + STATE]
            kernel_grad[own] = got[place + LAGS : place + GRADS] * wide[peer : peer + 1, :]
        readout_grad[:, part] = grads[part].T * by_channel(scales[1], spot)

    high = got[pl.ds(STATE, peers, stride=ROWS), :]
    low = got[pl.ds(STATE + 1, peers, stride=ROWS), :]
    total = jnp.sum((high + low * (1.0 / 256.0)) * scales[2], axis=0, keepdims=True)
    states = state_grad.shape[1]
    state_grad[0:1] = total[:, :states]
    state_grad[1:2] = total[:, states:]
    high, low = (
        jnp.take_along_axis(singles, lane % SUBLANES + first, axis=1) for first in STEP_LANES
    )
    value = (high + low * (1.0 / 256.0)) * scales[3]
    for spot in range(0, peers, per_row):
        part = slice(spot * SUBLANES, (spot + per_row) * SUBLANES)
        step_grad[part] = by_channel(value, spot).reshape(LANES)


def kernel_device(inputs, out_grad, readout, log_step, decay_log, rotation):
    owners, groups = lax.axis_size("seq"), lax.axis_size("ch")
    peers = owners * groups
    channels, length = inputs.shape
    states = decay_log.shape[0]
    part_count = channels // owners
    pairs = part_count // 2
    norm_scale = 1.0 / math.sqrt(owners * length)
    vmem = pl.BlockSpec(memory_space=pltpu.VMEM)
    memory = pltpu.CompilerParams(vmem_limit_bytes=32 * 1024 * 1024)
    f32, bf16 = jnp.float32, jnp.bfloat16

    def exchange(value):
        rows = value.shape[0] // peers
        value = value.reshape(peers, rows // 2, 2, LANES)
        value = lax.all_to_all(value, ("ch", "seq"), split_axis=0, concat_axis=0, tiled=True)
        return value.reshape(peers * rows, LANES)

    anywhere = pl.BlockSpec(memory_space=pl.ANY)
    held = [jnp.asarray(table) for table in transform_tables(owners, length, norm_scale)]
    held += [decay_log[None], rotation[None]]
    sources = (
        inputs, out_grad, readout.transpose(0, 2, 1).reshape(LANES, channels), log_step[None], *held
    )
    pieces, *held = pl.pallas_call(
        pack_kernel,
        out_shape=[jax.ShapeDtypeStruct((peers * OUT_ROWS, LANES), bf16)]
        + [jax.ShapeDtypeStruct(value.shape, value.dtype) for value in held],
        in_specs=[anywhere] * len(sources),
        out_specs=[vmem] * (1 + len(held)),
        scratch_shapes=[
            pltpu.VMEM((2, channels, LANES), bf16),
            pltpu.VMEM((LANES, channels), f32),
            pltpu.VMEM((1, channels), f32),
            pltpu.VMEM((channels, LANES), f32),
            pltpu.VMEM((peers * OUT_ROWS, LANES), f32),
            pltpu.SemaphoreType.DMA((len(sources),)),
        ],
        compiler_params=memory,
    )(*(pltpu.with_memory_space_constraint(value, pltpu.HBM) for value in sources))
    got = exchange(pieces)
    sent = pl.pallas_call(
        functools.partial(main_kernel, owners, norm_scale),
        out_shape=jax.ShapeDtypeStruct((peers * ROWS, LANES), f32),
        in_specs=[vmem] * 5,
        out_specs=vmem,
        scratch_shapes=[
            pltpu.VMEM((peers * OUT_ROWS, LANES), f32),
            pltpu.VMEM((2, (owners + 1) * 2 * part_count, 2 * LANES), bf16),
            pltpu.VMEM(((owners + 1) * 2 * part_count, 2 * LANES), f32),
            pltpu.VMEM(((owners + 1) * part_count, 2 * LANES), f32),
            pltpu.VMEM((14, pairs, LANES), f32),
            pltpu.VMEM((2 * (owners * length).bit_length(), pairs, LANES), f32),
            pltpu.VMEM((pairs, 4, owners, LANES), f32),
            pltpu.VMEM((2 * pairs * length, 2 * LANES), bf16),
            pltpu.VMEM((2 * pairs * length + 2 * (owners + 1) * part_count, 2 * LANES), bf16),
            pltpu.VMEM((owners * part_count, length), f32),
            pltpu.VMEM((4, pairs, LANES), f32),
        ],
        compiler_params=memory,
    )(got, *held)
    back = exchange(sent.astype(jnp.float16))
    kernel_grad, readout_grad, step_grad, state_grad = pl.pallas_call(
        unpack_kernel,
        out_shape=[
            jax.ShapeDtypeStruct((channels, length), f32),
            jax.ShapeDtypeStruct((LANES, channels), f32),
            jax.ShapeDtypeStruct((channels,), f32),
            jax.ShapeDtypeStruct((2, states), f32),
        ],
        in_specs=[vmem],
        out_specs=[vmem] * 4,
        scratch_shapes=[
            pltpu.VMEM((peers, LANES), f32),
            pltpu.VMEM((channels, LANES), f32),
        ],
        compiler_params=memory,
    )(back.astype(f32))
    readout_grad = readout_grad.reshape(2, states, channels).transpose(0, 2, 1)
    return kernel_grad, readout_grad, step_grad, state_grad


def kernel_fits(mesh, inputs, decay_log):
    owners, groups = mesh.shape["seq"], mesh.shape["ch"]
    channels = inputs.shape[0] // groups
    return (
        inputs.shape[1] == owners * LANES
        and 2 * decay_log.shape[0] == LANES
        and owners == SUBLANES
        and groups % 2 == 0
        and channels == owners * groups * SUBLANES
        and channels % LANES == 0
    )


def solution(mesh):
    def whole(inputs, out_grad, readout, log_step, decay_log, rotation):
        fits = kernel_fits(mesh, inputs, decay_log)
        return jax.shard_map(
            kernel_device if fits else general_device,
            mesh=mesh,
            in_specs=(P("ch", "seq"), P("ch", "seq"), P(None, "ch", None), P("ch"), P(), P()),
            out_specs=(P("ch", "seq"), P(None, "ch", None), P("ch"), P()),
            check_vma=False,
        )(inputs, out_grad, readout, log_step, decay_log, rotation)

    return whole
```

```python
import functools
import math

import jax
import jax.numpy as jnp
import numpy as np
from jax import lax
from jax.experimental import pallas as pl
from jax.experimental.pallas import tpu as pltpu
from jax.sharding import PartitionSpec as P

precise = lax.Precision.HIGHEST
two_pi = 2.0 * math.pi
LANES = 128
SUBLANES = 8


def angle_table(left_index, right_index, modulus, orient):
    product = left_index[:, None] * right_index[None, :] % modulus
    return orient * two_pi * product.astype(jnp.float32) / modulus


def rotate(real_part, imag_part, angles):
    cosine_table = jnp.cos(angles)
    sine_table = jnp.sin(angles)
    return (
        real_part * cosine_table - imag_part * sine_table,
        real_part * sine_table + imag_part * cosine_table,
    )


def last_transform(real_part, imag_part, orient):
    length = real_part.shape[-1]
    counter = jnp.arange(length, dtype=jnp.int32)
    angles = angle_table(counter, counter, length, orient)
    cosine_table = jnp.cos(angles)
    sine_table = jnp.sin(angles)
    dot = functools.partial(jnp.dot, precision=precise, preferred_element_type=jnp.float32)
    return (
        dot(real_part, cosine_table) - dot(imag_part, sine_table),
        dot(imag_part, cosine_table) + dot(real_part, sine_table),
    )


def discretize(readout, log_step, decay_log, rotation):
    step_size = jnp.exp(log_step)[:, None]
    pole_real = -jnp.exp(decay_log)[None, :]
    pole_imag = rotation[None, :]
    rate_real = step_size * pole_real
    rate_imag = step_size * pole_imag
    lift_real = jnp.expm1(rate_real) * jnp.cos(rate_imag) - 2.0 * jnp.sin(0.5 * rate_imag) ** 2
    lift_imag = jnp.exp(rate_real) * jnp.sin(rate_imag)
    pole_norm = pole_real * pole_real + pole_imag * pole_imag
    ratio_real = (lift_real * pole_real + lift_imag * pole_imag) / pole_norm
    ratio_imag = (lift_imag * pole_real - lift_real * pole_imag) / pole_norm
    coef_real = readout[0] * ratio_real - readout[1] * ratio_imag
    coef_imag = readout[0] * ratio_imag + readout[1] * ratio_real
    return (coef_real, coef_imag, rate_real, rate_imag)


def parameter_grads(primal, backward, totals):
    coef_real, coef_imag = (primal[0], primal[1])
    cotangents = (
        2.0 * totals[0],
        -2.0 * totals[1],
        2.0 * (coef_real * totals[2] - coef_imag * totals[3]),
        -2.0 * (coef_real * totals[3] + coef_imag * totals[2]),
    )
    return backward(cotangents)


def shifted_totals(raw_sums, rate_real, rate_imag, block_start, norm_scale):
    decays = jnp.exp(rate_real * block_start)
    phases = rate_imag * block_start
    base_real = decays * jnp.cos(phases)
    base_imag = decays * jnp.sin(phases)
    near_real = block_start * raw_sums[0] + raw_sums[2]
    near_imag = block_start * raw_sums[1] + raw_sums[3]
    return jnp.stack(
        [
            norm_scale * (base_real * raw_sums[0] - base_imag * raw_sums[1]),
            norm_scale * (base_real * raw_sums[1] + base_imag * raw_sums[0]),
            norm_scale * (base_real * near_real - base_imag * near_imag),
            norm_scale * (base_real * near_imag + base_imag * near_real),
        ]
    )


def whole_channel_totals(lag_rows, rate_real, rate_imag, norm_scale):
    owners, length = (lag_rows.shape[1], lag_rows.shape[2])
    offsets = jnp.arange(length, dtype=jnp.int32).astype(jnp.float32)
    decays = jnp.exp(rate_real[:, :, None] * offsets)
    phases = rate_imag[:, :, None] * offsets
    power_real = decays * jnp.cos(phases)
    power_imag = decays * jnp.sin(phases)
    weighted = lag_rows * offsets
    raw_sums = jnp.stack(
        [
            jnp.einsum("cbj,cnj->cnb", lag_rows, power_real, precision=precise),
            jnp.einsum("cbj,cnj->cnb", lag_rows, power_imag, precision=precise),
            jnp.einsum("cbj,cnj->cnb", weighted, power_real, precision=precise),
            jnp.einsum("cbj,cnj->cnb", weighted, power_imag, precision=precise),
        ]
    )
    starts = (jnp.arange(owners, dtype=jnp.int32) * length).astype(jnp.float32)
    totals = shifted_totals(
        raw_sums, rate_real[:, :, None], rate_imag[:, :, None], starts, norm_scale
    )
    return jnp.sum(totals, axis=-1)


def general_lags(whole, norm_scale):
    part_count, owners, length = whole.shape[1:]
    freq_width = 2 * owners
    modulus = freq_width * length
    row_index = jnp.arange(owners, dtype=jnp.int32)
    outer_index = jnp.arange(freq_width, dtype=jnp.int32)
    inner_index = jnp.arange(length, dtype=jnp.int32)
    first = angle_table(row_index, outer_index, freq_width, -1.0)
    spec_real = jnp.einsum("scba,bk->scka", whole, jnp.cos(first), precision=precise)
    spec_imag = jnp.einsum("scba,bk->scka", whole, jnp.sin(first), precision=precise)
    spec_real, spec_imag = rotate(
        spec_real, spec_imag, angle_table(outer_index, inner_index, modulus, -1.0)
    )
    freq_real, freq_imag = last_transform(spec_real, spec_imag, -1.0)
    prod_real = freq_real[1] * freq_real[0] + freq_imag[1] * freq_imag[0]
    prod_imag = freq_imag[1] * freq_real[0] - freq_real[1] * freq_imag[0]
    back_real, back_imag = last_transform(prod_real, prod_imag, 1.0)
    back_real, back_imag = rotate(
        back_real, back_imag, angle_table(outer_index, inner_index, modulus, 1.0)
    )
    final = angle_table(outer_index, row_index, freq_width, 1.0)
    lag_rows = jnp.einsum("cka,kb->cba", back_real, jnp.cos(final), precision=precise) - jnp.einsum(
        "cka,kb->cba", back_imag, jnp.sin(final), precision=precise
    )
    return lag_rows * (norm_scale / modulus)


def general_device(inputs, out_grad, readout, log_step, decay_log, rotation):
    owners = lax.axis_size("seq")
    channels, length = inputs.shape
    states = decay_log.shape[0]
    part_count = channels // owners
    norm_scale = 1.0 / math.sqrt(owners * length)
    pieces = jnp.concatenate(
        [a.reshape(owners, part_count, length) for a in (inputs, out_grad)], axis=1
    )
    pieces = lax.all_to_all(pieces, "seq", split_axis=0, concat_axis=0, tiled=True)
    whole = pieces.astype(jnp.float32).reshape(owners, 2, part_count, length)
    lag_rows = general_lags(whole.transpose(1, 2, 0, 3), norm_scale)
    first_channel = lax.axis_index("seq") * part_count
    own_readout = lax.dynamic_slice_in_dim(readout, first_channel, part_count, 1)
    own_step = lax.dynamic_slice_in_dim(log_step, first_channel, part_count, 0)
    primal, backward = jax.vjp(discretize, own_readout, own_step, decay_log, rotation)
    totals = whole_channel_totals(lag_rows, primal[2], primal[3], norm_scale)
    readout_part, step_part, decay_part, rotation_part = parameter_grads(primal, backward, totals)
    shared = jnp.concatenate(
        [readout_part.reshape(-1), step_part, decay_part, rotation_part]
    )
    sent = jnp.concatenate(
        [
            lag_rows.transpose(1, 0, 2).reshape(owners, -1),
            jnp.broadcast_to(shared, (owners, shared.shape[0])),
        ],
        axis=1,
    )
    got = lax.all_to_all(sent, "seq", split_axis=0, concat_axis=0, tiled=True)
    cuts = np.cumsum([part_count * length, 2 * part_count * states, part_count])
    lags, readouts, steps, state = jnp.split(got, cuts, axis=1)
    readouts = readouts.reshape(owners, 2, part_count, states).transpose(1, 0, 2, 3)
    return (
        lags.reshape(channels, length),
        readouts.reshape(2, channels, states),
        steps.reshape(channels),
        lax.psum(jnp.sum(state, axis=0), "ch").reshape(2, states),
    )


def split_halves(value):
    high = value.astype(jnp.bfloat16)
    return high, (value - high.astype(jnp.float32)).astype(jnp.bfloat16)


def cos_sin(angle):
    turns = jnp.floor(angle * (2.0 / math.pi) + 0.5)
    rest = angle - turns * 1.5703125
    rest = rest - turns * 4.837512969970703125e-4
    rest = rest - turns * 7.54978995489188216e-8
    quarter = turns.astype(jnp.int32)
    square = rest * rest
    sine = rest + rest * square * (
        -1.6666654611e-1 + square * (8.3321608736e-3 - square * 1.9515295891e-4)
    )
    cosine = (
        1.0
        - 0.5 * square
        + square
        * square
        * (
            4.166664568298827e-2
            + square * (-1.388731625493765e-3 + square * 2.443315711809948e-5)
        )
    )
    odd = (quarter & 1) == 1
    out_cos = jnp.where(odd, sine, cosine)
    out_sin = jnp.where(odd, cosine, sine)
    out_cos = jnp.where(((quarter + 1) & 2) == 2, -out_cos, out_cos)
    out_sin = jnp.where((quarter & 2) == 2, -out_sin, out_sin)
    return out_cos, out_sin


def grow(value):
    series = 1.0
    for term in range(9, 1, -1):
        series = 1.0 + series * value * (1.0 / term)
    return jnp.where(jnp.abs(value) < 0.35, series * value, jnp.exp(value) - 1.0)


def power(rate_real, rate_imag, offset):
    size = jnp.exp(rate_real * offset)
    cosine, sine = cos_sin(rate_imag * offset)
    return size * cosine, size * sine


def times(left, right):
    return (
        left[0] * right[0] - left[1] * right[1],
        left[0] * right[1] + left[1] * right[0],
    )


def blocks_forward(x):
    root = math.sqrt(0.5)
    cosine, sine = math.cos(math.pi / 8), math.sin(math.pi / 8)
    total = [x[s] + x[s + 4] for s in range(4)]
    gap = [x[s] - x[s + 4] for s in range(4)]
    even, odd = total[0] + total[2], total[1] + total[3]
    real, imag = [None] * 9, [None] * 9
    real[0], real[8] = even + odd, even - odd
    imag[0] = imag[8] = jnp.zeros_like(even)
    real[4], imag[4] = total[0] - total[2], total[3] - total[1]
    less, more = root * (gap[1] - gap[3]), root * (gap[1] + gap[3])
    real[2], imag[2] = gap[0] + less, -gap[2] - more
    real[6], imag[6] = gap[0] - less, gap[2] - more
    less, more = root * (x[2] - x[6]), root * (x[2] + x[6])
    even1 = (x[0] + less, -x[4] - more)
    even3 = (x[0] - less, x[4] - more)
    p, q, r, t = x[1] - x[7], x[3] - x[5], x[1] + x[7], x[3] + x[5]
    odd1 = (cosine * p + sine * q, -sine * r - cosine * t)
    odd3 = (sine * p - cosine * q, sine * t - cosine * r)
    real[1], imag[1] = even1[0] + odd1[0], even1[1] + odd1[1]
    real[7], imag[7] = even1[0] - odd1[0], odd1[1] - even1[1]
    real[3], imag[3] = even3[0] + odd3[0], even3[1] + odd3[1]
    real[5], imag[5] = even3[0] - odd3[0], odd3[1] - even3[1]
    return list(zip(real, imag))


def blocks_back(z):
    root = math.sqrt(0.5)
    cosine, sine = math.cos(math.pi / 8), math.sin(math.pi / 8)
    real, imag = [v[0] for v in z], [v[1] for v in z]
    even, odd = real[0] + real[8], real[0] - real[8]
    total = [even + real[4], odd + imag[4], even - real[4], odd - imag[4]]
    less, more = root * (real[2] - real[6]), root * (imag[2] + imag[6])
    gap = [real[2] + real[6], less + more, imag[2] - imag[6], more - less]
    x = [total[s] + gap[s] for s in range(4)] + [total[s] - gap[s] for s in range(4)]
    even1 = (real[1] + real[7], imag[7] - imag[1])
    even3 = (real[3] + real[5], imag[5] - imag[3])
    odd1 = (real[1] - real[7], imag[1] + imag[7])
    odd3 = (real[3] - real[5], imag[3] + imag[5])
    less, more = root * (even1[0] - even3[0]), root * (even1[1] + even3[1])
    p = cosine * odd1[0] + sine * odd3[0]
    q = sine * odd1[0] - cosine * odd3[0]
    r = sine * odd1[1] + cosine * odd3[1]
    t = cosine * odd1[1] - sine * odd3[1]
    extra = [
        even1[0] + even3[0],
        p + r,
        less - more,
        q + t,
        even3[1] - even1[1],
        t - q,
        -less - more,
        r - p,
    ]
    return [v + w for v, w in zip(x, extra)]


def transform_tables(owners, length, norm_scale):
    width = 2 * owners
    counter = np.arange(length)
    angles = two_pi * (counter[:, None] * counter[None, :] % length) / length
    cosine, sine = np.cos(angles), np.sin(angles)
    matrix = np.block([[cosine, -sine], [sine, cosine]]).astype(np.float32)
    high = matrix.astype(jnp.bfloat16)
    low = (matrix - high.astype(np.float32)).astype(jnp.bfloat16)
    outer = np.arange(owners + 1)
    angles = two_pi * (outer[:, None] * counter[None, :]) / (width * length)
    twiddle = np.stack([np.cos(angles), -np.sin(angles)], axis=1)
    weight = np.where(outer % owners == 0, 1.0, 2.0) * norm_scale / (width * length)
    twiddle = np.concatenate([twiddle, twiddle * weight[:, None, None]], axis=1)
    return np.stack([high, low]), twiddle.astype(np.float32)


def three_pieces(value):
    pieces = []
    for _ in range(3):
        piece = value.astype(jnp.bfloat16).astype(jnp.float32)
        pieces.append(piece)
        value = value - piece
    return pieces


def swap(value):
    return pltpu.roll(value, LANES // 2, 1)


def rest_lanes(lane):
    return lane < 3, (lane >= LANES // 2) & (lane < LANES // 2 + 3)


def rest_steps(value):
    high = value.astype(jnp.bfloat16).astype(jnp.float32)
    steps = jnp.where(high == 0.0, 0.0, (value - high) / jnp.where(high == 0.0, 1.0, high))
    return jnp.floor(steps * (256.0 * REST_STEPS) + 0.5)


def unpack_rests(high, rest):
    lane = lax.broadcasted_iota(jnp.int32, high.shape, 1)
    shared, replaced = rest_lanes(lane)
    step = sum(rest[:, LANES // 2 + i : LANES // 2 + i + 1] for i in range(3))
    both = jnp.where(shared, rest, swap(rest))
    first = jnp.floor(both * (1.0 / (2.0 * REST_STEPS + 1.0)) + 0.5)
    second = both - first * (2.0 * REST_STEPS + 1.0)
    steps = jnp.where(shared, first, second) * (1.0 / (256.0 * REST_STEPS))
    return jnp.where(shared | replaced, high * steps, rest), jnp.broadcast_to(step, high.shape)


def transposed(value):
    return jnp.concatenate(
        [value[:, spot : spot + LANES].T for spot in range(0, value.shape[1], LANES)], axis=0
    )


READ, REST, OUT_ROWS = 16, 17, 18
REST_STEPS = 7.0
ROWS = 20
LAGS, GRADS, STATE, SINGLES = 0, 8, 16, 18
STEP_LANES, SCALE_LANES = (0, 8), (16, 17, 18, 19)
SPARE = 15.0
PARTS = 4
EARLY = 9
FRESH = 5


def pack_kernel(inputs, out_grad, readout, log_step, *refs):
    count = (len(refs) - 7) // 2
    sources, (out, *held) = refs[:count], refs[count : 2 * count + 1]
    signals, read, step, turned, rows, sems = refs[2 * count + 1 :]
    peers = out.shape[0] // OUT_ROWS
    copies = [
        pltpu.make_async_copy(source, target, sems.at[i])
        for i, (source, target) in enumerate(
            (
                (readout, read),
                (log_step, step),
                (inputs, signals.at[0]),
                (out_grad, signals.at[1]),
                *zip(sources, held),
            )
        )
    ]
    for copy in copies:
        copy.start()
    for copy in copies[:4]:
        copy.wait()
    own = lax.axis_index("seq")
    turned[...] = transposed(read[...])
    channels = step.shape[1]
    peer = lax.broadcasted_iota(jnp.int32, (peers, channels), 0)
    channel = lax.broadcasted_iota(jnp.int32, (peers, channels), 1)
    sent_channel = channel == peer * SUBLANES + own

    def pick(row):
        value = jnp.sum(jnp.where(sent_channel, row, 0.0), axis=1, keepdims=True)
        return jnp.broadcast_to(value, (peers, LANES))

    half = LANES // 2
    shared = rest_steps(read[0:SUBLANES]) * (2.0 * REST_STEPS + 1.0)
    shared = shared + rest_steps(read[half : half + SUBLANES])
    pieces = three_pieces(pick(step[...]))
    placed = [(i, pick(shared[i : i + 1])) for i in range(3)]
    placed += [(half + i, piece) for i, piece in enumerate(pieces)]
    for place, signal in enumerate((signals[0], signals[1])):
        value = signal.astype(jnp.float32)
        for peer in range(peers):
            spot = peer * OUT_ROWS + place * SUBLANES
            rows[spot : spot + SUBLANES] = value[peer * SUBLANES : (peer + 1) * SUBLANES]
    value = turned[pl.ds(own, peers, stride=SUBLANES), :]
    high = value.astype(jnp.bfloat16).astype(jnp.float32)
    rows[pl.ds(READ, peers, stride=OUT_ROWS), :] = high
    rest = value - high
    lane = lax.broadcasted_iota(jnp.int32, (peers, LANES), 1)
    for place, other in placed:
        rest = jnp.where(lane == place, other, rest)
    rows[pl.ds(REST, peers, stride=OUT_ROWS), :] = rest
    out[...] = rows[...].astype(jnp.bfloat16)
    for copy in copies[4:]:
        copy.wait()


def exponent_of(bound):
    return jnp.floor(jnp.log(jnp.maximum(bound, 1e-30)) * (1.0 / math.log(2.0))) + (2.0 - SPARE)


def greatest(value):
    return jnp.max(jnp.max(value, axis=1, keepdims=True), axis=0, keepdims=True)


def size_of(value):
    return jnp.abs(value[0]) + jnp.abs(value[1])


def two_pieces(value):
    high = value.astype(jnp.bfloat16).astype(jnp.float32)
    return high, (value - high) * 256.0


def main_kernel(
    owners,
    norm_scale,
    got,
    matrix,
    twiddle,
    decay_log,
    rotation,
    sent,
    rows_in,
    spectra,
    freq,
    back,
    params,
    doubled,
    bases,
    powers,
    early_powers,
    lags,
    sums,
):
    peers, length = got.shape[0] // OUT_ROWS, got.shape[1]
    groups = peers // owners
    part_count = groups * SUBLANES
    rows = 2 * part_count
    pairs = part_count // 2
    half = pairs // SUBLANES
    reach = length // 2
    lane = lax.broadcasted_iota(jnp.int32, (pairs, LANES), 1)
    left = lane < LANES // 2
    row = lax.broadcasted_iota(jnp.int32, (SUBLANES, LANES), 0)

    def lanes_of(side):
        return slice(side * LANES, (side + 1) * LANES)

    def collect(spot):
        tiles = [
            rows_in[pl.ds(group * owners * OUT_ROWS + spot, owners, stride=OUT_ROWS), :]
            for group in range(groups)
        ]
        return jnp.concatenate(tiles[:half], axis=0), jnp.concatenate(tiles[half:], axis=0)

    def make_params():
        sides = []
        for high, rest in zip(collect(READ), collect(REST)):
            rest, step = unpack_rests(high, rest)
            sides.append((high + rest, step))
        (lower, lower_step), (upper, upper_step) = sides
        read = (jnp.where(left, lower, swap(upper)), jnp.where(left, swap(lower), upper))
        step = jnp.exp(jnp.where(left, lower_step, upper_step))
        decay_row = jnp.concatenate([decay_log[...], decay_log[...]], axis=1)
        rotation_row = jnp.concatenate([rotation[...], rotation[...]], axis=1)
        pole = (
            jnp.broadcast_to(-jnp.exp(decay_row), step.shape),
            jnp.broadcast_to(rotation_row, step.shape),
        )
        rate = (step * pole[0], step * pole[1])
        place, size = 0, 1
        while size < owners * length:
            if place // 2 % FRESH == 0:
                value = power(rate[0], rate[1], float(size))
            else:
                value = (value[0] * value[0] - value[1] * value[1], 2.0 * value[0] * value[1])
            doubled[place], doubled[place + 1] = value
            place, size = place + 2, size * 2
        sine = cos_sin(0.5 * rate[1])[1]
        cosine = 1.0 - 2.0 * sine * sine
        lift = (grow(rate[0]) * cosine - 2.0 * sine * sine, doubled[1])
        norm = 1.0 / (pole[0] * pole[0] + pole[1] * pole[1])
        inverse = (pole[0] * norm, -pole[1] * norm)
        ratio = times(lift, inverse)
        coef = times(read, ratio)
        lifted = times((doubled[0], doubled[1]), inverse)
        values = (rate, ratio, coef, times(read, lifted), pole, times(coef, inverse), (step, step))
        for place, value in enumerate(values):
            params[2 * place], params[2 * place + 1] = value

    early = min(EARLY, pairs)
    products = 4 * early * reach
    nothing = twiddle[0, 1, 0].astype(jnp.int32) * (2 * SUBLANES)
    block_bit, reach_bit = length.bit_length() - 1, reach.bit_length() - 1
    bits = [(row & (1 << i)) != 0 for i in range(SUBLANES.bit_length() - 1)]

    def doubled_row(p, i):
        return doubled[2 * i, p : p + 1, :], doubled[2 * i + 1, p : p + 1, :]

    def by_rows(p, first):
        out = None
        for i, bit in enumerate(bits):
            real, imag = doubled_row(p, first + i)
            value = (jnp.where(bit, real, 1.0), jnp.where(bit, imag, 0.0))
            out = value if out is None else times(out, value)
        return out

    def make_tables():
        for p in range(pairs):
            table = [by_rows(p, 0)]
            for i in range(len(bits), reach_bit):
                table += [times(block, doubled_row(p, i)) for block in table]
            for place in range(0, len(table), 2):
                for side in range(2):
                    value = jnp.concatenate([table[place][side], table[place + 1][side]], axis=0)
                    for i, piece in enumerate(split_halves(value)):
                        for spot in (2 * i * reach, (2 * i + 1) * reach):
                            spot += p * 4 * reach + place * SUBLANES
                            if p < early:
                                rows_at = pl.multiple_of(nothing + spot, 2 * SUBLANES)
                                early_powers[pl.ds(rows_at, 2 * SUBLANES), lanes_of(side)] = piece
                            else:
                                powers[spot : spot + 2 * SUBLANES, lanes_of(side)] = piece
            base = by_rows(p, block_bit)
            bases[p, 0], bases[p, 1] = base
            bases[p, 2], bases[p, 3] = times(base, doubled_row(p, reach_bit))

    def transform(pieces, target, count):
        dot = functools.partial(jnp.dot, preferred_element_type=jnp.float32)
        cuts = [(owners + 1) * i // PARTS * count for i in range(PARTS + 1)]
        for part in map(slice, cuts, cuts[1:]):
            high, low = pieces(part)
            target[part] = dot(high, matrix[0]) + dot(low, matrix[0]) + dot(high, matrix[1])

    def spread_blocks():
        rows_in[...] = got[...].astype(jnp.float32)
        blocks = []
        for s in range(owners):
            spots = [(group * owners + s) * OUT_ROWS for group in range(groups)]
            blocks.append(
                jnp.concatenate(
                    [rows_in[spot : spot + SUBLANES] for spot in spots]
                    + [rows_in[spot + SUBLANES : spot + 2 * SUBLANES] for spot in spots],
                    axis=0,
                )
            )
        for k, value in enumerate(blocks_forward(blocks)):
            if k:
                value = times(value, (twiddle[k, 0:1], twiddle[k, 1:2]))
            for side in range(2):
                for i, piece in enumerate(split_halves(value[side])):
                    spectra[i, k * rows : (k + 1) * rows, lanes_of(side)] = piece

    def to_frequencies():
        transform(lambda part: (spectra[0, part], spectra[1, part]), freq, rows)
        make_params()
        make_tables()

    def to_lags():
        for k in range(owners + 1):
            at_in = freq[k * rows : k * rows + part_count]
            at_out = freq[k * rows + part_count : (k + 1) * rows]
            ur, ui = at_in[:, :length], at_in[:, length:]
            gr, gi = at_out[:, :length], at_out[:, length:]
            for side, value in enumerate((gr * ur + gi * ui, gr * ui - gi * ur)):
                for i, piece in enumerate(split_halves(value)):
                    spot = products + (i * (owners + 1) + k) * part_count
                    early_powers[spot : spot + part_count, lanes_of(side)] = piece

        def pieces(part):
            low = products + (owners + 1) * part_count
            return tuple(
                early_powers[first + part.start : first + part.stop] for first in (products, low)
            )

        transform(pieces, back, part_count)

    def finish():
        turned = []
        for k in range(owners + 1):
            spots = slice(k * part_count, (k + 1) * part_count)
            value = (back[spots, lanes_of(0)], back[spots, lanes_of(1)])
            turned.append(times(value, (twiddle[k, 2:3], twiddle[k, 3:4])))
        blocks = blocks_back(turned)

        most = jnp.zeros((part_count, LANES), jnp.float32)
        for b, block in enumerate(blocks):
            most = jnp.maximum(most, jnp.abs(block))

        for group in range(groups):
            spots = slice(group * SUBLANES, (group + 1) * SUBLANES)
            tiles = jnp.stack([block[spots] for block in blocks])
            lags[group * owners * SUBLANES : (group + 1) * owners * SUBLANES] = jnp.swapaxes(
                tiles, 0, 1
            ).reshape(owners * SUBLANES, length)

        def param(place):
            return params[2 * place], params[2 * place + 1]

        rate, ratio, coef, through, pole, direct, (step, _) = (param(i) for i in range(7))
        most = greatest(most)
        whole = 2.0 * math.sqrt(owners * length)
        on_rate = size_of(coef) * float(owners * length) + size_of(through)
        on_pole = step * on_rate + size_of(direct)
        lag_exponent = exponent_of(most)
        grad_exponent = exponent_of(most * (whole * greatest(size_of(ratio))))
        state_exponent = exponent_of(
            most * (whole * part_count * greatest(on_pole * (1.0 - pole[0])))
        )
        step_exponent = exponent_of(
            most * (whole * (LANES // 2) * greatest(on_rate * size_of(rate)))
        )
        lag_scale = jnp.exp2(-lag_exponent)
        for b, block in enumerate(blocks):
            for group in range(groups):
                place = (group * owners + b) * ROWS
                value = block[group * SUBLANES : (group + 1) * SUBLANES]
                sent[place + LAGS : place + GRADS] = value * lag_scale

        start = row.astype(jnp.float32) * float(length)
        first = left[:owners]
        wide = lax.broadcasted_iota(jnp.int32, (4 * owners, LANES), 1)
        wide_left = wide < reach
        offset = jnp.where(wide_left, wide, wide - reach).astype(jnp.float32)
        both_left = wide_left[: 2 * owners]
        for p in range(pairs):
            both = jnp.concatenate(
                [
                    lags[channel * owners : (channel + 1) * owners]
                    for channel in (p, pairs + p)
                ],
                axis=0,
            )
            swapped = swap(both)
            plain = jnp.concatenate(
                [jnp.where(both_left, both, swapped), jnp.where(both_left, swapped, both)], axis=0
            )
            factor = []
            for value in (plain, plain * offset):
                high = value.astype(jnp.bfloat16).astype(jnp.float32)
                factor.append(jnp.where(wide_left, high, value - high))
            factor = jnp.concatenate(factor, axis=0).astype(jnp.bfloat16)
            raw = jnp.dot(
                jnp.concatenate([factor, factor], axis=1),
                (early_powers if p < early else powers)[p * 4 * reach : (p + 1) * 4 * reach],
                preferred_element_type=jnp.float32,
            )

            def pick(place, side):
                top = raw[2 * place * owners : (2 * place + 1) * owners, lanes_of(side)]
                bottom = raw[(2 * place + 1) * owners : (2 * place + 2) * owners, lanes_of(side)]
                return jnp.where(first, top, bottom)

            found = None
            for part in range(2):
                base = (bases[p, 2 * part], bases[p, 2 * part + 1])
                near = start + float(part * reach)
                value = (pick(part, 0), pick(part, 1))
                lagged = (near * value[0] + pick(2 + part, 0), near * value[1] + pick(2 + part, 1))
                terms = times(base, value) + times(base, lagged)
                found = terms if found is None else [x + y for x, y in zip(found, terms)]
            for place, value in enumerate(found):
                sums[place, p : p + 1] = jnp.sum(value, axis=0, keepdims=True)

        total = (sums[0] * (2.0 * norm_scale), sums[1] * (2.0 * norm_scale))
        lag_total = (sums[2] * (2.0 * norm_scale), sums[3] * (2.0 * norm_scale))
        on_read = times(total, ratio)
        on_read = (on_read[0], -on_read[1])
        on_rate = times(coef, lag_total)
        more = times(total, through)
        on_rate = (on_rate[0] + more[0], on_rate[1] + more[1])
        less = times(total, direct)
        on_pole = (step * on_rate[0] - less[0], step * on_rate[1] - less[1])
        on_step = times(on_rate, rate)[0]
        on_decay = jnp.sum(on_pole[0] * pole[0], axis=0, keepdims=True)
        on_rotation = -jnp.sum(on_pole[1], axis=0, keepdims=True)
        on_decay = on_decay + swap(on_decay)
        on_rotation = on_rotation + swap(on_rotation)
        state = jnp.where(left[0:1], on_decay, on_rotation) * jnp.exp2(-state_exponent)

        grad_scale = jnp.exp2(-grad_exponent)
        on_read = (on_read[0] * grad_scale, on_read[1] * grad_scale)
        lower = jnp.where(left, on_read[0], swap(on_read[1]))
        upper = jnp.where(left, swap(on_read[0]), on_read[1])
        grads = jnp.concatenate([lower, upper], axis=0)
        step_scale = jnp.broadcast_to(jnp.exp2(-step_exponent), (pairs, LANES))
        step_columns = [
            jnp.broadcast_to(jnp.sum(value, axis=1, keepdims=True), (pairs, LANES)) * step_scale
            for value in (jnp.where(left, on_step, 0.0), jnp.where(left, 0.0, on_step))
        ]
        place_lane = lax.broadcasted_iota(jnp.int32, (SUBLANES, LANES), 1)
        scales = jnp.zeros((1, LANES), jnp.float32)
        for spot, value in zip(
            SCALE_LANES, (lag_exponent, grad_exponent, state_exponent, step_exponent)
        ):
            scales = jnp.where(place_lane[0:1] == spot, value, scales)
        state_high, state_low = two_pieces(state)
        tails = []
        for group in range(groups):
            spot = group % half * SUBLANES
            pieces = two_pieces(step_columns[group // half][spot : spot + SUBLANES])
            spread = jnp.zeros((SUBLANES, LANES), jnp.float32)
            for spot, piece in zip(STEP_LANES, pieces):
                spread = jnp.where(place_lane == row + spot, piece, spread)
            singles = scales + jnp.sum(spread, axis=0, keepdims=True)
            tails.append(jnp.concatenate([state_high, state_low, singles, singles], axis=0))
        for b in range(owners):
            for group in range(groups):
                place = (group * owners + b) * ROWS
                sent[place + GRADS : place + STATE] = grads[
                    group * SUBLANES : (group + 1) * SUBLANES
                ]
                sent[place + STATE : place + ROWS] = tails[group]

    for section in (spread_blocks, to_frequencies, to_lags, finish):
        section()


def unpack_kernel(got, kernel_grad, readout_grad, step_grad, state_grad, wide, grads):
    peers = got.shape[0] // ROWS
    per_row = LANES // SUBLANES
    singles = got[pl.ds(SINGLES, peers, stride=ROWS), :]
    exponents = [jnp.broadcast_to(singles[:, spot : spot + 1], (peers, LANES)) for spot in SCALE_LANES]
    scales = [jnp.exp2(value) for value in exponents]
    wide[...] = scales[0]
    lane = lax.broadcasted_iota(jnp.int32, (peers, LANES), 1)
    row = lax.broadcasted_iota(jnp.int32, (peers, LANES), 0)

    def by_channel(value, spot):
        mine = jnp.where(row - spot == lane // SUBLANES, value, 0.0)
        return jnp.sum(mine, axis=0, keepdims=True)

    for spot in range(0, peers, per_row):
        part = slice(spot * SUBLANES, (spot + per_row) * SUBLANES)
        for peer in range(spot, spot + per_row):
            place, own = peer * ROWS, slice(peer * SUBLANES, (peer + 1) * SUBLANES)
            grads[own] = got[place + GRADS : place + STATE]
            kernel_grad[own] = got[place + LAGS : place + GRADS] * wide[peer : peer + 1, :]
        readout_grad[:, part] = grads[part].T * by_channel(scales[1], spot)

    high = got[pl.ds(STATE, peers, stride=ROWS), :]
    low = got[pl.ds(STATE + 1, peers, stride=ROWS), :]
    total = jnp.sum((high + low * (1.0 / 256.0)) * scales[2], axis=0, keepdims=True)
    states = state_grad.shape[1]
    state_grad[0:1] = total[:, :states]
    state_grad[1:2] = total[:, states:]
    high, low = (
        jnp.take_along_axis(singles, lane % SUBLANES + first, axis=1) for first in STEP_LANES
    )
    value = (high + low * (1.0 / 256.0)) * scales[3]
    for spot in range(0, peers, per_row):
        part = slice(spot * SUBLANES, (spot + per_row) * SUBLANES)
        step_grad[part] = by_channel(value, spot).reshape(LANES)


def kernel_device(inputs, out_grad, readout, log_step, decay_log, rotation):
    owners, groups = lax.axis_size("seq"), lax.axis_size("ch")
    peers = owners * groups
    channels, length = inputs.shape
    states = decay_log.shape[0]
    part_count = channels // owners
    pairs = part_count // 2
    norm_scale = 1.0 / math.sqrt(owners * length)
    vmem = pl.BlockSpec(memory_space=pltpu.VMEM)
    memory = pltpu.CompilerParams(vmem_limit_bytes=32 * 1024 * 1024)
    f32, bf16 = jnp.float32, jnp.bfloat16

    def exchange(value):
        rows = value.shape[0] // peers
        value = value.reshape(peers, rows // 2, 2, LANES)
        value = lax.all_to_all(value, ("ch", "seq"), split_axis=0, concat_axis=0, tiled=True)
        return value.reshape(peers * rows, LANES)

    anywhere = pl.BlockSpec(memory_space=pl.ANY)
    held = [jnp.asarray(table) for table in transform_tables(owners, length, norm_scale)]
    held += [decay_log[None], rotation[None]]
    sources = (
        inputs, out_grad, readout.transpose(0, 2, 1).reshape(LANES, channels), log_step[None], *held
    )
    pieces, *held = pl.pallas_call(
        pack_kernel,
        out_shape=[jax.ShapeDtypeStruct((peers * OUT_ROWS, LANES), bf16)]
        + [jax.ShapeDtypeStruct(value.shape, value.dtype) for value in held],
        in_specs=[anywhere] * len(sources),
        out_specs=[vmem] * (1 + len(held)),
        scratch_shapes=[
            pltpu.VMEM((2, channels, LANES), bf16),
            pltpu.VMEM((LANES, channels), f32),
            pltpu.VMEM((1, channels), f32),
            pltpu.VMEM((channels, LANES), f32),
            pltpu.VMEM((peers * OUT_ROWS, LANES), f32),
            pltpu.SemaphoreType.DMA((len(sources),)),
        ],
        compiler_params=memory,
    )(*(pltpu.with_memory_space_constraint(value, pltpu.HBM) for value in sources))
    got = exchange(pieces)
    sent = pl.pallas_call(
        functools.partial(main_kernel, owners, norm_scale),
        out_shape=jax.ShapeDtypeStruct((peers * ROWS, LANES), f32),
        in_specs=[vmem] * 5,
        out_specs=vmem,
        scratch_shapes=[
            pltpu.VMEM((peers * OUT_ROWS, LANES), f32),
            pltpu.VMEM((2, (owners + 1) * 2 * part_count, 2 * LANES), bf16),
            pltpu.VMEM(((owners + 1) * 2 * part_count, 2 * LANES), f32),
            pltpu.VMEM(((owners + 1) * part_count, 2 * LANES), f32),
            pltpu.VMEM((14, pairs, LANES), f32),
            pltpu.VMEM((2 * (owners * length).bit_length(), pairs, LANES), f32),
            pltpu.VMEM((pairs, 4, owners, LANES), f32),
            pltpu.VMEM((2 * pairs * length, 2 * LANES), bf16),
            pltpu.VMEM((2 * pairs * length + 2 * (owners + 1) * part_count, 2 * LANES), bf16),
            pltpu.VMEM((owners * part_count, length), f32),
            pltpu.VMEM((4, pairs, LANES), f32),
        ],
        compiler_params=memory,
    )(got, *held)
    back = exchange(sent.astype(jnp.float16))
    kernel_grad, readout_grad, step_grad, state_grad = pl.pallas_call(
        unpack_kernel,
        out_shape=[
            jax.ShapeDtypeStruct((channels, length), f32),
            jax.ShapeDtypeStruct((LANES, channels), f32),
            jax.ShapeDtypeStruct((channels,), f32),
            jax.ShapeDtypeStruct((2, states), f32),
        ],
        in_specs=[vmem],
        out_specs=[vmem] * 4,
        scratch_shapes=[
            pltpu.VMEM((peers, LANES), f32),
            pltpu.VMEM((channels, LANES), f32),
        ],
        compiler_params=memory,
    )(back.astype(f32))
    readout_grad = readout_grad.reshape(2, states, channels).transpose(0, 2, 1)
    return kernel_grad, readout_grad, step_grad, state_grad


def kernel_fits(mesh, inputs, decay_log):
    owners, groups = mesh.shape["seq"], mesh.shape["ch"]
    channels = inputs.shape[0] // groups
    return (
        inputs.shape[1] == owners * LANES
        and 2 * decay_log.shape[0] == LANES
        and owners == SUBLANES
        and groups % 2 == 0
        and channels == owners * groups * SUBLANES
        and channels % LANES == 0
    )


def solution(mesh):
    def whole(inputs, out_grad, readout, log_step, decay_log, rotation):
        fits = kernel_fits(mesh, inputs, decay_log)
        return jax.shard_map(
            kernel_device if fits else general_device,
            mesh=mesh,
            in_specs=(P("ch", "seq"), P("ch", "seq"), P(None, "ch", None), P("ch"), P(), P()),
            out_specs=(P("ch", "seq"), P(None, "ch", None), P("ch"), P()),
            check_vma=False,
        )(inputs, out_grad, readout, log_step, decay_log, rotation)

    return whole
```

```python
import functools
import math

import jax
import jax.numpy as jnp
import numpy as np
from jax import lax
from jax.experimental import pallas as pl
from jax.experimental.pallas import tpu as pltpu
from jax.sharding import PartitionSpec as P

precise = lax.Precision.HIGHEST
two_pi = 2.0 * math.pi
LANES = 128
SUBLANES = 8


def angle_table(left_index, right_index, modulus, orient):
    product = left_index[:, None] * right_index[None, :] % modulus
    return orient * two_pi * product.astype(jnp.float32) / modulus


def rotate(real_part, imag_part, angles):
    cosine_table = jnp.cos(angles)
    sine_table = jnp.sin(angles)
    return (
        real_part * cosine_table - imag_part * sine_table,
        real_part * sine_table + imag_part * cosine_table,
    )


def last_transform(real_part, imag_part, orient):
    length = real_part.shape[-1]
    counter = jnp.arange(length, dtype=jnp.int32)
    angles = angle_table(counter, counter, length, orient)
    cosine_table = jnp.cos(angles)
    sine_table = jnp.sin(angles)
    dot = functools.partial(jnp.dot, precision=precise, preferred_element_type=jnp.float32)
    return (
        dot(real_part, cosine_table) - dot(imag_part, sine_table),
        dot(imag_part, cosine_table) + dot(real_part, sine_table),
    )


def discretize(readout, log_step, decay_log, rotation):
    step_size = jnp.exp(log_step)[:, None]
    pole_real = -jnp.exp(decay_log)[None, :]
    pole_imag = rotation[None, :]
    rate_real = step_size * pole_real
    rate_imag = step_size * pole_imag
    lift_real = jnp.expm1(rate_real) * jnp.cos(rate_imag) - 2.0 * jnp.sin(0.5 * rate_imag) ** 2
    lift_imag = jnp.exp(rate_real) * jnp.sin(rate_imag)
    pole_norm = pole_real * pole_real + pole_imag * pole_imag
    ratio_real = (lift_real * pole_real + lift_imag * pole_imag) / pole_norm
    ratio_imag = (lift_imag * pole_real - lift_real * pole_imag) / pole_norm
    coef_real = readout[0] * ratio_real - readout[1] * ratio_imag
    coef_imag = readout[0] * ratio_imag + readout[1] * ratio_real
    return (coef_real, coef_imag, rate_real, rate_imag)


def parameter_grads(primal, backward, totals):
    coef_real, coef_imag = (primal[0], primal[1])
    cotangents = (
        2.0 * totals[0],
        -2.0 * totals[1],
        2.0 * (coef_real * totals[2] - coef_imag * totals[3]),
        -2.0 * (coef_real * totals[3] + coef_imag * totals[2]),
    )
    return backward(cotangents)


def shifted_totals(raw_sums, rate_real, rate_imag, block_start, norm_scale):
    decays = jnp.exp(rate_real * block_start)
    phases = rate_imag * block_start
    base_real = decays * jnp.cos(phases)
    base_imag = decays * jnp.sin(phases)
    near_real = block_start * raw_sums[0] + raw_sums[2]
    near_imag = block_start * raw_sums[1] + raw_sums[3]
    return jnp.stack(
        [
            norm_scale * (base_real * raw_sums[0] - base_imag * raw_sums[1]),
            norm_scale * (base_real * raw_sums[1] + base_imag * raw_sums[0]),
            norm_scale * (base_real * near_real - base_imag * near_imag),
            norm_scale * (base_real * near_imag + base_imag * near_real),
        ]
    )


def whole_channel_totals(lag_rows, rate_real, rate_imag, norm_scale):
    owners, length = (lag_rows.shape[1], lag_rows.shape[2])
    offsets = jnp.arange(length, dtype=jnp.int32).astype(jnp.float32)
    decays = jnp.exp(rate_real[:, :, None] * offsets)
    phases = rate_imag[:, :, None] * offsets
    power_real = decays * jnp.cos(phases)
    power_imag = decays * jnp.sin(phases)
    weighted = lag_rows * offsets
    raw_sums = jnp.stack(
        [
            jnp.einsum("cbj,cnj->cnb", lag_rows, power_real, precision=precise),
            jnp.einsum("cbj,cnj->cnb", lag_rows, power_imag, precision=precise),
            jnp.einsum("cbj,cnj->cnb", weighted, power_real, precision=precise),
            jnp.einsum("cbj,cnj->cnb", weighted, power_imag, precision=precise),
        ]
    )
    starts = (jnp.arange(owners, dtype=jnp.int32) * length).astype(jnp.float32)
    totals = shifted_totals(
        raw_sums, rate_real[:, :, None], rate_imag[:, :, None], starts, norm_scale
    )
    return jnp.sum(totals, axis=-1)


def general_lags(whole, norm_scale):
    part_count, owners, length = whole.shape[1:]
    freq_width = 2 * owners
    modulus = freq_width * length
    row_index = jnp.arange(owners, dtype=jnp.int32)
    outer_index = jnp.arange(freq_width, dtype=jnp.int32)
    inner_index = jnp.arange(length, dtype=jnp.int32)
    first = angle_table(row_index, outer_index, freq_width, -1.0)
    spec_real = jnp.einsum("scba,bk->scka", whole, jnp.cos(first), precision=precise)
    spec_imag = jnp.einsum("scba,bk->scka", whole, jnp.sin(first), precision=precise)
    spec_real, spec_imag = rotate(
        spec_real, spec_imag, angle_table(outer_index, inner_index, modulus, -1.0)
    )
    freq_real, freq_imag = last_transform(spec_real, spec_imag, -1.0)
    prod_real = freq_real[1] * freq_real[0] + freq_imag[1] * freq_imag[0]
    prod_imag = freq_imag[1] * freq_real[0] - freq_real[1] * freq_imag[0]
    back_real, back_imag = last_transform(prod_real, prod_imag, 1.0)
    back_real, back_imag = rotate(
        back_real, back_imag, angle_table(outer_index, inner_index, modulus, 1.0)
    )
    final = angle_table(outer_index, row_index, freq_width, 1.0)
    lag_rows = jnp.einsum("cka,kb->cba", back_real, jnp.cos(final), precision=precise) - jnp.einsum(
        "cka,kb->cba", back_imag, jnp.sin(final), precision=precise
    )
    return lag_rows * (norm_scale / modulus)


def general_device(inputs, out_grad, readout, log_step, decay_log, rotation):
    owners = lax.axis_size("seq")
    channels, length = inputs.shape
    states = decay_log.shape[0]
    part_count = channels // owners
    norm_scale = 1.0 / math.sqrt(owners * length)
    pieces = jnp.concatenate(
        [a.reshape(owners, part_count, length) for a in (inputs, out_grad)], axis=1
    )
    pieces = lax.all_to_all(pieces, "seq", split_axis=0, concat_axis=0, tiled=True)
    whole = pieces.astype(jnp.float32).reshape(owners, 2, part_count, length)
    lag_rows = general_lags(whole.transpose(1, 2, 0, 3), norm_scale)
    first_channel = lax.axis_index("seq") * part_count
    own_readout = lax.dynamic_slice_in_dim(readout, first_channel, part_count, 1)
    own_step = lax.dynamic_slice_in_dim(log_step, first_channel, part_count, 0)
    primal, backward = jax.vjp(discretize, own_readout, own_step, decay_log, rotation)
    totals = whole_channel_totals(lag_rows, primal[2], primal[3], norm_scale)
    readout_part, step_part, decay_part, rotation_part = parameter_grads(primal, backward, totals)
    shared = jnp.concatenate(
        [readout_part.reshape(-1), step_part, decay_part, rotation_part]
    )
    sent = jnp.concatenate(
        [
            lag_rows.transpose(1, 0, 2).reshape(owners, -1),
            jnp.broadcast_to(shared, (owners, shared.shape[0])),
        ],
        axis=1,
    )
    got = lax.all_to_all(sent, "seq", split_axis=0, concat_axis=0, tiled=True)
    cuts = np.cumsum([part_count * length, 2 * part_count * states, part_count])
    lags, readouts, steps, state = jnp.split(got, cuts, axis=1)
    readouts = readouts.reshape(owners, 2, part_count, states).transpose(1, 0, 2, 3)
    return (
        lags.reshape(channels, length),
        readouts.reshape(2, channels, states),
        steps.reshape(channels),
        lax.psum(jnp.sum(state, axis=0), "ch").reshape(2, states),
    )


def split_halves(value):
    high = value.astype(jnp.bfloat16)
    return high, (value - high.astype(jnp.float32)).astype(jnp.bfloat16)


def cos_sin(angle):
    turns = jnp.floor(angle * (2.0 / math.pi) + 0.5)
    rest = angle - turns * 1.5703125
    rest = rest - turns * 4.837512969970703125e-4
    rest = rest - turns * 7.54978995489188216e-8
    quarter = turns.astype(jnp.int32)
    square = rest * rest
    sine = rest + rest * square * (
        -1.6666654611e-1 + square * (8.3321608736e-3 - square * 1.9515295891e-4)
    )
    cosine = (
        1.0
        - 0.5 * square
        + square
        * square
        * (
            4.166664568298827e-2
            + square * (-1.388731625493765e-3 + square * 2.443315711809948e-5)
        )
    )
    odd = (quarter & 1) == 1
    out_cos = jnp.where(odd, sine, cosine)
    out_sin = jnp.where(odd, cosine, sine)
    out_cos = jnp.where(((quarter + 1) & 2) == 2, -out_cos, out_cos)
    out_sin = jnp.where((quarter & 2) == 2, -out_sin, out_sin)
    return out_cos, out_sin


def grow(value):
    series = 1.0
    for term in range(9, 1, -1):
        series = 1.0 + series * value * (1.0 / term)
    return jnp.where(jnp.abs(value) < 0.35, series * value, jnp.exp(value) - 1.0)


def power(rate_real, rate_imag, offset):
    size = jnp.exp(rate_real * offset)
    cosine, sine = cos_sin(rate_imag * offset)
    return size * cosine, size * sine


def times(left, right):
    return (
        left[0] * right[0] - left[1] * right[1],
        left[0] * right[1] + left[1] * right[0],
    )


def blocks_forward(x):
    root = math.sqrt(0.5)
    cosine, sine = math.cos(math.pi / 8), math.sin(math.pi / 8)
    total = [x[s] + x[s + 4] for s in range(4)]
    gap = [x[s] - x[s + 4] for s in range(4)]
    even, odd = total[0] + total[2], total[1] + total[3]
    real, imag = [None] * 9, [None] * 9
    real[0], real[8] = even + odd, even - odd
    imag[0] = imag[8] = jnp.zeros_like(even)
    real[4], imag[4] = total[0] - total[2], total[3] - total[1]
    less, more = root * (gap[1] - gap[3]), root * (gap[1] + gap[3])
    real[2], imag[2] = gap[0] + less, -gap[2] - more
    real[6], imag[6] = gap[0] - less, gap[2] - more
    less, more = root * (x[2] - x[6]), root * (x[2] + x[6])
    even1 = (x[0] + less, -x[4] - more)
    even3 = (x[0] - less, x[4] - more)
    p, q, r, t = x[1] - x[7], x[3] - x[5], x[1] + x[7], x[3] + x[5]
    odd1 = (cosine * p + sine * q, -sine * r - cosine * t)
    odd3 = (sine * p - cosine * q, sine * t - cosine * r)
    real[1], imag[1] = even1[0] + odd1[0], even1[1] + odd1[1]
    real[7], imag[7] = even1[0] - odd1[0], odd1[1] - even1[1]
    real[3], imag[3] = even3[0] + odd3[0], even3[1] + odd3[1]
    real[5], imag[5] = even3[0] - odd3[0], odd3[1] - even3[1]
    return list(zip(real, imag))


def blocks_back(z):
    root = math.sqrt(0.5)
    cosine, sine = math.cos(math.pi / 8), math.sin(math.pi / 8)
    real, imag = [v[0] for v in z], [v[1] for v in z]
    even, odd = real[0] + real[8], real[0] - real[8]
    total = [even + real[4], odd + imag[4], even - real[4], odd - imag[4]]
    less, more = root * (real[2] - real[6]), root * (imag[2] + imag[6])
    gap = [real[2] + real[6], less + more, imag[2] - imag[6], more - less]
    x = [total[s] + gap[s] for s in range(4)] + [total[s] - gap[s] for s in range(4)]
    even1 = (real[1] + real[7], imag[7] - imag[1])
    even3 = (real[3] + real[5], imag[5] - imag[3])
    odd1 = (real[1] - real[7], imag[1] + imag[7])
    odd3 = (real[3] - real[5], imag[3] + imag[5])
    less, more = root * (even1[0] - even3[0]), root * (even1[1] + even3[1])
    p = cosine * odd1[0] + sine * odd3[0]
    q = sine * odd1[0] - cosine * odd3[0]
    r = sine * odd1[1] + cosine * odd3[1]
    t = cosine * odd1[1] - sine * odd3[1]
    extra = [
        even1[0] + even3[0],
        p + r,
        less - more,
        q + t,
        even3[1] - even1[1],
        t - q,
        -less - more,
        r - p,
    ]
    return [v + w for v, w in zip(x, extra)]


def transform_tables(owners, length, norm_scale):
    width = 2 * owners
    counter = np.arange(length)
    angles = two_pi * (counter[:, None] * counter[None, :] % length) / length
    cosine, sine = np.cos(angles), np.sin(angles)
    matrix = np.block([[cosine, -sine], [sine, cosine]]).astype(np.float32)
    high = matrix.astype(jnp.bfloat16)
    low = (matrix - high.astype(np.float32)).astype(jnp.bfloat16)
    outer = np.arange(owners + 1)
    angles = two_pi * (outer[:, None] * counter[None, :]) / (width * length)
    twiddle = np.stack([np.cos(angles), -np.sin(angles)], axis=1)
    weight = np.where(outer % owners == 0, 1.0, 2.0) * norm_scale / (width * length)
    twiddle = np.concatenate([twiddle, twiddle * weight[:, None, None]], axis=1)
    return np.stack([high, low]), twiddle.astype(np.float32)


def three_pieces(value):
    pieces = []
    for _ in range(3):
        piece = value.astype(jnp.bfloat16).astype(jnp.float32)
        pieces.append(piece)
        value = value - piece
    return pieces


def swap(value):
    return pltpu.roll(value, LANES // 2, 1)


def rest_lanes(lane):
    return lane < 3, (lane >= LANES // 2) & (lane < LANES // 2 + 3)


def rest_steps(value):
    high = value.astype(jnp.bfloat16).astype(jnp.float32)
    steps = jnp.where(high == 0.0, 0.0, (value - high) / jnp.where(high == 0.0, 1.0, high))
    return jnp.floor(steps * (256.0 * REST_STEPS) + 0.5)


def unpack_rests(high, rest):
    lane = lax.broadcasted_iota(jnp.int32, high.shape, 1)
    shared, replaced = rest_lanes(lane)
    step = sum(rest[:, LANES // 2 + i : LANES // 2 + i + 1] for i in range(3))
    both = jnp.where(shared, rest, swap(rest))
    first = jnp.floor(both * (1.0 / (2.0 * REST_STEPS + 1.0)) + 0.5)
    second = both - first * (2.0 * REST_STEPS + 1.0)
    steps = jnp.where(shared, first, second) * (1.0 / (256.0 * REST_STEPS))
    return jnp.where(shared | replaced, high * steps, rest), jnp.broadcast_to(step, high.shape)


def transposed(value):
    return jnp.concatenate(
        [value[:, spot : spot + LANES].T for spot in range(0, value.shape[1], LANES)], axis=0
    )


READ, REST, OUT_ROWS = 16, 17, 18
REST_STEPS = 7.0
ROWS = 20
LAGS, GRADS, STATE, SINGLES = 0, 8, 16, 18
STEP_LANES, SCALE_LANES = (0, 8), (16, 17, 18, 19)
SPARE = 15.0
PARTS = 4
FRESH = 5


def pack_kernel(inputs, out_grad, readout, log_step, *refs):
    count = (len(refs) - 7) // 2
    sources, (out, *held) = refs[:count], refs[count : 2 * count + 1]
    signals, read, step, turned, rows, sems = refs[2 * count + 1 :]
    peers = out.shape[0] // OUT_ROWS
    copies = [
        pltpu.make_async_copy(source, target, sems.at[i])
        for i, (source, target) in enumerate(
            (
                (readout, read),
                (log_step, step),
                (inputs, signals.at[0]),
                (out_grad, signals.at[1]),
                *zip(sources, held),
            )
        )
    ]
    for copy in copies:
        copy.start()
    for copy in copies[:4]:
        copy.wait()
    own = lax.axis_index("seq")
    turned[...] = transposed(read[...])
    channels = step.shape[1]
    peer = lax.broadcasted_iota(jnp.int32, (peers, channels), 0)
    channel = lax.broadcasted_iota(jnp.int32, (peers, channels), 1)
    sent_channel = channel == peer * SUBLANES + own

    def pick(row):
        value = jnp.sum(jnp.where(sent_channel, row, 0.0), axis=1, keepdims=True)
        return jnp.broadcast_to(value, (peers, LANES))

    half = LANES // 2
    shared = rest_steps(read[0:SUBLANES]) * (2.0 * REST_STEPS + 1.0)
    shared = shared + rest_steps(read[half : half + SUBLANES])
    pieces = three_pieces(pick(step[...]))
    placed = [(i, pick(shared[i : i + 1])) for i in range(3)]
    placed += [(half + i, piece) for i, piece in enumerate(pieces)]
    for place, signal in enumerate((signals[0], signals[1])):
        value = signal.astype(jnp.float32)
        for peer in range(peers):
            spot = peer * OUT_ROWS + place * SUBLANES
            rows[spot : spot + SUBLANES] = value[peer * SUBLANES : (peer + 1) * SUBLANES]
    value = turned[pl.ds(own, peers, stride=SUBLANES), :]
    high = value.astype(jnp.bfloat16).astype(jnp.float32)
    rows[pl.ds(READ, peers, stride=OUT_ROWS), :] = high
    rest = value - high
    lane = lax.broadcasted_iota(jnp.int32, (peers, LANES), 1)
    for place, other in placed:
        rest = jnp.where(lane == place, other, rest)
    rows[pl.ds(REST, peers, stride=OUT_ROWS), :] = rest
    out[...] = rows[...].astype(jnp.bfloat16)
    for copy in copies[4:]:
        copy.wait()


def exponent_of(bound):
    return jnp.floor(jnp.log(jnp.maximum(bound, 1e-30)) * (1.0 / math.log(2.0))) + (2.0 - SPARE)


def greatest(value):
    return jnp.max(jnp.max(value, axis=1, keepdims=True), axis=0, keepdims=True)


def size_of(value):
    return jnp.abs(value[0]) + jnp.abs(value[1])


def two_pieces(value):
    high = value.astype(jnp.bfloat16).astype(jnp.float32)
    return high, (value - high) * 256.0


def main_kernel(
    owners,
    norm_scale,
    got,
    matrix,
    twiddle,
    decay_log,
    rotation,
    sent,
    rows_in,
    spectra,
    freq,
    back,
    params,
    doubled,
    bases,
    powers,
    lags,
    sums,
):
    peers, length = got.shape[0] // OUT_ROWS, got.shape[1]
    groups = peers // owners
    part_count = groups * SUBLANES
    rows = 2 * part_count
    pairs = part_count // 2
    half = pairs // SUBLANES
    reach = length // 2
    lane = lax.broadcasted_iota(jnp.int32, (pairs, LANES), 1)
    left = lane < LANES // 2
    row = lax.broadcasted_iota(jnp.int32, (SUBLANES, LANES), 0)

    def lanes_of(side):
        return slice(side * LANES, (side + 1) * LANES)

    def collect(spot):
        tiles = [
            rows_in[pl.ds(group * owners * OUT_ROWS + spot, owners, stride=OUT_ROWS), :]
            for group in range(groups)
        ]
        return jnp.concatenate(tiles[:half], axis=0), jnp.concatenate(tiles[half:], axis=0)

    def make_params():
        sides = []
        for high, rest in zip(collect(READ), collect(REST)):
            rest, step = unpack_rests(high, rest)
            sides.append((high + rest, step))
        (lower, lower_step), (upper, upper_step) = sides
        read = (jnp.where(left, lower, swap(upper)), jnp.where(left, swap(lower), upper))
        step = jnp.exp(jnp.where(left, lower_step, upper_step))
        decay_row = jnp.concatenate([decay_log[...], decay_log[...]], axis=1)
        rotation_row = jnp.concatenate([rotation[...], rotation[...]], axis=1)
        pole = (
            jnp.broadcast_to(-jnp.exp(decay_row), step.shape),
            jnp.broadcast_to(rotation_row, step.shape),
        )
        rate = (step * pole[0], step * pole[1])
        place, size = 0, 1
        while size < owners * length:
            if place // 2 % FRESH == 0:
                value = power(rate[0], rate[1], float(size))
            else:
                value = (value[0] * value[0] - value[1] * value[1], 2.0 * value[0] * value[1])
            doubled[place], doubled[place + 1] = value
            place, size = place + 2, size * 2
        sine = cos_sin(0.5 * rate[1])[1]
        cosine = 1.0 - 2.0 * sine * sine
        lift = (grow(rate[0]) * cosine - 2.0 * sine * sine, doubled[1])
        norm = 1.0 / (pole[0] * pole[0] + pole[1] * pole[1])
        inverse = (pole[0] * norm, -pole[1] * norm)
        ratio = times(lift, inverse)
        coef = times(read, ratio)
        lifted = times((doubled[0], doubled[1]), inverse)
        values = (rate, ratio, coef, times(read, lifted), pole, times(coef, inverse), (step, step))
        for place, value in enumerate(values):
            params[2 * place], params[2 * place + 1] = value

    block_bit, reach_bit = length.bit_length() - 1, reach.bit_length() - 1
    bits = [(row & (1 << i)) != 0 for i in range(SUBLANES.bit_length() - 1)]

    def doubled_row(p, i):
        return doubled[2 * i, p : p + 1, :], doubled[2 * i + 1, p : p + 1, :]

    def by_rows(p, first):
        out = None
        for i, bit in enumerate(bits):
            real, imag = doubled_row(p, first + i)
            value = (jnp.where(bit, real, 1.0), jnp.where(bit, imag, 0.0))
            out = value if out is None else times(out, value)
        return out

    def make_tables():
        for p in range(pairs):
            table = [by_rows(p, 0)]
            for i in range(len(bits), reach_bit):
                table += [times(block, doubled_row(p, i)) for block in table]
            for place in range(0, len(table), 2):
                for side in range(2):
                    value = jnp.concatenate([table[place][side], table[place + 1][side]], axis=0)
                    for i, piece in enumerate(split_halves(value)):
                        spot = 2 * i * reach + place * SUBLANES
                        powers[p, spot : spot + 2 * SUBLANES, lanes_of(side)] = piece
                        spot += reach
                        powers[p, spot : spot + 2 * SUBLANES, lanes_of(side)] = piece
            base = by_rows(p, block_bit)
            bases[p, 0], bases[p, 1] = base
            bases[p, 2], bases[p, 3] = times(base, doubled_row(p, reach_bit))

    def transform(source, target, count):
        dot = functools.partial(jnp.dot, preferred_element_type=jnp.float32)
        cuts = [(owners + 1) * i // PARTS * count for i in range(PARTS + 1)]
        for part in map(slice, cuts, cuts[1:]):
            low = source[1, part]
            target[part] = (
                dot(source[0, part], matrix[0]) + dot(low, matrix[0]) + dot(source[0, part], matrix[1])
            )

    def spread_blocks():
        rows_in[...] = got[...].astype(jnp.float32)
        blocks = []
        for s in range(owners):
            spots = [(group * owners + s) * OUT_ROWS for group in range(groups)]
            blocks.append(
                jnp.concatenate(
                    [rows_in[spot : spot + SUBLANES] for spot in spots]
                    + [rows_in[spot + SUBLANES : spot + 2 * SUBLANES] for spot in spots],
                    axis=0,
                )
            )
        for k, value in enumerate(blocks_forward(blocks)):
            if k:
                value = times(value, (twiddle[k, 0:1], twiddle[k, 1:2]))
            for side in range(2):
                for i, piece in enumerate(split_halves(value[side])):
                    spectra[i, k * rows : (k + 1) * rows, lanes_of(side)] = piece

    def to_frequencies():
        transform(spectra, freq, rows)
        make_params()
        make_tables()

    def to_lags():
        for k in range(owners + 1):
            at_in = freq[k * rows : k * rows + part_count]
            at_out = freq[k * rows + part_count : (k + 1) * rows]
            ur, ui = at_in[:, :length], at_in[:, length:]
            gr, gi = at_out[:, :length], at_out[:, length:]
            for side, value in enumerate((gr * ur + gi * ui, gr * ui - gi * ur)):
                for i, piece in enumerate(split_halves(value)):
                    spectra[i, k * part_count : (k + 1) * part_count, lanes_of(side)] = piece
        transform(spectra, back, part_count)

    def finish():
        turned = []
        for k in range(owners + 1):
            spots = slice(k * part_count, (k + 1) * part_count)
            value = (back[spots, lanes_of(0)], back[spots, lanes_of(1)])
            turned.append(times(value, (twiddle[k, 2:3], twiddle[k, 3:4])))
        blocks = blocks_back(turned)

        most = jnp.zeros((part_count, LANES), jnp.float32)
        for b, block in enumerate(blocks):
            most = jnp.maximum(most, jnp.abs(block))

        for group in range(groups):
            spots = slice(group * SUBLANES, (group + 1) * SUBLANES)
            tiles = jnp.stack([block[spots] for block in blocks])
            lags[group * owners * SUBLANES : (group + 1) * owners * SUBLANES] = jnp.swapaxes(
                tiles, 0, 1
            ).reshape(owners * SUBLANES, length)

        def param(place):
            return params[2 * place], params[2 * place + 1]

        rate, ratio, coef, through, pole, direct, (step, _) = (param(i) for i in range(7))
        most = greatest(most)
        whole = 2.0 * math.sqrt(owners * length)
        on_rate = size_of(coef) * float(owners * length) + size_of(through)
        on_pole = step * on_rate + size_of(direct)
        lag_exponent = exponent_of(most)
        grad_exponent = exponent_of(most * (whole * greatest(size_of(ratio))))
        state_exponent = exponent_of(
            most * (whole * part_count * greatest(on_pole * (1.0 - pole[0])))
        )
        step_exponent = exponent_of(
            most * (whole * (LANES // 2) * greatest(on_rate * size_of(rate)))
        )
        lag_scale = jnp.exp2(-lag_exponent)
        for b, block in enumerate(blocks):
            for group in range(groups):
                place = (group * owners + b) * ROWS
                value = block[group * SUBLANES : (group + 1) * SUBLANES]
                sent[place + LAGS : place + GRADS] = value * lag_scale

        start = row.astype(jnp.float32) * float(length)
        first = left[:owners]
        wide = lax.broadcasted_iota(jnp.int32, (4 * owners, LANES), 1)
        wide_left = wide < reach
        offset = jnp.where(wide_left, wide, wide - reach).astype(jnp.float32)
        both_left = wide_left[: 2 * owners]
        for p in range(pairs):
            both = jnp.concatenate(
                [
                    lags[channel * owners : (channel + 1) * owners]
                    for channel in (p, pairs + p)
                ],
                axis=0,
            )
            swapped = swap(both)
            plain = jnp.concatenate(
                [jnp.where(both_left, both, swapped), jnp.where(both_left, swapped, both)], axis=0
            )
            factor = []
            for value in (plain, plain * offset):
                high = value.astype(jnp.bfloat16).astype(jnp.float32)
                factor.append(jnp.where(wide_left, high, value - high))
            factor = jnp.concatenate(factor, axis=0).astype(jnp.bfloat16)
            raw = jnp.dot(
                jnp.concatenate([factor, factor], axis=1),
                powers[p],
                preferred_element_type=jnp.float32,
            )

            def pick(place, side):
                top = raw[2 * place * owners : (2 * place + 1) * owners, lanes_of(side)]
                bottom = raw[(2 * place + 1) * owners : (2 * place + 2) * owners, lanes_of(side)]
                return jnp.where(first, top, bottom)

            found = None
            for part in range(2):
                base = (bases[p, 2 * part], bases[p, 2 * part + 1])
                near = start + float(part * reach)
                value = (pick(part, 0), pick(part, 1))
                lagged = (near * value[0] + pick(2 + part, 0), near * value[1] + pick(2 + part, 1))
                terms = times(base, value) + times(base, lagged)
                found = terms if found is None else [x + y for x, y in zip(found, terms)]
            for place, value in enumerate(found):
                sums[place, p : p + 1] = jnp.sum(value, axis=0, keepdims=True)

        total = (sums[0] * (2.0 * norm_scale), sums[1] * (2.0 * norm_scale))
        lag_total = (sums[2] * (2.0 * norm_scale), sums[3] * (2.0 * norm_scale))
        on_read = times(total, ratio)
        on_read = (on_read[0], -on_read[1])
        on_rate = times(coef, lag_total)
        more = times(total, through)
        on_rate = (on_rate[0] + more[0], on_rate[1] + more[1])
        less = times(total, direct)
        on_pole = (step * on_rate[0] - less[0], step * on_rate[1] - less[1])
        on_step = times(on_rate, rate)[0]
        on_decay = jnp.sum(on_pole[0] * pole[0], axis=0, keepdims=True)
        on_rotation = -jnp.sum(on_pole[1], axis=0, keepdims=True)
        on_decay = on_decay + swap(on_decay)
        on_rotation = on_rotation + swap(on_rotation)
        state = jnp.where(left[0:1], on_decay, on_rotation) * jnp.exp2(-state_exponent)

        grad_scale = jnp.exp2(-grad_exponent)
        on_read = (on_read[0] * grad_scale, on_read[1] * grad_scale)
        lower = jnp.where(left, on_read[0], swap(on_read[1]))
        upper = jnp.where(left, swap(on_read[0]), on_read[1])
        grads = jnp.concatenate([lower, upper], axis=0)
        step_scale = jnp.broadcast_to(jnp.exp2(-step_exponent), (pairs, LANES))
        step_columns = [
            jnp.broadcast_to(jnp.sum(value, axis=1, keepdims=True), (pairs, LANES)) * step_scale
            for value in (jnp.where(left, on_step, 0.0), jnp.where(left, 0.0, on_step))
        ]
        place_lane = lax.broadcasted_iota(jnp.int32, (SUBLANES, LANES), 1)
        scales = jnp.zeros((1, LANES), jnp.float32)
        for spot, value in zip(
            SCALE_LANES, (lag_exponent, grad_exponent, state_exponent, step_exponent)
        ):
            scales = jnp.where(place_lane[0:1] == spot, value, scales)
        state_high, state_low = two_pieces(state)
        tails = []
        for group in range(groups):
            spot = group % half * SUBLANES
            pieces = two_pieces(step_columns[group // half][spot : spot + SUBLANES])
            spread = jnp.zeros((SUBLANES, LANES), jnp.float32)
            for spot, piece in zip(STEP_LANES, pieces):
                spread = jnp.where(place_lane == row + spot, piece, spread)
            singles = scales + jnp.sum(spread, axis=0, keepdims=True)
            tails.append(jnp.concatenate([state_high, state_low, singles, singles], axis=0))
        for b in range(owners):
            for group in range(groups):
                place = (group * owners + b) * ROWS
                sent[place + GRADS : place + STATE] = grads[
                    group * SUBLANES : (group + 1) * SUBLANES
                ]
                sent[place + STATE : place + ROWS] = tails[group]

    for section in (spread_blocks, to_frequencies, to_lags, finish):
        section()


def unpack_kernel(got, kernel_grad, readout_grad, step_grad, state_grad, wide, grads):
    peers = got.shape[0] // ROWS
    per_row = LANES // SUBLANES
    singles = got[pl.ds(SINGLES, peers, stride=ROWS), :]
    exponents = [jnp.broadcast_to(singles[:, spot : spot + 1], (peers, LANES)) for spot in SCALE_LANES]
    scales = [jnp.exp2(value) for value in exponents]
    wide[...] = scales[0]
    lane = lax.broadcasted_iota(jnp.int32, (peers, LANES), 1)
    row = lax.broadcasted_iota(jnp.int32, (peers, LANES), 0)

    def by_channel(value, spot):
        mine = jnp.where(row - spot == lane // SUBLANES, value, 0.0)
        return jnp.sum(mine, axis=0, keepdims=True)

    for spot in range(0, peers, per_row):
        part = slice(spot * SUBLANES, (spot + per_row) * SUBLANES)
        for peer in range(spot, spot + per_row):
            place, own = peer * ROWS, slice(peer * SUBLANES, (peer + 1) * SUBLANES)
            grads[own] = got[place + GRADS : place + STATE]
            kernel_grad[own] = got[place + LAGS : place + GRADS] * wide[peer : peer + 1, :]
        readout_grad[:, part] = grads[part].T * by_channel(scales[1], spot)

    high = got[pl.ds(STATE, peers, stride=ROWS), :]
    low = got[pl.ds(STATE + 1, peers, stride=ROWS), :]
    total = jnp.sum((high + low * (1.0 / 256.0)) * scales[2], axis=0, keepdims=True)
    states = state_grad.shape[1]
    state_grad[0:1] = total[:, :states]
    state_grad[1:2] = total[:, states:]
    high, low = (
        jnp.take_along_axis(singles, lane % SUBLANES + first, axis=1) for first in STEP_LANES
    )
    value = (high + low * (1.0 / 256.0)) * scales[3]
    for spot in range(0, peers, per_row):
        part = slice(spot * SUBLANES, (spot + per_row) * SUBLANES)
        step_grad[part] = by_channel(value, spot).reshape(LANES)


def kernel_device(inputs, out_grad, readout, log_step, decay_log, rotation):
    owners, groups = lax.axis_size("seq"), lax.axis_size("ch")
    peers = owners * groups
    channels, length = inputs.shape
    states = decay_log.shape[0]
    part_count = channels // owners
    pairs = part_count // 2
    norm_scale = 1.0 / math.sqrt(owners * length)
    vmem = pl.BlockSpec(memory_space=pltpu.VMEM)
    memory = pltpu.CompilerParams(vmem_limit_bytes=32 * 1024 * 1024)
    f32, bf16 = jnp.float32, jnp.bfloat16

    def exchange(value):
        rows = value.shape[0] // peers
        value = value.reshape(peers, rows // 2, 2, LANES)
        value = lax.all_to_all(value, ("ch", "seq"), split_axis=0, concat_axis=0, tiled=True)
        return value.reshape(peers * rows, LANES)

    anywhere = pl.BlockSpec(memory_space=pl.ANY)
    held = [jnp.asarray(table) for table in transform_tables(owners, length, norm_scale)]
    held += [decay_log[None], rotation[None]]
    sources = (
        inputs, out_grad, readout.transpose(0, 2, 1).reshape(LANES, channels), log_step[None], *held
    )
    pieces, *held = pl.pallas_call(
        pack_kernel,
        out_shape=[jax.ShapeDtypeStruct((peers * OUT_ROWS, LANES), bf16)]
        + [jax.ShapeDtypeStruct(value.shape, value.dtype) for value in held],
        in_specs=[anywhere] * len(sources),
        out_specs=[vmem] * (1 + len(held)),
        scratch_shapes=[
            pltpu.VMEM((2, channels, LANES), bf16),
            pltpu.VMEM((LANES, channels), f32),
            pltpu.VMEM((1, channels), f32),
            pltpu.VMEM((channels, LANES), f32),
            pltpu.VMEM((peers * OUT_ROWS, LANES), f32),
            pltpu.SemaphoreType.DMA((len(sources),)),
        ],
        compiler_params=memory,
    )(*(pltpu.with_memory_space_constraint(value, pltpu.HBM) for value in sources))
    got = exchange(pieces)
    sent = pl.pallas_call(
        functools.partial(main_kernel, owners, norm_scale),
        out_shape=jax.ShapeDtypeStruct((peers * ROWS, LANES), f32),
        in_specs=[vmem] * 5,
        out_specs=vmem,
        scratch_shapes=[
            pltpu.VMEM((peers * OUT_ROWS, LANES), f32),
            pltpu.VMEM((2, (owners + 1) * 2 * part_count, 2 * LANES), bf16),
            pltpu.VMEM(((owners + 1) * 2 * part_count, 2 * LANES), f32),
            pltpu.VMEM(((owners + 1) * part_count, 2 * LANES), f32),
            pltpu.VMEM((14, pairs, LANES), f32),
            pltpu.VMEM((2 * (owners * length).bit_length(), pairs, LANES), f32),
            pltpu.VMEM((pairs, 4, owners, LANES), f32),
            pltpu.VMEM((pairs, 2 * length, 2 * LANES), bf16),
            pltpu.VMEM((owners * part_count, length), f32),
            pltpu.VMEM((4, pairs, LANES), f32),
        ],
        compiler_params=memory,
    )(got, *held)
    back = exchange(sent.astype(jnp.float16))
    kernel_grad, readout_grad, step_grad, state_grad = pl.pallas_call(
        unpack_kernel,
        out_shape=[
            jax.ShapeDtypeStruct((channels, length), f32),
            jax.ShapeDtypeStruct((LANES, channels), f32),
            jax.ShapeDtypeStruct((channels,), f32),
            jax.ShapeDtypeStruct((2, states), f32),
        ],
        in_specs=[vmem],
        out_specs=[vmem] * 4,
        scratch_shapes=[
            pltpu.VMEM((peers, LANES), f32),
            pltpu.VMEM((channels, LANES), f32),
        ],
        compiler_params=memory,
    )(back.astype(f32))
    readout_grad = readout_grad.reshape(2, states, channels).transpose(0, 2, 1)
    return kernel_grad, readout_grad, step_grad, state_grad


def kernel_fits(mesh, inputs, decay_log):
    owners, groups = mesh.shape["seq"], mesh.shape["ch"]
    channels = inputs.shape[0] // groups
    return (
        inputs.shape[1] == owners * LANES
        and 2 * decay_log.shape[0] == LANES
        and owners == SUBLANES
        and groups % 2 == 0
        and channels == owners * groups * SUBLANES
        and channels % LANES == 0
    )


def solution(mesh):
    def whole(inputs, out_grad, readout, log_step, decay_log, rotation):
        fits = kernel_fits(mesh, inputs, decay_log)
        return jax.shard_map(
            kernel_device if fits else general_device,
            mesh=mesh,
            in_specs=(P("ch", "seq"), P("ch", "seq"), P(None, "ch", None), P("ch"), P(), P()),
            out_specs=(P("ch", "seq"), P(None, "ch", None), P("ch"), P()),
            check_vma=False,
        )(inputs, out_grad, readout, log_step, decay_log, rotation)

    return whole
```

```python
import functools
import math

import jax
import jax.numpy as jnp
import numpy as np
from jax import lax
from jax.experimental import pallas as pl
from jax.experimental.pallas import tpu as pltpu
from jax.sharding import PartitionSpec as P

precise = lax.Precision.HIGHEST
two_pi = 2.0 * math.pi
LANES = 128
SUBLANES = 8


def angle_table(left_index, right_index, modulus, orient):
    product = left_index[:, None] * right_index[None, :] % modulus
    return orient * two_pi * product.astype(jnp.float32) / modulus


def rotate(real_part, imag_part, angles):
    cosine_table = jnp.cos(angles)
    sine_table = jnp.sin(angles)
    return (
        real_part * cosine_table - imag_part * sine_table,
        real_part * sine_table + imag_part * cosine_table,
    )


def last_transform(real_part, imag_part, orient):
    length = real_part.shape[-1]
    counter = jnp.arange(length, dtype=jnp.int32)
    angles = angle_table(counter, counter, length, orient)
    cosine_table = jnp.cos(angles)
    sine_table = jnp.sin(angles)
    dot = functools.partial(jnp.dot, precision=precise, preferred_element_type=jnp.float32)
    return (
        dot(real_part, cosine_table) - dot(imag_part, sine_table),
        dot(imag_part, cosine_table) + dot(real_part, sine_table),
    )


def discretize(readout, log_step, decay_log, rotation):
    step_size = jnp.exp(log_step)[:, None]
    pole_real = -jnp.exp(decay_log)[None, :]
    pole_imag = rotation[None, :]
    rate_real = step_size * pole_real
    rate_imag = step_size * pole_imag
    lift_real = jnp.expm1(rate_real) * jnp.cos(rate_imag) - 2.0 * jnp.sin(0.5 * rate_imag) ** 2
    lift_imag = jnp.exp(rate_real) * jnp.sin(rate_imag)
    pole_norm = pole_real * pole_real + pole_imag * pole_imag
    ratio_real = (lift_real * pole_real + lift_imag * pole_imag) / pole_norm
    ratio_imag = (lift_imag * pole_real - lift_real * pole_imag) / pole_norm
    coef_real = readout[0] * ratio_real - readout[1] * ratio_imag
    coef_imag = readout[0] * ratio_imag + readout[1] * ratio_real
    return (coef_real, coef_imag, rate_real, rate_imag)


def parameter_grads(primal, backward, totals):
    coef_real, coef_imag = (primal[0], primal[1])
    cotangents = (
        2.0 * totals[0],
        -2.0 * totals[1],
        2.0 * (coef_real * totals[2] - coef_imag * totals[3]),
        -2.0 * (coef_real * totals[3] + coef_imag * totals[2]),
    )
    return backward(cotangents)


def shifted_totals(raw_sums, rate_real, rate_imag, block_start, norm_scale):
    decays = jnp.exp(rate_real * block_start)
    phases = rate_imag * block_start
    base_real = decays * jnp.cos(phases)
    base_imag = decays * jnp.sin(phases)
    near_real = block_start * raw_sums[0] + raw_sums[2]
    near_imag = block_start * raw_sums[1] + raw_sums[3]
    return jnp.stack(
        [
            norm_scale * (base_real * raw_sums[0] - base_imag * raw_sums[1]),
            norm_scale * (base_real * raw_sums[1] + base_imag * raw_sums[0]),
            norm_scale * (base_real * near_real - base_imag * near_imag),
            norm_scale * (base_real * near_imag + base_imag * near_real),
        ]
    )


def whole_channel_totals(lag_rows, rate_real, rate_imag, norm_scale):
    owners, length = (lag_rows.shape[1], lag_rows.shape[2])
    offsets = jnp.arange(length, dtype=jnp.int32).astype(jnp.float32)
    decays = jnp.exp(rate_real[:, :, None] * offsets)
    phases = rate_imag[:, :, None] * offsets
    power_real = decays * jnp.cos(phases)
    power_imag = decays * jnp.sin(phases)
    weighted = lag_rows * offsets
    raw_sums = jnp.stack(
        [
            jnp.einsum("cbj,cnj->cnb", lag_rows, power_real, precision=precise),
            jnp.einsum("cbj,cnj->cnb", lag_rows, power_imag, precision=precise),
            jnp.einsum("cbj,cnj->cnb", weighted, power_real, precision=precise),
            jnp.einsum("cbj,cnj->cnb", weighted, power_imag, precision=precise),
        ]
    )
    starts = (jnp.arange(owners, dtype=jnp.int32) * length).astype(jnp.float32)
    totals = shifted_totals(
        raw_sums, rate_real[:, :, None], rate_imag[:, :, None], starts, norm_scale
    )
    return jnp.sum(totals, axis=-1)


def general_lags(whole, norm_scale):
    part_count, owners, length = whole.shape[1:]
    freq_width = 2 * owners
    modulus = freq_width * length
    row_index = jnp.arange(owners, dtype=jnp.int32)
    outer_index = jnp.arange(freq_width, dtype=jnp.int32)
    inner_index = jnp.arange(length, dtype=jnp.int32)
    first = angle_table(row_index, outer_index, freq_width, -1.0)
    spec_real = jnp.einsum("scba,bk->scka", whole, jnp.cos(first), precision=precise)
    spec_imag = jnp.einsum("scba,bk->scka", whole, jnp.sin(first), precision=precise)
    spec_real, spec_imag = rotate(
        spec_real, spec_imag, angle_table(outer_index, inner_index, modulus, -1.0)
    )
    freq_real, freq_imag = last_transform(spec_real, spec_imag, -1.0)
    prod_real = freq_real[1] * freq_real[0] + freq_imag[1] * freq_imag[0]
    prod_imag = freq_imag[1] * freq_real[0] - freq_real[1] * freq_imag[0]
    back_real, back_imag = last_transform(prod_real, prod_imag, 1.0)
    back_real, back_imag = rotate(
        back_real, back_imag, angle_table(outer_index, inner_index, modulus, 1.0)
    )
    final = angle_table(outer_index, row_index, freq_width, 1.0)
    lag_rows = jnp.einsum("cka,kb->cba", back_real, jnp.cos(final), precision=precise) - jnp.einsum(
        "cka,kb->cba", back_imag, jnp.sin(final), precision=precise
    )
    return lag_rows * (norm_scale / modulus)


def general_device(inputs, out_grad, readout, log_step, decay_log, rotation):
    owners = lax.axis_size("seq")
    channels, length = inputs.shape
    states = decay_log.shape[0]
    part_count = channels // owners
    norm_scale = 1.0 / math.sqrt(owners * length)
    pieces = jnp.concatenate(
        [a.reshape(owners, part_count, length) for a in (inputs, out_grad)], axis=1
    )
    pieces = lax.all_to_all(pieces, "seq", split_axis=0, concat_axis=0, tiled=True)
    whole = pieces.astype(jnp.float32).reshape(owners, 2, part_count, length)
    lag_rows = general_lags(whole.transpose(1, 2, 0, 3), norm_scale)
    first_channel = lax.axis_index("seq") * part_count
    own_readout = lax.dynamic_slice_in_dim(readout, first_channel, part_count, 1)
    own_step = lax.dynamic_slice_in_dim(log_step, first_channel, part_count, 0)
    primal, backward = jax.vjp(discretize, own_readout, own_step, decay_log, rotation)
    totals = whole_channel_totals(lag_rows, primal[2], primal[3], norm_scale)
    readout_part, step_part, decay_part, rotation_part = parameter_grads(primal, backward, totals)
    shared = jnp.concatenate(
        [readout_part.reshape(-1), step_part, decay_part, rotation_part]
    )
    sent = jnp.concatenate(
        [
            lag_rows.transpose(1, 0, 2).reshape(owners, -1),
            jnp.broadcast_to(shared, (owners, shared.shape[0])),
        ],
        axis=1,
    )
    got = lax.all_to_all(sent, "seq", split_axis=0, concat_axis=0, tiled=True)
    cuts = np.cumsum([part_count * length, 2 * part_count * states, part_count])
    lags, readouts, steps, state = jnp.split(got, cuts, axis=1)
    readouts = readouts.reshape(owners, 2, part_count, states).transpose(1, 0, 2, 3)
    return (
        lags.reshape(channels, length),
        readouts.reshape(2, channels, states),
        steps.reshape(channels),
        lax.psum(jnp.sum(state, axis=0), "ch").reshape(2, states),
    )


def split_halves(value):
    high = value.astype(jnp.bfloat16)
    return high, (value - high.astype(jnp.float32)).astype(jnp.bfloat16)


def cos_sin(angle):
    turns = jnp.floor(angle * (2.0 / math.pi) + 0.5)
    rest = angle - turns * 1.5703125
    rest = rest - turns * 4.837512969970703125e-4
    rest = rest - turns * 7.54978995489188216e-8
    quarter = turns.astype(jnp.int32)
    square = rest * rest
    sine = rest + rest * square * (
        -1.6666654611e-1 + square * (8.3321608736e-3 - square * 1.9515295891e-4)
    )
    cosine = (
        1.0
        - 0.5 * square
        + square
        * square
        * (
            4.166664568298827e-2
            + square * (-1.388731625493765e-3 + square * 2.443315711809948e-5)
        )
    )
    odd = (quarter & 1) == 1
    out_cos = jnp.where(odd, sine, cosine)
    out_sin = jnp.where(odd, cosine, sine)
    out_cos = jnp.where(((quarter + 1) & 2) == 2, -out_cos, out_cos)
    out_sin = jnp.where((quarter & 2) == 2, -out_sin, out_sin)
    return out_cos, out_sin


def grow(value):
    series = 1.0
    for term in range(9, 1, -1):
        series = 1.0 + series * value * (1.0 / term)
    return jnp.where(jnp.abs(value) < 0.35, series * value, jnp.exp(value) - 1.0)


def power(rate_real, rate_imag, offset):
    size = jnp.exp(rate_real * offset)
    cosine, sine = cos_sin(rate_imag * offset)
    return size * cosine, size * sine


def times(left, right):
    return (
        left[0] * right[0] - left[1] * right[1],
        left[0] * right[1] + left[1] * right[0],
    )


def blocks_forward(x):
    root = math.sqrt(0.5)
    cosine, sine = math.cos(math.pi / 8), math.sin(math.pi / 8)
    total = [x[s] + x[s + 4] for s in range(4)]
    gap = [x[s] - x[s + 4] for s in range(4)]
    even, odd = total[0] + total[2], total[1] + total[3]
    real, imag = [None] * 9, [None] * 9
    real[0], real[8] = even + odd, even - odd
    imag[0] = imag[8] = jnp.zeros_like(even)
    real[4], imag[4] = total[0] - total[2], total[3] - total[1]
    less, more = root * (gap[1] - gap[3]), root * (gap[1] + gap[3])
    real[2], imag[2] = gap[0] + less, -gap[2] - more
    real[6], imag[6] = gap[0] - less, gap[2] - more
    less, more = root * (x[2] - x[6]), root * (x[2] + x[6])
    even1 = (x[0] + less, -x[4] - more)
    even3 = (x[0] - less, x[4] - more)
    p, q, r, t = x[1] - x[7], x[3] - x[5], x[1] + x[7], x[3] + x[5]
    odd1 = (cosine * p + sine * q, -sine * r - cosine * t)
    odd3 = (sine * p - cosine * q, sine * t - cosine * r)
    real[1], imag[1] = even1[0] + odd1[0], even1[1] + odd1[1]
    real[7], imag[7] = even1[0] - odd1[0], odd1[1] - even1[1]
    real[3], imag[3] = even3[0] + odd3[0], even3[1] + odd3[1]
    real[5], imag[5] = even3[0] - odd3[0], odd3[1] - even3[1]
    return list(zip(real, imag))


def blocks_back(z):
    root = math.sqrt(0.5)
    cosine, sine = math.cos(math.pi / 8), math.sin(math.pi / 8)
    real, imag = [v[0] for v in z], [v[1] for v in z]
    even, odd = real[0] + real[8], real[0] - real[8]
    total = [even + real[4], odd + imag[4], even - real[4], odd - imag[4]]
    less, more = root * (real[2] - real[6]), root * (imag[2] + imag[6])
    gap = [real[2] + real[6], less + more, imag[2] - imag[6], more - less]
    x = [total[s] + gap[s] for s in range(4)] + [total[s] - gap[s] for s in range(4)]
    even1 = (real[1] + real[7], imag[7] - imag[1])
    even3 = (real[3] + real[5], imag[5] - imag[3])
    odd1 = (real[1] - real[7], imag[1] + imag[7])
    odd3 = (real[3] - real[5], imag[3] + imag[5])
    less, more = root * (even1[0] - even3[0]), root * (even1[1] + even3[1])
    p = cosine * odd1[0] + sine * odd3[0]
    q = sine * odd1[0] - cosine * odd3[0]
    r = sine * odd1[1] + cosine * odd3[1]
    t = cosine * odd1[1] - sine * odd3[1]
    extra = [
        even1[0] + even3[0],
        p + r,
        less - more,
        q + t,
        even3[1] - even1[1],
        t - q,
        -less - more,
        r - p,
    ]
    return [v + w for v, w in zip(x, extra)]


def transform_tables(owners, length, norm_scale):
    width = 2 * owners
    counter = np.arange(length)
    angles = two_pi * (counter[:, None] * counter[None, :] % length) / length
    cosine, sine = np.cos(angles), np.sin(angles)
    matrix = np.block([[cosine, -sine], [sine, cosine]]).astype(np.float32)
    high = matrix.astype(jnp.bfloat16)
    low = (matrix - high.astype(np.float32)).astype(jnp.bfloat16)
    outer = np.arange(owners + 1)
    angles = two_pi * (outer[:, None] * counter[None, :]) / (width * length)
    twiddle = np.stack([np.cos(angles), -np.sin(angles)], axis=1)
    weight = np.where(outer % owners == 0, 1.0, 2.0) * norm_scale / (width * length)
    twiddle = np.concatenate([twiddle, twiddle * weight[:, None, None]], axis=1)
    return np.stack([high, low]), twiddle.astype(np.float32)


def three_pieces(value):
    pieces = []
    for _ in range(3):
        piece = value.astype(jnp.bfloat16).astype(jnp.float32)
        pieces.append(piece)
        value = value - piece
    return pieces


def swap(value):
    return pltpu.roll(value, LANES // 2, 1)


def rest_lanes(lane):
    return lane < 3, (lane >= LANES // 2) & (lane < LANES // 2 + 3)


def rest_steps(value):
    high = value.astype(jnp.bfloat16).astype(jnp.float32)
    steps = jnp.where(high == 0.0, 0.0, (value - high) / jnp.where(high == 0.0, 1.0, high))
    return jnp.floor(steps * (256.0 * REST_STEPS) + 0.5)


def unpack_rests(high, rest):
    lane = lax.broadcasted_iota(jnp.int32, high.shape, 1)
    shared, replaced = rest_lanes(lane)
    step = sum(rest[:, LANES // 2 + i : LANES // 2 + i + 1] for i in range(3))
    both = jnp.where(shared, rest, swap(rest))
    first = jnp.floor(both * (1.0 / (2.0 * REST_STEPS + 1.0)) + 0.5)
    second = both - first * (2.0 * REST_STEPS + 1.0)
    steps = jnp.where(shared, first, second) * (1.0 / (256.0 * REST_STEPS))
    return jnp.where(shared | replaced, high * steps, rest), jnp.broadcast_to(step, high.shape)


def transposed(value):
    return jnp.concatenate(
        [value[:, spot : spot + LANES].T for spot in range(0, value.shape[1], LANES)], axis=0
    )


READ, REST, OUT_ROWS = 16, 17, 18
REST_STEPS = 7.0
ROWS = 20
LAGS, GRADS, STATE, SINGLES = 0, 8, 16, 18
STEP_LANES, SCALE_LANES = (0, 8), (16, 17, 18, 19)
SPARE = 15.0
PARTS = 3
EARLY = 9
FRESH = 5


def pack_kernel(inputs, out_grad, readout, log_step, *refs):
    count = (len(refs) - 7) // 2
    sources, (out, *held) = refs[:count], refs[count : 2 * count + 1]
    signals, read, step, turned, rows, sems = refs[2 * count + 1 :]
    peers = out.shape[0] // OUT_ROWS
    copies = [
        pltpu.make_async_copy(source, target, sems.at[i])
        for i, (source, target) in enumerate(
            (
                (readout, read),
                (log_step, step),
                (inputs, signals.at[0]),
                (out_grad, signals.at[1]),
                *zip(sources, held),
            )
        )
    ]
    for copy in copies:
        copy.start()
    for copy in copies[:4]:
        copy.wait()
    own = lax.axis_index("seq")
    turned[...] = transposed(read[...])
    channels = step.shape[1]
    peer = lax.broadcasted_iota(jnp.int32, (peers, channels), 0)
    channel = lax.broadcasted_iota(jnp.int32, (peers, channels), 1)
    sent_channel = channel == peer * SUBLANES + own

    def pick(row):
        value = jnp.sum(jnp.where(sent_channel, row, 0.0), axis=1, keepdims=True)
        return jnp.broadcast_to(value, (peers, LANES))

    half = LANES // 2
    shared = rest_steps(read[0:SUBLANES]) * (2.0 * REST_STEPS + 1.0)
    shared = shared + rest_steps(read[half : half + SUBLANES])
    pieces = three_pieces(pick(step[...]))
    placed = [(i, pick(shared[i : i + 1])) for i in range(3)]
    placed += [(half + i, piece) for i, piece in enumerate(pieces)]
    for place, signal in enumerate((signals[0], signals[1])):
        value = signal.astype(jnp.float32)
        for peer in range(peers):
            spot = peer * OUT_ROWS + place * SUBLANES
            rows[spot : spot + SUBLANES] = value[peer * SUBLANES : (peer + 1) * SUBLANES]
    value = turned[pl.ds(own, peers, stride=SUBLANES), :]
    high = value.astype(jnp.bfloat16).astype(jnp.float32)
    rows[pl.ds(READ, peers, stride=OUT_ROWS), :] = high
    rest = value - high
    lane = lax.broadcasted_iota(jnp.int32, (peers, LANES), 1)
    for place, other in placed:
        rest = jnp.where(lane == place, other, rest)
    rows[pl.ds(REST, peers, stride=OUT_ROWS), :] = rest
    out[...] = rows[...].astype(jnp.bfloat16)
    for copy in copies[4:]:
        copy.wait()


def exponent_of(bound):
    return jnp.floor(jnp.log(jnp.maximum(bound, 1e-30)) * (1.0 / math.log(2.0))) + (2.0 - SPARE)


def greatest(value):
    return jnp.max(jnp.max(value, axis=1, keepdims=True), axis=0, keepdims=True)


def size_of(value):
    return jnp.abs(value[0]) + jnp.abs(value[1])


def two_pieces(value):
    high = value.astype(jnp.bfloat16).astype(jnp.float32)
    return high, (value - high) * 256.0


def main_kernel(
    owners,
    norm_scale,
    got,
    matrix,
    twiddle,
    decay_log,
    rotation,
    sent,
    rows_in,
    spectra,
    freq,
    back,
    params,
    doubled,
    bases,
    powers,
    early_powers,
    lags,
    sums,
):
    peers, length = got.shape[0] // OUT_ROWS, got.shape[1]
    groups = peers // owners
    part_count = groups * SUBLANES
    rows = 2 * part_count
    pairs = part_count // 2
    half = pairs // SUBLANES
    reach = length // 2
    lane = lax.broadcasted_iota(jnp.int32, (pairs, LANES), 1)
    left = lane < LANES // 2
    row = lax.broadcasted_iota(jnp.int32, (SUBLANES, LANES), 0)

    def lanes_of(side):
        return slice(side * LANES, (side + 1) * LANES)

    def collect(spot):
        tiles = [
            rows_in[pl.ds(group * owners * OUT_ROWS + spot, owners, stride=OUT_ROWS), :]
            for group in range(groups)
        ]
        return jnp.concatenate(tiles[:half], axis=0), jnp.concatenate(tiles[half:], axis=0)

    def make_params():
        sides = []
        for high, rest in zip(collect(READ), collect(REST)):
            rest, step = unpack_rests(high, rest)
            sides.append((high + rest, step))
        (lower, lower_step), (upper, upper_step) = sides
        read = (jnp.where(left, lower, swap(upper)), jnp.where(left, swap(lower), upper))
        step = jnp.exp(jnp.where(left, lower_step, upper_step))
        decay_row = jnp.concatenate([decay_log[...], decay_log[...]], axis=1)
        rotation_row = jnp.concatenate([rotation[...], rotation[...]], axis=1)
        pole = (
            jnp.broadcast_to(-jnp.exp(decay_row), step.shape),
            jnp.broadcast_to(rotation_row, step.shape),
        )
        rate = (step * pole[0], step * pole[1])
        place, size = 0, 1
        while size < owners * length:
            if place // 2 % FRESH == 0:
                value = power(rate[0], rate[1], float(size))
            else:
                value = (value[0] * value[0] - value[1] * value[1], 2.0 * value[0] * value[1])
            doubled[place], doubled[place + 1] = value
            place, size = place + 2, size * 2
        sine = cos_sin(0.5 * rate[1])[1]
        cosine = 1.0 - 2.0 * sine * sine
        lift = (grow(rate[0]) * cosine - 2.0 * sine * sine, doubled[1])
        norm = 1.0 / (pole[0] * pole[0] + pole[1] * pole[1])
        inverse = (pole[0] * norm, -pole[1] * norm)
        ratio = times(lift, inverse)
        coef = times(read, ratio)
        lifted = times((doubled[0], doubled[1]), inverse)
        values = (rate, ratio, coef, times(read, lifted), pole, times(coef, inverse), (step, step))
        for place, value in enumerate(values):
            params[2 * place], params[2 * place + 1] = value

    early = min(EARLY, pairs)
    products = 4 * early * reach
    nothing = twiddle[0, 1, 0].astype(jnp.int32) * (2 * SUBLANES)
    block_bit, reach_bit = length.bit_length() - 1, reach.bit_length() - 1
    bits = [(row & (1 << i)) != 0 for i in range(SUBLANES.bit_length() - 1)]

    def doubled_row(p, i):
        return doubled[2 * i, p : p + 1, :], doubled[2 * i + 1, p : p + 1, :]

    def by_rows(p, first):
        out = None
        for i, bit in enumerate(bits):
            real, imag = doubled_row(p, first + i)
            value = (jnp.where(bit, real, 1.0), jnp.where(bit, imag, 0.0))
            out = value if out is None else times(out, value)
        return out

    def make_tables():
        for p in range(pairs):
            table = [by_rows(p, 0)]
            for i in range(len(bits), reach_bit):
                table += [times(block, doubled_row(p, i)) for block in table]
            for place in range(0, len(table), 2):
                for side in range(2):
                    value = jnp.concatenate([table[place][side], table[place + 1][side]], axis=0)
                    for i, piece in enumerate(split_halves(value)):
                        for spot in (2 * i * reach, (2 * i + 1) * reach):
                            spot += p * 4 * reach + place * SUBLANES
                            if p < early:
                                rows_at = pl.multiple_of(nothing + spot, 2 * SUBLANES)
                                early_powers[pl.ds(rows_at, 2 * SUBLANES), lanes_of(side)] = piece
                            else:
                                powers[spot : spot + 2 * SUBLANES, lanes_of(side)] = piece
            base = by_rows(p, block_bit)
            bases[p, 0], bases[p, 1] = base
            bases[p, 2], bases[p, 3] = times(base, doubled_row(p, reach_bit))

    def transform(pieces, target, count):
        dot = functools.partial(jnp.dot, preferred_element_type=jnp.float32)
        cuts = [(owners + 1) * i // PARTS * count for i in range(PARTS + 1)]
        for part in map(slice, cuts, cuts[1:]):
            high, low = pieces(part)
            target[part] = dot(high, matrix[0]) + dot(low, matrix[0]) + dot(high, matrix[1])

    def spread_blocks():
        rows_in[...] = got[...].astype(jnp.float32)
        blocks = []
        for s in range(owners):
            spots = [(group * owners + s) * OUT_ROWS for group in range(groups)]
            blocks.append(
                jnp.concatenate(
                    [rows_in[spot : spot + SUBLANES] for spot in spots]
                    + [rows_in[spot + SUBLANES : spot + 2 * SUBLANES] for spot in spots],
                    axis=0,
                )
            )
        for k, value in enumerate(blocks_forward(blocks)):
            if k:
                value = times(value, (twiddle[k, 0:1], twiddle[k, 1:2]))
            for side in range(2):
                for i, piece in enumerate(split_halves(value[side])):
                    spectra[i, k * rows : (k + 1) * rows, lanes_of(side)] = piece

    def to_frequencies():
        transform(lambda part: (spectra[0, part], spectra[1, part]), freq, rows)
        make_params()
        make_tables()

    def to_lags():
        for k in range(owners + 1):
            at_in = freq[k * rows : k * rows + part_count]
            at_out = freq[k * rows + part_count : (k + 1) * rows]
            ur, ui = at_in[:, :length], at_in[:, length:]
            gr, gi = at_out[:, :length], at_out[:, length:]
            for side, value in enumerate((gr * ur + gi * ui, gr * ui - gi * ur)):
                for i, piece in enumerate(split_halves(value)):
                    spot = products + (i * (owners + 1) + k) * part_count
                    early_powers[spot : spot + part_count, lanes_of(side)] = piece

        def pieces(part):
            low = products + (owners + 1) * part_count
            return tuple(
                early_powers[first + part.start : first + part.stop] for first in (products, low)
            )

        transform(pieces, back, part_count)

    def finish():
        turned = []
        for k in range(owners + 1):
            spots = slice(k * part_count, (k + 1) * part_count)
            value = (back[spots, lanes_of(0)], back[spots, lanes_of(1)])
            turned.append(times(value, (twiddle[k, 2:3], twiddle[k, 3:4])))
        blocks = blocks_back(turned)

        most = jnp.zeros((part_count, LANES), jnp.float32)
        for b, block in enumerate(blocks):
            most = jnp.maximum(most, jnp.abs(block))

        for group in range(groups):
            spots = slice(group * SUBLANES, (group + 1) * SUBLANES)
            tiles = jnp.stack([block[spots] for block in blocks])
            lags[group * owners * SUBLANES : (group + 1) * owners * SUBLANES] = jnp.swapaxes(
                tiles, 0, 1
            ).reshape(owners * SUBLANES, length)

        def param(place):
            return params[2 * place], params[2 * place + 1]

        rate, ratio, coef, through, pole, direct, (step, _) = (param(i) for i in range(7))
        most = greatest(most)
        whole = 2.0 * math.sqrt(owners * length)
        on_rate = size_of(coef) * float(owners * length) + size_of(through)
        on_pole = step * on_rate + size_of(direct)
        lag_exponent = exponent_of(most)
        grad_exponent = exponent_of(most * (whole * greatest(size_of(ratio))))
        state_exponent = exponent_of(
            most * (whole * part_count * greatest(on_pole * (1.0 - pole[0])))
        )
        step_exponent = exponent_of(
            most * (whole * (LANES // 2) * greatest(on_rate * size_of(rate)))
        )
        lag_scale = jnp.exp2(-lag_exponent)
        for b, block in enumerate(blocks):
            for group in range(groups):
                place = (group * owners + b) * ROWS
                value = block[group * SUBLANES : (group + 1) * SUBLANES]
                sent[place + LAGS : place + GRADS] = value * lag_scale

        start = row.astype(jnp.float32) * float(length)
        first = left[:owners]
        wide = lax.broadcasted_iota(jnp.int32, (4 * owners, LANES), 1)
        wide_left = wide < reach
        offset = jnp.where(wide_left, wide, wide - reach).astype(jnp.float32)
        both_left = wide_left[: 2 * owners]
        for p in range(pairs):
            both = jnp.concatenate(
                [
                    lags[channel * owners : (channel + 1) * owners]
                    for channel in (p, pairs + p)
                ],
                axis=0,
            )
            swapped = swap(both)
            plain = jnp.concatenate(
                [jnp.where(both_left, both, swapped), jnp.where(both_left, swapped, both)], axis=0
            )
            factor = []
            for value in (plain, plain * offset):
                high = value.astype(jnp.bfloat16).astype(jnp.float32)
                factor.append(jnp.where(wide_left, high, value - high))
            factor = jnp.concatenate(factor, axis=0).astype(jnp.bfloat16)
            raw = jnp.dot(
                jnp.concatenate([factor, factor], axis=1),
                (early_powers if p < early else powers)[p * 4 * reach : (p + 1) * 4 * reach],
                preferred_element_type=jnp.float32,
            )

            def pick(place, side):
                top = raw[2 * place * owners : (2 * place + 1) * owners, lanes_of(side)]
                bottom = raw[(2 * place + 1) * owners : (2 * place + 2) * owners, lanes_of(side)]
                return jnp.where(first, top, bottom)

            found = None
            for part in range(2):
                base = (bases[p, 2 * part], bases[p, 2 * part + 1])
                near = start + float(part * reach)
                value = (pick(part, 0), pick(part, 1))
                lagged = (near * value[0] + pick(2 + part, 0), near * value[1] + pick(2 + part, 1))
                terms = times(base, value) + times(base, lagged)
                found = terms if found is None else [x + y for x, y in zip(found, terms)]
            for place, value in enumerate(found):
                sums[place, p : p + 1] = jnp.sum(value, axis=0, keepdims=True)

        total = (sums[0] * (2.0 * norm_scale), sums[1] * (2.0 * norm_scale))
        lag_total = (sums[2] * (2.0 * norm_scale), sums[3] * (2.0 * norm_scale))
        on_read = times(total, ratio)
        on_read = (on_read[0], -on_read[1])
        on_rate = times(coef, lag_total)
        more = times(total, through)
        on_rate = (on_rate[0] + more[0], on_rate[1] + more[1])
        less = times(total, direct)
        on_pole = (step * on_rate[0] - less[0], step * on_rate[1] - less[1])
        on_step = times(on_rate, rate)[0]
        on_decay = jnp.sum(on_pole[0] * pole[0], axis=0, keepdims=True)
        on_rotation = -jnp.sum(on_pole[1], axis=0, keepdims=True)
        on_decay = on_decay + swap(on_decay)
        on_rotation = on_rotation + swap(on_rotation)
        state = jnp.where(left[0:1], on_decay, on_rotation) * jnp.exp2(-state_exponent)

        grad_scale = jnp.exp2(-grad_exponent)
        on_read = (on_read[0] * grad_scale, on_read[1] * grad_scale)
        lower = jnp.where(left, on_read[0], swap(on_read[1]))
        upper = jnp.where(left, swap(on_read[0]), on_read[1])
        grads = jnp.concatenate([lower, upper], axis=0)
        step_scale = jnp.broadcast_to(jnp.exp2(-step_exponent), (pairs, LANES))
        step_columns = [
            jnp.broadcast_to(jnp.sum(value, axis=1, keepdims=True), (pairs, LANES)) * step_scale
            for value in (jnp.where(left, on_step, 0.0), jnp.where(left, 0.0, on_step))
        ]
        place_lane = lax.broadcasted_iota(jnp.int32, (SUBLANES, LANES), 1)
        scales = jnp.zeros((1, LANES), jnp.float32)
        for spot, value in zip(
            SCALE_LANES, (lag_exponent, grad_exponent, state_exponent, step_exponent)
        ):
            scales = jnp.where(place_lane[0:1] == spot, value, scales)
        state_high, state_low = two_pieces(state)
        tails = []
        for group in range(groups):
            spot = group % half * SUBLANES
            pieces = two_pieces(step_columns[group // half][spot : spot + SUBLANES])
            spread = jnp.zeros((SUBLANES, LANES), jnp.float32)
            for spot, piece in zip(STEP_LANES, pieces):
                spread = jnp.where(place_lane == row + spot, piece, spread)
            singles = scales + jnp.sum(spread, axis=0, keepdims=True)
            tails.append(jnp.concatenate([state_high, state_low, singles, singles], axis=0))
        for b in range(owners):
            for group in range(groups):
                place = (group * owners + b) * ROWS
                sent[place + GRADS : place + STATE] = grads[
                    group * SUBLANES : (group + 1) * SUBLANES
                ]
                sent[place + STATE : place + ROWS] = tails[group]

    for section in (spread_blocks, to_frequencies, to_lags, finish):
        section()


def unpack_kernel(got, kernel_grad, readout_grad, step_grad, state_grad, wide, grads):
    peers = got.shape[0] // ROWS
    per_row = LANES // SUBLANES
    singles = got[pl.ds(SINGLES, peers, stride=ROWS), :]
    exponents = [jnp.broadcast_to(singles[:, spot : spot + 1], (peers, LANES)) for spot in SCALE_LANES]
    scales = [jnp.exp2(value) for value in exponents]
    wide[...] = scales[0]
    lane = lax.broadcasted_iota(jnp.int32, (peers, LANES), 1)
    row = lax.broadcasted_iota(jnp.int32, (peers, LANES), 0)

    def by_channel(value, spot):
        mine = jnp.where(row - spot == lane // SUBLANES, value, 0.0)
        return jnp.sum(mine, axis=0, keepdims=True)

    for spot in range(0, peers, per_row):
        part = slice(spot * SUBLANES, (spot + per_row) * SUBLANES)
        for peer in range(spot, spot + per_row):
            place, own = peer * ROWS, slice(peer * SUBLANES, (peer + 1) * SUBLANES)
            grads[own] = got[place + GRADS : place + STATE]
            kernel_grad[own] = got[place + LAGS : place + GRADS] * wide[peer : peer + 1, :]
        readout_grad[:, part] = grads[part].T * by_channel(scales[1], spot)

    high = got[pl.ds(STATE, peers, stride=ROWS), :]
    low = got[pl.ds(STATE + 1, peers, stride=ROWS), :]
    total = jnp.sum((high + low * (1.0 / 256.0)) * scales[2], axis=0, keepdims=True)
    states = state_grad.shape[1]
    state_grad[0:1] = total[:, :states]
    state_grad[1:2] = total[:, states:]
    high, low = (
        jnp.take_along_axis(singles, lane % SUBLANES + first, axis=1) for first in STEP_LANES
    )
    value = (high + low * (1.0 / 256.0)) * scales[3]
    for spot in range(0, peers, per_row):
        part = slice(spot * SUBLANES, (spot + per_row) * SUBLANES)
        step_grad[part] = by_channel(value, spot).reshape(LANES)


def kernel_device(inputs, out_grad, readout, log_step, decay_log, rotation):
    owners, groups = lax.axis_size("seq"), lax.axis_size("ch")
    peers = owners * groups
    channels, length = inputs.shape
    states = decay_log.shape[0]
    part_count = channels // owners
    pairs = part_count // 2
    norm_scale = 1.0 / math.sqrt(owners * length)
    vmem = pl.BlockSpec(memory_space=pltpu.VMEM)
    memory = pltpu.CompilerParams(vmem_limit_bytes=32 * 1024 * 1024)
    f32, bf16 = jnp.float32, jnp.bfloat16

    def exchange(value):
        rows = value.shape[0] // peers
        value = value.reshape(peers, rows // 2, 2, LANES)
        value = lax.all_to_all(value, ("ch", "seq"), split_axis=0, concat_axis=0, tiled=True)
        return value.reshape(peers * rows, LANES)

    anywhere = pl.BlockSpec(memory_space=pl.ANY)
    held = [jnp.asarray(table) for table in transform_tables(owners, length, norm_scale)]
    held += [decay_log[None], rotation[None]]
    sources = (
        inputs, out_grad, readout.transpose(0, 2, 1).reshape(LANES, channels), log_step[None], *held
    )
    pieces, *held = pl.pallas_call(
        pack_kernel,
        out_shape=[jax.ShapeDtypeStruct((peers * OUT_ROWS, LANES), bf16)]
        + [jax.ShapeDtypeStruct(value.shape, value.dtype) for value in held],
        in_specs=[anywhere] * len(sources),
        out_specs=[vmem] * (1 + len(held)),
        scratch_shapes=[
            pltpu.VMEM((2, channels, LANES), bf16),
            pltpu.VMEM((LANES, channels), f32),
            pltpu.VMEM((1, channels), f32),
            pltpu.VMEM((channels, LANES), f32),
            pltpu.VMEM((peers * OUT_ROWS, LANES), f32),
            pltpu.SemaphoreType.DMA((len(sources),)),
        ],
        compiler_params=memory,
    )(*(pltpu.with_memory_space_constraint(value, pltpu.HBM) for value in sources))
    got = exchange(pieces)
    sent = pl.pallas_call(
        functools.partial(main_kernel, owners, norm_scale),
        out_shape=jax.ShapeDtypeStruct((peers * ROWS, LANES), f32),
        in_specs=[vmem] * 5,
        out_specs=vmem,
        scratch_shapes=[
            pltpu.VMEM((peers * OUT_ROWS, LANES), f32),
            pltpu.VMEM((2, (owners + 1) * 2 * part_count, 2 * LANES), bf16),
            pltpu.VMEM(((owners + 1) * 2 * part_count, 2 * LANES), f32),
            pltpu.VMEM(((owners + 1) * part_count, 2 * LANES), f32),
            pltpu.VMEM((14, pairs, LANES), f32),
            pltpu.VMEM((2 * (owners * length).bit_length(), pairs, LANES), f32),
            pltpu.VMEM((pairs, 4, owners, LANES), f32),
            pltpu.VMEM((2 * pairs * length, 2 * LANES), bf16),
            pltpu.VMEM((2 * pairs * length + 2 * (owners + 1) * part_count, 2 * LANES), bf16),
            pltpu.VMEM((owners * part_count, length), f32),
            pltpu.VMEM((4, pairs, LANES), f32),
        ],
        compiler_params=memory,
    )(got, *held)
    back = exchange(sent.astype(jnp.float16))
    kernel_grad, readout_grad, step_grad, state_grad = pl.pallas_call(
        unpack_kernel,
        out_shape=[
            jax.ShapeDtypeStruct((channels, length), f32),
            jax.ShapeDtypeStruct((LANES, channels), f32),
            jax.ShapeDtypeStruct((channels,), f32),
            jax.ShapeDtypeStruct((2, states), f32),
        ],
        in_specs=[vmem],
        out_specs=[vmem] * 4,
        scratch_shapes=[
            pltpu.VMEM((peers, LANES), f32),
            pltpu.VMEM((channels, LANES), f32),
        ],
        compiler_params=memory,
    )(back.astype(f32))
    readout_grad = readout_grad.reshape(2, states, channels).transpose(0, 2, 1)
    return kernel_grad, readout_grad, step_grad, state_grad


def kernel_fits(mesh, inputs, decay_log):
    owners, groups = mesh.shape["seq"], mesh.shape["ch"]
    channels = inputs.shape[0] // groups
    return (
        inputs.shape[1] == owners * LANES
        and 2 * decay_log.shape[0] == LANES
        and owners == SUBLANES
        and groups % 2 == 0
        and channels == owners * groups * SUBLANES
        and channels % LANES == 0
    )


def solution(mesh):
    def whole(inputs, out_grad, readout, log_step, decay_log, rotation):
        fits = kernel_fits(mesh, inputs, decay_log)
        return jax.shard_map(
            kernel_device if fits else general_device,
            mesh=mesh,
            in_specs=(P("ch", "seq"), P("ch", "seq"), P(None, "ch", None), P("ch"), P(), P()),
            out_specs=(P("ch", "seq"), P(None, "ch", None), P("ch"), P()),
            check_vma=False,
        )(inputs, out_grad, readout, log_step, decay_log, rotation)

    return whole
```
